32 devices in a mesh: sec: 4 (over z), depth: 4 (over y, x), segment: 2 (over core).
Axes of the slice: x: 2, y: 2, z: 4, core: 2. Of those that a mesh axis runs over, the one named last changes fastest.
Arguments:
- fields: float32 [2, 9, 8, 64, 128], P('segment', None, 'sec', 'depth'), may hold values from -6 to 6
- block_ids: int32 [2, 8, 64, 128], P('segment', 'sec', 'depth'), may hold values from 0 to 15
- buoyancy: float32 [16], replicated, may hold values from 0.5 to 1
- lame_lambda: float32 [16], replicated, may hold values from 0.2 to 0.6
- lame_mu: float32 [16], replicated, may hold values from 0.1 to 0.3
- moments: float32 [6, 16384], P(None, ('sec', 'depth')), may hold values from -12 to 12
- moment_owner: int32 [16384, 1], P(('sec', 'depth')), may hold values from 0 to 3; in each aligned block of 1024 rows (0 to 1023, 1024 to 2047, ...) at most 512 rows name the same one
- moment_cells: int32 [16384], P(('sec', 'depth')), may hold values from 0 to 4095
- drm_rows: int32 [32768], P(('sec', 'depth')), may hold values from 0 to 4095
Outputs:
- final_fields: float32 [2, 9, 8, 64, 128], P('segment', None, 'sec', 'depth')
The draws below stay inside these ranges and needn't reach their ends.
Inputs may be any that keep to these rules, and one draw needn't show every extreme that they name: `moment_owner`: in the entries of one section and slab at most 512 name the same section, a bound that some block reaches of them.
All inputs are finite; a program needn't handle non-finite values.
Results may differ from the reference program's by a relative error of at most 0.00002.
Values sent between devices are 32-bit elements; how exact they have to be, the bound alone decides.
No kernel may reach another device: no remote copies, remote signals or barrier semaphores. Data moves between devices by JAX's collectives and lax.ppermute only.
A program may use at most 64 MiB of HBM per device.

```python
import math
import jax
import jax.numpy as jnp
import numpy as np
from jax import lax

CX = 2
CZ = 16
CY = 128
STEPS = 4
NBLK = 16
ENT = 1024
R = 2048
CAP = 512
CELLS = 4096
NX = 8
NZ = 64
ENTS = 16384
ROWS = 32768
N_SEC = 4
N_DEPTH = 4


def with_ends(array, rng, low, top_value):
    spot = [jax.random.randint(jax.random.fold_in(rng, axis), (), 0, length) for axis, length in enumerate(array.shape)]
    longest = array.shape.index(max(array.shape))
    neighbour = spot[:longest] + [(spot[longest] + 1) % array.shape[longest]] + spot[longest + 1:]
    return array.at[tuple(spot)].set(low).at[tuple(neighbour)].set(top_value)


def levels(key, shape, shards, smallest, high):
    gain, own = 1.0, jax.random.fold_in(key, 6)
    for position, shards_of in shards:
        draws = jnp.exp(jax.random.uniform(jax.random.fold_in(own, position), (shards_of,), jnp.float32, smallest / len(shards), high / len(shards)))
        gain = gain * jnp.repeat(draws, shape[position] // shards_of).reshape([-1 if axis == position else 1 for axis in range(len(shape))])
    return gain


def shared_out(rng, own, number, rows, number_of, top, limit, slope):
    sequence = jax.random.permutation(rng, number_of)
    crowded, usual = load_shares(number_of, rows * top, limit, slope, True), load_shares(number_of, rows * top, limit, slope, False)
    places = jnp.arange(number_of)

    def named(tallies, offset_by):
        used = int((tallies > 0).sum())
        fixed = max(1, used // 4)
        passed = fixed + (places - fixed + offset_by * (used - fixed)) % max(1, number_of - fixed)
        return jnp.zeros((number_of,), jnp.int32).at[sequence[jnp.where(places < fixed, places, passed)]].set(jnp.asarray(tallies, jnp.int32))

    tallies = jnp.where(number % 4 == 0, named(crowded, number // 4), named(usual, number - number // 4 - 1))
    mixed = jax.random.permutation(jax.random.fold_in(own, 3), number_of)
    donor, sink = mixed[0:number_of // 2 * 2:2], mixed[1:number_of // 2 * 2:2]
    room = jnp.minimum(tallies[donor] - 1, limit - tallies[sink]) // 2
    room = jnp.where((donor == sequence[0]) | (sink == sequence[0]) | (tallies[sink] == 0), 0, jnp.maximum(room, 0))
    passed = jax.random.randint(jax.random.fold_in(own, 4), (number_of // 2,), 0, 1 << 20) % (room + 1)
    tallies = tallies.at[donor].add(-passed).at[sink].add(passed)
    members = jnp.searchsorted(jnp.cumsum(tallies), jnp.arange(rows * top), side="right").astype(jnp.int32)
    listing = members.reshape(top, rows).T
    listing = listing[jax.random.permutation(jax.random.fold_in(own, 1), rows)]
    offset_by = jax.random.randint(jax.random.fold_in(own, 2), (rows, 1), 0, top)
    return jnp.take_along_axis(listing, (jnp.arange(top)[None, :] + offset_by) % top, axis=1)


def load_shares(count, total, most, slope, full):
    weights = [(1 << 20) // math.isqrt(standing ** slope) + 1 for standing in range(1, count + 1)]
    largest = most if full else min(most, max(-(-total // count), total * weights[0] // sum(weights)))
    least = 1 if total - largest >= count - 1 else 0
    given, surplus = [largest] + [least] * (count - 1), total - largest - least * (count - 1)
    while surplus > 0:
        candidates = [i for i in range(1, count) if given[i] < largest] or [i for i in range(1, count) if given[i] < most]
        mass, left = sum([weights[i] for i in candidates]), surplus
        for i in candidates:
            extra = min(most - given[i], max(1, left * weights[i] // mass), surplus)
            given[i] = given[i] + extra
            surplus = surplus - extra
    return np.array(given)


def noise(rng, dims, scale, limit, cuts=(), kind=jnp.bfloat16):
    values = jax.random.normal(rng, dims, jnp.float32) * scale
    if len(cuts) > 0:
        values = levels(rng, dims, cuts, -0.22, 0.18) * values
    return jnp.clip(values, min=-limit, max=limit).astype(kind)


def setup_inputs(seed: int = 0) -> dict:
    key_list = jax.random.split(jax.random.key(seed), 10)
    fields = noise(key_list[0], (2, 9, NX, NZ, CY), 1.0, 6.0, ((0, 2), (2, 4), (3, 4)), jnp.float32)
    block_ids = with_ends(jax.random.randint(key_list[1], (2, NX, NZ, CY), 0, NBLK), jax.random.fold_in(key_list[1], 1), 0, NBLK - 1).astype(jnp.int32)
    buoyancy = jnp.clip(jnp.exp(jax.random.uniform(key_list[2], (NBLK,), jnp.float32, math.log(0.5), math.log(1.0))), 0.5, 1.0)
    lame_lambda = jnp.clip(jax.random.uniform(key_list[3], (NBLK,), jnp.float32, 0.2, 0.6), 0.2, 0.6)
    lame_mu = jnp.clip(jax.random.uniform(key_list[4], (NBLK,), jnp.float32, 0.1, 0.3), 0.1, 0.3)
    moments = noise(key_list[5], (6, ENTS), 2.0, 12.0, ((1, 16),), jnp.float32)
    moment_owner_keys = jax.random.split(jax.random.fold_in(key_list[6], 1), ENTS // ENT)
    moment_owner_turns = jax.random.permutation(jax.random.fold_in(key_list[6], 3), ENTS // ENT)
    moment_owner = jax.vmap(lambda own, number: shared_out(jax.random.fold_in(key_list[6], 2), own, number, ENT, N_SEC, 1, CAP, 2))(moment_owner_keys, moment_owner_turns).reshape((ENTS, 1))
    moment_cells = with_ends(jax.random.randint(key_list[7], (ENTS,), 0, CELLS), jax.random.fold_in(key_list[7], 1), 0, CELLS - 1).astype(jnp.int32)
    drm_rows = with_ends(jax.random.randint(key_list[8], (ROWS,), 0, CELLS), jax.random.fold_in(key_list[8], 1), 0, CELLS - 1).astype(jnp.int32)
    return {"fields": fields, "block_ids": block_ids, "buoyancy": buoyancy, "lame_lambda": lame_lambda, "lame_mu": lame_mu, "moments": moments, "moment_owner": moment_owner, "moment_cells": moment_cells, "drm_rows": drm_rows}


HALF_STEP = 0.5


def lookup(block_ids, table):
    result = jnp.zeros(block_ids.shape, jnp.float32)
    for entry in range(table.shape[0]):
        result = result + jnp.where(block_ids == entry, table[entry], jnp.float32(0.0))
    return result


def back_diff(field, axis):
    count = field.shape[axis]
    first = jnp.zeros_like(lax.slice_in_dim(field, 0, 1, axis=axis))
    before = jnp.concatenate([first, lax.slice_in_dim(field, 0, count - 1, axis=axis)], axis)
    return field - before


def fore_diff(field, axis):
    count = field.shape[axis]
    last = jnp.zeros_like(lax.slice_in_dim(field, 0, 1, axis=axis))
    after = jnp.concatenate([lax.slice_in_dim(field, 1, count, axis=axis), last], axis)
    return after - field


def reference(fields, block_ids, buoyancy, lame_lambda, lame_mu, moments, moment_owner, moment_cells, drm_rows):
    buoy = lookup(block_ids, buoyancy)
    lam = lookup(block_ids, lame_lambda)
    shear = lookup(block_ids, lame_mu)
    entries = jnp.arange(ENTS, dtype=jnp.int32)
    slab = (entries // ENT) % N_DEPTH
    gx = moment_owner[:, 0] * CX + moment_cells // (CZ * CY)
    gz = slab * CZ + (moment_cells // CY) % CZ
    gy = moment_cells % CY
    target = ((gx * NZ + gz) * CY + gy).astype(jnp.int32)
    stress = fields[0, 3:].reshape(6, -1).at[:, target].add(moments)
    state = fields.at[0, 3:].set(stress.reshape(6, NX, NZ, CY))
    rows = jnp.arange(ROWS, dtype=jnp.int32)
    owner_dev = rows // R
    rsec = owner_dev // N_DEPTH
    rslab = owner_dev % N_DEPTH
    rx = rsec * CX + drm_rows // (CZ * CY)
    rz = rslab * CZ + (drm_rows // CY) % CZ
    ry = drm_rows % CY
    boundary = ((rx * NZ + rz) * CY + ry).astype(jnp.int32)
    for step in range(STEPS):
        vx, vy, vz = state[:, 0], state[:, 1], state[:, 2]
        sxx, syy, szz, syz, sxz, sxy = (state[:, k] for k in range(3, 9))
        nvx = vx + HALF_STEP * buoy * (back_diff(sxx, 1) + back_diff(sxy, 3) + back_diff(sxz, 2))
        nvy = vy + HALF_STEP * buoy * (back_diff(sxy, 1) + back_diff(syy, 3) + back_diff(syz, 2))
        nvz = vz + HALF_STEP * buoy * (back_diff(sxz, 1) + back_diff(syz, 3) + back_diff(szz, 2))
        newv = jnp.stack([nvx, nvy, nvz], axis=1)
        oldv = state[:, :3]
        increment = (newv[0] - oldv[0]).reshape(3, -1)[:, boundary]
        basin = newv[1].reshape(3, -1).at[:, boundary].add(increment)
        newv = jnp.stack([newv[0], basin.reshape(3, NX, NZ, CY)], axis=0)
        vx, vy, vz = newv[:, 0], newv[:, 1], newv[:, 2]
        exx = fore_diff(vx, 1)
        eyy = fore_diff(vy, 3)
        ezz = fore_diff(vz, 2)
        trace = exx + eyy + ezz
        sxx = sxx + HALF_STEP * (lam * trace + 2.0 * shear * exx)
        syy = syy + HALF_STEP * (lam * trace + 2.0 * shear * eyy)
        szz = szz + HALF_STEP * (lam * trace + 2.0 * shear * ezz)
        syz = syz + HALF_STEP * shear * (fore_diff(vy, 2) + fore_diff(vz, 3))
        sxz = sxz + HALF_STEP * shear * (fore_diff(vx, 2) + fore_diff(vz, 1))
        sxy = sxy + HALF_STEP * shear * (fore_diff(vx, 3) + fore_diff(vy, 1))
        state = jnp.stack([vx, vy, vz, sxx, syy, szz, syz, sxz, sxy], axis=1)
    return state
```

```python
import functools

import jax
import jax.numpy as jnp
from jax import lax
from jax.experimental import pallas as pl
from jax.experimental.pallas import tpu as pltpu
from jax.sharding import PartitionSpec as P

STEPS = 4
MARGIN = 8
F32 = jnp.float32
BF16 = jnp.bfloat16
NT = (((1,), (1,)), ((), ()))


def one_hot(index, count):
    rows = lax.broadcasted_iota(jnp.int32, (count, index.shape[-1]), 0)
    return jnp.where(rows == index, F32(1.0), F32(0.0)).astype(BF16)


def split3(value):
    high = value.astype(BF16)
    rest = value - high.astype(F32)
    mid = rest.astype(BF16)
    low = (rest - mid.astype(F32)).astype(BF16)
    return high, mid, low


def pack_kernel(fields, ids, moments, cells, rows, payload, entries):
    cx, cz, cy = fields.shape[2:]
    payload[0:9] = fields[0]
    payload[9] = (ids[0] + 1).astype(F32)
    lines = [rows[i : i + 1, :] for i in range(rows.shape[0])]
    line = jnp.concatenate(lines, axis=1)
    high = one_hot(line // cy, cx * cz)
    low = one_hot(line % cy, cy)
    count = lax.dot_general(high, low, NT, preferred_element_type=F32)
    payload[10] = count.reshape(cx, cz, cy)
    entries[0:6] = moments[...]
    width = cells.shape[1]
    for i in range(cells.shape[0]):
        entries[6:7, i * width : (i + 1) * width] = cells[i : i + 1, :].astype(F32)
        entries[7:8, i * width : (i + 1) * width] = jnp.zeros((1, width), F32)


def moment_kernel(sizes, entries, window, acc):
    cx, cz, cy, reach, sections, slabs = sizes
    planes = window.shape[1]
    section = lax.axis_index("sec")
    slab = lax.axis_index("depth")
    first_plane = (section - reach) * cx
    window[...] = jnp.zeros_like(window)

    def gather(depth_index, first_row, row_count, at_row):
        acc[0 : 6 * planes * row_count, :] = jnp.zeros((6 * planes * row_count, cy), F32)

        @pl.loop(0, sections)
        def _(source):
            block = entries[source * slabs + depth_index]
            cell = block[6:7, :].astype(jnp.int32)
            row = cell // cy
            z = row % cz - first_row
            plane = row // cz - first_plane
            inside = (z >= 0) & (z < row_count)
            place = jnp.where(inside, plane * row_count + z, -1)
            high = one_hot(place, planes * row_count)
            low = one_hot(cell % cy, cy)
            parts = split3(block[0:6, :])
            for comp in range(6):
                total = jnp.zeros((planes * row_count, cy), F32)
                for part in parts:
                    total = total + lax.dot_general(
                        high * part[comp : comp + 1, :], low, NT, preferred_element_type=F32
                    )
                span = slice(comp * planes * row_count, (comp + 1) * planes * row_count)
                acc[span, :] = acc[span, :] + total

        for comp in range(6):
            span = slice(comp * planes * row_count, (comp + 1) * planes * row_count)
            window[comp, :, at_row : at_row + row_count, :] = acc[span, :].reshape(
                planes, row_count, cy
            )

    gather(slab, 0, cz, MARGIN)

    @pl.when(slab > 0)
    def _():
        gather(slab - 1, cz - MARGIN, MARGIN, 0)

    @pl.when(slab < slabs - 1)
    def _():
        gather(slab + 1, 0, MARGIN, MARGIN + cz)


def step_kernel(sizes, gathered, window, buoyancy, lame_lambda, lame_mu, out, state, coef, sem):
    cx, cz, cy, reach, sections, slabs = sizes
    planes, rows = state.shape[2], state.shape[3]
    section = lax.axis_index("sec")
    slab = lax.axis_index("depth")
    segment = lax.axis_index("segment")
    state[...] = jnp.zeros_like(state)

    def pieces(act):
        for i in range(2 * reach + 1):
            source = section - reach + i
            for k, (first, count, at) in enumerate(
                ((cz - MARGIN, MARGIN, 0), (0, cz, MARGIN), (0, MARGIN, MARGIN + cz))
            ):
                depth = slab - 1 + k

                @pl.when((source >= 0) & (source < sections) & (depth >= 0) & (depth < slabs))
                def _():
                    for model in range(2):
                        device = (source * slabs + depth) * 2 + model
                        act(
                            pltpu.make_async_copy(
                                gathered.at[device, :, :, pl.ds(first, count), :],
                                state.at[model, :, pl.ds(i * cx, cx), pl.ds(at, count), :],
                                sem.at[i, k, model],
                            )
                        )

    pieces(lambda copy: copy.start())
    pieces(lambda copy: copy.wait())

    @pl.loop(0, planes)
    def _(x):
        for model in range(2):
            ids = state[model, 9, x]
            found = [jnp.zeros((rows, cy), F32)] * 3
            for entry in range(buoyancy.shape[0]):
                hit = ids == F32(entry + 1)
                found = [
                    jnp.where(hit, F32(0.5) * table[entry], value)
                    for table, value in zip((buoyancy, lame_lambda, lame_mu), found)
                ]
            for number in range(3):
                coef[model, number, x] = found[number]
        for comp in range(6):
            state[0, 3 + comp, x] = state[0, 3 + comp, x] + window[comp, x]

    lane = lax.broadcasted_iota(jnp.int32, (rows, cy), 1)
    first_lane, last_lane = lane == 0, lane == cy - 1

    def back_y(f):
        return f - jnp.where(first_lane, F32(0.0), pltpu.roll(f, 1, 1))

    def back_z(f):
        return f - pltpu.roll(f, 1, 0)

    def fore_y(f):
        return jnp.where(last_lane, F32(0.0), pltpu.roll(f, cy - 1, 1)) - f

    def fore_z(f):
        return pltpu.roll(f, rows - 1, 0) - f

    own = reach * cx
    for step in range(STEPS):
        left = STEPS - 1 - step
        low, high = own - left, own + cx + left

        @pl.loop(low, high + 1)
        def _(x):
            inc = [None, None]
            for model in range(2):
                sxx, syy, szz, syz, sxz, sxy = (state[model, 3 + k, x] for k in range(6))
                sxx_p, sxz_p, sxy_p = (state[model, k, x - 1] for k in (3, 7, 8))
                hb = coef[model, 0, x]
                inc[model] = (
                    hb * ((sxx - sxx_p) + back_y(sxy) + back_z(sxz)),
                    hb * ((sxy - sxy_p) + back_y(syy) + back_z(syz)),
                    hb * ((sxz - sxz_p) + back_y(syz) + back_z(szz)),
                )
            times = state[1, 10, x]
            for k in range(3):
                state[0, k, x] = state[0, k, x] + inc[0][k]
                state[1, k, x] = (state[1, k, x] + inc[1][k]) + times * inc[0][k]

        @pl.loop(low, high)
        def _(x):
            for model in range(2):
                vx, vy, vz = (state[model, k, x] for k in range(3))
                vx_n, vy_n, vz_n = (state[model, k, x + 1] for k in range(3))
                hl, hm = coef[model, 1, x], coef[model, 2, x]
                exx, eyy, ezz = vx_n - vx, fore_y(vy), fore_z(vz)
                pressure = hl * (exx + eyy + ezz)
                twice = hm + hm
                state[model, 3, x] = state[model, 3, x] + (pressure + twice * exx)
                state[model, 4, x] = state[model, 4, x] + (pressure + twice * eyy)
                state[model, 5, x] = state[model, 5, x] + (pressure + twice * ezz)
                state[model, 6, x] = state[model, 6, x] + hm * (fore_z(vy) + fore_y(vz))
                state[model, 7, x] = state[model, 7, x] + hm * (fore_z(vx) + (vz_n - vz))
                state[model, 8, x] = state[model, 8, x] + hm * (fore_y(vx) + (vy_n - vy))

    out[0] = state[segment, 0:9, own : own + cx, MARGIN : MARGIN + cz, :]


VMEM = pl.BlockSpec(memory_space=pltpu.VMEM)
SMEM = pl.BlockSpec(memory_space=pltpu.SMEM)
ANY = pl.BlockSpec(memory_space=pl.ANY)
LIMIT = pltpu.CompilerParams(vmem_limit_bytes=40 * 2**20)


def on_device(
    fields, block_ids, buoyancy, lame_lambda, lame_mu, moments, moment_owner, moment_cells, drm_rows
):
    sections, slabs = lax.axis_size("sec"), lax.axis_size("depth")
    cx, cz, cy = fields.shape[2:]
    cells_here = cx * cz * cy
    count = moment_cells.shape[0]
    reach = -(-STEPS // cx)
    planes, rows = (2 * reach + 1) * cx, cz + 2 * MARGIN
    sizes = (cx, cz, cy, reach, sections, slabs)
    cells = (moment_owner[:, 0] * cells_here + moment_cells).reshape(-1, cy)
    payload, entries = pl.pallas_call(
        pack_kernel,
        out_shape=(
            jax.ShapeDtypeStruct((11, cx, cz, cy), F32),
            jax.ShapeDtypeStruct((8, count), F32),
        ),
        in_specs=[VMEM] * 5,
        out_specs=(VMEM, VMEM),
        compiler_params=LIMIT,
        name="pack",
    )(fields, block_ids, moments, cells, drm_rows.reshape(-1, cy))
    all_entries = lax.all_gather(entries, ("sec", "depth"))
    gathered = lax.all_gather(payload, ("sec", "depth", "segment"))
    window = pl.pallas_call(
        functools.partial(moment_kernel, sizes),
        out_shape=jax.ShapeDtypeStruct((6, planes, rows, cy), F32),
        in_specs=[VMEM],
        out_specs=VMEM,
        scratch_shapes=[pltpu.VMEM((6 * planes * max(cz, MARGIN), cy), F32)],
        compiler_params=LIMIT,
        name="moments_in_window",
    )(all_entries)
    return pl.pallas_call(
        functools.partial(step_kernel, sizes),
        out_shape=jax.ShapeDtypeStruct(fields.shape, F32),
        in_specs=[ANY, VMEM, SMEM, SMEM, SMEM],
        out_specs=VMEM,
        scratch_shapes=[
            pltpu.VMEM((2, 11, planes, rows, cy), F32),
            pltpu.VMEM((2, 3, planes, rows, cy), F32),
            pltpu.SemaphoreType.DMA((2 * reach + 1, 3, 2)),
        ],
        compiler_params=LIMIT,
        name="steps",
    )(gathered, window, buoyancy, lame_lambda, lame_mu)


def solution(mesh):
    in_specs = (
        P("segment", None, "sec", "depth", None),
        P("segment", "sec", "depth", None),
        P(),
        P(),
        P(),
        P(None, ("sec", "depth")),
        P(("sec", "depth"), None),
        P(("sec", "depth")),
        P(("sec", "depth")),
    )
    out_specs = P("segment", None, "sec", "depth", None)
    return jax.shard_map(
        on_device, mesh=mesh, in_specs=in_specs, out_specs=out_specs, check_vma=False
    )
```

```python
import functools

import jax
import jax.numpy as jnp
from jax import lax
from jax.experimental import pallas as pl
from jax.experimental.pallas import tpu as pltpu
from jax.sharding import PartitionSpec as P

STEPS = 4
F32 = jnp.float32
BF16 = jnp.bfloat16
NT = (((1,), (1,)), ((), ()))


def one_hot(index, count):
    rows = lax.broadcasted_iota(jnp.int32, (count, index.shape[-1]), 0)
    return jnp.where(rows == index, F32(1.0), F32(0.0))


def split3(value):
    high = value.astype(BF16).astype(F32)
    rest = value - high
    mid = rest.astype(BF16).astype(F32)
    return high, mid, rest - mid


def copy_all(sem, pairs):
    copies = [pltpu.make_async_copy(a, b, sem.at[i]) for i, (a, b) in enumerate(pairs)]
    for copy in copies:
        copy.start()
    for copy in copies:
        copy.wait()


def in_line(rows):
    return jnp.concatenate([rows[i : i + 1, :] for i in range(rows.shape[0])], axis=1)


def aux_kernel(ids_in, moments_in, owner_in, cells_in, rows_in, aux, ids, moments, owner, cells, rows, sem):
    copy_all(
        sem,
        [(ids_in, ids), (moments_in, moments), (owner_in, owner), (cells_in, cells), (rows_in, rows)],
    )
    cx, cz, cy = ids.shape[1:]
    lines = cx * cz
    aux[0:lines] = (ids[0] + 1).astype(F32).reshape(lines, cy)
    line = in_line(rows[...])
    high = one_hot(line // cy, lines).astype(BF16)
    low = one_hot(line % cy, cy).astype(BF16)
    aux[lines : 2 * lines] = lax.dot_general(high, low, NT, preferred_element_type=F32)
    for i in range(cells.shape[0]):
        at = 2 * lines + 8 * i
        aux[at : at + 6] = moments[:, i * cy : (i + 1) * cy]
        aux[at + 6 : at + 7] = owner[i : i + 1, :].astype(F32)
        aux[at + 7 : at + 8] = cells[i : i + 1, :].astype(F32)


def widen_kernel(cx, sections, *refs):
    fields, left, right = refs[0:3]
    auxes = refs[3 : 3 + sections]
    wide, top, bottom = refs[3 + sections : 6 + sections]
    block, aux, acc, sem = refs[6 + sections :]
    section = lax.axis_index("sec")
    segment = lax.axis_index("segment")
    comps, planes, cz, cy = wide.shape
    lines = cx * cz
    copy_all(
        sem,
        [(fields.at[0], block.at[:, pl.ds(cx, cx)])]
        + [(left.at[0], block.at[:, pl.ds(0, cx)]), (right.at[0], block.at[:, pl.ds(2 * cx, cx)])]
        + [(auxes[i], aux.at[i]) for i in range(sections)],
    )
    wide[0:9] = block[...]
    zeros = jnp.zeros((2, cx, cz, cy), F32)
    before, after = aux[sections - 1, 0 : 2 * lines], aux[1 % sections, 0 : 2 * lines]
    wide[9:11, 0:cx] = jnp.where(section > 0, before.reshape(2, cx, cz, cy), zeros)
    wide[9:11, cx : 2 * cx] = aux[0, 0 : 2 * lines].reshape(2, cx, cz, cy)
    wide[9:11, 2 * cx :] = jnp.where(section < sections - 1, after.reshape(2, cx, cz, cy), zeros)

    @pl.when(segment == 0)
    def _():
        half = planes * cz // 2
        acc[...] = jnp.zeros_like(acc)

        @pl.loop(0, sections)
        def _(source):
            groups = (aux.shape[1] - 2 * lines) // 8
            chunk = [aux[source, pl.ds(2 * lines + 8 * i, 8)] for i in range(groups)]
            entries = jnp.concatenate(chunk, axis=1)
            owner = entries[6:7].astype(jnp.int32)
            cell = entries[7:8].astype(jnp.int32)
            plane = (owner - section + 1) * cx + cell // (cz * cy)
            line = plane * cz + (cell // cy) % cz
            upper = line >= half
            high = one_hot(jnp.where(upper, line - half, line), half)
            low = one_hot(jnp.where(upper, cell % cy + cy, cell % cy), 2 * cy).astype(BF16)
            for part in split3(entries[0:6]):
                spread = [(high * part[c : c + 1]).astype(BF16) for c in range(6)]
                acc[...] += lax.dot_general(
                    jnp.concatenate(spread, axis=0), low, NT, preferred_element_type=F32
                )

        for c in range(6):
            span = slice(c * half, (c + 1) * half)
            for k in range(2):
                at = slice(k * planes // 2, (k + 1) * planes // 2)
                extra = acc[span, k * cy : (k + 1) * cy].reshape(planes // 2, cz, cy)
                wide[3 + c, at] = wide[3 + c, at] + extra

    for x in range(planes):
        top[:, x * STEPS : (x + 1) * STEPS] = wide[:, x, cz - STEPS :]
        bottom[:, x * STEPS : (x + 1) * STEPS] = wide[:, x, 0:STEPS]


def advance(cx, steps, state, coef, times):
    planes, rows, cy = state.shape[2:]
    lane = lax.broadcasted_iota(jnp.int32, (rows, cy), 1)
    first_lane, last_lane = lane == 0, lane == cy - 1

    def back_y(f):
        return f - jnp.where(first_lane, F32(0.0), pltpu.roll(f, 1, 1))

    def back_z(f):
        return f - pltpu.roll(f, 1, 0)

    def fore_y(f):
        return jnp.where(last_lane, F32(0.0), pltpu.roll(f, cy - 1, 1)) - f

    def fore_z(f):
        return pltpu.roll(f, rows - 1, 0) - f

    for step in range(steps):
        left = steps - 1 - step
        low, high = cx - left, 2 * cx + left

        @pl.loop(low, high + 1)
        def _(x):
            inc = [None, None]
            for model in range(2):
                sxx, syy, szz, syz, sxz, sxy = (state[model, 3 + k, x] for k in range(6))
                sxx_p, sxz_p, sxy_p = (state[model, k, x - 1] for k in (3, 7, 8))
                hb = coef[model, 0, x]
                inc[model] = (
                    hb * ((sxx - sxx_p) + back_y(sxy) + back_z(sxz)),
                    hb * ((sxy - sxy_p) + back_y(syy) + back_z(syz)),
                    hb * ((sxz - sxz_p) + back_y(syz) + back_z(szz)),
                )
            for k in range(3):
                state[0, k, x] = state[0, k, x] + inc[0][k]
                state[1, k, x] = (state[1, k, x] + inc[1][k]) + times[x] * inc[0][k]

        @pl.loop(low, high)
        def _(x):
            for model in range(2):
                vx, vy, vz = (state[model, k, x] for k in range(3))
                vx_n, vy_n, vz_n = (state[model, k, x + 1] for k in range(3))
                hl, hm = coef[model, 1, x], coef[model, 2, x]
                exx, eyy, ezz = vx_n - vx, fore_y(vy), fore_z(vz)
                pressure = hl * (exx + eyy + ezz)
                twice = hm + hm
                state[model, 3, x] = state[model, 3, x] + (pressure + twice * exx)
                state[model, 4, x] = state[model, 4, x] + (pressure + twice * eyy)
                state[model, 5, x] = state[model, 5, x] + (pressure + twice * ezz)
                state[model, 6, x] = state[model, 6, x] + hm * (fore_z(vy) + fore_y(vz))
                state[model, 7, x] = state[model, 7, x] + hm * (fore_z(vx) + (vz_n - vz))
                state[model, 8, x] = state[model, 8, x] + hm * (fore_y(vx) + (vy_n - vy))


def first_kernel(
    cx, steps, wide, above, below, r_wide, r_above, r_below, buoyancy, lame_lambda, lame_mu,
    sent, both, coef, times, mid, ends, state, tables, sem,
):
    segment = lax.axis_index("segment")
    planes, cz, cy = mid.shape[2:]
    rows = state.shape[3]
    copy_all(
        sem,
        [(wide, mid.at[0]), (above, ends.at[0, 0]), (below, ends.at[0, 1])]
        + [(r_wide, mid.at[1]), (r_above, ends.at[1, 0]), (r_below, ends.at[1, 1])]
        + [(t, tables.at[i]) for i, t in enumerate((buoyancy, lame_lambda, lame_mu))],
    )

    def join(model, source, first, count):
        for x in range(planes):
            span = slice(x * STEPS, (x + 1) * STEPS)
            to = state.at[model, first : first + count, x]
            at = slice(first, first + count)
            to[:, 0:STEPS] = ends[source, 0, at, span]
            to[:, STEPS : STEPS + cz] = mid[source, at, x]
            to[:, STEPS + cz :] = ends[source, 1, at, span]

    join(segment, 0, 0, 11)

    @pl.when(segment == 1)
    def _():
        join(0, 1, 0, 11)

    @pl.loop(0, planes)
    def _(x):
        for model in range(2):
            ids = state[model, 9, x]
            found = [jnp.zeros((rows, cy), F32)] * 3
            for entry in range(tables.shape[1]):
                hit = ids == F32(entry + 1)
                found = [
                    jnp.where(hit, F32(0.5) * tables[i, entry], found[i]) for i in range(3)
                ]
            for i in range(3):
                coef[model, i, x] = found[i]
        times[x] = state[1, 10, x]

    advance(cx, steps, state, coef, times)
    both[...] = state[:, 0:9, cx : 2 * cx]
    sent[...] = state[segment, 0:9, cx : 2 * cx]


def next_kernel(cx, steps, last, both_in, left, right, r_left, r_right, coef_in, times_in, *refs):
    segment = lax.axis_index("segment")
    sent, both = refs[0:2]
    state, coef, times, sem = refs[-4:]
    near = slice(0, cx), slice(2 * cx, 3 * cx)
    copy_all(
        sem,
        [(both_in, state.at[:, :, pl.ds(cx, cx)]), (coef_in, coef), (times_in, times)]
        + [(left, state.at[segment, :, pl.ds(0, cx)])]
        + [(right, state.at[segment, :, pl.ds(2 * cx, cx)])],
    )

    @pl.when(segment == 1)
    def _():
        copy_all(
            sem,
            [(r_left, state.at[0, :, pl.ds(0, cx)]), (r_right, state.at[0, :, pl.ds(2 * cx, cx)])],
        )

    advance(cx, steps, state, coef, times)
    if last:
        rows = state.shape[3]
        sent[0] = state[segment, :, cx : 2 * cx, STEPS : rows - STEPS]
    else:
        sent[...] = state[segment, :, cx : 2 * cx]
        both[...] = state[:, :, cx : 2 * cx]


VMEM = pl.BlockSpec(memory_space=pltpu.VMEM)
ANY = pl.BlockSpec(memory_space=pl.ANY)
LIMIT = pltpu.CompilerParams(vmem_limit_bytes=40 * 2**20)


def call(kernel, name, operands, outs, scratch, copies):
    return pl.pallas_call(
        kernel,
        out_shape=[jax.ShapeDtypeStruct(shape, F32) for shape in outs],
        in_specs=[ANY] * len(operands),
        out_specs=[VMEM] * len(outs),
        scratch_shapes=scratch + [pltpu.SemaphoreType.DMA((copies,))],
        compiler_params=LIMIT,
        name=name,
    )(*operands)


def on_device(
    fields, block_ids, buoyancy, lame_lambda, lame_mu, moments, moment_owner, moment_cells, drm_rows
):
    sections, slabs = lax.axis_size("sec"), lax.axis_size("depth")
    cx, cz, cy = fields.shape[2:]
    planes, rows = 3 * cx, cz + 2 * STEPS
    around = range(sections)

    def along(block, axis, distance):
        size = lax.axis_size(axis)
        route = [(i, i + distance) for i in range(size) if 0 <= i + distance < size]
        return lax.ppermute(block, axis, route)

    def to_basin(block, axis, distance):
        size = lax.axis_size(axis)
        route = [
            (2 * i, 2 * (i + distance) + 1) for i in range(size) if 0 <= i + distance < size
        ]
        return lax.ppermute(block, (axis, "segment"), route)

    owner = moment_owner.reshape(-1, cy)
    cells = moment_cells.reshape(-1, cy)
    boundary = drm_rows.reshape(-1, cy)
    left, right = along(fields, "sec", 1), along(fields, "sec", -1)
    ids_and_entries = (block_ids, moments, owner, cells, boundary)
    aux_shape = (2 * cx * cz + 8 * cells.shape[0], cy)
    (aux,) = call(
        aux_kernel,
        "ids_counts_entries",
        ids_and_entries,
        [aux_shape],
        [pltpu.VMEM(a.shape, a.dtype) for a in ids_and_entries],
        len(ids_and_entries),
    )
    auxes = [aux] + [
        lax.ppermute(aux, "sec", [((i + k) % sections, i) for i in around]) for k in around[1:]
    ]
    wide, top, bottom = call(
        functools.partial(widen_kernel, cx, sections),
        "widen_and_moments",
        (fields, left, right, *auxes),
        [(11, planes, cz, cy), (11, planes * STEPS, cy), (11, planes * STEPS, cy)],
        [
            pltpu.VMEM((9, planes, cz, cy), F32),
            pltpu.VMEM((sections, *aux_shape), F32),
            pltpu.VMEM((6 * planes * cz // 2, 2 * cy), F32),
        ],
        3 + sections,
    )
    above, below = along(top, "depth", 1), along(bottom, "depth", -1)
    r_wide = lax.ppermute(wide, "segment", [(0, 1)])
    r_above, r_below = to_basin(top, "depth", 1), to_basin(bottom, "depth", -1)
    plan = [cx] * (STEPS // cx) + [STEPS % cx] * (STEPS % cx > 0)
    window = pltpu.VMEM((2, 9, planes, rows, cy), F32)
    block_shape = (9, cx, rows, cy)
    coef_shape, times_shape = (2, 3, planes, rows, cy), (planes, rows, cy)
    sent, both, coef, times = call(
        functools.partial(first_kernel, cx, plan[0]),
        "first_steps",
        (wide, above, below, r_wide, r_above, r_below, buoyancy, lame_lambda, lame_mu),
        [block_shape, (2, *block_shape), coef_shape, times_shape],
        [
            pltpu.VMEM((2, 11, planes, cz, cy), F32),
            pltpu.VMEM((2, 2, 11, planes * STEPS, cy), F32),
            pltpu.VMEM((2, 11, planes, rows, cy), F32),
            pltpu.SMEM((3, buoyancy.shape[0]), F32),
        ],
        9,
    )
    for number, steps in enumerate(plan[1:]):
        last = number == len(plan) - 2
        left, right = along(sent, "sec", 1), along(sent, "sec", -1)
        r_left, r_right = to_basin(sent, "sec", 1), to_basin(sent, "sec", -1)
        outs = [fields.shape] if last else [block_shape, (2, *block_shape)]
        got = call(
            functools.partial(next_kernel, cx, steps, last),
            "next_steps",
            (both, left, right, r_left, r_right, coef, times),
            outs,
            [window, pltpu.VMEM(coef_shape, F32), pltpu.VMEM(times_shape, F32)],
            5,
        )
        sent, both = got[0], got[-1]
    return sent


def solution(mesh):
    in_specs = (
        P("segment", None, "sec", "depth", None),
        P("segment", "sec", "depth", None),
        P(),
        P(),
        P(),
        P(None, ("sec", "depth")),
        P(("sec", "depth"), None),
        P(("sec", "depth")),
        P(("sec", "depth")),
    )
    out_specs = P("segment", None, "sec", "depth", None)
    return jax.shard_map(
        on_device, mesh=mesh, in_specs=in_specs, out_specs=out_specs, check_vma=False
    )
```

```python
import functools

import jax
import jax.numpy as jnp
from jax import lax
from jax.experimental import pallas as pl
from jax.experimental.pallas import tpu as pltpu
from jax.sharding import PartitionSpec as P

STEPS = 4
F32 = jnp.float32
BF16 = jnp.bfloat16
NT = (((1,), (1,)), ((), ()))


def one_hot(index, count):
    rows = lax.broadcasted_iota(jnp.int32, (count, index.shape[-1]), 0)
    return jnp.where(rows == index, F32(1.0), F32(0.0))


def split3(value):
    high = value.astype(BF16).astype(F32)
    rest = value - high
    mid = rest.astype(BF16).astype(F32)
    return high, mid, rest - mid


def copy_all(sem, pairs):
    copies = [pltpu.make_async_copy(a, b, sem.at[i]) for i, (a, b) in enumerate(pairs)]
    for copy in copies:
        copy.start()
    for copy in copies:
        copy.wait()


def in_line(rows):
    return jnp.concatenate([rows[i : i + 1, :] for i in range(rows.shape[0])], axis=1)


def pack_kernel(layout, fields_in, ids_in, moments_in, owner_in, cells_in, rows_in, packed, entries, *scratch):
    cx, cz, cy = layout
    ids, moments, owner, cells, rows, sem = scratch
    lines = cx * cz
    copies = [(ids_in, ids), (moments_in, moments), (owner_in, owner), (cells_in, cells), (rows_in, rows)]
    copies += [
        (fields_in.at[0, k, x], packed.at[pl.ds((k * cx + x) * cz, cz)])
        for k in range(9)
        for x in range(cx)
    ]
    copy_all(sem, copies)
    packed[9 * lines : 10 * lines] = (ids[0] + 1).astype(F32).reshape(lines, cy)
    line = in_line(rows[...])
    high = one_hot(line // cy, lines).astype(BF16)
    low = one_hot(line % cy, cy).astype(BF16)
    packed[10 * lines : 11 * lines] = lax.dot_general(high, low, NT, preferred_element_type=F32)
    for i in range(cells.shape[0]):
        at = 8 * i
        entries[at : at + 6] = moments[:, i * cy : (i + 1) * cy]
        entries[at + 6 : at + 7] = owner[i : i + 1, :].astype(F32)
        entries[at + 7 : at + 8] = cells[i : i + 1, :].astype(F32)
    packed[11 * lines :] = entries[...]


def widen_kernel(layout, *refs):
    cx, cz, cy = layout
    packs, others = refs[0:3], refs[3:-6]
    kept, swapped, near, far, wide, acc = refs[-6:]
    section = lax.axis_index("sec")
    segment = lax.axis_index("segment")
    planes = 3 * cx
    lines = cx * cz
    for i, pack in enumerate(packs):
        wide[:, i * cx : (i + 1) * cx] = pack[0 : 11 * lines].reshape(11, cx, cz, cy)

    @pl.when(segment == 0)
    def _():
        half = planes * cz // 2
        acc[...] = jnp.zeros_like(acc)
        for entries in [pack.at[pl.ds(11 * lines, pack.shape[0] - 11 * lines)] for pack in packs] + list(others):
            groups = entries.shape[0] // 8
            chunk = [entries[8 * i : 8 * i + 8] for i in range(groups)]
            entry = jnp.concatenate(chunk, axis=1)
            owner = entry[6:7].astype(jnp.int32)
            cell = entry[7:8].astype(jnp.int32)
            plane = (owner - section + 1) * cx + cell // (cz * cy)
            line = plane * cz + (cell // cy) % cz
            upper = line >= half
            high = one_hot(jnp.where(upper, line - half, line), half)
            low = one_hot(jnp.where(upper, cell % cy + cy, cell % cy), 2 * cy).astype(BF16)
            for part in split3(entry[0:6]):
                spread = [(high * part[c : c + 1]).astype(BF16) for c in range(6)]
                acc[...] += lax.dot_general(
                    jnp.concatenate(spread, axis=0), low, NT, preferred_element_type=F32
                )

        for c in range(6):
            span = slice(c * half, (c + 1) * half)
            for k in range(2):
                at = slice(k * planes // 2, (k + 1) * planes // 2)
                extra = acc[span, k * cy : (k + 1) * cy].reshape(planes // 2, cz, cy)
                wide[3 + c, at] = wide[3 + c, at] + extra

    def cut(to, first, count):
        for x in range(planes):
            to[:, x * count : (x + 1) * count] = wide[:, x, first : first + count]

    reach = cz // 2 + STEPS

    @pl.when(segment == 0)
    def _():
        cut(kept, 0, reach)
        cut(swapped, cz - reach, reach)
        cut(near, cz - STEPS, STEPS)
        cut(far, 0, STEPS)

    @pl.when(segment == 1)
    def _():
        cut(kept, cz - reach, reach)
        cut(swapped, 0, reach)
        cut(near, 0, STEPS)
        cut(far, cz - STEPS, STEPS)


def advance(cx, steps, state, coef, times):
    planes, rows, cy = state.shape[2:]
    lane = lax.broadcasted_iota(jnp.int32, (rows, cy), 1)
    first_lane, last_lane = lane == 0, lane == cy - 1

    def back_y(f):
        return f - jnp.where(first_lane, F32(0.0), pltpu.roll(f, 1, 1))

    def back_z(f):
        return f - pltpu.roll(f, 1, 0)

    def fore_y(f):
        return jnp.where(last_lane, F32(0.0), pltpu.roll(f, cy - 1, 1)) - f

    def fore_z(f):
        return pltpu.roll(f, rows - 1, 0) - f

    for step in range(steps):
        left = steps - 1 - step
        low, high = cx - left, 2 * cx + left

        @pl.loop(low, high + 1)
        def _(x):
            inc = [None, None]
            for model in range(2):
                sxx, syy, szz, syz, sxz, sxy = (state[model, 3 + k, x] for k in range(6))
                sxx_p, sxz_p, sxy_p = (state[model, k, x - 1] for k in (3, 7, 8))
                hb = coef[model, 0, x]
                inc[model] = (
                    hb * ((sxx - sxx_p) + back_y(sxy) + back_z(sxz)),
                    hb * ((sxy - sxy_p) + back_y(syy) + back_z(syz)),
                    hb * ((sxz - sxz_p) + back_y(syz) + back_z(szz)),
                )
            for k in range(3):
                state[0, k, x] = state[0, k, x] + inc[0][k]
                state[1, k, x] = (state[1, k, x] + inc[1][k]) + times[x] * inc[0][k]

        @pl.loop(low, high)
        def _(x):
            for model in range(2):
                vx, vy, vz = (state[model, k, x] for k in range(3))
                vx_n, vy_n, vz_n = (state[model, k, x + 1] for k in range(3))
                hl, hm = coef[model, 1, x], coef[model, 2, x]
                exx, eyy, ezz = vx_n - vx, fore_y(vy), fore_z(vz)
                pressure = hl * (exx + eyy + ezz)
                twice = hm + hm
                state[model, 3, x] = state[model, 3, x] + (pressure + twice * exx)
                state[model, 4, x] = state[model, 4, x] + (pressure + twice * eyy)
                state[model, 5, x] = state[model, 5, x] + (pressure + twice * ezz)
                state[model, 6, x] = state[model, 6, x] + hm * (fore_z(vy) + fore_y(vz))
                state[model, 7, x] = state[model, 7, x] + hm * (fore_z(vx) + (vz_n - vz))
                state[model, 8, x] = state[model, 8, x] + hm * (fore_y(vx) + (vy_n - vy))


def first_kernel(
    cx, steps, kept, swapped, near, far, buoyancy, lame_lambda, lame_mu,
    sent, both, coef, times, state, tables, sem,
):
    segment = lax.axis_index("segment")
    planes, rows, cy = state.shape[2:]
    reach = rows - STEPS
    copy_all(sem, [(t, tables.at[i]) for i, t in enumerate((buoyancy, lame_lambda, lame_mu))])

    def join(model, body, halo, upper):
        for x in range(planes):
            inner, outer = slice(x * reach, (x + 1) * reach), slice(x * STEPS, (x + 1) * STEPS)
            if upper:
                state[model, :, x, 0:STEPS] = halo[:, outer]
                state[model, :, x, STEPS:] = body[:, inner]
            else:
                state[model, :, x, 0:reach] = body[:, inner]
                state[model, :, x, reach:] = halo[:, outer]

    @pl.when(segment == 0)
    def _():
        join(0, kept, near, True)
        join(1, swapped, far, True)

    @pl.when(segment == 1)
    def _():
        join(1, kept, near, False)
        join(0, swapped, far, False)

    @pl.loop(0, planes)
    def _(x):
        for model in range(2):
            ids = state[model, 9, x]
            found = [jnp.zeros((rows, cy), F32)] * 3
            for entry in range(tables.shape[1]):
                hit = ids == F32(entry + 1)
                found = [
                    jnp.where(hit, F32(0.5) * tables[i, entry], found[i]) for i in range(3)
                ]
            for i in range(3):
                coef[model, i, x] = found[i]
        times[x] = state[1, 10, x]

    advance(cx, steps, state, coef, times)
    both[...] = state[:, 0:9, cx : 2 * cx]
    cut_edges(cx, steps, state, sent)


def cut_edges(cx, done, state, sent):
    rows = state.shape[3]
    count = rows - 2 * done
    for x in range(cx):
        sent[:, :, x * count : (x + 1) * count] = state[:, 0:9, cx + x, done : rows - done]


def next_kernel(cx, done, steps, both_in, left, right, coef, times, *refs):
    segment = lax.axis_index("segment")
    first, second, state = refs
    rows = state.shape[3]
    count = rows - 2 * done
    state[:, :, cx : 2 * cx] = both_in[...]
    for x in range(cx):
        span = slice(x * count, (x + 1) * count)
        state[:, :, x, done : rows - done] = left[:, :, span]
        state[:, :, 2 * cx + x, done : rows - done] = right[:, :, span]
    advance(cx, steps, state, coef, times)
    if done + steps == STEPS:
        first[...] = state[segment, :, cx : 2 * cx, STEPS : rows - STEPS]
        second[...] = state[1 - segment, :, cx : 2 * cx, STEPS : rows - STEPS]
    else:
        first[...] = state[:, :, cx : 2 * cx]
        cut_edges(cx, done + steps, state, second)


def home_kernel(mine, brought, out):
    half = mine.shape[2]
    segment = lax.axis_index("segment")

    @pl.when(segment == 0)
    def _():
        out[0, :, :, 0:half] = mine[...]
        out[0, :, :, half:] = brought[...]

    @pl.when(segment == 1)
    def _():
        out[0, :, :, half:] = mine[...]
        out[0, :, :, 0:half] = brought[...]


VMEM = pl.BlockSpec(memory_space=pltpu.VMEM)
HBM = pl.BlockSpec(memory_space=pltpu.HBM)
LIMIT = pltpu.CompilerParams(vmem_limit_bytes=40 * 2**20)


def call(kernel, name, in_hbm, in_vmem, outs, scratch, copies=0):
    sems = [pltpu.SemaphoreType.DMA((copies,))] * (copies > 0)
    return pl.pallas_call(
        kernel,
        out_shape=[jax.ShapeDtypeStruct(shape, F32) for shape in outs],
        in_specs=[VMEM] * len(in_vmem) + [HBM] * len(in_hbm),
        out_specs=[VMEM] * len(outs),
        scratch_shapes=scratch + sems,
        compiler_params=LIMIT,
        name=name,
    )(*in_vmem, *in_hbm)


def on_device(
    fields, block_ids, buoyancy, lame_lambda, lame_mu, moments, moment_owner, moment_cells, drm_rows
):
    sections, slabs = lax.axis_size("sec"), lax.axis_size("depth")
    layout = cx, cz, cy = fields.shape[2:]
    planes = 3 * cx
    reach, rows = cz // 2 + STEPS, cz // 2 + 2 * STEPS
    plan = [cx] * (STEPS // cx) + [STEPS % cx] * (STEPS % cx > 0)

    def along_x(block, distance):
        route = [(i, i + distance) for i in range(sections) if 0 <= i + distance < sections]
        return lax.ppermute(block, "sec", route)

    def halo(block, core_zero_goes, flip):
        route = []
        for i in range(slabs):
            for core in range(2):
                to = i + (core_zero_goes if core == 0 else -core_zero_goes)
                if 0 <= to < slabs:
                    route.append((2 * i + core, 2 * to + (1 - core if flip else core)))
        return lax.ppermute(block, ("depth", "segment"), route)

    def swap(block):
        return lax.ppermute(block, "segment", [(0, 1), (1, 0)])

    owner = moment_owner.reshape(-1, cy)
    cells = moment_cells.reshape(-1, cy)
    boundary = drm_rows.reshape(-1, cy)
    small = (block_ids, moments, owner, cells, boundary)
    lines = cx * cz
    entry_lines = 8 * cells.shape[0]
    packed, entries = call(
        functools.partial(pack_kernel, layout),
        "pack",
        (fields, *small),
        (),
        [(11 * lines + entry_lines, cy), (entry_lines, cy)],
        [pltpu.VMEM(a.shape, a.dtype) for a in small],
        len(small) + 9 * cx,
    )
    routes = [
        [((i + k) % sections, i) for i in range(sections)] for k in range(2, sections - 1)
    ] + [[(0, sections - 1), (sections - 1, 0)]] * (sections > 2)
    others = [lax.ppermute(entries, "sec", route) for route in routes]
    left, right = along_x(packed, 1), along_x(packed, -1)
    kept, swapped, near, far = call(
        functools.partial(widen_kernel, layout),
        "widen_and_moments",
        (),
        (left, packed, right, *others),
        [(11, planes * reach, cy)] * 2 + [(11, planes * STEPS, cy)] * 2,
        [pltpu.VMEM((11, planes, cz, cy), F32), pltpu.VMEM((6 * planes * cz // 2, 2 * cy), F32)],
    )
    near, far, swapped = halo(near, 1, False), halo(far, -1, True), swap(swapped)
    both_shape = (2, 9, cx, rows, cy)
    coef_shape, times_shape = (2, 3, planes, rows, cy), (planes, rows, cy)

    def edge_shape(done):
        return (2, 9, cx * (rows - 2 * done), cy)

    done = plan[0]
    sent, both, coef, times = call(
        functools.partial(first_kernel, cx, plan[0]),
        "first_steps",
        (buoyancy, lame_lambda, lame_mu),
        (kept, swapped, near, far),
        [edge_shape(done), both_shape, coef_shape, times_shape],
        [
            pltpu.VMEM((2, 11, planes, rows, cy), F32),
            pltpu.SMEM((3, buoyancy.shape[0]), F32),
        ],
        3,
    )
    for steps in plan[1:]:
        left, right = along_x(sent, 1), along_x(sent, -1)
        after = done + steps
        half_block = (9, cx, cz // 2, cy)
        both, sent = call(
            functools.partial(next_kernel, cx, done, steps),
            "next_steps",
            (),
            (both, left, right, coef, times),
            [half_block] * 2 if after == STEPS else [both_shape, edge_shape(after)],
            [pltpu.VMEM((2, 9, planes, rows, cy), F32)],
        )
        done = after
    (out,) = call(home_kernel, "home", (), (both, swap(sent)), [fields.shape], [])
    return out


def solution(mesh):
    in_specs = (
        P("segment", None, "sec", "depth", None),
        P("segment", "sec", "depth", None),
        P(),
        P(),
        P(),
        P(None, ("sec", "depth")),
        P(("sec", "depth"), None),
        P(("sec", "depth")),
        P(("sec", "depth")),
    )
    out_specs = P("segment", None, "sec", "depth", None)
    return jax.shard_map(
        on_device, mesh=mesh, in_specs=in_specs, out_specs=out_specs, check_vma=False
    )
```

```python
import functools

import jax
import jax.numpy as jnp
from jax import lax
from jax.experimental import pallas as pl
from jax.experimental.pallas import tpu as pltpu
from jax.sharding import PartitionSpec as P

STEPS = 4
F32 = jnp.float32
BF16 = jnp.bfloat16
NT = (((1,), (1,)), ((), ()))


def one_hot(index, count):
    rows = lax.broadcasted_iota(jnp.int32, (count, index.shape[-1]), 0)
    return jnp.where(rows == index, F32(1.0), F32(0.0))


def split3(value):
    high = value.astype(BF16).astype(F32)
    rest = value - high
    mid = rest.astype(BF16).astype(F32)
    return high, mid, rest - mid


def copy_all(sem, pairs):
    copies = [pltpu.make_async_copy(a, b, sem.at[i]) for i, (a, b) in enumerate(pairs)]
    for copy in copies:
        copy.start()
    for copy in copies:
        copy.wait()


def in_line(rows):
    return jnp.concatenate([rows[i : i + 1, :] for i in range(rows.shape[0])], axis=1)


def pack_kernel(layout, fields_in, ids_in, moments_in, owner_in, cells_in, rows_in, packed, entries, *scratch):
    cx, cz, cy = layout
    ids, moments, owner, cells, rows, sem = scratch
    lines = cx * cz
    copies = [(ids_in, ids), (moments_in, moments), (owner_in, owner), (cells_in, cells), (rows_in, rows)]
    copies += [
        (fields_in.at[0, k, x], packed.at[pl.ds((k * cx + x) * cz, cz)])
        for k in range(9)
        for x in range(cx)
    ]
    copy_all(sem, copies)
    packed[9 * lines : 10 * lines] = (ids[0] + 1).astype(F32).reshape(lines, cy)
    line = in_line(rows[...])
    high = one_hot(line // cy, lines).astype(BF16)
    low = one_hot(line % cy, cy).astype(BF16)
    packed[10 * lines : 11 * lines] = lax.dot_general(high, low, NT, preferred_element_type=F32)
    for i in range(cells.shape[0]):
        at = 8 * i
        entries[at : at + 6] = moments[:, i * cy : (i + 1) * cy]
        entries[at + 6 : at + 7] = owner[i : i + 1, :].astype(F32)
        entries[at + 7 : at + 8] = cells[i : i + 1, :].astype(F32)


def moment_kernel(layout, *refs):
    cx, cz, cy = layout
    blocks, dense, acc = refs[:-2], refs[-2], refs[-1]
    section = lax.axis_index("sec")
    planes = 3 * cx
    half = planes * cz // 2

    @pl.when(lax.axis_index("segment") == 0)
    def _():
        acc[...] = jnp.zeros_like(acc)
        for entries in blocks:
            groups = entries.shape[0] // 8
            chunk = [entries[8 * i : 8 * i + 8] for i in range(groups)]
            entry = jnp.concatenate(chunk, axis=1)
            owner = entry[6:7].astype(jnp.int32)
            cell = entry[7:8].astype(jnp.int32)
            plane = (owner - section + 1) * cx + cell // (cz * cy)
            line = plane * cz + (cell // cy) % cz
            upper = line >= half
            high = one_hot(jnp.where(upper, line - half, line), half)
            low = one_hot(jnp.where(upper, cell % cy + cy, cell % cy), 2 * cy).astype(BF16)
            for part in split3(entry[0:6]):
                spread = [(high * part[c : c + 1]).astype(BF16) for c in range(6)]
                acc[...] += lax.dot_general(
                    jnp.concatenate(spread, axis=0), low, NT, preferred_element_type=F32
                )
        for c in range(6):
            for k in range(2):
                at = slice(k * planes // 2, (k + 1) * planes // 2)
                got = acc[c * half : (c + 1) * half, k * cy : (k + 1) * cy]
                dense[c, at] = got.reshape(planes // 2, cz, cy)


def by_parity(even, odd, act):
    parity = lax.axis_index("sec") % 2

    @pl.when(parity == 0)
    def _():
        act(*even)

    @pl.when(parity == 1)
    def _():
        act(*odd)


def widen_kernel(layout, packed, first, second, dense, kept, swapped, near, far, wide):
    cx, cz, cy = layout
    segment = lax.axis_index("segment")
    planes = 3 * cx

    def place(left, right):
        for i, pack in enumerate((left, packed, right)):
            wide[:, i * cx : (i + 1) * cx] = pack[...].reshape(11, cx, cz, cy)

    by_parity((second, first), (first, second), place)

    @pl.when(segment == 0)
    def _():
        wide[3:9] = wide[3:9] + dense[...]

    def cut(to, first, count):
        for x in range(planes):
            to[:, x * count : (x + 1) * count] = wide[:, x, first : first + count]

    reach = cz // 2 + STEPS

    @pl.when(segment == 0)
    def _():
        cut(kept, 0, reach)
        cut(swapped, cz - reach, reach)
        cut(near, cz - STEPS, STEPS)
        cut(far, 0, STEPS)

    @pl.when(segment == 1)
    def _():
        cut(kept, cz - reach, reach)
        cut(swapped, 0, reach)
        cut(near, 0, STEPS)
        cut(far, cz - STEPS, STEPS)


def advance(cx, steps, state, coef, times, given_top=False):
    planes, rows, cy = state.shape[2:]
    lane = lax.broadcasted_iota(jnp.int32, (rows, cy), 1)
    first_lane, last_lane = lane == 0, lane == cy - 1

    def back_y(f):
        return f - jnp.where(first_lane, F32(0.0), pltpu.roll(f, 1, 1))

    def back_z(f):
        return f - pltpu.roll(f, 1, 0)

    def fore_y(f):
        return jnp.where(last_lane, F32(0.0), pltpu.roll(f, cy - 1, 1)) - f

    def fore_z(f):
        return pltpu.roll(f, rows - 1, 0) - f

    def velocity(x):
        inc = [None, None]
        for model in range(2):
            sxx, syy, szz, syz, sxz, sxy = (state[model, 3 + k, x] for k in range(6))
            sxx_p, sxz_p, sxy_p = (state[model, k, x - 1] for k in (3, 7, 8))
            hb = coef[model, 0, x]
            inc[model] = (
                hb * ((sxx - sxx_p) + back_y(sxy) + back_z(sxz)),
                hb * ((sxy - sxy_p) + back_y(syy) + back_z(syz)),
                hb * ((sxz - sxz_p) + back_y(syz) + back_z(szz)),
            )
        for k in range(3):
            state[0, k, x] = state[0, k, x] + inc[0][k]
            state[1, k, x] = (state[1, k, x] + inc[1][k]) + times[x] * inc[0][k]

    for step in range(steps):
        left = steps - 1 - step
        low, high = cx - left, 2 * cx + left
        pl.loop(low, high + 1 - (given_top and step == 0))(velocity)

        @pl.loop(low, high)
        def _(x):
            for model in range(2):
                vx, vy, vz = (state[model, k, x] for k in range(3))
                vx_n, vy_n, vz_n = (state[model, k, x + 1] for k in range(3))
                hl, hm = coef[model, 1, x], coef[model, 2, x]
                exx, eyy, ezz = vx_n - vx, fore_y(vy), fore_z(vz)
                pressure = hl * (exx + eyy + ezz)
                twice = hm + hm
                state[model, 3, x] = state[model, 3, x] + (pressure + twice * exx)
                state[model, 4, x] = state[model, 4, x] + (pressure + twice * eyy)
                state[model, 5, x] = state[model, 5, x] + (pressure + twice * ezz)
                state[model, 6, x] = state[model, 6, x] + hm * (fore_z(vy) + fore_y(vz))
                state[model, 7, x] = state[model, 7, x] + hm * (fore_z(vx) + (vz_n - vz))
                state[model, 8, x] = state[model, 8, x] + hm * (fore_y(vx) + (vy_n - vy))

    return velocity


def first_kernel(
    cx, steps, kept, swapped, near, far, buoyancy, lame_lambda, lame_mu,
    to_first, to_second, both, coef, times, state, tables, sem,
):
    segment = lax.axis_index("segment")
    planes, rows, cy = state.shape[2:]
    reach = rows - STEPS
    copy_all(sem, [(t, tables.at[i]) for i, t in enumerate((buoyancy, lame_lambda, lame_mu))])

    def join(model, body, halo, upper):
        for x in range(planes):
            inner, outer = slice(x * reach, (x + 1) * reach), slice(x * STEPS, (x + 1) * STEPS)
            if upper:
                state[model, :, x, 0:STEPS] = halo[:, outer]
                state[model, :, x, STEPS:] = body[:, inner]
            else:
                state[model, :, x, 0:reach] = body[:, inner]
                state[model, :, x, reach:] = halo[:, outer]

    @pl.when(segment == 0)
    def _():
        join(0, kept, near, True)
        join(1, swapped, far, True)

    @pl.when(segment == 1)
    def _():
        join(1, kept, near, False)
        join(0, swapped, far, False)

    @pl.loop(0, planes)
    def _(x):
        for model in range(2):
            ids = state[model, 9, x]
            found = [jnp.zeros((rows, cy), F32)] * 3
            for entry in range(tables.shape[1]):
                hit = ids == F32(entry + 1)
                found = [
                    jnp.where(hit, F32(0.5) * tables[i, entry], found[i]) for i in range(3)
                ]
            for i in range(3):
                coef[model, i, x] = found[i]
        times[x] = state[1, 10, x]

    velocity = advance(cx, steps, state, coef, times)
    both[...] = state[:, 0:9, cx : 2 * cx]
    cut_edges(cx, steps, velocity, state, to_first, to_second)


def cut_edges(cx, done, velocity, state, to_first, to_second):
    rows = state.shape[3]
    at = slice(done, rows - done)
    count = rows - 2 * done

    def put(to, place, x, comps):
        for k in comps:
            to[:, place * count : (place + 1) * count] = state[:, k, x, at]
            place += 1
        return place

    def rightward(to):
        place = 0
        for x in range(1, cx):
            place = put(to, place, cx + x, range(9))
        put(to, place, cx, (3, 7, 8))

    def leftward(to):
        place = 0
        for x in range(cx - 1):
            place = put(to, place, cx + x, range(9))
        put(to, place, 2 * cx - 1, range(3))

    by_parity((to_second, to_first), (to_first, to_second), lambda left, right: rightward(right))
    velocity(2 * cx - 1)
    by_parity((to_second, to_first), (to_first, to_second), lambda left, right: leftward(left))


def next_kernel(cx, done, steps, both_in, from_first, from_second, coef, times, *refs):
    segment = lax.axis_index("segment")
    state = refs[-1]
    rows = state.shape[3]
    at = slice(done, rows - done)
    count = rows - 2 * done
    state[:, :, cx : 2 * cx] = both_in[...]

    def get(edge, place, x, comps):
        for k in comps:
            state[:, k, x, at] = edge[:, place * count : (place + 1) * count]
            place += 1
        return place

    def place_edges(left, right):
        place = 0
        for x in range(1, cx):
            place = get(left, place, x, range(9))
        get(left, place, 0, (3, 7, 8))
        place = 0
        for x in range(cx - 1):
            place = get(right, place, 2 * cx + x, range(9))
        get(right, place, 3 * cx - 1, range(3))

    by_parity((from_second, from_first), (from_first, from_second), place_edges)
    velocity = advance(cx, steps, state, coef, times, given_top=True)
    if done + steps == STEPS:
        refs[0][...] = state[segment, :, cx : 2 * cx, STEPS : rows - STEPS]
        refs[1][...] = state[1 - segment, :, cx : 2 * cx, STEPS : rows - STEPS]
    else:
        refs[2][...] = state[:, :, cx : 2 * cx]
        cut_edges(cx, done + steps, velocity, state, refs[0], refs[1])


def home_kernel(mine, brought, out):
    half = mine.shape[2]
    segment = lax.axis_index("segment")

    @pl.when(segment == 0)
    def _():
        out[0, :, :, 0:half] = mine[...]
        out[0, :, :, half:] = brought[...]

    @pl.when(segment == 1)
    def _():
        out[0, :, :, half:] = mine[...]
        out[0, :, :, 0:half] = brought[...]


VMEM = pl.BlockSpec(memory_space=pltpu.VMEM)
HBM = pl.BlockSpec(memory_space=pltpu.HBM)


def call(kernel, name, in_hbm, in_vmem, outs, scratch, copies=0, limit=40 * 2**20, flops=10**7):
    sems = [pltpu.SemaphoreType.DMA((copies,))] * (copies > 0)
    return pl.pallas_call(
        kernel,
        out_shape=[jax.ShapeDtypeStruct(shape, F32) for shape in outs],
        in_specs=[VMEM] * len(in_vmem) + [HBM] * len(in_hbm),
        out_specs=[VMEM] * len(outs),
        scratch_shapes=scratch + sems,
        compiler_params=pltpu.CompilerParams(vmem_limit_bytes=limit),
        cost_estimate=pl.CostEstimate(flops=flops, bytes_accessed=2**20, transcendentals=0),
        name=name,
    )(*in_vmem, *in_hbm)


def on_device(
    fields, block_ids, buoyancy, lame_lambda, lame_mu, moments, moment_owner, moment_cells, drm_rows
):
    sections, slabs = lax.axis_size("sec"), lax.axis_size("depth")
    layout = cx, cz, cy = fields.shape[2:]
    planes = 3 * cx
    reach, rows = cz // 2 + STEPS, cz // 2 + 2 * STEPS
    assert cx > 1 and STEPS % cx == 0

    def pairs(block, start):
        route = [(i, i + 1) for i in range(start, sections - 1, 2)]
        return lax.ppermute(block, "sec", route + [(j, i) for i, j in route])

    def other(section, k):
        return section ^ k if sections & (sections - 1) == 0 else (section + k) % sections

    def halo(block, core_zero_goes, flip):
        route = []
        for i in range(slabs):
            for core in range(2):
                to = i + (core_zero_goes if core == 0 else -core_zero_goes)
                if 0 <= to < slabs:
                    route.append((2 * i + core, 2 * to + (1 - core if flip else core)))
        return lax.ppermute(block, ("depth", "segment"), route)

    def swap(block):
        return lax.ppermute(block, "segment", [(0, 1), (1, 0)])

    owner = moment_owner.reshape(-1, cy)
    cells = moment_cells.reshape(-1, cy)
    boundary = drm_rows.reshape(-1, cy)
    small = (block_ids, moments, owner, cells, boundary)
    lines = cx * cz
    entry_lines = 8 * cells.shape[0]
    packed, entries = call(
        functools.partial(pack_kernel, layout),
        "pack",
        (fields, *small),
        (),
        [(11 * lines, cy), (entry_lines, cy)],
        [pltpu.VMEM(a.shape, a.dtype) for a in small],
        len(small) + 9 * cx,
        limit=64 * 2**20,
    )
    blocks = [entries] + [
        lax.ppermute(
            entries, ("sec", "segment"), [(2 * other(i, k), 2 * i) for i in range(sections)]
        )
        for k in range(1, sections)
    ]
    first, second = pairs(packed, 0), pairs(packed, 1)
    half = planes * cz // 2
    (dense,) = call(
        functools.partial(moment_kernel, layout),
        "moments",
        (),
        blocks,
        [(6, planes, cz, cy)],
        [pltpu.VMEM((6 * half, 2 * cy), F32)],
        flops=2 * 18 * half * 2 * cy * sections * moments.shape[1],
    )
    kept, swapped, near, far = call(
        functools.partial(widen_kernel, layout),
        "widen",
        (),
        (packed, first, second, dense),
        [(11, planes * reach, cy)] * 2 + [(11, planes * STEPS, cy)] * 2,
        [pltpu.VMEM((11, planes, cz, cy), F32)],
    )
    near, far, swapped = halo(near, 1, False), halo(far, -1, True), swap(swapped)
    both_shape = (2, 9, cx, rows, cy)
    coef_shape, times_shape = (2, 3, planes, rows, cy), (planes, rows, cy)

    def edge_shape(done):
        return (2, (9 * (cx - 1) + 3) * (rows - 2 * done), cy)

    done = cx
    to_first, to_second, both, coef, times = call(
        functools.partial(first_kernel, cx, cx),
        "first_steps",
        (buoyancy, lame_lambda, lame_mu),
        (kept, swapped, near, far),
        [edge_shape(done)] * 2 + [both_shape, coef_shape, times_shape],
        [
            pltpu.VMEM((2, 11, planes, rows, cy), F32),
            pltpu.SMEM((3, buoyancy.shape[0]), F32),
        ],
        3,
    )
    while done < STEPS:
        first, second = pairs(to_first, 0), pairs(to_second, 1)
        after = done + cx
        half_block = (9, cx, cz // 2, cy)
        got = call(
            functools.partial(next_kernel, cx, done, cx),
            "next_steps",
            (),
            (both, first, second, coef, times),
            [half_block] * 2 if after == STEPS else [edge_shape(after)] * 2 + [both_shape],
            [pltpu.VMEM((2, 9, planes, rows, cy), F32)],
        )
        to_first, to_second, both = got[0], got[1], got[-1]
        done = after
    (out,) = call(home_kernel, "home", (), (to_first, swap(to_second)), [fields.shape], [])
    return out


def solution(mesh):
    in_specs = (
        P("segment", None, "sec", "depth", None),
        P("segment", "sec", "depth", None),
        P(),
        P(),
        P(),
        P(None, ("sec", "depth")),
        P(("sec", "depth"), None),
        P(("sec", "depth")),
        P(("sec", "depth")),
    )
    out_specs = P("segment", None, "sec", "depth", None)
    return jax.shard_map(
        on_device, mesh=mesh, in_specs=in_specs, out_specs=out_specs, check_vma=False
    )
```

```python
import functools

import jax
import jax.numpy as jnp
from jax import lax
from jax.experimental import pallas as pl
from jax.experimental.pallas import tpu as pltpu
from jax.sharding import PartitionSpec as P

STEPS = 4
F32 = jnp.float32
BF16 = jnp.bfloat16
NT = (((1,), (1,)), ((), ()))


def one_hot(index, count):
    rows = lax.broadcasted_iota(jnp.int32, (count, index.shape[-1]), 0)
    return jnp.where(rows == index, F32(1.0), F32(0.0))


def split3(value):
    high = value.astype(BF16).astype(F32)
    rest = value - high
    mid = rest.astype(BF16).astype(F32)
    return high, mid, rest - mid


def copy_all(sem, pairs):
    copies = [pltpu.make_async_copy(a, b, sem.at[i]) for i, (a, b) in enumerate(pairs)]
    for copy in copies:
        copy.start()
    for copy in copies:
        copy.wait()


def in_line(rows):
    return jnp.concatenate([rows[i : i + 1, :] for i in range(rows.shape[0])], axis=1)


def pack_kernel(layout, fields_in, ids_in, moments_in, owner_in, cells_in, rows_in, packed, entries, *scratch):
    cx, cz, cy = layout
    ids, moments, owner, cells, rows, sem = scratch
    lines = cx * cz
    copies = [(ids_in, ids), (moments_in, moments), (owner_in, owner), (cells_in, cells), (rows_in, rows)]
    copies += [(fields_in.at[0], packed.at[pl.ds(0, 9)])]
    copy_all(sem, copies)
    packed[9] = (ids[0] + 1).astype(F32)
    line = in_line(rows[...])
    high = one_hot(line // cy, lines).astype(BF16)
    low = one_hot(line % cy, cy).astype(BF16)
    count = lax.dot_general(high, low, NT, preferred_element_type=F32)
    packed[10] = count.reshape(cx, cz, cy)
    for i in range(cells.shape[0]):
        at = 8 * i
        entries[at : at + 6] = moments[:, i * cy : (i + 1) * cy]
        entries[at + 6 : at + 7] = owner[i : i + 1, :].astype(F32)
        entries[at + 7 : at + 8] = cells[i : i + 1, :].astype(F32)


def moment_kernel(layout, *refs):
    cx, cz, cy = layout
    blocks, own_in, dense, acc, own, sem = refs[:-5], *refs[-5:]
    section = lax.axis_index("sec")
    planes = 3 * cx
    half = planes * cz // 2

    @pl.when(lax.axis_index("segment") == 0)
    def _():
        copy = pltpu.make_async_copy(own_in, own, sem.at[0])
        copy.start()
        acc[...] = jnp.zeros_like(acc)
        for entries in (*blocks, own):
            if entries is own:
                copy.wait()
            groups = entries.shape[0] // 8
            chunk = [entries[8 * i : 8 * i + 8] for i in range(groups)]
            entry = jnp.concatenate(chunk, axis=1)
            owner = entry[6:7].astype(jnp.int32)
            cell = entry[7:8].astype(jnp.int32)
            plane = (owner - section + 1) * cx + cell // (cz * cy)
            line = plane * cz + (cell // cy) % cz
            upper = line >= half
            high = one_hot(jnp.where(upper, line - half, line), half)
            low = one_hot(jnp.where(upper, cell % cy + cy, cell % cy), 2 * cy).astype(BF16)
            for part in split3(entry[0:6]):
                spread = [(high * part[c : c + 1]).astype(BF16) for c in range(6)]
                acc[...] += lax.dot_general(
                    jnp.concatenate(spread, axis=0), low, NT, preferred_element_type=F32
                )
        for c in range(6):
            for k in range(2):
                at = slice(k * planes // 2, (k + 1) * planes // 2)
                got = acc[c * half : (c + 1) * half, k * cy : (k + 1) * cy]
                dense[c, at] = got.reshape(planes // 2, cz, cy)


def by_parity(even, odd, act):
    parity = lax.axis_index("sec") % 2

    @pl.when(parity == 0)
    def _():
        act(*even)

    @pl.when(parity == 1)
    def _():
        act(*odd)


def widen_kernel(layout, packed, first, second, dense, kept, swapped, near, far, wide):
    cx, cz, cy = layout
    segment = lax.axis_index("segment")
    planes = 3 * cx

    def place(left, right):
        for i, pack in enumerate((left, packed, right)):
            wide[:, i * cx : (i + 1) * cx] = pack[...]

    by_parity((second, first), (first, second), place)

    @pl.when(segment == 0)
    def _():
        wide[3:9] = wide[3:9] + dense[...]

    def cut(to, first, count):
        for x in range(planes):
            to[:, x * count : (x + 1) * count] = wide[:, x, first : first + count]

    def cut_halo(to, upward):
        spans, lines = halo_rows(cx, upward)
        for x, at, rows in spans:
            first = cz - rows if upward else 0
            for k in range(11):
                to[k * lines + at : k * lines + at + rows] = wide[k, x, first : first + rows]

    reach = cz // 2 + STEPS

    @pl.when(segment == 0)
    def _():
        cut(kept, 0, reach)
        cut(swapped, cz - reach, reach)
        cut_halo(near, True)
        cut_halo(far, False)

    @pl.when(segment == 1)
    def _():
        cut(kept, cz - reach, reach)
        cut(swapped, 0, reach)
        cut_halo(near, False)
        cut_halo(far, True)


def halo_rows(cx, upward):
    found, at = [], 0
    for x in range(3 * cx):
        beyond = max(0, cx - x) if upward else max(0, x - 2 * cx + 1)
        found.append((x, at, STEPS - beyond))
        at += STEPS - beyond
    return found, at


def advance(cx, steps, state, coef, times, given_top=False):
    planes, rows, cy = state.shape[2:]
    lane = lax.broadcasted_iota(jnp.int32, (rows, cy), 1)
    first_lane, last_lane = lane == 0, lane == cy - 1

    def back_y(f):
        return f - jnp.where(first_lane, F32(0.0), pltpu.roll(f, 1, 1))

    def back_z(f):
        return f - pltpu.roll(f, 1, 0)

    def fore_y(f):
        return jnp.where(last_lane, F32(0.0), pltpu.roll(f, cy - 1, 1)) - f

    def fore_z(f):
        return pltpu.roll(f, rows - 1, 0) - f

    def velocity(x):
        inc = [None, None]
        for model in range(2):
            sxx, syy, szz, syz, sxz, sxy = (state[model, 3 + k, x] for k in range(6))
            sxx_p, sxz_p, sxy_p = (state[model, k, x - 1] for k in (3, 7, 8))
            hb = coef[model, 0, x]
            inc[model] = (
                hb * ((sxx - sxx_p) + back_y(sxy) + back_z(sxz)),
                hb * ((sxy - sxy_p) + back_y(syy) + back_z(syz)),
                hb * ((sxz - sxz_p) + back_y(syz) + back_z(szz)),
            )
        for k in range(3):
            state[0, k, x] = state[0, k, x] + inc[0][k]
            state[1, k, x] = (state[1, k, x] + inc[1][k]) + times[x] * inc[0][k]

    for step in range(steps):
        left = steps - 1 - step
        low, high = cx - left, 2 * cx + left
        pl.loop(low, high + 1 - (given_top and step == 0))(velocity)

        @pl.loop(low, high)
        def _(x):
            for model in range(2):
                vx, vy, vz = (state[model, k, x] for k in range(3))
                vx_n, vy_n, vz_n = (state[model, k, x + 1] for k in range(3))
                hl, hm = coef[model, 1, x], coef[model, 2, x]
                exx, eyy, ezz = vx_n - vx, fore_y(vy), fore_z(vz)
                pressure = hl * (exx + eyy + ezz)
                twice = hm + hm
                state[model, 3, x] = state[model, 3, x] + (pressure + twice * exx)
                state[model, 4, x] = state[model, 4, x] + (pressure + twice * eyy)
                state[model, 5, x] = state[model, 5, x] + (pressure + twice * ezz)
                state[model, 6, x] = state[model, 6, x] + hm * (fore_z(vy) + fore_y(vz))
                state[model, 7, x] = state[model, 7, x] + hm * (fore_z(vx) + (vz_n - vz))
                state[model, 8, x] = state[model, 8, x] + hm * (fore_y(vx) + (vy_n - vy))

    return velocity


def first_kernel(
    cx, steps, kept, swapped, near, far, buoyancy, lame_lambda, lame_mu,
    to_first, to_second, both, coef, times, state, tables, sem,
):
    segment = lax.axis_index("segment")
    planes, rows, cy = state.shape[2:]
    reach = rows - STEPS
    copy_all(sem, [(t, tables.at[i]) for i, t in enumerate((buoyancy, lame_lambda, lame_mu))])

    def join(model, body, halo, upper):
        spans, lines = halo_rows(cx, upper)
        for x, at, count in spans:
            inner = slice(x * reach, (x + 1) * reach)
            first = STEPS if upper else 0
            state[model, :, x, first : first + reach] = body[:, inner]
            first = STEPS - count if upper else reach
            for k in range(11):
                outer = slice(k * lines + at, k * lines + at + count)
                state[model, k, x, first : first + count] = halo[outer]

    @pl.when(segment == 0)
    def _():
        join(0, kept, near, True)
        join(1, swapped, far, True)

    @pl.when(segment == 1)
    def _():
        join(1, kept, near, False)
        join(0, swapped, far, False)

    @pl.loop(0, planes)
    def _(x):
        for model in range(2):
            ids = state[model, 9, x]
            found = [jnp.zeros((rows, cy), F32)] * 3
            for entry in range(tables.shape[1]):
                hit = ids == F32(entry + 1)
                found = [
                    jnp.where(hit, F32(0.5) * tables[i, entry], found[i]) for i in range(3)
                ]
            for i in range(3):
                coef[model, i, x] = found[i]
        times[x] = state[1, 10, x]

    velocity = advance(cx, steps, state, coef, times)
    both[...] = state[:, 0:9, cx : 2 * cx]
    cut_edges(cx, steps, velocity, state, to_first, to_second)


def cut_edges(cx, done, velocity, state, to_first, to_second):
    rows = state.shape[3]
    at = slice(done, rows - done)
    count = rows - 2 * done

    def put(to, place, x, comps):
        for k in comps:
            to[:, place * count : (place + 1) * count] = state[:, k, x, at]
            place += 1
        return place

    def rightward(to):
        place = 0
        for x in range(1, cx):
            place = put(to, place, cx + x, range(9))
        put(to, place, cx, (3, 7, 8))

    def leftward(to):
        place = 0
        for x in range(cx - 1):
            place = put(to, place, cx + x, range(9))
        put(to, place, 2 * cx - 1, range(3))

    by_parity((to_second, to_first), (to_first, to_second), lambda left, right: rightward(right))
    velocity(2 * cx - 1)
    by_parity((to_second, to_first), (to_first, to_second), lambda left, right: leftward(left))


def next_kernel(cx, done, steps, both_in, from_first, from_second, coef, times, *refs):
    segment = lax.axis_index("segment")
    state = refs[-1]
    rows = state.shape[3]
    at = slice(done, rows - done)
    count = rows - 2 * done
    state[:, :, cx : 2 * cx] = both_in[...]

    def get(edge, place, x, comps):
        for k in comps:
            state[:, k, x, at] = edge[:, place * count : (place + 1) * count]
            place += 1
        return place

    def place_edges(left, right):
        place = 0
        for x in range(1, cx):
            place = get(left, place, x, range(9))
        get(left, place, 0, (3, 7, 8))
        place = 0
        for x in range(cx - 1):
            place = get(right, place, 2 * cx + x, range(9))
        get(right, place, 3 * cx - 1, range(3))

    by_parity((from_second, from_first), (from_first, from_second), place_edges)
    velocity = advance(cx, steps, state, coef, times, given_top=True)
    if done + steps == STEPS:
        refs[0][...] = state[segment, :, cx : 2 * cx, STEPS : rows - STEPS]
        refs[1][...] = state[1 - segment, :, cx : 2 * cx, STEPS : rows - STEPS]
    else:
        refs[2][...] = state[:, :, cx : 2 * cx]
        cut_edges(cx, done + steps, velocity, state, refs[0], refs[1])


def home_kernel(mine, brought, out):
    half = mine.shape[2]
    segment = lax.axis_index("segment")

    @pl.when(segment == 0)
    def _():
        out[0, :, :, 0:half] = mine[...]
        out[0, :, :, half:] = brought[...]

    @pl.when(segment == 1)
    def _():
        out[0, :, :, half:] = mine[...]
        out[0, :, :, 0:half] = brought[...]


VMEM = pl.BlockSpec(memory_space=pltpu.VMEM)
HBM = pl.BlockSpec(memory_space=pltpu.HBM)


def call(kernel, name, in_hbm, in_vmem, outs, scratch, copies=0, limit=40 * 2**20, flops=10**7):
    sems = [pltpu.SemaphoreType.DMA((copies,))] * (copies > 0)
    return pl.pallas_call(
        kernel,
        out_shape=[jax.ShapeDtypeStruct(shape, F32) for shape in outs],
        in_specs=[VMEM] * len(in_vmem) + [HBM] * len(in_hbm),
        out_specs=[VMEM] * len(outs),
        scratch_shapes=scratch + sems,
        compiler_params=pltpu.CompilerParams(vmem_limit_bytes=limit),
        cost_estimate=pl.CostEstimate(flops=flops, bytes_accessed=2**20, transcendentals=0),
        name=name,
    )(*in_vmem, *in_hbm)


def on_device(
    fields, block_ids, buoyancy, lame_lambda, lame_mu, moments, moment_owner, moment_cells, drm_rows
):
    sections, slabs = lax.axis_size("sec"), lax.axis_size("depth")
    layout = cx, cz, cy = fields.shape[2:]
    planes = 3 * cx
    reach, rows = cz // 2 + STEPS, cz // 2 + 2 * STEPS
    assert cx > 1 and STEPS % cx == 0

    def pairs(block, start):
        route = [(i, i + 1) for i in range(start, sections - 1, 2)]
        return lax.ppermute(block, "sec", route + [(j, i) for i, j in route])

    def other(section, k):
        return section ^ k if sections & (sections - 1) == 0 else (section + k) % sections

    def halo(block, core_zero_goes, flip):
        route = []
        for i in range(slabs):
            for core in range(2):
                to = i + (core_zero_goes if core == 0 else -core_zero_goes)
                if 0 <= to < slabs:
                    route.append((2 * i + core, 2 * to + (1 - core if flip else core)))
        return lax.ppermute(block, ("depth", "segment"), route)

    def swap(block):
        return lax.ppermute(block, "segment", [(0, 1), (1, 0)])

    owner = moment_owner.reshape(-1, cy)
    cells = moment_cells.reshape(-1, cy)
    boundary = drm_rows.reshape(-1, cy)
    small = (block_ids, moments, owner, cells, boundary)
    entry_lines = 8 * cells.shape[0]
    packed, entries = call(
        functools.partial(pack_kernel, layout),
        "pack",
        (fields, *small),
        (),
        [(11, cx, cz, cy), (entry_lines, cy)],
        [pltpu.VMEM(a.shape, a.dtype) for a in small],
        len(small) + 1,
        limit=64 * 2**20,
    )
    blocks = [
        lax.ppermute(entries, "sec", [(other(i, k), i) for i in range(sections)])
        for k in range(1, sections)
    ]
    first, second = pairs(packed, 0), pairs(packed, 1)
    half = planes * cz // 2
    halo_lines = -(-11 * halo_rows(cx, True)[1] // 8) * 8
    (dense,) = call(
        functools.partial(moment_kernel, layout),
        "moments",
        (entries,),
        blocks,
        [(6, planes, cz, cy)],
        [pltpu.VMEM((6 * half, 2 * cy), F32), pltpu.VMEM((entry_lines, cy), F32)],
        1,
        flops=2 * 18 * half * 2 * cy * sections * moments.shape[1],
    )
    kept, swapped, near, far = call(
        functools.partial(widen_kernel, layout),
        "widen",
        (),
        (packed, first, second, dense),
        [(11, planes * reach, cy)] * 2 + [(halo_lines, cy)] * 2,
        [pltpu.VMEM((11, planes, cz, cy), F32)],
    )
    near, far, swapped = halo(near, 1, False), halo(far, -1, True), swap(swapped)
    both_shape = (2, 9, cx, rows, cy)
    coef_shape, times_shape = (2, 3, planes, rows, cy), (planes, rows, cy)

    def edge_shape(done):
        return (2, (9 * (cx - 1) + 3) * (rows - 2 * done), cy)

    done = cx
    to_first, to_second, both, coef, times = call(
        functools.partial(first_kernel, cx, cx),
        "first_steps",
        (buoyancy, lame_lambda, lame_mu),
        (kept, swapped, near, far),
        [edge_shape(done)] * 2 + [both_shape, coef_shape, times_shape],
        [
            pltpu.VMEM((2, 11, planes, rows, cy), F32),
            pltpu.SMEM((3, buoyancy.shape[0]), F32),
        ],
        3,
    )
    while done < STEPS:
        first, second = pairs(to_first, 0), pairs(to_second, 1)
        after = done + cx
        half_block = (9, cx, cz // 2, cy)
        got = call(
            functools.partial(next_kernel, cx, done, cx),
            "next_steps",
            (),
            (both, first, second, coef, times),
            [half_block] * 2 if after == STEPS else [edge_shape(after)] * 2 + [both_shape],
            [pltpu.VMEM((2, 9, planes, rows, cy), F32)],
        )
        to_first, to_second, both = got[0], got[1], got[-1]
        done = after
    (out,) = call(home_kernel, "home", (), (to_first, swap(to_second)), [fields.shape], [])
    return out


def solution(mesh):
    in_specs = (
        P("segment", None, "sec", "depth", None),
        P("segment", "sec", "depth", None),
        P(),
        P(),
        P(),
        P(None, ("sec", "depth")),
        P(("sec", "depth"), None),
        P(("sec", "depth")),
        P(("sec", "depth")),
    )
    out_specs = P("segment", None, "sec", "depth", None)
    return jax.shard_map(
        on_device, mesh=mesh, in_specs=in_specs, out_specs=out_specs, check_vma=False
    )
```

```python
import functools

import jax
import jax.numpy as jnp
from jax import lax
from jax.experimental import pallas as pl
from jax.experimental.pallas import tpu as pltpu
from jax.sharding import PartitionSpec as P

STEPS = 4
F32 = jnp.float32
BF16 = jnp.bfloat16
NT = (((1,), (1,)), ((), ()))


def one_hot(index, count):
    rows = lax.broadcasted_iota(jnp.int32, (count, index.shape[-1]), 0)
    return jnp.where(rows == index, F32(1.0), F32(0.0))


def split3(value):
    high = value.astype(BF16).astype(F32)
    rest = value - high
    mid = rest.astype(BF16).astype(F32)
    return high, mid, rest - mid


def copy_all(sem, pairs):
    copies = [pltpu.make_async_copy(a, b, sem.at[i]) for i, (a, b) in enumerate(pairs)]
    for copy in copies:
        copy.start()
    for copy in copies:
        copy.wait()


def in_line(rows):
    return jnp.concatenate([rows[i : i + 1, :] for i in range(rows.shape[0])], axis=1)


def pack_kernel(layout, fields_in, ids_in, moments_in, owner_in, cells_in, rows_in, packed, entries, *scratch):
    cx, cz, cy = layout
    ids, moments, owner, cells, rows, extra, lines, sem = scratch
    arguments = [(ids_in, ids), (moments_in, moments), (owner_in, owner), (cells_in, cells), (rows_in, rows)]
    fields = pltpu.make_async_copy(fields_in.at[0], packed.at[pl.ds(0, 9)], sem.at[5])
    fields.start()
    copy_all(sem, arguments)
    for i in range(cells.shape[0]):
        at = 8 * i
        lines[at : at + 6] = moments[:, i * cy : (i + 1) * cy]
        lines[at + 6 : at + 7] = owner[i : i + 1, :].astype(F32)
        lines[at + 7 : at + 8] = cells[i : i + 1, :].astype(F32)
    sent = pltpu.make_async_copy(lines, entries, sem.at[6])
    sent.start()
    extra[0] = (ids[0] + 1).astype(F32)
    line = in_line(rows[...])
    high = one_hot(line // cy, cx * cz).astype(BF16)
    low = one_hot(line % cy, cy).astype(BF16)
    count = lax.dot_general(high, low, NT, preferred_element_type=F32)
    extra[1] = count.reshape(cx, cz, cy)
    added = pltpu.make_async_copy(extra, packed.at[pl.ds(9, 2)], sem.at[7])
    added.start()
    for copy in (fields, sent, added):
        copy.wait()


def moment_kernel(layout, *refs):
    cx, cz, cy = layout
    blocks, dense, acc = refs[:-2], *refs[-2:]
    section = lax.axis_index("sec")
    planes = 3 * cx
    half = planes * cz // 2

    @pl.when(lax.axis_index("segment") == 0)
    def _():
        acc[...] = jnp.zeros_like(acc)
        for entries in blocks:
            groups = entries.shape[0] // 8
            chunk = [entries[8 * i : 8 * i + 8] for i in range(groups)]
            entry = jnp.concatenate(chunk, axis=1)
            owner = entry[6:7].astype(jnp.int32)
            cell = entry[7:8].astype(jnp.int32)
            plane = (owner - section + 1) * cx + cell // (cz * cy)
            line = plane * cz + (cell // cy) % cz
            upper = line >= half
            high = one_hot(jnp.where(upper, line - half, line), half)
            low = one_hot(jnp.where(upper, cell % cy + cy, cell % cy), 2 * cy).astype(BF16)
            for part in split3(entry[0:6]):
                spread = [(high * part[c : c + 1]).astype(BF16) for c in range(6)]
                acc[...] += lax.dot_general(
                    jnp.concatenate(spread, axis=0), low, NT, preferred_element_type=F32
                )
        for c in range(6):
            for k in range(2):
                at = slice(k * planes // 2, (k + 1) * planes // 2)
                got = acc[c * half : (c + 1) * half, k * cy : (k + 1) * cy]
                dense[c, at] = got.reshape(planes // 2, cz, cy)


def by_parity(even, odd, act):
    parity = lax.axis_index("sec") % 2

    @pl.when(parity == 0)
    def _():
        act(*even)

    @pl.when(parity == 1)
    def _():
        act(*odd)


def widen_kernel(layout, packed, first, second, dense, kept, swapped, near, far, wide):
    cx, cz, cy = layout
    segment = lax.axis_index("segment")
    planes = 3 * cx

    def place(left, right):
        for i, pack in enumerate((left, packed, right)):
            wide[:, i * cx : (i + 1) * cx] = pack[...]

    by_parity((second, first), (first, second), place)

    @pl.when(segment == 0)
    def _():
        wide[3:9] = wide[3:9] + dense[...]

    def cut(to, first, count):
        comps = to.shape[0]
        for x in range(planes):
            to[:, x * count : (x + 1) * count] = wide[0:comps, x, first : first + count]

    def cut_halo(to, upward):
        spans, lines = halo_rows(cx, upward)
        comps = to.shape[0] // lines
        for x, at, rows in spans:
            first = cz - rows if upward else 0
            for k in range(comps):
                to[k * lines + at : k * lines + at + rows] = wide[k, x, first : first + rows]

    reach = cz // 2 + STEPS

    @pl.when(segment == 0)
    def _():
        cut(kept, 0, reach)
        cut(swapped, cz - reach, reach)
        cut_halo(near, True)
        cut_halo(far, False)

    @pl.when(segment == 1)
    def _():
        cut(kept, cz - reach, reach)
        cut(swapped, 0, reach)
        cut_halo(near, False)
        cut_halo(far, True)


def hold_kernel(block, after, same):
    pass


def halo_rows(cx, upward):
    found, at = [], 0
    for x in range(3 * cx):
        beyond = max(0, cx - x) if upward else max(0, x - 2 * cx + 1)
        found.append((x, at, STEPS - beyond))
        at += STEPS - beyond
    return found, at


def advance(cx, steps, state, coef, times, given_top=False):
    planes, rows, cy = state.shape[2:]
    lane = lax.broadcasted_iota(jnp.int32, (rows, cy), 1)
    first_lane, last_lane = lane == 0, lane == cy - 1

    def back_y(f):
        return f - jnp.where(first_lane, F32(0.0), pltpu.roll(f, 1, 1))

    def back_z(f):
        return f - pltpu.roll(f, 1, 0)

    def fore_y(f):
        return jnp.where(last_lane, F32(0.0), pltpu.roll(f, cy - 1, 1)) - f

    def fore_z(f):
        return pltpu.roll(f, rows - 1, 0) - f

    def velocity(x):
        inc = [None, None]
        for model in range(2):
            sxx, syy, szz, syz, sxz, sxy = (state[model, 3 + k, x] for k in range(6))
            sxx_p, sxz_p, sxy_p = (state[model, k, x - 1] for k in (3, 7, 8))
            hb = coef[model, 0, x]
            inc[model] = (
                hb * ((sxx - sxx_p) + back_y(sxy) + back_z(sxz)),
                hb * ((sxy - sxy_p) + back_y(syy) + back_z(syz)),
                hb * ((sxz - sxz_p) + back_y(syz) + back_z(szz)),
            )
        for k in range(3):
            state[0, k, x] = state[0, k, x] + inc[0][k]
            state[1, k, x] = (state[1, k, x] + inc[1][k]) + times[x] * inc[0][k]

    for step in range(steps):
        left = steps - 1 - step
        low, high = cx - left, 2 * cx + left
        pl.loop(low, high + 1 - (given_top and step == 0))(velocity)

        @pl.loop(low, high)
        def _(x):
            for model in range(2):
                vx, vy, vz = (state[model, k, x] for k in range(3))
                vx_n, vy_n, vz_n = (state[model, k, x + 1] for k in range(3))
                hl, hm = coef[model, 1, x], coef[model, 2, x]
                exx, eyy, ezz = vx_n - vx, fore_y(vy), fore_z(vz)
                pressure = hl * (exx + eyy + ezz)
                twice = hm + hm
                state[model, 3, x] = state[model, 3, x] + (pressure + twice * exx)
                state[model, 4, x] = state[model, 4, x] + (pressure + twice * eyy)
                state[model, 5, x] = state[model, 5, x] + (pressure + twice * ezz)
                state[model, 6, x] = state[model, 6, x] + hm * (fore_z(vy) + fore_y(vz))
                state[model, 7, x] = state[model, 7, x] + hm * (fore_z(vx) + (vz_n - vz))
                state[model, 8, x] = state[model, 8, x] + hm * (fore_y(vx) + (vy_n - vy))

    return velocity


def first_kernel(
    cx, steps, kept, near, far, swapped, buoyancy, lame_lambda, lame_mu,
    to_first, to_second, both, coef, times, state, tables, sem,
):
    segment = lax.axis_index("segment")
    planes, rows, cy = state.shape[2:]
    reach = rows - STEPS
    copies = [
        pltpu.make_async_copy(table, tables.at[i], sem.at[i])
        for i, table in enumerate((buoyancy, lame_lambda, lame_mu))
    ]
    for copy in copies:
        copy.start()

    def join(model, body, halo, upper):
        spans, lines = halo_rows(cx, upper)
        for x, at, count in spans:
            inner = slice(x * reach, (x + 1) * reach)
            to = slice(STEPS, rows) if upper else slice(0, reach)
            edge = slice(STEPS - count, STEPS) if upper else slice(reach, reach + count)
            state[model, :, x, to] = body[0:10, inner]
            for k in range(10):
                state[model, k, x, edge] = halo[k * lines + at : k * lines + at + count]
            if body.shape[0] == 11:
                times[x, to] = body[10, inner]
                times[x, edge] = halo[10 * lines + at : 10 * lines + at + count]

    @pl.when(segment == 0)
    def _():
        join(0, kept, near, True)
        join(1, swapped, far, True)

    @pl.when(segment == 1)
    def _():
        join(1, kept, near, False)
        join(0, swapped, far, False)

    for copy in copies:
        copy.wait()

    @pl.loop(0, planes)
    def _(x):
        for model in range(2):
            ids = state[model, 9, x]
            found = [jnp.zeros((rows, cy), F32)] * 3
            for entry in range(tables.shape[1]):
                hit = ids == F32(entry + 1)
                found = [
                    jnp.where(hit, F32(0.5) * tables[i, entry], found[i]) for i in range(3)
                ]
            for i in range(3):
                coef[model, i, x] = found[i]

    velocity = advance(cx, steps, state, coef, times)
    both[...] = state[:, 0:9, cx : 2 * cx]
    cut_edges(cx, steps, velocity, state, to_first, to_second)


def cut_edges(cx, done, velocity, state, to_first, to_second):
    rows = state.shape[3]
    at = slice(done, rows - done)
    count = rows - 2 * done

    def put(to, place, x, comps):
        for k in comps:
            to[:, place * count : (place + 1) * count] = state[:, k, x, at]
            place += 1
        return place

    def rightward(to):
        place = 0
        for x in range(1, cx):
            place = put(to, place, cx + x, range(9))
        put(to, place, cx, (3, 7, 8))

    def leftward(to):
        place = 0
        for x in range(cx - 1):
            place = put(to, place, cx + x, range(9))
        put(to, place, 2 * cx - 1, range(3))

    by_parity((to_second, to_first), (to_first, to_second), lambda left, right: rightward(right))
    velocity(2 * cx - 1)
    by_parity((to_second, to_first), (to_first, to_second), lambda left, right: leftward(left))


def next_kernel(cx, done, steps, both_in, from_first, from_second, coef, times, *refs):
    segment = lax.axis_index("segment")
    state = refs[-1]
    rows = state.shape[3]
    at = slice(done, rows - done)
    count = rows - 2 * done
    state[:, :, cx : 2 * cx] = both_in[...]

    def get(edge, place, x, comps):
        for k in comps:
            state[:, k, x, at] = edge[:, place * count : (place + 1) * count]
            place += 1
        return place

    def place_edges(left, right):
        place = 0
        for x in range(1, cx):
            place = get(left, place, x, range(9))
        get(left, place, 0, (3, 7, 8))
        place = 0
        for x in range(cx - 1):
            place = get(right, place, 2 * cx + x, range(9))
        get(right, place, 3 * cx - 1, range(3))

    by_parity((from_second, from_first), (from_first, from_second), place_edges)
    velocity = advance(cx, steps, state, coef, times, given_top=True)
    if done + steps == STEPS:
        refs[0][...] = state[segment, :, cx : 2 * cx, STEPS : rows - STEPS]
        refs[1][...] = state[1 - segment, :, cx : 2 * cx, STEPS : rows - STEPS]
    else:
        refs[2][...] = state[:, :, cx : 2 * cx]
        cut_edges(cx, done + steps, velocity, state, refs[0], refs[1])


def home_kernel(mine, brought, out):
    half = mine.shape[2]
    segment = lax.axis_index("segment")

    @pl.when(segment == 0)
    def _():
        out[0, :, :, 0:half] = mine[...]
        out[0, :, :, half:] = brought[...]

    @pl.when(segment == 1)
    def _():
        out[0, :, :, half:] = mine[...]
        out[0, :, :, 0:half] = brought[...]


VMEM = pl.BlockSpec(memory_space=pltpu.VMEM)
HBM = pl.BlockSpec(memory_space=pltpu.HBM)
ANY = pl.BlockSpec(memory_space=pl.ANY)


def call(kernel, name, in_hbm, in_vmem, outs, scratch, copies=0, limit=40 * 2**20, flops=10**7, out_space=VMEM):
    sems = [pltpu.SemaphoreType.DMA((copies,))] * (copies > 0)
    return pl.pallas_call(
        kernel,
        out_shape=[jax.ShapeDtypeStruct(shape, F32) for shape in outs],
        in_specs=[VMEM] * len(in_vmem) + [HBM] * len(in_hbm),
        out_specs=[out_space] * len(outs),
        scratch_shapes=scratch + sems,
        compiler_params=pltpu.CompilerParams(vmem_limit_bytes=limit),
        cost_estimate=pl.CostEstimate(flops=flops, bytes_accessed=2**20, transcendentals=0),
        name=name,
    )(*in_vmem, *in_hbm)


def on_device(
    fields, block_ids, buoyancy, lame_lambda, lame_mu, moments, moment_owner, moment_cells, drm_rows
):
    sections, slabs = lax.axis_size("sec"), lax.axis_size("depth")
    layout = cx, cz, cy = fields.shape[2:]
    planes = 3 * cx
    reach, rows = cz // 2 + STEPS, cz // 2 + 2 * STEPS
    assert cx > 1 and STEPS % cx == 0

    def pairs(block, start):
        route = [(i, i + 1) for i in range(start, sections - 1, 2)]
        return lax.ppermute(block, "sec", route + [(j, i) for i, j in route])

    def other(section, k):
        return section ^ k if sections & (sections - 1) == 0 else (section + k) % sections

    def halo(block, core_zero_goes, flip):
        route = []
        for i in range(slabs):
            for core in range(2):
                to = i + (core_zero_goes if core == 0 else -core_zero_goes)
                if 0 <= to < slabs:
                    route.append((2 * i + core, 2 * to + (1 - core if flip else core)))
        return lax.ppermute(block, ("depth", "segment"), route)

    def swap(block):
        return lax.ppermute(block, "segment", [(0, 1), (1, 0)])

    owner = moment_owner.reshape(-1, cy)
    cells = moment_cells.reshape(-1, cy)
    boundary = drm_rows.reshape(-1, cy)
    small = (block_ids, moments, owner, cells, boundary)
    entry_lines = 8 * cells.shape[0]
    packed, entries = call(
        functools.partial(pack_kernel, layout),
        "pack",
        (fields, *small),
        (),
        [(11, cx, cz, cy), (entry_lines, cy)],
        [pltpu.VMEM(a.shape, a.dtype) for a in small]
        + [pltpu.VMEM((2, cx, cz, cy), F32), pltpu.VMEM((entry_lines, cy), F32)],
        8,
        limit=64 * 2**20,
        out_space=HBM,
    )
    blocks = [
        lax.ppermute(entries, "sec", [(other(i, k), i) for i in range(sections)])
        for k in range(1, sections)
    ]
    first, second = pairs(packed, 0), pairs(packed, 1)
    half = planes * cz // 2

    def halo_shape(comps):
        return (-(-comps * halo_rows(cx, True)[1] // 8) * 8, cy)

    (dense,) = call(
        functools.partial(moment_kernel, layout),
        "moments",
        (),
        [entries, *blocks],
        [(6, planes, cz, cy)],
        [pltpu.VMEM((6 * half, 2 * cy), F32)],
        flops=2 * 18 * half * 2 * cy * sections * moments.shape[1],
    )
    kept, swapped, near, far = call(
        functools.partial(widen_kernel, layout),
        "widen",
        (),
        (packed, first, second, dense),
        [(11, planes * reach, cy), (10, planes * reach, cy), halo_shape(11), halo_shape(10)],
        [pltpu.VMEM((11, planes, cz, cy), F32)],
    )
    near, far = halo(near, 1, False), halo(far, -1, True)
    swapped = pl.pallas_call(
        hold_kernel,
        out_shape=jax.ShapeDtypeStruct(swapped.shape, F32),
        in_specs=[ANY, ANY],
        out_specs=ANY,
        input_output_aliases={0: 0},
        name="hold",
    )(swapped, near)
    swapped = swap(swapped)
    both_shape = (2, 9, cx, rows, cy)
    coef_shape, times_shape = (2, 3, planes, rows, cy), (planes, rows, cy)

    def edge_shape(done):
        return (2, (9 * (cx - 1) + 3) * (rows - 2 * done), cy)

    done = cx
    to_first, to_second, both, coef, times = call(
        functools.partial(first_kernel, cx, cx),
        "first_steps",
        (buoyancy, lame_lambda, lame_mu),
        (kept, near, far, swapped),
        [edge_shape(done)] * 2 + [both_shape, coef_shape, times_shape],
        [
            pltpu.VMEM((2, 10, planes, rows, cy), F32),
            pltpu.SMEM((3, buoyancy.shape[0]), F32),
        ],
        3,
    )
    while done < STEPS:
        first, second = pairs(to_first, 0), pairs(to_second, 1)
        after = done + cx
        half_block = (9, cx, cz // 2, cy)
        got = call(
            functools.partial(next_kernel, cx, done, cx),
            "next_steps",
            (),
            (both, first, second, coef, times),
            [half_block] * 2 if after == STEPS else [edge_shape(after)] * 2 + [both_shape],
            [pltpu.VMEM((2, 9, planes, rows, cy), F32)],
        )
        to_first, to_second, both = got[0], got[1], got[-1]
        done = after
    (out,) = call(home_kernel, "home", (), (to_first, swap(to_second)), [fields.shape], [])
    return out


def solution(mesh):
    in_specs = (
        P("segment", None, "sec", "depth", None),
        P("segment", "sec", "depth", None),
        P(),
        P(),
        P(),
        P(None, ("sec", "depth")),
        P(("sec", "depth"), None),
        P(("sec", "depth")),
        P(("sec", "depth")),
    )
    out_specs = P("segment", None, "sec", "depth", None)
    return jax.shard_map(
        on_device, mesh=mesh, in_specs=in_specs, out_specs=out_specs, check_vma=False
    )
```

```python
import functools

import jax
import jax.numpy as jnp
from jax import lax
from jax.experimental import pallas as pl
from jax.experimental.pallas import tpu as pltpu
from jax.sharding import PartitionSpec as P

STEPS = 4
F32 = jnp.float32
BF16 = jnp.bfloat16
NT = (((1,), (1,)), ((), ()))


def one_hot(index, count):
    rows = lax.broadcasted_iota(jnp.int32, (count, index.shape[-1]), 0)
    return jnp.where(rows == index, F32(1.0), F32(0.0))


def split3(value):
    high = value.astype(BF16).astype(F32)
    rest = value - high
    mid = rest.astype(BF16).astype(F32)
    return high, mid, rest - mid


def copy_all(sem, pairs):
    copies = [pltpu.make_async_copy(a, b, sem.at[i]) for i, (a, b) in enumerate(pairs)]
    for copy in copies:
        copy.start()
    for copy in copies:
        copy.wait()


def in_line(rows):
    return jnp.concatenate([rows[i : i + 1, :] for i in range(rows.shape[0])], axis=1)


def reach_of(cz):
    return cz // 2 + STEPS


def pack_kernel(
    fields_in, ids_in, moments_in, owner_in, cells_in, rows_in, buoyancy, lame_lambda, lame_mu,
    entries, kept, given, fields, ids, moments, owner, cells, rows, wide, tables, sem,
):
    cx, cz, cy = ids.shape[1:]
    arguments = [(fields_in, fields), (ids_in, ids), (moments_in, moments), (owner_in, owner)]
    arguments += [(cells_in, cells), (rows_in, rows)]
    arguments += [(t, tables.at[i]) for i, t in enumerate((buoyancy, lame_lambda, lame_mu))]
    copy_all(sem, arguments)
    for i in range(cells.shape[0]):
        at = 8 * i
        entries[at : at + 6] = moments[:, i * cy : (i + 1) * cy]
        entries[at + 6 : at + 7] = owner[i : i + 1, :].astype(F32)
        entries[at + 7 : at + 8] = cells[i : i + 1, :].astype(F32)
    wide[0] = (ids[0] + 1).astype(F32)
    line = in_line(rows[...])
    high = one_hot(line // cy, cx * cz).astype(BF16)
    low = one_hot(line % cy, cy).astype(BF16)
    count = lax.dot_general(high, low, NT, preferred_element_type=F32)
    wide[1] = count.reshape(cx, cz, cy)
    reach = reach_of(cz)
    lines = 11 * cx * reach
    lane = lax.broadcasted_iota(jnp.int32, (1, cy), 1)
    for i in range(3):
        found = jnp.zeros((1, cy), F32)
        for entry in range(tables.shape[1]):
            found = jnp.where(lane == entry + 1, F32(0.5) * tables[i, entry], found)
        kept[lines + i : lines + i + 1] = found
    kept[lines + 3 : lines + 8] = jnp.zeros((5, cy), F32)
    kept[lines + 8 :] = entries[...]

    def cut(first, other):
        for x in range(cx):
            at = slice(x * reach, (x + 1) * reach)
            for k in range(11):
                source = fields.at[0, k] if k < 9 else wide.at[k - 9]
                line = (k * cx + x) * reach
                kept[line : line + reach] = source[x, first : first + reach]
            given[0:9, at] = fields[0, :, x, other : other + reach]
            given[9, at] = wide[0, x, other : other + reach]

    @pl.when(lax.axis_index("segment") == 0)
    def _():
        cut(0, cz - reach)

    @pl.when(lax.axis_index("segment") == 1)
    def _():
        cut(cz - reach, 0)


def add_moments(layout, blocks, acc):
    cx, cz, cy = layout
    section = lax.axis_index("sec")
    half = cx * cz // 2
    for entries in blocks:
        chunk = [entries[8 * i : 8 * i + 8] for i in range(entries.shape[0] // 8)]
        entry = jnp.concatenate(chunk, axis=1)
        owner = entry[6:7].astype(jnp.int32)
        cell = entry[7:8].astype(jnp.int32)
        line = jnp.where(owner == section, cell // cy, -1)
        upper = line >= half
        high = one_hot(jnp.where(upper, line - half, line), half)
        low = one_hot(jnp.where(upper, cell % cy + cy, cell % cy), 2 * cy).astype(BF16)
        for part in split3(entry[0:6]):
            spread = [(high * part[c : c + 1]).astype(BF16) for c in range(6)]
            acc[...] += lax.dot_general(
                jnp.concatenate(spread, axis=0), low, NT, preferred_element_type=F32
            )


def own_kernel(layout, kept, out, tables, acc):
    lines = out.shape[0] * out.shape[1]
    out[...] = kept[0:lines].reshape(out.shape)
    tables[...] = kept[lines : lines + 8]
    acc[...] = jnp.zeros_like(acc)
    add_moments(layout, [kept.at[pl.ds(lines + 8, kept.shape[0] - lines - 8)]], acc)


def join_kernel(layout, *refs):
    cx, cz, cy = layout
    kept, got, started, blocks = refs[0], refs[1], refs[2], refs[3:-5]
    body, count, edge, acc, dense = refs[-5:]
    reach = reach_of(cz)
    half = cx * cz // 2
    acc[...] = started[...]
    add_moments(layout, blocks, acc)
    for c in range(6):
        for k in range(2):
            added = acc[c * half : (c + 1) * half, k * cy : (k + 1) * cy]
            dense[c, k * half : (k + 1) * half] = added
    count[...] = kept[10]

    def join(mine, first, sent):
        body[mine] = kept[0:10]
        body[1 - mine] = got[...]
        for x in range(cx):
            at = slice(x * reach, (x + 1) * reach)
            added = dense[:, x * cz + first : x * cz + first + reach]
            body[0, 3:9, at] = body[0, 3:9, at] + added
        for x in range(cx):
            row = x * reach + sent
            for k in range(21):
                at = slice((k * cx + x) * STEPS, (k * cx + x + 1) * STEPS)
                if k < 20:
                    edge[at] = body[k // 10, k % 10, row : row + STEPS]
                else:
                    edge[at] = count[row : row + STEPS]

    @pl.when(lax.axis_index("segment") == 0)
    def _():
        join(0, 0, 0)

    @pl.when(lax.axis_index("segment") == 1)
    def _():
        join(1, cz - reach, reach - STEPS)


def by_parity(even, odd, act):
    parity = lax.axis_index("sec") % 2

    @pl.when(parity == 0)
    def _():
        act(*even)

    @pl.when(parity == 1)
    def _():
        act(*odd)


def advance(cx, steps, state, coef, times, given_top=False):
    planes, rows, cy = state.shape[2:]
    lane = lax.broadcasted_iota(jnp.int32, (rows, cy), 1)
    first_lane, last_lane = lane == 0, lane == cy - 1

    def back_y(f):
        return f - jnp.where(first_lane, F32(0.0), pltpu.roll(f, 1, 1))

    def back_z(f):
        return f - pltpu.roll(f, 1, 0)

    def fore_y(f):
        return jnp.where(last_lane, F32(0.0), pltpu.roll(f, cy - 1, 1)) - f

    def fore_z(f):
        return pltpu.roll(f, rows - 1, 0) - f

    def velocity(x):
        inc = [None, None]
        for model in range(2):
            sxx, syy, szz, syz, sxz, sxy = (state[model, 3 + k, x] for k in range(6))
            sxx_p, sxz_p, sxy_p = (state[model, k, x - 1] for k in (3, 7, 8))
            hb = coef[model, 0, x]
            inc[model] = (
                hb * ((sxx - sxx_p) + back_y(sxy) + back_z(sxz)),
                hb * ((sxy - sxy_p) + back_y(syy) + back_z(syz)),
                hb * ((sxz - sxz_p) + back_y(syz) + back_z(szz)),
            )
        for k in range(3):
            state[0, k, x] = state[0, k, x] + inc[0][k]
            state[1, k, x] = (state[1, k, x] + inc[1][k]) + times[x] * inc[0][k]

    for step in range(steps):
        left = steps - 1 - step
        low, high = cx - left, 2 * cx + left
        pl.loop(low, high + 1 - (given_top and step == 0))(velocity)

        @pl.loop(low, high)
        def _(x):
            for model in range(2):
                vx, vy, vz = (state[model, k, x] for k in range(3))
                vx_n, vy_n, vz_n = (state[model, k, x + 1] for k in range(3))
                hl, hm = coef[model, 1, x], coef[model, 2, x]
                exx, eyy, ezz = vx_n - vx, fore_y(vy), fore_z(vz)
                pressure = hl * (exx + eyy + ezz)
                twice = hm + hm
                state[model, 3, x] = state[model, 3, x] + (pressure + twice * exx)
                state[model, 4, x] = state[model, 4, x] + (pressure + twice * eyy)
                state[model, 5, x] = state[model, 5, x] + (pressure + twice * ezz)
                state[model, 6, x] = state[model, 6, x] + hm * (fore_z(vy) + fore_y(vz))
                state[model, 7, x] = state[model, 7, x] + hm * (fore_z(vx) + (vz_n - vz))
                state[model, 8, x] = state[model, 8, x] + hm * (fore_y(vx) + (vy_n - vy))

    return velocity


def look_up(tables, ids):
    lanes = ids.astype(jnp.int32)
    wide = [jnp.broadcast_to(tables[i : i + 1], ids.shape) for i in range(3)]
    return [jnp.take_along_axis(table, lanes, axis=1) for table in wide]


def edge_units(cx, with_ids):
    right, left = [], []
    for model in range(2):
        whole = list(range(10 if with_ids else 9)) + [10] * (with_ids and model == 1)
        for x in range(cx - 1):
            right += [(model, what, x + 1) for what in whole]
            left += [(model, what, x) for what in whole]
        right += [(model, what, 0) for what in (3, 7, 8)]
        left += [(model, what, cx - 1) for what in range(3)]
    return right, left


def cut_edges(cx, done, with_ids, velocity, state, ids, times, to_first, to_second):
    rows = state.shape[3]
    at = slice(done, rows - done)
    count = rows - 2 * done
    right_units, left_units = edge_units(cx, with_ids)

    def put(to, units):
        for i, (model, what, x) in enumerate(units):
            line = slice(i * count, (i + 1) * count)
            if what == 10:
                to[line] = times[cx + x, at]
            elif what == 9:
                to[line] = ids[model, cx + x, at]
            else:
                to[line] = state[model, what, cx + x, at]

    holders = (to_second, to_first), (to_first, to_second)
    by_parity(*holders, lambda left, right: put(right, right_units))
    velocity(2 * cx - 1)
    by_parity(*holders, lambda left, right: put(left, left_units))


def planes_kernel(
    cx, body, count, halo, tables,
    to_first, to_second, both, coef_out, times_out, state, ids, coef, times,
):
    rows = state.shape[3]
    reach = rows - STEPS

    def join(main, edge):
        for x in range(cx):
            inner = slice(x * reach, (x + 1) * reach)
            for k in range(21):
                outer = halo[(k * cx + x) * STEPS : (k * cx + x + 1) * STEPS]
                model, what = k // 10, k % 10
                if k == 20:
                    times[cx + x, main] = count[inner]
                    times[cx + x, edge] = outer
                elif what == 9:
                    ids[model, cx + x, main] = body[model, what, inner]
                    ids[model, cx + x, edge] = outer
                else:
                    state[model, what, cx + x, main] = body[model, what, inner]
                    state[model, what, cx + x, edge] = outer

    @pl.when(lax.axis_index("segment") == 0)
    def _():
        join(slice(STEPS, rows), slice(0, STEPS))

    @pl.when(lax.axis_index("segment") == 1)
    def _():
        join(slice(0, reach), slice(reach, rows))

    for model in range(2):
        for x in range(cx, 2 * cx):
            for i, found in enumerate(look_up(tables, ids[model, x])):
                coef[model, i, x] = found
    own = slice(cx, 2 * cx)
    both[...] = state[:, :, own]
    coef_out[...] = coef[:, :, own]
    times_out[...] = times[own]
    velocity = advance(cx, 0, state, coef, times)
    cut_edges(cx, 0, True, velocity, state, ids, times, to_first, to_second)


def next_kernel(cx, done, *refs):
    first = done == 0
    both_in, from_first, from_second, coef_in, times_in = refs[0:5]
    if first:
        tables = refs[5]
        state, ids, coef, times = refs[-4:]
    else:
        state, coef, times = refs[-1], coef_in, times_in
    outs = refs[6 if first else 5 :]
    segment = lax.axis_index("segment")
    rows = state.shape[3]
    at = slice(done, rows - done)
    count = rows - 2 * done
    own = slice(cx, 2 * cx)
    state[:, :, own] = both_in[...]
    right_units, left_units = edge_units(cx, first)

    def get(edge, units, start):
        for i, (model, what, x) in enumerate(units):
            line = edge[i * count : (i + 1) * count]
            if what == 10:
                times[start + x, at] = line
            elif what == 9:
                ids[model, start + x, at] = line
            else:
                state[model, what, start + x, at] = line

    def place(left, right):
        get(left, right_units, 0)
        get(right, left_units, 2 * cx)

    by_parity((from_second, from_first), (from_first, from_second), place)
    if first:
        coef[:, :, own] = coef_in[...]
        times[own] = times_in[...]
        for model in range(2):
            for x in (*range(1, cx), *range(2 * cx, 3 * cx - 1)):
                for i, found in enumerate(look_up(tables, ids[model, x])):
                    coef[model, i, x] = found
    velocity = advance(cx, cx, state, coef, times, given_top=True)
    if done + cx == STEPS:
        outs[0][...] = state[segment, :, own, STEPS : rows - STEPS]
        outs[1][...] = state[1 - segment, :, own, STEPS : rows - STEPS]
    else:
        outs[2][...] = state[:, :, own]
        if first:
            outs[3][...] = coef[...]
            outs[4][...] = times[...]
        cut_edges(cx, done + cx, False, velocity, state, None, times, outs[0], outs[1])


def home_kernel(mine, brought, out):
    half = mine.shape[2]
    segment = lax.axis_index("segment")

    @pl.when(segment == 0)
    def _():
        out[0, :, :, 0:half] = mine[...]
        out[0, :, :, half:] = brought[...]

    @pl.when(segment == 1)
    def _():
        out[0, :, :, half:] = mine[...]
        out[0, :, :, 0:half] = brought[...]


VMEM = pl.BlockSpec(memory_space=pltpu.VMEM)
HBM = pl.BlockSpec(memory_space=pltpu.HBM)


def call(kernel, name, in_vmem, in_hbm, outs, scratch, copies=0, limit=40 * 2**20, flops=10**7):
    sems = [pltpu.SemaphoreType.DMA((copies,))] * (copies > 0)
    return pl.pallas_call(
        kernel,
        out_shape=[jax.ShapeDtypeStruct(shape, F32) for shape in outs],
        in_specs=[VMEM] * len(in_vmem) + [HBM] * len(in_hbm),
        out_specs=[VMEM] * len(outs),
        scratch_shapes=[pltpu.VMEM(s, F32) if isinstance(s, tuple) else s for s in scratch] + sems,
        compiler_params=pltpu.CompilerParams(vmem_limit_bytes=limit),
        cost_estimate=pl.CostEstimate(flops=flops, bytes_accessed=2**20, transcendentals=0),
        name=name,
    )(*in_vmem, *in_hbm)


def on_device(
    fields, block_ids, buoyancy, lame_lambda, lame_mu, moments, moment_owner, moment_cells, drm_rows
):
    sections, slabs = lax.axis_size("sec"), lax.axis_size("depth")
    layout = cx, cz, cy = fields.shape[2:]
    reach, rows = reach_of(cz), cz // 2 + 2 * STEPS
    assert cx > 1 and STEPS % cx == 0

    def pairs(block, start):
        route = [(i, i + 1) for i in range(start, sections - 1, 2)]
        return lax.ppermute(block, "sec", route + [(j, i) for i, j in route])

    def other(section, k):
        return section ^ k if sections & (sections - 1) == 0 else (section + k) % sections

    def along_depth(block):
        down = [(2 * i + 1, 2 * (i + 1)) for i in range(slabs - 1)]
        return lax.ppermute(block, ("depth", "segment"), down + [(j, i) for i, j in down])

    def swap(block):
        return lax.ppermute(block, "segment", [(0, 1), (1, 0)])

    owner = moment_owner.reshape(-1, cy)
    cells = moment_cells.reshape(-1, cy)
    arguments = (fields, block_ids, moments, owner, cells, drm_rows.reshape(-1, cy))
    entry_lines = 8 * cells.shape[0]
    entries, kept, given = call(
        pack_kernel,
        "pack",
        (),
        (*arguments, buoyancy, lame_lambda, lame_mu),
        [(entry_lines, cy), (11 * cx * reach + 8 + entry_lines, cy), (10, cx * reach, cy)],
        [pltpu.VMEM(a.shape, a.dtype) for a in arguments]
        + [(2, cx, cz, cy), pltpu.SMEM((3, buoyancy.shape[0]), F32)],
        len(arguments) + 3,
        limit=64 * 2**20,
    )
    blocks = [
        lax.ppermute(entries, "sec", [(other(i, k), i) for i in range(sections)])
        for k in range(1, sections)
    ]
    got = swap(given)
    acc_shape = (6 * cx * cz // 2, 2 * cy)
    kept, tables, started = call(
        functools.partial(own_kernel, layout),
        "own_moments",
        (kept,),
        (),
        [(11, cx * reach, cy), (8, cy), acc_shape],
        [],
        flops=10**9,
    )
    body, count, edge = call(
        functools.partial(join_kernel, layout),
        "join_and_moments",
        (kept, got, started, *blocks),
        (),
        [(2, 10, cx * reach, cy), (cx * reach, cy), (21 * cx * STEPS, cy)],
        [acc_shape, (6, cx * cz, cy)],
    )
    halo = along_depth(edge)
    own = (cx, rows, cy)
    window = (3 * cx, rows, cy)

    def edges(done):
        units = edge_units(cx, done == 0)[0]
        return [(len(units) * (rows - 2 * done), cy)] * 2

    to_first, to_second, both, coef, times = call(
        functools.partial(planes_kernel, cx),
        "own_planes",
        (body, count, halo, tables),
        (),
        edges(0) + [(2, 9, *own), (2, 3, *own), own],
        [(2, 9, *window), (2, *window), (2, 3, *window), window],
    )
    for done in range(0, STEPS, cx):
        from_first, from_second = pairs(to_first, 0), pairs(to_second, 1)
        first, last = done == 0, done + cx == STEPS
        outs = [(9, cx, cz // 2, cy)] * 2 if last else edges(done + cx) + [(2, 9, *own)]
        if first:
            outs = outs + [(2, 3, *window), window]
        space = [(2, 9, *window)]
        if first:
            space += [(2, *window), (2, 3, *window), window]
        done_now = call(
            functools.partial(next_kernel, cx, done),
            "steps",
            (both, from_first, from_second, coef, times) + (tables,) * first,
            (),
            outs,
            space,
        )
        to_first, to_second = done_now[0:2]
        if first:
            coef, times = done_now[3:5]
        both = done_now[-1] if not first else done_now[2]
    (out,) = call(home_kernel, "home", (to_first, swap(to_second)), (), [fields.shape], [])
    return out


def solution(mesh):
    in_specs = (
        P("segment", None, "sec", "depth", None),
        P("segment", "sec", "depth", None),
        P(),
        P(),
        P(),
        P(None, ("sec", "depth")),
        P(("sec", "depth"), None),
        P(("sec", "depth")),
        P(("sec", "depth")),
    )
    out_specs = P("segment", None, "sec", "depth", None)
    return jax.shard_map(
        on_device, mesh=mesh, in_specs=in_specs, out_specs=out_specs, check_vma=False
    )
```

```python
import functools

import jax
import jax.numpy as jnp
from jax import lax
from jax.experimental import pallas as pl
from jax.experimental.pallas import tpu as pltpu
from jax.sharding import PartitionSpec as P

STEPS = 4
F32 = jnp.float32
BF16 = jnp.bfloat16
NT = (((1,), (1,)), ((), ()))


def one_hot(index, count):
    rows = lax.broadcasted_iota(jnp.int32, (count, index.shape[-1]), 0)
    return jnp.where(rows == index, F32(1.0), F32(0.0))


def split3(value):
    high = value.astype(BF16).astype(F32)
    rest = value - high
    mid = rest.astype(BF16).astype(F32)
    return high, mid, rest - mid


def copy_all(sem, pairs):
    copies = [pltpu.make_async_copy(a, b, sem.at[i]) for i, (a, b) in enumerate(pairs)]
    for copy in copies:
        copy.start()
    for copy in copies:
        copy.wait()


def in_line(rows):
    return jnp.concatenate([rows[i : i + 1, :] for i in range(rows.shape[0])], axis=1)


def reach_of(cz):
    return cz // 2 + STEPS


def pack_kernel(
    fields_in, ids_in, moments_in, owner_in, cells_in, rows_in, buoyancy, lame_lambda, lame_mu,
    entries, kept, given, fields, ids, moments, owner, cells, rows, wide, tables, sem,
):
    cx, cz, cy = ids.shape[1:]
    arguments = [(fields_in, fields), (ids_in, ids), (moments_in, moments), (owner_in, owner)]
    arguments += [(cells_in, cells), (rows_in, rows)]
    arguments += [(t, tables.at[i]) for i, t in enumerate((buoyancy, lame_lambda, lame_mu))]
    copy_all(sem, arguments)
    for i in range(cells.shape[0]):
        at = 8 * i
        entries[at : at + 6] = moments[:, i * cy : (i + 1) * cy]
        entries[at + 6 : at + 7] = owner[i : i + 1, :].astype(F32)
        entries[at + 7 : at + 8] = cells[i : i + 1, :].astype(F32)
    wide[0] = (ids[0] + 1).astype(F32)
    line = in_line(rows[...])
    high = one_hot(line // cy, cx * cz).astype(BF16)
    low = one_hot(line % cy, cy).astype(BF16)
    count = lax.dot_general(high, low, NT, preferred_element_type=F32)
    wide[1] = count.reshape(cx, cz, cy)
    reach = reach_of(cz)
    lines = 11 * cx * reach
    lane = lax.broadcasted_iota(jnp.int32, (1, cy), 1)
    for i in range(3):
        found = jnp.zeros((1, cy), F32)
        for entry in range(tables.shape[1]):
            found = jnp.where(lane == entry + 1, F32(0.5) * tables[i, entry], found)
        kept[lines + i : lines + i + 1] = found
    kept[lines + 3 : lines + 8] = jnp.zeros((5, cy), F32)
    kept[lines + 8 :] = entries[...]

    def cut(first, other):
        for x in range(cx):
            at = slice(x * reach, (x + 1) * reach)
            for k in range(11):
                source = fields.at[0, k] if k < 9 else wide.at[k - 9]
                line = (k * cx + x) * reach
                kept[line : line + reach] = source[x, first : first + reach]
            given[0:9, at] = fields[0, :, x, other : other + reach]
            given[9, at] = wide[0, x, other : other + reach]

    @pl.when(lax.axis_index("segment") == 0)
    def _():
        cut(0, cz - reach)

    @pl.when(lax.axis_index("segment") == 1)
    def _():
        cut(cz - reach, 0)


def add_moments(layout, blocks, acc):
    cx, cz, cy = layout
    section = lax.axis_index("sec")
    half = cx * cz // 2
    for entries in blocks:
        chunk = [entries[8 * i : 8 * i + 8] for i in range(entries.shape[0] // 8)]
        entry = jnp.concatenate(chunk, axis=1)
        owner = entry[6:7].astype(jnp.int32)
        cell = entry[7:8].astype(jnp.int32)
        line = jnp.where(owner == section, cell // cy, -1)
        upper = line >= half
        high = one_hot(jnp.where(upper, line - half, line), half)
        low = one_hot(jnp.where(upper, cell % cy + cy, cell % cy), 2 * cy).astype(BF16)
        for part in split3(entry[0:6]):
            spread = [(high * part[c : c + 1]).astype(BF16) for c in range(6)]
            acc[...] += lax.dot_general(
                jnp.concatenate(spread, axis=0), low, NT, preferred_element_type=F32
            )


def own_kernel(layout, kept, out, tables, acc):
    lines = out.shape[0] * out.shape[1]
    out[...] = kept[0:lines].reshape(out.shape)
    tables[...] = kept[lines : lines + 8]
    acc[...] = jnp.zeros_like(acc)
    add_moments(layout, [kept.at[pl.ds(lines + 8, kept.shape[0] - lines - 8)]], acc)


def by_core(act):
    segment = lax.axis_index("segment")

    @pl.when(segment == 0)
    def _():
        act(0, lambda reach: slice(STEPS, STEPS + reach), lambda reach: slice(0, STEPS))

    @pl.when(segment == 1)
    def _():
        act(1, lambda reach: slice(0, reach), lambda reach: slice(reach, reach + STEPS))


def join_kernel(layout, *refs):
    cx, cz, cy = layout
    kept, got, started, blocks = refs[0], refs[1], refs[2], refs[3:-6]
    state, ids, times, edge, acc, dense = refs[-6:]
    reach = reach_of(cz)
    half = cx * cz // 2
    acc[...] = started[...]
    add_moments(layout, blocks, acc)
    for c in range(6):
        for k in range(2):
            added = acc[c * half : (c + 1) * half, k * cy : (k + 1) * cy]
            dense[c, k * half : (k + 1) * half] = added

    def join(mine, main, outer):
        main, outer = main(reach), outer(reach)
        first = 0 if mine == 0 else cz - reach
        last = main.start if mine == 0 else main.stop - STEPS
        gone = slice(last, last + STEPS)
        for x in range(cx):
            at = slice(x * reach, (x + 1) * reach)
            for model in range(2):
                rows = kept if model == mine else got
                state[model, :, x, main] = rows[0:9, at]
                ids[model, x, main] = rows[9, at]
            added = dense[:, x * cz + first : x * cz + first + reach]
            state[0, 3:9, x, main] = state[0, 3:9, x, main] + added
            times[x, main] = kept[10, at]
            state[:, :, x, outer] = jnp.zeros((2, 9, STEPS, cy), F32)
            ids[:, x, outer] = jnp.zeros((2, STEPS, cy), F32)
            times[x, outer] = jnp.zeros((STEPS, cy), F32)
            for k in range(21):
                line = slice((k * cx + x) * STEPS, (k * cx + x + 1) * STEPS)
                if k == 20:
                    edge[line] = times[x, gone]
                elif k % 10 == 9:
                    edge[line] = ids[k // 10, x, gone]
                else:
                    edge[line] = state[k // 10, k % 10, x, gone]

    by_core(join)


def by_parity(even, odd, act):
    parity = lax.axis_index("sec") % 2

    @pl.when(parity == 0)
    def _():
        act(*even)

    @pl.when(parity == 1)
    def _():
        act(*odd)


def advance(cx, steps, state, coef, times, given_top=False):
    planes, rows, cy = state.shape[2:]
    lane = lax.broadcasted_iota(jnp.int32, (rows, cy), 1)
    first_lane, last_lane = lane == 0, lane == cy - 1

    def back_y(f):
        return f - jnp.where(first_lane, F32(0.0), pltpu.roll(f, 1, 1))

    def back_z(f):
        return f - pltpu.roll(f, 1, 0)

    def fore_y(f):
        return jnp.where(last_lane, F32(0.0), pltpu.roll(f, cy - 1, 1)) - f

    def fore_z(f):
        return pltpu.roll(f, rows - 1, 0) - f

    def velocity(x):
        inc = [None, None]
        for model in range(2):
            sxx, syy, szz, syz, sxz, sxy = (state[model, 3 + k, x] for k in range(6))
            sxx_p, sxz_p, sxy_p = (state[model, k, x - 1] for k in (3, 7, 8))
            hb = coef[model, 0, x]
            inc[model] = (
                hb * ((sxx - sxx_p) + back_y(sxy) + back_z(sxz)),
                hb * ((sxy - sxy_p) + back_y(syy) + back_z(syz)),
                hb * ((sxz - sxz_p) + back_y(syz) + back_z(szz)),
            )
        for k in range(3):
            state[0, k, x] = state[0, k, x] + inc[0][k]
            state[1, k, x] = (state[1, k, x] + inc[1][k]) + times[x] * inc[0][k]

    for step in range(steps):
        left = steps - 1 - step
        low, high = cx - left, 2 * cx + left
        pl.loop(low, high + 1 - (given_top and step == 0))(velocity)

        @pl.loop(low, high)
        def _(x):
            for model in range(2):
                vx, vy, vz = (state[model, k, x] for k in range(3))
                vx_n, vy_n, vz_n = (state[model, k, x + 1] for k in range(3))
                hl, hm = coef[model, 1, x], coef[model, 2, x]
                exx, eyy, ezz = vx_n - vx, fore_y(vy), fore_z(vz)
                pressure = hl * (exx + eyy + ezz)
                twice = hm + hm
                state[model, 3, x] = state[model, 3, x] + (pressure + twice * exx)
                state[model, 4, x] = state[model, 4, x] + (pressure + twice * eyy)
                state[model, 5, x] = state[model, 5, x] + (pressure + twice * ezz)
                state[model, 6, x] = state[model, 6, x] + hm * (fore_z(vy) + fore_y(vz))
                state[model, 7, x] = state[model, 7, x] + hm * (fore_z(vx) + (vz_n - vz))
                state[model, 8, x] = state[model, 8, x] + hm * (fore_y(vx) + (vy_n - vy))

    return velocity


def look_up(tables, ids):
    lanes = ids.astype(jnp.int32)
    wide = [jnp.broadcast_to(tables[i : i + 1], ids.shape) for i in range(3)]
    return [jnp.take_along_axis(table, lanes, axis=1) for table in wide]


def edge_units(cx, with_ids):
    right, left = [], []
    for model in range(2):
        whole = list(range(10 if with_ids else 9)) + [10] * (with_ids and model == 1)
        for x in range(cx - 1):
            right += [(model, what, x + 1) for what in whole]
            left += [(model, what, x) for what in whole]
        right += [(model, what, 0) for what in (3, 7, 8)]
        left += [(model, what, cx - 1) for what in range(3)]
    return right, left


def cut_edges(cx, rows_of, with_ids, velocity, state, ids, times, to_first, to_second):
    right_units, left_units = edge_units(cx, with_ids)

    def put(to, units, new_plane):
        for i, (model, what, x) in enumerate(units):
            at = rows_of(x == new_plane)
            count = at.stop - at.start
            line = slice(i * count, (i + 1) * count)
            if what == 10:
                to[line] = times[cx + x, at]
            elif what == 9:
                to[line] = ids[model, cx + x, at]
            else:
                to[line] = state[model, what, cx + x, at]

    holders = (to_second, to_first), (to_first, to_second)
    by_parity(*holders, lambda left, right: put(right, right_units, -1))
    velocity(2 * cx - 1)
    by_parity(*holders, lambda left, right: put(left, left_units, cx - 1))


def outer_rows(mine, outer):
    def rows_of(new):
        shift = 1 if new and mine == 0 else 0
        return slice(outer.start + shift, outer.stop + shift)

    return rows_of


def coefficients(cx, planes, tables, ids, coef):
    for model in range(2):
        for x in planes:
            for i, found in enumerate(look_up(tables, ids[model, x])):
                coef[model, i, x] = found


def inner_kernel(cx, own_state, own_ids, own_times, tables, to_first, to_second, state, ids, coef, times):
    own = slice(cx, 2 * cx)
    reach = state.shape[3] - STEPS
    state[:, :, own], ids[:, own], times[own] = own_state[...], own_ids[...], own_times[...]
    coefficients(cx, range(2 * cx - 1, 2 * cx), tables, ids, coef)
    velocity = advance(cx, 0, state, coef, times)

    def cut(mine, main, outer):
        rows_of = lambda new: main(reach)
        cut_edges(cx, rows_of, True, velocity, state, ids, times, to_first, to_second)

    by_core(cut)


def outer_kernel(
    cx, own_state, own_ids, own_times, halo, tables,
    to_first, to_second, both, coef_out, times_out, state, ids, coef, times,
):
    own = slice(cx, 2 * cx)
    reach = state.shape[3] - STEPS
    state[:, :, own], ids[:, own], times[own] = own_state[...], own_ids[...], own_times[...]

    def join(mine, main, outer):
        for x in range(cx):
            for k in range(21):
                line = halo[(k * cx + x) * STEPS : (k * cx + x + 1) * STEPS]
                if k == 20:
                    times[cx + x, outer(reach)] = line
                elif k % 10 == 9:
                    ids[k // 10, cx + x, outer(reach)] = line
                else:
                    state[k // 10, k % 10, cx + x, outer(reach)] = line

    by_core(join)
    coefficients(cx, range(cx, 2 * cx), tables, ids, coef)
    both[...] = state[:, :, own]
    coef_out[...] = coef[:, :, own]
    times_out[...] = times[own]
    velocity = advance(cx, 0, state, coef, times)

    def cut(mine, main, outer):
        rows_of = outer_rows(mine, outer(reach))
        cut_edges(cx, rows_of, True, velocity, state, ids, times, to_first, to_second)

    by_core(cut)


def next_kernel(cx, done, *refs):
    first = done == 0
    parts = 2 if first else 1
    both_in, coef_in, times_in = refs[0:3]
    edges, refs = refs[3 : 3 + 2 * parts], refs[3 + 2 * parts :]
    if first:
        tables, outs = refs[0], refs[1:]
        state, ids, coef, times = refs[-4:]
    else:
        ids, outs = None, refs
        state, coef, times = refs[-1], coef_in, times_in
    segment = lax.axis_index("segment")
    rows = state.shape[3]
    own = slice(cx, 2 * cx)
    state[:, :, own] = both_in[...]
    right_units, left_units = edge_units(cx, first)

    def get(edge, units, start, rows_of, new_plane):
        for i, (model, what, x) in enumerate(units):
            at = rows_of(x == new_plane)
            count = at.stop - at.start
            line = edge[i * count : (i + 1) * count]
            if what == 10:
                times[start + x, at] = line
            elif what == 9:
                ids[model, start + x, at] = line
            else:
                state[model, what, start + x, at] = line

    def place(rows_of, pair):
        def put(left, right):
            get(left, right_units, 0, rows_of, -1)
            get(right, left_units, 2 * cx, rows_of, cx - 1)

        by_parity((pair[1], pair[0]), pair, put)

    if first:

        def place_both(mine, main, outer):
            reach = rows - STEPS
            place(lambda new: main(reach), edges[0:2])
            place(outer_rows(mine, outer(reach)), edges[2:4])

        by_core(place_both)
        coef[:, :, own] = coef_in[...]
        times[own] = times_in[...]
        coefficients(cx, (*range(1, cx), *range(2 * cx, 3 * cx - 1)), tables, ids, coef)
    else:
        place(lambda new: slice(done, rows - done), edges)
    velocity = advance(cx, cx, state, coef, times, given_top=True)
    if done + cx == STEPS:
        outs[0][...] = state[segment, :, own, STEPS : rows - STEPS]
        outs[1][...] = state[1 - segment, :, own, STEPS : rows - STEPS]
    else:
        outs[2][...] = state[:, :, own]
        if first:
            outs[3][...] = coef[...]
            outs[4][...] = times[...]
        left = slice(done + cx, rows - done - cx)
        cut_edges(cx, lambda new: left, False, velocity, state, None, times, outs[0], outs[1])


def home_kernel(mine, brought, out):
    half = mine.shape[2]
    segment = lax.axis_index("segment")

    @pl.when(segment == 0)
    def _():
        out[0, :, :, 0:half] = mine[...]
        out[0, :, :, half:] = brought[...]

    @pl.when(segment == 1)
    def _():
        out[0, :, :, half:] = mine[...]
        out[0, :, :, 0:half] = brought[...]


VMEM = pl.BlockSpec(memory_space=pltpu.VMEM)
HBM = pl.BlockSpec(memory_space=pltpu.HBM)


def call(kernel, name, in_vmem, in_hbm, outs, scratch, copies=0, limit=40 * 2**20, flops=10**7):
    sems = [pltpu.SemaphoreType.DMA((copies,))] * (copies > 0)
    return pl.pallas_call(
        kernel,
        out_shape=[jax.ShapeDtypeStruct(shape, F32) for shape in outs],
        in_specs=[VMEM] * len(in_vmem) + [HBM] * len(in_hbm),
        out_specs=[VMEM] * len(outs),
        scratch_shapes=[pltpu.VMEM(s, F32) if isinstance(s, tuple) else s for s in scratch] + sems,
        compiler_params=pltpu.CompilerParams(vmem_limit_bytes=limit),
        cost_estimate=pl.CostEstimate(flops=flops, bytes_accessed=2**20, transcendentals=0),
        name=name,
    )(*in_vmem, *in_hbm)


def on_device(
    fields, block_ids, buoyancy, lame_lambda, lame_mu, moments, moment_owner, moment_cells, drm_rows
):
    sections, slabs = lax.axis_size("sec"), lax.axis_size("depth")
    layout = cx, cz, cy = fields.shape[2:]
    reach, rows = reach_of(cz), cz // 2 + 2 * STEPS
    assert cx > 1 and STEPS % cx == 0

    def pairs(block, start):
        route = [(i, i + 1) for i in range(start, sections - 1, 2)]
        return lax.ppermute(block, "sec", route + [(j, i) for i, j in route])

    def other(section, k):
        return section ^ k if sections & (sections - 1) == 0 else (section + k) % sections

    def along_depth(block):
        down = [(2 * i + 1, 2 * (i + 1)) for i in range(slabs - 1)]
        return lax.ppermute(block, ("depth", "segment"), down + [(j, i) for i, j in down])

    def swap(block):
        return lax.ppermute(block, "segment", [(0, 1), (1, 0)])

    owner = moment_owner.reshape(-1, cy)
    cells = moment_cells.reshape(-1, cy)
    arguments = (fields, block_ids, moments, owner, cells, drm_rows.reshape(-1, cy))
    entry_lines = 8 * cells.shape[0]
    entries, kept, given = call(
        pack_kernel,
        "pack",
        (),
        (*arguments, buoyancy, lame_lambda, lame_mu),
        [(entry_lines, cy), (11 * cx * reach + 8 + entry_lines, cy), (10, cx * reach, cy)],
        [pltpu.VMEM(a.shape, a.dtype) for a in arguments]
        + [(2, cx, cz, cy), pltpu.SMEM((3, buoyancy.shape[0]), F32)],
        len(arguments) + 3,
        limit=64 * 2**20,
    )
    blocks = [
        lax.ppermute(entries, "sec", [(other(i, k), i) for i in range(sections)])
        for k in range(1, sections)
    ]
    got = swap(given)
    acc_shape = (6 * cx * cz // 2, 2 * cy)
    kept, tables, started = call(
        functools.partial(own_kernel, layout),
        "own_moments",
        (kept,),
        (),
        [(11, cx * reach, cy), (8, cy), acc_shape],
        [],
        flops=10**9,
    )
    own = (cx, rows, cy)
    window = (3 * cx, rows, cy)
    state, ids, times, edge = call(
        functools.partial(join_kernel, layout),
        "join_and_moments",
        (kept, got, started, *blocks),
        (),
        [(2, 9, *own), (2, *own), own, (21 * cx * STEPS, cy)],
        [acc_shape, (6, cx * cz, cy)],
    )
    halo = along_depth(edge)
    work = [(2, 9, *window), (2, *window), (2, 3, *window), window]

    def edges(count, with_ids):
        return [(len(edge_units(cx, with_ids)[0]) * count, cy)] * 2

    def exchange(pair):
        return [pairs(pair[0], 0), pairs(pair[1], 1)]

    inner = call(
        functools.partial(inner_kernel, cx),
        "inner_edges",
        (state, ids, times, tables),
        (),
        edges(reach, True),
        work,
        flops=10**9,
    )
    got_edges = exchange(inner)
    *outer, both, coef, times = call(
        functools.partial(outer_kernel, cx),
        "outer_edges",
        (state, ids, times, halo, tables),
        (),
        edges(STEPS, True) + [(2, 9, *own), (2, 3, *own), own],
        work,
        flops=4 * 10**9,
    )
    got_edges += exchange(outer)
    for done in range(0, STEPS, cx):
        first, last = done == 0, done + cx == STEPS
        after = done + cx
        outs = [(9, cx, cz // 2, cy)] * 2
        if not last:
            outs = edges(rows - 2 * after, False) + [(2, 9, *own)]
            outs += [(2, 3, *window), window] * first
        pair = call(
            functools.partial(next_kernel, cx, done),
            "steps",
            (both, coef, times, *got_edges) + (tables,) * first,
            (),
            outs,
            work if first else work[0:1],
        )
        if not last:
            got_edges = exchange(pair[0:2])
            both = pair[2]
            if first:
                coef, times = pair[3:5]
    to_first, to_second = pair[0:2]
    (out,) = call(home_kernel, "home", (to_first, swap(to_second)), (), [fields.shape], [])
    return out


def solution(mesh):
    in_specs = (
        P("segment", None, "sec", "depth", None),
        P("segment", "sec", "depth", None),
        P(),
        P(),
        P(),
        P(None, ("sec", "depth")),
        P(("sec", "depth"), None),
        P(("sec", "depth")),
        P(("sec", "depth")),
    )
    out_specs = P("segment", None, "sec", "depth", None)
    return jax.shard_map(
        on_device, mesh=mesh, in_specs=in_specs, out_specs=out_specs, check_vma=False
    )
```

```python
import functools

import jax
import jax.numpy as jnp
from jax import lax
from jax.experimental import pallas as pl
from jax.experimental.pallas import tpu as pltpu
from jax.sharding import PartitionSpec as P

STEPS = 4
F32 = jnp.float32
BF16 = jnp.bfloat16
NT = (((1,), (1,)), ((), ()))


def one_hot(index, count):
    rows = lax.broadcasted_iota(jnp.int32, (count, index.shape[-1]), 0)
    return jnp.where(rows == index, F32(1.0), F32(0.0))


def split3(value):
    high = value.astype(BF16).astype(F32)
    rest = value - high
    mid = rest.astype(BF16).astype(F32)
    return high, mid, rest - mid


def copy_all(sem, pairs):
    copies = [pltpu.make_async_copy(a, b, sem.at[i]) for i, (a, b) in enumerate(pairs)]
    for copy in copies:
        copy.start()
    for copy in copies:
        copy.wait()


def in_line(rows):
    return jnp.concatenate([rows[i : i + 1, :] for i in range(rows.shape[0])], axis=1)


def reach_of(cz):
    return cz // 2 + STEPS


def entries_kernel(moments_in, owner_in, cells_in, entries, moments, owner, cells, sem):
    copy_all(sem, [(moments_in, moments), (owner_in, owner), (cells_in, cells)])
    cy = cells.shape[1]
    for i in range(cells.shape[0]):
        at = 8 * i
        entries[at : at + 6] = moments[:, i * cy : (i + 1) * cy]
        entries[at + 6 : at + 7] = owner[i : i + 1, :].astype(F32)
        entries[at + 7 : at + 8] = cells[i : i + 1, :].astype(F32)


def pack_kernel(
    fields_in, ids_in, rows_in, entries_in, buoyancy, lame_lambda, lame_mu,
    kept, given, fields, ids, rows, entries, wide, tables, sem,
):
    cx, cz, cy = ids.shape[1:]
    arguments = [(fields_in, fields), (ids_in, ids), (rows_in, rows), (entries_in, entries)]
    arguments += [(t, tables.at[i]) for i, t in enumerate((buoyancy, lame_lambda, lame_mu))]
    copy_all(sem, arguments)
    wide[0] = (ids[0] + 1).astype(F32)
    line = in_line(rows[...])
    high = one_hot(line // cy, cx * cz).astype(BF16)
    low = one_hot(line % cy, cy).astype(BF16)
    count = lax.dot_general(high, low, NT, preferred_element_type=F32)
    wide[1] = count.reshape(cx, cz, cy)
    reach = reach_of(cz)
    lines = 11 * cx * reach
    lane = lax.broadcasted_iota(jnp.int32, (1, cy), 1)
    for i in range(3):
        found = jnp.zeros((1, cy), F32)
        for entry in range(tables.shape[1]):
            found = jnp.where(lane == entry + 1, F32(0.5) * tables[i, entry], found)
        kept[lines + i : lines + i + 1] = found
    kept[lines + 3 : lines + 8] = jnp.zeros((5, cy), F32)
    kept[lines + 8 :] = entries[...]

    def cut(first, other):
        for x in range(cx):
            at = slice(x * reach, (x + 1) * reach)
            for k in range(11):
                source = fields.at[0, k] if k < 9 else wide.at[k - 9]
                line = (k * cx + x) * reach
                kept[line : line + reach] = source[x, first : first + reach]
            given[0:9, at] = fields[0, :, x, other : other + reach]
            given[9, at] = wide[0, x, other : other + reach]

    @pl.when(lax.axis_index("segment") == 0)
    def _():
        cut(0, cz - reach)

    @pl.when(lax.axis_index("segment") == 1)
    def _():
        cut(cz - reach, 0)


def moments_of(layout, entries):
    cx, cz, cy = layout
    section = lax.axis_index("sec")
    half = cx * cz // 2
    chunk = [entries[8 * i : 8 * i + 8] for i in range(entries.shape[0] // 8)]
    entry = jnp.concatenate(chunk, axis=1)
    owner = entry[6:7].astype(jnp.int32)
    cell = entry[7:8].astype(jnp.int32)
    line = jnp.where(owner == section, cell // cy, -1)
    upper = line >= half
    high = one_hot(jnp.where(upper, line - half, line), half)
    low = one_hot(jnp.where(upper, cell % cy + cy, cell % cy), 2 * cy).astype(BF16)
    total = jnp.zeros((6 * half, 2 * cy), F32)
    for part in split3(entry[0:6]):
        spread = jnp.concatenate([(high * part[c : c + 1]).astype(BF16) for c in range(6)], axis=0)
        total = total + lax.dot_general(spread, low, NT, preferred_element_type=F32)
    return total


def own_kernel(layout, kept, out, tables, acc):
    lines = out.shape[0] * out.shape[1]
    out[...] = kept[0:lines].reshape(out.shape)
    tables[...] = kept[lines : lines + 8]
    acc[...] = moments_of(layout, kept[lines + 8 :])


def more_kernel(layout, started, entries, acc):
    acc[...] = started[...] + moments_of(layout, entries[...])


def by_core(act):
    segment = lax.axis_index("segment")

    @pl.when(segment == 0)
    def _():
        act(0, lambda reach: slice(STEPS, STEPS + reach), lambda reach: slice(0, STEPS))

    @pl.when(segment == 1)
    def _():
        act(1, lambda reach: slice(0, reach), lambda reach: slice(reach, reach + STEPS))


def join_kernel(layout, *refs):
    cx, cz, cy = layout
    kept, got, started, entries, state, ids, times, edge, dense = refs
    reach = reach_of(cz)
    half = cx * cz // 2
    total = started[...] + moments_of(layout, entries[...])
    for c in range(6):
        for k in range(2):
            added = total[c * half : (c + 1) * half, k * cy : (k + 1) * cy]
            dense[c, k * half : (k + 1) * half] = added

    def join(mine, main, outer):
        main, outer = main(reach), outer(reach)
        first = 0 if mine == 0 else cz - reach
        last = main.start if mine == 0 else main.stop - STEPS
        gone = slice(last, last + STEPS)
        for x in range(cx):
            at = slice(x * reach, (x + 1) * reach)
            for model in range(2):
                rows = kept if model == mine else got
                state[model, :, x, main] = rows[0:9, at]
                ids[model, x, main] = rows[9, at]
            added = dense[:, x * cz + first : x * cz + first + reach]
            state[0, 3:9, x, main] = state[0, 3:9, x, main] + added
            times[x, main] = kept[10, at]
            state[:, :, x, outer] = jnp.zeros((2, 9, STEPS, cy), F32)
            ids[:, x, outer] = jnp.zeros((2, STEPS, cy), F32)
            times[x, outer] = jnp.zeros((STEPS, cy), F32)
            for k in range(21):
                line = slice((k * cx + x) * STEPS, (k * cx + x + 1) * STEPS)
                if k == 20:
                    edge[line] = times[x, gone]
                elif k % 10 == 9:
                    edge[line] = ids[k // 10, x, gone]
                else:
                    edge[line] = state[k // 10, k % 10, x, gone]

    by_core(join)


def by_parity(even, odd, act):
    parity = lax.axis_index("sec") % 2

    @pl.when(parity == 0)
    def _():
        act(*even)

    @pl.when(parity == 1)
    def _():
        act(*odd)


def advance(cx, steps, state, coef, times, given_top=False):
    planes, rows, cy = state.shape[2:]
    lane = lax.broadcasted_iota(jnp.int32, (rows, cy), 1)
    first_lane, last_lane = lane == 0, lane == cy - 1

    def back_y(f):
        return f - jnp.where(first_lane, F32(0.0), pltpu.roll(f, 1, 1))

    def back_z(f):
        return f - pltpu.roll(f, 1, 0)

    def fore_y(f):
        return jnp.where(last_lane, F32(0.0), pltpu.roll(f, cy - 1, 1)) - f

    def fore_z(f):
        return pltpu.roll(f, rows - 1, 0) - f

    def velocity(x):
        inc = [None, None]
        for model in range(2):
            sxx, syy, szz, syz, sxz, sxy = (state[model, 3 + k, x] for k in range(6))
            sxx_p, sxz_p, sxy_p = (state[model, k, x - 1] for k in (3, 7, 8))
            hb = coef[model, 0, x]
            inc[model] = (
                hb * ((sxx - sxx_p) + back_y(sxy) + back_z(sxz)),
                hb * ((sxy - sxy_p) + back_y(syy) + back_z(syz)),
                hb * ((sxz - sxz_p) + back_y(syz) + back_z(szz)),
            )
        for k in range(3):
            state[0, k, x] = state[0, k, x] + inc[0][k]
            state[1, k, x] = (state[1, k, x] + inc[1][k]) + times[x] * inc[0][k]

    for step in range(steps):
        left = steps - 1 - step
        low, high = cx - left, 2 * cx + left
        for x in range(low, high + 1 - (given_top and step == 0)):
            velocity(x)
        for x in range(low, high):
            for model in range(2):
                vx, vy, vz = (state[model, k, x] for k in range(3))
                vx_n, vy_n, vz_n = (state[model, k, x + 1] for k in range(3))
                hl, hm = coef[model, 1, x], coef[model, 2, x]
                exx, eyy, ezz = vx_n - vx, fore_y(vy), fore_z(vz)
                pressure = hl * (exx + eyy + ezz)
                twice = hm + hm
                state[model, 3, x] = state[model, 3, x] + (pressure + twice * exx)
                state[model, 4, x] = state[model, 4, x] + (pressure + twice * eyy)
                state[model, 5, x] = state[model, 5, x] + (pressure + twice * ezz)
                state[model, 6, x] = state[model, 6, x] + hm * (fore_z(vy) + fore_y(vz))
                state[model, 7, x] = state[model, 7, x] + hm * (fore_z(vx) + (vz_n - vz))
                state[model, 8, x] = state[model, 8, x] + hm * (fore_y(vx) + (vy_n - vy))

    return velocity


def look_up(tables, ids):
    lanes = ids.astype(jnp.int32)
    wide = [jnp.broadcast_to(tables[i : i + 1], ids.shape) for i in range(3)]
    return [jnp.take_along_axis(table, lanes, axis=1) for table in wide]


def edge_units(cx, with_ids):
    right, left = [], []
    for model in range(2):
        whole = list(range(10 if with_ids else 9)) + [10] * (with_ids and model == 1)
        for x in range(cx - 1):
            right += [(model, what, x + 1) for what in whole]
            left += [(model, what, x) for what in whole]
        right += [(model, what, 0) for what in (3, 7, 8)]
        left += [(model, what, cx - 1) for what in range(3)]
    return right, left


def cut_edges(cx, rows_of, with_ids, velocity, state, ids, times, to_first, to_second):
    right_units, left_units = edge_units(cx, with_ids)

    def put(to, units, far, right):
        line = slice(0, 0)
        for model, what, x in units:
            at = rows_of(x == far, right)
            line = slice(line.stop, line.stop + at.stop - at.start)
            if what == 10:
                to[line] = times[cx + x, at]
            elif what == 9:
                to[line] = ids[model, cx + x, at]
            else:
                to[line] = state[model, what, cx + x, at]

    holders = (to_second, to_first), (to_first, to_second)
    by_parity(*holders, lambda left, right: put(right, right_units, 0, True))
    velocity(2 * cx - 1)
    by_parity(*holders, lambda left, right: put(left, left_units, cx - 1, False))


def outer_rows(mine, outer):
    def rows_of(far, right):
        shift = 1 if far and not right and mine == 0 else 0
        return slice(outer.start + shift, outer.stop + shift)

    return rows_of


def reached_rows(cx, done, rows):
    def rows_of(far, right):
        first, last = done, rows - done
        if right:
            return slice(first + (cx if far else 1), last)
        return slice(first + far, last - (cx if far else 1))

    return rows_of


def coefficients(cx, planes, tables, ids, coef):
    for model in range(2):
        for x in planes:
            for i, found in enumerate(look_up(tables, ids[model, x])):
                coef[model, i, x] = found


def inner_kernel(cx, own_state, own_ids, own_times, tables, to_first, to_second, state, ids, coef, times):
    own = slice(cx, 2 * cx)
    reach = state.shape[3] - STEPS
    state[:, :, own], ids[:, own], times[own] = own_state[...], own_ids[...], own_times[...]
    coefficients(cx, range(2 * cx - 1, 2 * cx), tables, ids, coef)
    velocity = advance(cx, 0, state, coef, times)

    def cut(mine, main, outer):
        rows_of = lambda far, right: main(reach)
        cut_edges(cx, rows_of, True, velocity, state, ids, times, to_first, to_second)

    by_core(cut)


def outer_kernel(
    cx, own_state, own_ids, own_times, halo, tables,
    to_first, to_second, both, coef_out, times_out, state, ids, coef, times,
):
    own = slice(cx, 2 * cx)
    reach = state.shape[3] - STEPS
    state[:, :, own], ids[:, own], times[own] = own_state[...], own_ids[...], own_times[...]

    def join(mine, main, outer):
        for x in range(cx):
            for k in range(21):
                line = halo[(k * cx + x) * STEPS : (k * cx + x + 1) * STEPS]
                if k == 20:
                    times[cx + x, outer(reach)] = line
                elif k % 10 == 9:
                    ids[k // 10, cx + x, outer(reach)] = line
                else:
                    state[k // 10, k % 10, cx + x, outer(reach)] = line

    by_core(join)
    coefficients(cx, range(cx, 2 * cx), tables, ids, coef)
    both[...] = state[:, :, own]
    coef_out[...] = coef[:, :, own]
    times_out[...] = times[own]
    velocity = advance(cx, 0, state, coef, times)

    def cut(mine, main, outer):
        rows_of = outer_rows(mine, outer(reach))
        cut_edges(cx, rows_of, True, velocity, state, ids, times, to_first, to_second)

    by_core(cut)


def next_kernel(cx, done, *refs):
    first = done == 0
    parts = 2 if first else 1
    both_in, coef_in, times_in = refs[0:3]
    edges, refs = refs[3 : 3 + 2 * parts], refs[3 + 2 * parts :]
    if first:
        tables, outs = refs[0], refs[1:]
        state, ids, coef, times = refs[-4:]
    else:
        ids, outs = None, refs
        state, coef, times = refs[-1], coef_in, times_in
    segment = lax.axis_index("segment")
    rows = state.shape[3]
    own = slice(cx, 2 * cx)
    state[:, :, own] = both_in[...]
    right_units, left_units = edge_units(cx, first)

    def get(edge, units, start, rows_of, far, right):
        last = 0
        for model, what, x in units:
            at = rows_of(x == far, right)
            first, last = last, last + at.stop - at.start
            line = edge[first:last]
            if what == 10:
                times[start + x, at] = line
            elif what == 9:
                ids[model, start + x, at] = line
            else:
                state[model, what, start + x, at] = line

    def place(rows_of, pair):
        def put(left, right):
            get(left, right_units, 0, rows_of, 0, True)
            get(right, left_units, 2 * cx, rows_of, cx - 1, False)

        by_parity((pair[1], pair[0]), pair, put)

    if first:

        def place_both(mine, main, outer):
            reach = rows - STEPS
            place(lambda far, right: main(reach), edges[0:2])
            place(outer_rows(mine, outer(reach)), edges[2:4])

        by_core(place_both)
        coef[:, :, own] = coef_in[...]
        times[own] = times_in[...]
        coefficients(cx, (*range(1, cx), *range(2 * cx, 3 * cx - 1)), tables, ids, coef)
    else:
        place(reached_rows(cx, done, rows), edges)
    velocity = advance(cx, cx, state, coef, times, given_top=True)
    if done + cx == STEPS:
        outs[0][...] = state[segment, :, own, STEPS : rows - STEPS]
        outs[1][...] = state[1 - segment, :, own, STEPS : rows - STEPS]
    else:
        outs[2][...] = state[:, :, own]
        if first:
            outs[3][...] = coef[...]
            outs[4][...] = times[...]
        rows_of = reached_rows(cx, done + cx, rows)
        cut_edges(cx, rows_of, False, velocity, state, None, times, outs[0], outs[1])


def home_kernel(mine, brought, out):
    half = mine.shape[2]
    segment = lax.axis_index("segment")

    @pl.when(segment == 0)
    def _():
        out[0, :, :, 0:half] = mine[...]
        out[0, :, :, half:] = brought[...]

    @pl.when(segment == 1)
    def _():
        out[0, :, :, half:] = mine[...]
        out[0, :, :, 0:half] = brought[...]


VMEM = pl.BlockSpec(memory_space=pltpu.VMEM)
HBM = pl.BlockSpec(memory_space=pltpu.HBM)


def call(kernel, name, in_vmem, in_hbm, outs, scratch, copies=0, limit=40 * 2**20, flops=10**7):
    sems = [pltpu.SemaphoreType.DMA((copies,))] * (copies > 0)
    return pl.pallas_call(
        kernel,
        out_shape=[jax.ShapeDtypeStruct(shape, F32) for shape in outs],
        in_specs=[VMEM] * len(in_vmem) + [HBM] * len(in_hbm),
        out_specs=[VMEM] * len(outs),
        scratch_shapes=[pltpu.VMEM(s, F32) if isinstance(s, tuple) else s for s in scratch] + sems,
        compiler_params=pltpu.CompilerParams(vmem_limit_bytes=limit),
        cost_estimate=pl.CostEstimate(flops=flops, bytes_accessed=2**20, transcendentals=0),
        name=name,
    )(*in_vmem, *in_hbm)


def on_device(
    fields, block_ids, buoyancy, lame_lambda, lame_mu, moments, moment_owner, moment_cells, drm_rows
):
    sections, slabs = lax.axis_size("sec"), lax.axis_size("depth")
    layout = cx, cz, cy = fields.shape[2:]
    reach, rows = reach_of(cz), cz // 2 + 2 * STEPS
    assert cx > 1 and STEPS % cx == 0

    def pairs(block, start):
        route = [(i, i + 1) for i in range(start, sections - 1, 2)]
        return lax.ppermute(block, "sec", route + [(j, i) for i, j in route])

    def other(section, k):
        return section ^ k if sections & (sections - 1) == 0 else (section + k) % sections

    def along_depth(block):
        down = [(2 * i + 1, 2 * (i + 1)) for i in range(slabs - 1)]
        return lax.ppermute(block, ("depth", "segment"), down + [(j, i) for i, j in down])

    def swap(block):
        return lax.ppermute(block, "segment", [(0, 1), (1, 0)])

    owner = moment_owner.reshape(-1, cy)
    cells = moment_cells.reshape(-1, cy)
    boundary = drm_rows.reshape(-1, cy)
    entry_lines = 8 * cells.shape[0]
    (entries,) = call(
        entries_kernel,
        "entries",
        (),
        (moments, owner, cells),
        [(entry_lines, cy)],
        [pltpu.VMEM(a.shape, a.dtype) for a in (moments, owner, cells)],
        3,
        limit=64 * 2**20,
    )
    blocks = [
        lax.ppermute(entries, "sec", [(other(i, k), i) for i in range(sections)])
        for k in range(1, sections)
    ]
    arguments = (fields, block_ids, boundary, entries)
    kept, given = call(
        pack_kernel,
        "pack",
        (),
        (*arguments, buoyancy, lame_lambda, lame_mu),
        [(11 * cx * reach + 8 + entry_lines, cy), (10, cx * reach, cy)],
        [pltpu.VMEM(a.shape, a.dtype) for a in arguments]
        + [(2, cx, cz, cy), pltpu.SMEM((3, buoyancy.shape[0]), F32)],
        len(arguments) + 3,
        limit=64 * 2**20,
    )
    got = swap(given)
    acc_shape = (6 * cx * cz // 2, 2 * cy)
    kept, tables, started = call(
        functools.partial(own_kernel, layout),
        "own_moments",
        (kept,),
        (),
        [(11, cx * reach, cy), (8, cy), acc_shape],
        [],
        flops=10**9,
    )
    for block in blocks[:-1]:
        (started,) = call(
            functools.partial(more_kernel, layout),
            "more_moments",
            (started, block),
            (),
            [acc_shape],
            [],
            flops=10**9,
        )
    own = (cx, rows, cy)
    window = (3 * cx, rows, cy)
    state, ids, times, edge = call(
        functools.partial(join_kernel, layout),
        "join_and_moments",
        (kept, got, started, blocks[-1]),
        (),
        [(2, 9, *own), (2, *own), own, (21 * cx * STEPS, cy)],
        [(6, cx * cz, cy)],
    )
    halo = along_depth(edge)
    work = [(2, 9, *window), (2, *window), (2, 3, *window), window]

    def edges(count, with_ids):
        return [(len(edge_units(cx, with_ids)[0]) * count, cy)] * 2

    def reached_edges(done):
        rows_of = reached_rows(cx, done, rows)
        whole, far = rows_of(False, True), rows_of(True, True)
        lines = 18 * (cx - 1) * (whole.stop - whole.start) + 6 * (far.stop - far.start)
        return [(-(-lines // 8) * 8, cy)] * 2

    def exchange(pair):
        return [pairs(pair[0], 0), pairs(pair[1], 1)]

    inner = call(
        functools.partial(inner_kernel, cx),
        "inner_edges",
        (state, ids, times, tables),
        (),
        edges(reach, True),
        work,
        flops=10**9,
    )
    got_edges = exchange(inner)
    *outer, both, coef, times = call(
        functools.partial(outer_kernel, cx),
        "outer_edges",
        (state, ids, times, halo, tables),
        (),
        edges(STEPS, True) + [(2, 9, *own), (2, 3, *own), own],
        work,
        flops=4 * 10**9,
    )
    got_edges += exchange(outer)
    for done in range(0, STEPS, cx):
        first, last = done == 0, done + cx == STEPS
        after = done + cx
        outs = [(9, cx, cz // 2, cy)] * 2
        if not last:
            outs = reached_edges(after) + [(2, 9, *own)]
            outs += [(2, 3, *window), window] * first
        pair = call(
            functools.partial(next_kernel, cx, done),
            "steps",
            (both, coef, times, *got_edges) + (tables,) * first,
            (),
            outs,
            work if first else work[0:1],
        )
        if not last:
            got_edges = exchange(pair[0:2])
            both = pair[2]
            if first:
                coef, times = pair[3:5]
    to_first, to_second = pair[0:2]
    (out,) = call(home_kernel, "home", (to_first, swap(to_second)), (), [fields.shape], [])
    return out


def solution(mesh):
    in_specs = (
        P("segment", None, "sec", "depth", None),
        P("segment", "sec", "depth", None),
        P(),
        P(),
        P(),
        P(None, ("sec", "depth")),
        P(("sec", "depth"), None),
        P(("sec", "depth")),
        P(("sec", "depth")),
    )
    out_specs = P("segment", None, "sec", "depth", None)
    return jax.shard_map(
        on_device, mesh=mesh, in_specs=in_specs, out_specs=out_specs, check_vma=False
    )
```

```python
import functools

import jax
import jax.numpy as jnp
from jax import lax
from jax.experimental import pallas as pl
from jax.experimental.pallas import tpu as pltpu
from jax.sharding import PartitionSpec as P

STEPS = 4
F32 = jnp.float32
BF16 = jnp.bfloat16
NT = (((1,), (1,)), ((), ()))


def one_hot(index, count):
    rows = lax.broadcasted_iota(jnp.int32, (count, index.shape[-1]), 0)
    return jnp.where(rows == index, F32(1.0), F32(0.0))


def split3(value):
    high = value.astype(BF16).astype(F32)
    rest = value - high
    mid = rest.astype(BF16).astype(F32)
    return high, mid, rest - mid


def copy_all(sem, pairs):
    copies = [pltpu.make_async_copy(a, b, sem.at[i]) for i, (a, b) in enumerate(pairs)]
    for copy in copies:
        copy.start()
    for copy in copies:
        copy.wait()


def in_line(rows):
    return jnp.concatenate([rows[i : i + 1, :] for i in range(rows.shape[0])], axis=1)


def reach_of(cz):
    return cz // 2 + STEPS


def pack_kernel(
    fields_in, ids_in, moments_in, owner_in, cells_in, rows_in, buoyancy, lame_lambda, lame_mu,
    entries, kept, given, fields, ids, moments, owner, cells, rows, wide, tables, sem,
):
    cx, cz, cy = ids.shape[1:]
    arguments = [(fields_in, fields), (ids_in, ids), (moments_in, moments), (owner_in, owner)]
    arguments += [(cells_in, cells), (rows_in, rows)]
    arguments += [(t, tables.at[i]) for i, t in enumerate((buoyancy, lame_lambda, lame_mu))]
    copy_all(sem, arguments)
    for i in range(cells.shape[0]):
        at = 8 * i
        entries[at : at + 6] = moments[:, i * cy : (i + 1) * cy]
        entries[at + 6 : at + 7] = owner[i : i + 1, :].astype(F32)
        entries[at + 7 : at + 8] = cells[i : i + 1, :].astype(F32)
    wide[0] = (ids[0] + 1).astype(F32)
    line = in_line(rows[...])
    high = one_hot(line // cy, cx * cz).astype(BF16)
    low = one_hot(line % cy, cy).astype(BF16)
    count = lax.dot_general(high, low, NT, preferred_element_type=F32)
    wide[1] = count.reshape(cx, cz, cy)
    reach = reach_of(cz)
    lines = 11 * cx * reach
    lane = lax.broadcasted_iota(jnp.int32, (1, cy), 1)
    for i in range(3):
        found = jnp.zeros((1, cy), F32)
        for entry in range(tables.shape[1]):
            found = jnp.where(lane == entry + 1, F32(0.5) * tables[i, entry], found)
        kept[lines + i : lines + i + 1] = found
    kept[lines + 3 : lines + 8] = jnp.zeros((5, cy), F32)
    kept[lines + 8 :] = entries[...]

    def cut(first, other):
        for x in range(cx):
            at = slice(x * reach, (x + 1) * reach)
            for k in range(11):
                source = fields.at[0, k] if k < 9 else wide.at[k - 9]
                line = (k * cx + x) * reach
                kept[line : line + reach] = source[x, first : first + reach]
            given[0:9, at] = fields[0, :, x, other : other + reach]
            given[9, at] = wide[0, x, other : other + reach]

    @pl.when(lax.axis_index("segment") == 0)
    def _():
        cut(0, cz - reach)

    @pl.when(lax.axis_index("segment") == 1)
    def _():
        cut(cz - reach, 0)


def moments_of(layout, entries):
    cx, cz, cy = layout
    section = lax.axis_index("sec")
    half = cx * cz // 2
    chunk = [entries[8 * i : 8 * i + 8] for i in range(entries.shape[0] // 8)]
    entry = jnp.concatenate(chunk, axis=1)
    owner = entry[6:7].astype(jnp.int32)
    cell = entry[7:8].astype(jnp.int32)
    line = jnp.where(owner == section, cell // cy, -1)
    upper = line >= half
    high = one_hot(jnp.where(upper, line - half, line), half)
    low = one_hot(jnp.where(upper, cell % cy + cy, cell % cy), 2 * cy).astype(BF16)
    total = jnp.zeros((6 * half, 2 * cy), F32)
    for part in split3(entry[0:6]):
        spread = jnp.concatenate([(high * part[c : c + 1]).astype(BF16) for c in range(6)], axis=0)
        total = total + lax.dot_general(spread, low, NT, preferred_element_type=F32)
    return total


def own_kernel(layout, kept, out, tables, acc):
    lines = out.shape[0] * out.shape[1]
    out[...] = kept[0:lines].reshape(out.shape)
    tables[...] = kept[lines : lines + 8]
    acc[...] = moments_of(layout, kept[lines + 8 :])


def more_kernel(layout, started, entries, acc):
    acc[...] = started[...] + moments_of(layout, entries[...])


def by_core(act):
    segment = lax.axis_index("segment")

    @pl.when(segment == 0)
    def _():
        act(0, lambda reach: slice(STEPS, STEPS + reach), lambda reach: slice(0, STEPS))

    @pl.when(segment == 1)
    def _():
        act(1, lambda reach: slice(0, reach), lambda reach: slice(reach, reach + STEPS))


def join_kernel(layout, *refs):
    cx, cz, cy = layout
    kept, got, started, entries, state, ids, times, edge, dense = refs
    reach = reach_of(cz)
    half = cx * cz // 2
    total = started[...] + moments_of(layout, entries[...])
    for c in range(6):
        for k in range(2):
            added = total[c * half : (c + 1) * half, k * cy : (k + 1) * cy]
            dense[c, k * half : (k + 1) * half] = added

    def join(mine, main, outer):
        main, outer = main(reach), outer(reach)
        first = 0 if mine == 0 else cz - reach
        last = main.start if mine == 0 else main.stop - STEPS
        gone = slice(last, last + STEPS)
        for x in range(cx):
            at = slice(x * reach, (x + 1) * reach)
            for model in range(2):
                rows = kept if model == mine else got
                state[model, :, x, main] = rows[0:9, at]
                ids[model, x, main] = rows[9, at]
            added = dense[:, x * cz + first : x * cz + first + reach]
            state[0, 3:9, x, main] = state[0, 3:9, x, main] + added
            times[x, main] = kept[10, at]
            state[:, :, x, outer] = jnp.zeros((2, 9, STEPS, cy), F32)
            ids[:, x, outer] = jnp.zeros((2, STEPS, cy), F32)
            times[x, outer] = jnp.zeros((STEPS, cy), F32)
            for k in range(21):
                line = slice((k * cx + x) * STEPS, (k * cx + x + 1) * STEPS)
                if k == 20:
                    edge[line] = times[x, gone]
                elif k % 10 == 9:
                    edge[line] = ids[k // 10, x, gone]
                else:
                    edge[line] = state[k // 10, k % 10, x, gone]

    by_core(join)


def by_parity(even, odd, act):
    parity = lax.axis_index("sec") % 2

    @pl.when(parity == 0)
    def _():
        act(*even)

    @pl.when(parity == 1)
    def _():
        act(*odd)


def advance(cx, steps, state, coef, times, given_top=False):
    planes, rows, cy = state.shape[2:]
    lane = lax.broadcasted_iota(jnp.int32, (rows, cy), 1)
    first_lane, last_lane = lane == 0, lane == cy - 1

    def back_y(f):
        return f - jnp.where(first_lane, F32(0.0), pltpu.roll(f, 1, 1))

    def back_z(f):
        return f - pltpu.roll(f, 1, 0)

    def fore_y(f):
        return jnp.where(last_lane, F32(0.0), pltpu.roll(f, cy - 1, 1)) - f

    def fore_z(f):
        return pltpu.roll(f, rows - 1, 0) - f

    def velocity(x):
        inc = [None, None]
        for model in range(2):
            sxx, syy, szz, syz, sxz, sxy = (state[model, 3 + k, x] for k in range(6))
            sxx_p, sxz_p, sxy_p = (state[model, k, x - 1] for k in (3, 7, 8))
            hb = coef[model, 0, x]
            inc[model] = (
                hb * ((sxx - sxx_p) + back_y(sxy) + back_z(sxz)),
                hb * ((sxy - sxy_p) + back_y(syy) + back_z(syz)),
                hb * ((sxz - sxz_p) + back_y(syz) + back_z(szz)),
            )
        for k in range(3):
            state[0, k, x] = state[0, k, x] + inc[0][k]
            state[1, k, x] = (state[1, k, x] + inc[1][k]) + times[x] * inc[0][k]

    for step in range(steps):
        left = steps - 1 - step
        low, high = cx - left, 2 * cx + left
        for x in range(low, high + 1 - (given_top and step == 0)):
            velocity(x)
        for x in range(low, high):
            for model in range(2):
                vx, vy, vz = (state[model, k, x] for k in range(3))
                vx_n, vy_n, vz_n = (state[model, k, x + 1] for k in range(3))
                hl, hm = coef[model, 1, x], coef[model, 2, x]
                exx, eyy, ezz = vx_n - vx, fore_y(vy), fore_z(vz)
                pressure = hl * (exx + eyy + ezz)
                twice = hm + hm
                state[model, 3, x] = state[model, 3, x] + (pressure + twice * exx)
                state[model, 4, x] = state[model, 4, x] + (pressure + twice * eyy)
                state[model, 5, x] = state[model, 5, x] + (pressure + twice * ezz)
                state[model, 6, x] = state[model, 6, x] + hm * (fore_z(vy) + fore_y(vz))
                state[model, 7, x] = state[model, 7, x] + hm * (fore_z(vx) + (vz_n - vz))
                state[model, 8, x] = state[model, 8, x] + hm * (fore_y(vx) + (vy_n - vy))

    return velocity


def look_up(tables, ids):
    lanes = ids.astype(jnp.int32)
    wide = [jnp.broadcast_to(tables[i : i + 1], ids.shape) for i in range(3)]
    return [jnp.take_along_axis(table, lanes, axis=1) for table in wide]


def edge_units(cx, with_ids):
    right, left = [], []
    for model in range(2):
        whole = list(range(10 if with_ids else 9)) + [10] * (with_ids and model == 1)
        for x in range(cx - 1):
            right += [(model, what, x + 1) for what in whole]
            left += [(model, what, x) for what in whole]
        right += [(model, what, 0) for what in (3, 7, 8)]
        left += [(model, what, cx - 1) for what in range(3)]
    return right, left


def cut_edges(cx, rows_of, with_ids, velocity, state, ids, times, to_first, to_second):
    right_units, left_units = edge_units(cx, with_ids)

    def put(to, units, far, right):
        line = slice(0, 0)
        for model, what, x in units:
            at = rows_of(x == far, right)
            line = slice(line.stop, line.stop + at.stop - at.start)
            if what == 10:
                to[line] = times[cx + x, at]
            elif what == 9:
                to[line] = ids[model, cx + x, at]
            else:
                to[line] = state[model, what, cx + x, at]

    holders = (to_second, to_first), (to_first, to_second)
    by_parity(*holders, lambda left, right: put(right, right_units, 0, True))
    velocity(2 * cx - 1)
    by_parity(*holders, lambda left, right: put(left, left_units, cx - 1, False))


def outer_rows(mine, outer):
    def rows_of(far, right):
        shift = 1 if far and not right and mine == 0 else 0
        return slice(outer.start + shift, outer.stop + shift)

    return rows_of


def reached_rows(cx, done, rows):
    def rows_of(far, right):
        first, last = done, rows - done
        if right:
            return slice(first + (cx if far else 1), last)
        return slice(first + far, last - (cx if far else 1))

    return rows_of


def coefficients(cx, planes, tables, ids, coef):
    for model in range(2):
        for x in planes:
            for i, found in enumerate(look_up(tables, ids[model, x])):
                coef[model, i, x] = found


def inner_kernel(cx, own_state, own_ids, own_times, tables, to_first, to_second, state, ids, coef, times):
    own = slice(cx, 2 * cx)
    reach = state.shape[3] - STEPS
    state[:, :, own], ids[:, own], times[own] = own_state[...], own_ids[...], own_times[...]
    coefficients(cx, range(2 * cx - 1, 2 * cx), tables, ids, coef)
    velocity = advance(cx, 0, state, coef, times)

    def cut(mine, main, outer):
        rows_of = lambda far, right: main(reach)
        cut_edges(cx, rows_of, True, velocity, state, ids, times, to_first, to_second)

    by_core(cut)


def outer_kernel(
    cx, own_state, own_ids, own_times, halo, tables,
    to_first, to_second, both, coef_out, times_out, state, ids, coef, times,
):
    own = slice(cx, 2 * cx)
    reach = state.shape[3] - STEPS
    state[:, :, own], ids[:, own], times[own] = own_state[...], own_ids[...], own_times[...]

    def join(mine, main, outer):
        for x in range(cx):
            for k in range(21):
                line = halo[(k * cx + x) * STEPS : (k * cx + x + 1) * STEPS]
                if k == 20:
                    times[cx + x, outer(reach)] = line
                elif k % 10 == 9:
                    ids[k // 10, cx + x, outer(reach)] = line
                else:
                    state[k // 10, k % 10, cx + x, outer(reach)] = line

    by_core(join)
    coefficients(cx, range(cx, 2 * cx), tables, ids, coef)
    both[...] = state[:, :, own]
    coef_out[...] = coef[:, :, own]
    times_out[...] = times[own]
    velocity = advance(cx, 0, state, coef, times)

    def cut(mine, main, outer):
        rows_of = outer_rows(mine, outer(reach))
        cut_edges(cx, rows_of, True, velocity, state, ids, times, to_first, to_second)

    by_core(cut)


def next_kernel(cx, done, *refs):
    first = done == 0
    parts = 2 if first else 1
    both_in, coef_in, times_in = refs[0:3]
    edges, refs = refs[3 : 3 + 2 * parts], refs[3 + 2 * parts :]
    if first:
        tables, outs = refs[0], refs[1:]
        state, ids, coef, times = refs[-4:]
    else:
        ids, outs = None, refs
        state, coef, times = refs[-1], coef_in, times_in
    segment = lax.axis_index("segment")
    rows = state.shape[3]
    own = slice(cx, 2 * cx)
    state[:, :, own] = both_in[...]
    right_units, left_units = edge_units(cx, first)

    def get(edge, units, start, rows_of, far, right):
        last = 0
        for model, what, x in units:
            at = rows_of(x == far, right)
            first, last = last, last + at.stop - at.start
            line = edge[first:last]
            if what == 10:
                times[start + x, at] = line
            elif what == 9:
                ids[model, start + x, at] = line
            else:
                state[model, what, start + x, at] = line

    def place(rows_of, pair):
        def put(left, right):
            get(left, right_units, 0, rows_of, 0, True)
            get(right, left_units, 2 * cx, rows_of, cx - 1, False)

        by_parity((pair[1], pair[0]), pair, put)

    if first:

        def place_both(mine, main, outer):
            reach = rows - STEPS
            place(lambda far, right: main(reach), edges[0:2])
            place(outer_rows(mine, outer(reach)), edges[2:4])

        by_core(place_both)
        coef[:, :, own] = coef_in[...]
        times[own] = times_in[...]
        coefficients(cx, (*range(1, cx), *range(2 * cx, 3 * cx - 1)), tables, ids, coef)
    else:
        place(reached_rows(cx, done, rows), edges)
    velocity = advance(cx, cx, state, coef, times, given_top=True)
    if done + cx == STEPS:
        outs[0][...] = state[segment, :, own, STEPS : rows - STEPS]
        outs[1][...] = state[1 - segment, :, own, STEPS : rows - STEPS]
    else:
        outs[2][...] = state[:, :, own]
        if first:
            outs[3][...] = coef[...]
            outs[4][...] = times[...]
        rows_of = reached_rows(cx, done + cx, rows)
        cut_edges(cx, rows_of, False, velocity, state, None, times, outs[0], outs[1])


def home_kernel(mine, brought, out):
    half = mine.shape[2]
    segment = lax.axis_index("segment")

    @pl.when(segment == 0)
    def _():
        out[0, :, :, 0:half] = mine[...]
        out[0, :, :, half:] = brought[...]

    @pl.when(segment == 1)
    def _():
        out[0, :, :, half:] = mine[...]
        out[0, :, :, 0:half] = brought[...]


VMEM = pl.BlockSpec(memory_space=pltpu.VMEM)
HBM = pl.BlockSpec(memory_space=pltpu.HBM)


def call(kernel, name, in_vmem, in_hbm, outs, scratch, copies=0, limit=40 * 2**20, flops=10**7):
    sems = [pltpu.SemaphoreType.DMA((copies,))] * (copies > 0)
    return pl.pallas_call(
        kernel,
        out_shape=[jax.ShapeDtypeStruct(shape, F32) for shape in outs],
        in_specs=[VMEM] * len(in_vmem) + [HBM] * len(in_hbm),
        out_specs=[VMEM] * len(outs),
        scratch_shapes=[pltpu.VMEM(s, F32) if isinstance(s, tuple) else s for s in scratch] + sems,
        compiler_params=pltpu.CompilerParams(vmem_limit_bytes=limit),
        cost_estimate=pl.CostEstimate(flops=flops, bytes_accessed=2**20, transcendentals=0),
        name=name,
    )(*in_vmem, *in_hbm)


def on_device(
    fields, block_ids, buoyancy, lame_lambda, lame_mu, moments, moment_owner, moment_cells, drm_rows
):
    sections, slabs = lax.axis_size("sec"), lax.axis_size("depth")
    layout = cx, cz, cy = fields.shape[2:]
    reach, rows = reach_of(cz), cz // 2 + 2 * STEPS
    assert cx > 1 and STEPS % cx == 0

    def pairs(block, start):
        route = [(i, i + 1) for i in range(start, sections - 1, 2)]
        return lax.ppermute(block, "sec", route + [(j, i) for i, j in route])

    def other(section, k):
        return section ^ k if sections & (sections - 1) == 0 else (section + k) % sections

    def along_depth(block):
        down = [(2 * i + 1, 2 * (i + 1)) for i in range(slabs - 1)]
        return lax.ppermute(block, ("depth", "segment"), down + [(j, i) for i, j in down])

    def swap(block):
        return lax.ppermute(block, "segment", [(0, 1), (1, 0)])

    owner = moment_owner.reshape(-1, cy)
    cells = moment_cells.reshape(-1, cy)
    arguments = (fields, block_ids, moments, owner, cells, drm_rows.reshape(-1, cy))
    entry_lines = 8 * cells.shape[0]
    entries, kept, given = call(
        pack_kernel,
        "pack",
        (),
        (*arguments, buoyancy, lame_lambda, lame_mu),
        [(entry_lines, cy), (11 * cx * reach + 8 + entry_lines, cy), (10, cx * reach, cy)],
        [pltpu.VMEM(a.shape, a.dtype) for a in arguments]
        + [(2, cx, cz, cy), pltpu.SMEM((3, buoyancy.shape[0]), F32)],
        len(arguments) + 3,
        limit=64 * 2**20,
    )
    blocks = [
        lax.ppermute(entries, "sec", [(other(i, k), i) for i in range(sections)])
        for k in range(1, sections)
    ]
    got = swap(given)
    acc_shape = (6 * cx * cz // 2, 2 * cy)
    kept, tables, started = call(
        functools.partial(own_kernel, layout),
        "own_moments",
        (kept,),
        (),
        [(11, cx * reach, cy), (8, cy), acc_shape],
        [],
        flops=10**9,
    )
    for block in blocks[:-1]:
        (started,) = call(
            functools.partial(more_kernel, layout),
            "more_moments",
            (started, block),
            (),
            [acc_shape],
            [],
            flops=10**9,
        )
    own = (cx, rows, cy)
    window = (3 * cx, rows, cy)
    state, ids, times, edge = call(
        functools.partial(join_kernel, layout),
        "join_and_moments",
        (kept, got, started, blocks[-1]),
        (),
        [(2, 9, *own), (2, *own), own, (21 * cx * STEPS, cy)],
        [(6, cx * cz, cy)],
    )
    halo = along_depth(edge)
    work = [(2, 9, *window), (2, *window), (2, 3, *window), window]

    def edges(count, with_ids):
        return [(len(edge_units(cx, with_ids)[0]) * count, cy)] * 2

    def reached_edges(done):
        rows_of = reached_rows(cx, done, rows)
        whole, far = rows_of(False, True), rows_of(True, True)
        lines = 18 * (cx - 1) * (whole.stop - whole.start) + 6 * (far.stop - far.start)
        return [(-(-lines // 8) * 8, cy)] * 2

    def exchange(pair):
        return [pairs(pair[0], 0), pairs(pair[1], 1)]

    inner = call(
        functools.partial(inner_kernel, cx),
        "inner_edges",
        (state, ids, times, tables),
        (),
        edges(reach, True),
        work,
        flops=10**9,
    )
    got_edges = exchange(inner)
    *outer, both, coef, times = call(
        functools.partial(outer_kernel, cx),
        "outer_edges",
        (state, ids, times, halo, tables),
        (),
        edges(STEPS, True) + [(2, 9, *own), (2, 3, *own), own],
        work,
        flops=4 * 10**9,
    )
    got_edges += exchange(outer)
    for done in range(0, STEPS, cx):
        first, last = done == 0, done + cx == STEPS
        after = done + cx
        outs = [(9, cx, cz // 2, cy)] * 2
        if not last:
            outs = reached_edges(after) + [(2, 9, *own)]
            outs += [(2, 3, *window), window] * first
        pair = call(
            functools.partial(next_kernel, cx, done),
            "steps",
            (both, coef, times, *got_edges) + (tables,) * first,
            (),
            outs,
            work if first else work[0:1],
        )
        if not last:
            got_edges = exchange(pair[0:2])
            both = pair[2]
            if first:
                coef, times = pair[3:5]
    to_first, to_second = pair[0:2]
    (out,) = call(home_kernel, "home", (to_first, swap(to_second)), (), [fields.shape], [])
    return out


def solution(mesh):
    in_specs = (
        P("segment", None, "sec", "depth", None),
        P("segment", "sec", "depth", None),
        P(),
        P(),
        P(),
        P(None, ("sec", "depth")),
        P(("sec", "depth"), None),
        P(("sec", "depth")),
        P(("sec", "depth")),
    )
    out_specs = P("segment", None, "sec", "depth", None)
    return jax.shard_map(
        on_device, mesh=mesh, in_specs=in_specs, out_specs=out_specs, check_vma=False
    )
```

```python
import functools

import jax
import jax.numpy as jnp
from jax import lax
from jax.experimental import pallas as pl
from jax.experimental.pallas import tpu as pltpu
from jax.sharding import PartitionSpec as P

STEPS = 4
F32 = jnp.float32
BF16 = jnp.bfloat16
NT = (((1,), (1,)), ((), ()))


def one_hot(index, count):
    rows = lax.broadcasted_iota(jnp.int32, (count, index.shape[-1]), 0)
    return jnp.where(rows == index, F32(1.0), F32(0.0))


def split3(value):
    high = value.astype(BF16).astype(F32)
    rest = value - high
    mid = rest.astype(BF16).astype(F32)
    return high, mid, rest - mid


def copy_all(sem, pairs):
    copies = [pltpu.make_async_copy(a, b, sem.at[i]) for i, (a, b) in enumerate(pairs)]
    for copy in copies:
        copy.start()
    for copy in copies:
        copy.wait()


def in_line(rows):
    return jnp.concatenate([rows[i : i + 1, :] for i in range(rows.shape[0])], axis=1)


def reach_of(cz):
    return cz // 2 + STEPS


def pack_kernel(
    fields_in, ids_in, moments_in, owner_in, cells_in, rows_in, buoyancy, lame_lambda, lame_mu,
    entries, kept, given, fields, ids, moments, owner, cells, rows, wide, tables, sem,
):
    cx, cz, cy = ids.shape[1:]
    arguments = [(fields_in, fields), (ids_in, ids), (moments_in, moments), (owner_in, owner)]
    arguments += [(cells_in, cells), (rows_in, rows)]
    arguments += [(t, tables.at[i]) for i, t in enumerate((buoyancy, lame_lambda, lame_mu))]
    copy_all(sem, arguments)
    for i in range(cells.shape[0]):
        at = 8 * i
        entries[at : at + 6] = moments[:, i * cy : (i + 1) * cy]
        entries[at + 6 : at + 7] = owner[i : i + 1, :].astype(F32)
        entries[at + 7 : at + 8] = cells[i : i + 1, :].astype(F32)
    wide[0] = (ids[0] + 1).astype(F32)
    line = in_line(rows[...])
    high = one_hot(line // cy, cx * cz).astype(BF16)
    low = one_hot(line % cy, cy).astype(BF16)
    count = lax.dot_general(high, low, NT, preferred_element_type=F32)
    wide[1] = count.reshape(cx, cz, cy)
    reach = reach_of(cz)
    lines = 11 * cx * reach
    lane = lax.broadcasted_iota(jnp.int32, (1, cy), 1)
    for i in range(3):
        found = jnp.zeros((1, cy), F32)
        for entry in range(tables.shape[1]):
            found = jnp.where(lane == entry + 1, F32(0.5) * tables[i, entry], found)
        kept[lines + i : lines + i + 1] = found
    kept[lines + 3 : lines + 8] = jnp.zeros((5, cy), F32)
    kept[lines + 8 :] = entries[...]

    def cut(first, other):
        for x in range(cx):
            at = slice(x * reach, (x + 1) * reach)
            for k in range(11):
                source = fields.at[0, k] if k < 9 else wide.at[k - 9]
                line = (k * cx + x) * reach
                kept[line : line + reach] = source[x, first : first + reach]
            given[0:9, at] = fields[0, :, x, other : other + reach]
            given[9, at] = wide[0, x, other : other + reach]

    @pl.when(lax.axis_index("segment") == 0)
    def _():
        cut(0, cz - reach)

    @pl.when(lax.axis_index("segment") == 1)
    def _():
        cut(cz - reach, 0)


def moments_of(layout, entries):
    cx, cz, cy = layout
    section = lax.axis_index("sec")
    half = cx * cz // 2
    chunk = [entries[8 * i : 8 * i + 8] for i in range(entries.shape[0] // 8)]
    entry = jnp.concatenate(chunk, axis=1)
    owner = entry[6:7].astype(jnp.int32)
    cell = entry[7:8].astype(jnp.int32)
    line = jnp.where(owner == section, cell // cy, -1)
    upper = line >= half
    high = one_hot(jnp.where(upper, line - half, line), half)
    low = one_hot(jnp.where(upper, cell % cy + cy, cell % cy), 2 * cy).astype(BF16)
    parts = split3(entry[0:6])
    spread = [(high * part[c : c + 1]).astype(BF16) for part in parts for c in range(6)]
    spread = jnp.concatenate(spread, axis=0)
    got = lax.dot_general(spread, low, NT, preferred_element_type=F32)
    lines = 6 * half
    return got[0:lines] + got[lines : 2 * lines] + got[2 * lines :]


def own_kernel(layout, kept, out, tables, acc):
    lines = out.shape[0] * out.shape[1]
    out[...] = kept[0:lines].reshape(out.shape)
    tables[...] = kept[lines : lines + 8]
    acc[...] = moments_of(layout, kept[lines + 8 :])


def more_kernel(layout, started, entries, acc):
    acc[...] = started[...] + moments_of(layout, entries[...])


def by_core(act):
    segment = lax.axis_index("segment")

    @pl.when(segment == 0)
    def _():
        act(0, lambda reach: slice(STEPS, STEPS + reach), lambda reach: slice(0, STEPS))

    @pl.when(segment == 1)
    def _():
        act(1, lambda reach: slice(0, reach), lambda reach: slice(reach, reach + STEPS))


def join_kernel(layout, *refs):
    cx, cz, cy = layout
    kept, got, started, entries, state, ids, times, edge, dense = refs
    reach = reach_of(cz)
    half = cx * cz // 2
    total = started[...] + moments_of(layout, entries[...])
    for c in range(6):
        for k in range(2):
            added = total[c * half : (c + 1) * half, k * cy : (k + 1) * cy]
            dense[c, k * half : (k + 1) * half] = added

    def join(mine, main, outer):
        main, outer = main(reach), outer(reach)
        first = 0 if mine == 0 else cz - reach
        last = main.start if mine == 0 else main.stop - STEPS
        gone = slice(last, last + STEPS)
        for x in range(cx):
            at = slice(x * reach, (x + 1) * reach)
            for model in range(2):
                rows = kept if model == mine else got
                state[model, :, x, main] = rows[0:9, at]
                ids[model, x, main] = rows[9, at]
            added = dense[:, x * cz + first : x * cz + first + reach]
            state[0, 3:9, x, main] = state[0, 3:9, x, main] + added
            times[x, main] = kept[10, at]
            state[:, :, x, outer] = jnp.zeros((2, 9, STEPS, cy), F32)
            ids[:, x, outer] = jnp.zeros((2, STEPS, cy), F32)
            times[x, outer] = jnp.zeros((STEPS, cy), F32)
            for k in range(21):
                line = slice((k * cx + x) * STEPS, (k * cx + x + 1) * STEPS)
                if k == 20:
                    edge[line] = times[x, gone]
                elif k % 10 == 9:
                    edge[line] = ids[k // 10, x, gone]
                else:
                    edge[line] = state[k // 10, k % 10, x, gone]

    by_core(join)


def by_parity(even, odd, act):
    parity = lax.axis_index("sec") % 2

    @pl.when(parity == 0)
    def _():
        act(*even)

    @pl.when(parity == 1)
    def _():
        act(*odd)


def advance(cx, steps, state, coef, times, given_top=False):
    planes, rows, cy = state.shape[2:]
    lane = lax.broadcasted_iota(jnp.int32, (rows, cy), 1)
    first_lane, last_lane = lane == 0, lane == cy - 1

    def back_y(f):
        return f - jnp.where(first_lane, F32(0.0), pltpu.roll(f, 1, 1))

    def back_z(f):
        return f - pltpu.roll(f, 1, 0)

    def fore_y(f):
        return jnp.where(last_lane, F32(0.0), pltpu.roll(f, cy - 1, 1)) - f

    def fore_z(f):
        return pltpu.roll(f, rows - 1, 0) - f

    def velocity(x):
        inc = [None, None]
        for model in range(2):
            sxx, syy, szz, syz, sxz, sxy = (state[model, 3 + k, x] for k in range(6))
            sxx_p, sxz_p, sxy_p = (state[model, k, x - 1] for k in (3, 7, 8))
            hb = coef[model, 0, x]
            inc[model] = (
                hb * ((sxx - sxx_p) + back_y(sxy) + back_z(sxz)),
                hb * ((sxy - sxy_p) + back_y(syy) + back_z(syz)),
                hb * ((sxz - sxz_p) + back_y(syz) + back_z(szz)),
            )
        for k in range(3):
            state[0, k, x] = state[0, k, x] + inc[0][k]
            state[1, k, x] = (state[1, k, x] + inc[1][k]) + times[x] * inc[0][k]

    for step in range(steps):
        left = steps - 1 - step
        low, high = cx - left, 2 * cx + left
        for x in range(low, high + 1 - (given_top and step == 0)):
            velocity(x)
        for x in range(low, high):
            for model in range(2):
                vx, vy, vz = (state[model, k, x] for k in range(3))
                vx_n, vy_n, vz_n = (state[model, k, x + 1] for k in range(3))
                hl, hm = coef[model, 1, x], coef[model, 2, x]
                exx, eyy, ezz = vx_n - vx, fore_y(vy), fore_z(vz)
                pressure = hl * (exx + eyy + ezz)
                twice = hm + hm
                state[model, 3, x] = state[model, 3, x] + (pressure + twice * exx)
                state[model, 4, x] = state[model, 4, x] + (pressure + twice * eyy)
                state[model, 5, x] = state[model, 5, x] + (pressure + twice * ezz)
                state[model, 6, x] = state[model, 6, x] + hm * (fore_z(vy) + fore_y(vz))
                state[model, 7, x] = state[model, 7, x] + hm * (fore_z(vx) + (vz_n - vz))
                state[model, 8, x] = state[model, 8, x] + hm * (fore_y(vx) + (vy_n - vy))

    return velocity


def look_up(tables, ids):
    lanes = ids.astype(jnp.int32)
    wide = [jnp.broadcast_to(tables[i : i + 1], ids.shape) for i in range(3)]
    return [jnp.take_along_axis(table, lanes, axis=1) for table in wide]


def edge_units(cx, with_ids):
    right, left = [], []
    for model in range(2):
        whole = list(range(10 if with_ids else 9)) + [10] * (with_ids and model == 1)
        for x in range(cx - 1):
            right += [(model, what, x + 1) for what in whole]
            left += [(model, what, x) for what in whole]
        right += [(model, what, 0) for what in (3, 7, 8)]
        left += [(model, what, cx - 1) for what in range(3)]
    return right, left


def cut_edges(cx, rows_of, with_ids, velocity, state, ids, times, to_first, to_second):
    right_units, left_units = edge_units(cx, with_ids)

    def put(to, units, far, right):
        line = slice(0, 0)
        for model, what, x in units:
            at = rows_of(x == far, right)
            line = slice(line.stop, line.stop + at.stop - at.start)
            if what == 10:
                to[line] = times[cx + x, at]
            elif what == 9:
                to[line] = ids[model, cx + x, at]
            else:
                to[line] = state[model, what, cx + x, at]

    holders = (to_second, to_first), (to_first, to_second)
    by_parity(*holders, lambda left, right: put(right, right_units, 0, True))
    velocity(2 * cx - 1)
    by_parity(*holders, lambda left, right: put(left, left_units, cx - 1, False))


def outer_rows(mine, outer):
    def rows_of(far, right):
        shift = 1 if far and not right and mine == 0 else 0
        return slice(outer.start + shift, outer.stop + shift)

    return rows_of


def reached_rows(cx, done, rows):
    def rows_of(far, right):
        first, last = done, rows - done
        if right:
            return slice(first + (cx if far else 1), last)
        return slice(first + far, last - (cx if far else 1))

    return rows_of


def coefficients(cx, planes, tables, ids, coef):
    for model in range(2):
        for x in planes:
            for i, found in enumerate(look_up(tables, ids[model, x])):
                coef[model, i, x] = found


def inner_kernel(cx, own_state, own_ids, own_times, tables, to_first, to_second, state, ids, coef, times):
    own = slice(cx, 2 * cx)
    reach = state.shape[3] - STEPS
    state[:, :, own], ids[:, own], times[own] = own_state[...], own_ids[...], own_times[...]
    coefficients(cx, range(2 * cx - 1, 2 * cx), tables, ids, coef)
    velocity = advance(cx, 0, state, coef, times)

    def cut(mine, main, outer):
        rows_of = lambda far, right: main(reach)
        cut_edges(cx, rows_of, True, velocity, state, ids, times, to_first, to_second)

    by_core(cut)


def outer_kernel(
    cx, own_state, own_ids, own_times, halo, tables,
    to_first, to_second, both, coef_out, times_out, state, ids, coef, times,
):
    own = slice(cx, 2 * cx)
    reach = state.shape[3] - STEPS
    state[:, :, own], ids[:, own], times[own] = own_state[...], own_ids[...], own_times[...]

    def join(mine, main, outer):
        for x in range(cx):
            for k in range(21):
                line = halo[(k * cx + x) * STEPS : (k * cx + x + 1) * STEPS]
                if k == 20:
                    times[cx + x, outer(reach)] = line
                elif k % 10 == 9:
                    ids[k // 10, cx + x, outer(reach)] = line
                else:
                    state[k // 10, k % 10, cx + x, outer(reach)] = line

    by_core(join)
    coefficients(cx, range(cx, 2 * cx), tables, ids, coef)
    both[...] = state[:, :, own]
    coef_out[...] = coef[:, :, own]
    times_out[...] = times[own]
    velocity = advance(cx, 0, state, coef, times)

    def cut(mine, main, outer):
        rows_of = outer_rows(mine, outer(reach))
        cut_edges(cx, rows_of, True, velocity, state, ids, times, to_first, to_second)

    by_core(cut)


def next_kernel(cx, done, *refs):
    first = done == 0
    parts = 2 if first else 1
    both_in, coef_in, times_in = refs[0:3]
    edges, refs = refs[3 : 3 + 2 * parts], refs[3 + 2 * parts :]
    if first:
        tables, outs = refs[0], refs[1:]
        state, ids, coef, times = refs[-4:]
    else:
        ids, outs = None, refs
        state, coef, times = refs[-1], coef_in, times_in
    segment = lax.axis_index("segment")
    rows = state.shape[3]
    own = slice(cx, 2 * cx)
    state[:, :, own] = both_in[...]
    right_units, left_units = edge_units(cx, first)

    def get(edge, units, start, rows_of, far, right):
        last = 0
        for model, what, x in units:
            at = rows_of(x == far, right)
            first, last = last, last + at.stop - at.start
            line = edge[first:last]
            if what == 10:
                times[start + x, at] = line
            elif what == 9:
                ids[model, start + x, at] = line
            else:
                state[model, what, start + x, at] = line

    def place(rows_of, pair):
        def put(left, right):
            get(left, right_units, 0, rows_of, 0, True)
            get(right, left_units, 2 * cx, rows_of, cx - 1, False)

        by_parity((pair[1], pair[0]), pair, put)

    if first:

        def place_both(mine, main, outer):
            reach = rows - STEPS
            place(lambda far, right: main(reach), edges[0:2])
            place(outer_rows(mine, outer(reach)), edges[2:4])

        by_core(place_both)
        coef[:, :, own] = coef_in[...]
        times[own] = times_in[...]
        coefficients(cx, (*range(1, cx), *range(2 * cx, 3 * cx - 1)), tables, ids, coef)
    else:
        place(reached_rows(cx, done, rows), edges)
    velocity = advance(cx, cx, state, coef, times, given_top=True)
    if done + cx == STEPS:
        outs[0][...] = state[segment, :, own, STEPS : rows - STEPS]
        outs[1][...] = state[1 - segment, :, own, STEPS : rows - STEPS]
    else:
        outs[2][...] = state[:, :, own]
        if first:
            outs[3][...] = coef[...]
            outs[4][...] = times[...]
        rows_of = reached_rows(cx, done + cx, rows)
        cut_edges(cx, rows_of, False, velocity, state, None, times, outs[0], outs[1])


def home_kernel(mine, brought, out):
    half = mine.shape[2]
    segment = lax.axis_index("segment")

    @pl.when(segment == 0)
    def _():
        out[0, :, :, 0:half] = mine[...]
        out[0, :, :, half:] = brought[...]

    @pl.when(segment == 1)
    def _():
        out[0, :, :, half:] = mine[...]
        out[0, :, :, 0:half] = brought[...]


VMEM = pl.BlockSpec(memory_space=pltpu.VMEM)
HBM = pl.BlockSpec(memory_space=pltpu.HBM)


def call(kernel, name, in_vmem, in_hbm, outs, scratch, copies=0, limit=40 * 2**20, flops=10**7):
    sems = [pltpu.SemaphoreType.DMA((copies,))] * (copies > 0)
    return pl.pallas_call(
        kernel,
        out_shape=[jax.ShapeDtypeStruct(shape, F32) for shape in outs],
        in_specs=[VMEM] * len(in_vmem) + [HBM] * len(in_hbm),
        out_specs=[VMEM] * len(outs),
        scratch_shapes=[pltpu.VMEM(s, F32) if isinstance(s, tuple) else s for s in scratch] + sems,
        compiler_params=pltpu.CompilerParams(vmem_limit_bytes=limit),
        cost_estimate=pl.CostEstimate(flops=flops, bytes_accessed=2**20, transcendentals=0),
        name=name,
    )(*in_vmem, *in_hbm)


def on_device(
    fields, block_ids, buoyancy, lame_lambda, lame_mu, moments, moment_owner, moment_cells, drm_rows
):
    sections, slabs = lax.axis_size("sec"), lax.axis_size("depth")
    layout = cx, cz, cy = fields.shape[2:]
    reach, rows = reach_of(cz), cz // 2 + 2 * STEPS
    assert cx > 1 and STEPS % cx == 0

    def pairs(block, start):
        route = [(i, i + 1) for i in range(start, sections - 1, 2)]
        return lax.ppermute(block, "sec", route + [(j, i) for i, j in route])

    def other(section, k):
        return section ^ k if sections & (sections - 1) == 0 else (section + k) % sections

    def along_depth(block):
        down = [(2 * i + 1, 2 * (i + 1)) for i in range(slabs - 1)]
        return lax.ppermute(block, ("depth", "segment"), down + [(j, i) for i, j in down])

    def swap(block):
        return lax.ppermute(block, "segment", [(0, 1), (1, 0)])

    owner = moment_owner.reshape(-1, cy)
    cells = moment_cells.reshape(-1, cy)
    arguments = (fields, block_ids, moments, owner, cells, drm_rows.reshape(-1, cy))
    entry_lines = 8 * cells.shape[0]
    entries, kept, given = call(
        pack_kernel,
        "pack",
        (),
        (*arguments, buoyancy, lame_lambda, lame_mu),
        [(entry_lines, cy), (11 * cx * reach + 8 + entry_lines, cy), (10, cx * reach, cy)],
        [pltpu.VMEM(a.shape, a.dtype) for a in arguments]
        + [(2, cx, cz, cy), pltpu.SMEM((3, buoyancy.shape[0]), F32)],
        len(arguments) + 3,
        limit=64 * 2**20,
    )
    blocks = [
        lax.ppermute(entries, "sec", [(other(i, k), i) for i in range(sections)])
        for k in (sections - 1, *range(1, sections - 1))
    ]
    got = swap(given)
    acc_shape = (6 * cx * cz // 2, 2 * cy)
    kept, tables, started = call(
        functools.partial(own_kernel, layout),
        "own_moments",
        (kept,),
        (),
        [(11, cx * reach, cy), (8, cy), acc_shape],
        [],
        flops=10**8,
    )
    for block in blocks[:-1]:
        (started,) = call(
            functools.partial(more_kernel, layout),
            "more_moments",
            (started, block),
            (),
            [acc_shape],
            [],
            flops=6 * 10**9,
        )
    own = (cx, rows, cy)
    window = (3 * cx, rows, cy)
    state, ids, times, edge = call(
        functools.partial(join_kernel, layout),
        "join_and_moments",
        (kept, got, started, blocks[-1]),
        (),
        [(2, 9, *own), (2, *own), own, (21 * cx * STEPS, cy)],
        [(6, cx * cz, cy)],
    )
    halo = along_depth(edge)
    work = [(2, 9, *window), (2, *window), (2, 3, *window), window]

    def edges(count, with_ids):
        return [(len(edge_units(cx, with_ids)[0]) * count, cy)] * 2

    def reached_edges(done):
        rows_of = reached_rows(cx, done, rows)
        whole, far = rows_of(False, True), rows_of(True, True)
        lines = 18 * (cx - 1) * (whole.stop - whole.start) + 6 * (far.stop - far.start)
        return [(-(-lines // 8) * 8, cy)] * 2

    def exchange(pair):
        return [pairs(pair[0], 0), pairs(pair[1], 1)]

    inner = call(
        functools.partial(inner_kernel, cx),
        "inner_edges",
        (state, ids, times, tables),
        (),
        edges(reach, True),
        work,
        flops=10**9,
    )
    got_edges = exchange(inner)
    *outer, both, coef, times = call(
        functools.partial(outer_kernel, cx),
        "outer_edges",
        (state, ids, times, halo, tables),
        (),
        edges(STEPS, True) + [(2, 9, *own), (2, 3, *own), own],
        work,
        flops=4 * 10**9,
    )
    got_edges += exchange(outer)
    for done in range(0, STEPS, cx):
        first, last = done == 0, done + cx == STEPS
        after = done + cx
        outs = [(9, cx, cz // 2, cy)] * 2
        if not last:
            outs = reached_edges(after) + [(2, 9, *own)]
            outs += [(2, 3, *window), window] * first
        pair = call(
            functools.partial(next_kernel, cx, done),
            "steps",
            (both, coef, times, *got_edges) + (tables,) * first,
            (),
            outs,
            work if first else work[0:1],
        )
        if not last:
            got_edges = exchange(pair[0:2])
            both = pair[2]
            if first:
                coef, times = pair[3:5]
    to_first, to_second = pair[0:2]
    (out,) = call(home_kernel, "home", (to_first, swap(to_second)), (), [fields.shape], [])
    return out


def solution(mesh):
    in_specs = (
        P("segment", None, "sec", "depth", None),
        P("segment", "sec", "depth", None),
        P(),
        P(),
        P(),
        P(None, ("sec", "depth")),
        P(("sec", "depth"), None),
        P(("sec", "depth")),
        P(("sec", "depth")),
    )
    out_specs = P("segment", None, "sec", "depth", None)
    return jax.shard_map(
        on_device, mesh=mesh, in_specs=in_specs, out_specs=out_specs, check_vma=False
    )
```

```python
import functools

import jax
import jax.numpy as jnp
from jax import lax
from jax.experimental import pallas as pl
from jax.experimental.pallas import tpu as pltpu
from jax.sharding import PartitionSpec as P

STEPS = 4
F32 = jnp.float32
BF16 = jnp.bfloat16
NT = (((1,), (1,)), ((), ()))


def one_hot(index, count):
    rows = lax.broadcasted_iota(jnp.int32, (count, index.shape[-1]), 0)
    return jnp.where(rows == index, F32(1.0), F32(0.0))


def split3(value):
    high = value.astype(BF16).astype(F32)
    rest = value - high
    mid = rest.astype(BF16).astype(F32)
    return high, mid, rest - mid


def copy_all(sem, pairs):
    copies = [pltpu.make_async_copy(a, b, sem.at[i]) for i, (a, b) in enumerate(pairs)]
    for copy in copies:
        copy.start()
    for copy in copies:
        copy.wait()


def in_line(rows):
    return jnp.concatenate([rows[i : i + 1, :] for i in range(rows.shape[0])], axis=1)


def reach_of(cz):
    return cz // 2 + STEPS


def pack_kernel(
    fields_in, ids_in, moments_in, owner_in, cells_in, rows_in, buoyancy, lame_lambda, lame_mu,
    entries, kept, given, fields, ids, moments, owner, cells, rows, wide, tables, sem,
):
    cx, cz, cy = ids.shape[1:]
    arguments = [(fields_in, fields), (ids_in, ids), (moments_in, moments), (owner_in, owner)]
    arguments += [(cells_in, cells), (rows_in, rows)]
    arguments += [(t, tables.at[i]) for i, t in enumerate((buoyancy, lame_lambda, lame_mu))]
    copy_all(sem, arguments)
    for i in range(cells.shape[0]):
        at = 8 * i
        entries[at : at + 6] = moments[:, i * cy : (i + 1) * cy]
        entries[at + 6 : at + 7] = owner[i : i + 1, :].astype(F32)
        entries[at + 7 : at + 8] = cells[i : i + 1, :].astype(F32)
    wide[0] = (ids[0] + 1).astype(F32)
    line = in_line(rows[...])
    high = one_hot(line // cy, cx * cz).astype(BF16)
    low = one_hot(line % cy, cy).astype(BF16)
    count = lax.dot_general(high, low, NT, preferred_element_type=F32)
    wide[1] = count.reshape(cx, cz, cy)
    reach = reach_of(cz)
    lines = 11 * cx * reach
    lane = lax.broadcasted_iota(jnp.int32, (1, cy), 1)
    for i in range(3):
        found = jnp.zeros((1, cy), F32)
        for entry in range(tables.shape[1]):
            found = jnp.where(lane == entry + 1, F32(0.5) * tables[i, entry], found)
        kept[lines + i : lines + i + 1] = found
    kept[lines + 3 : lines + 8] = jnp.zeros((5, cy), F32)
    kept[lines + 8 :] = entries[...]

    def cut(first, other):
        for x in range(cx):
            at = slice(x * reach, (x + 1) * reach)
            for k in range(11):
                source = fields.at[0, k] if k < 9 else wide.at[k - 9]
                line = (k * cx + x) * reach
                kept[line : line + reach] = source[x, first : first + reach]
            given[0:9, at] = fields[0, :, x, other : other + reach]
            given[9, at] = wide[0, x, other : other + reach]

    @pl.when(lax.axis_index("segment") == 0)
    def _():
        cut(0, cz - reach)

    @pl.when(lax.axis_index("segment") == 1)
    def _():
        cut(cz - reach, 0)


def moments_of(layout, entries):
    cx, cz, cy = layout
    section = lax.axis_index("sec")
    half = cx * cz // 2
    chunk = [entries[8 * i : 8 * i + 8] for i in range(entries.shape[0] // 8)]
    entry = jnp.concatenate(chunk, axis=1)
    owner = entry[6:7].astype(jnp.int32)
    cell = entry[7:8].astype(jnp.int32)
    line = jnp.where(owner == section, cell // cy, -1)
    upper = line >= half
    high = one_hot(jnp.where(upper, line - half, line), half)
    low = one_hot(jnp.where(upper, cell % cy + cy, cell % cy), 2 * cy).astype(BF16)
    parts = split3(entry[0:6])
    spread = [(high * part[c : c + 1]).astype(BF16) for part in parts for c in range(6)]
    spread = jnp.concatenate(spread, axis=0)
    got = lax.dot_general(spread, low, NT, preferred_element_type=F32)
    lines = 6 * half
    return got[0:lines] + got[lines : 2 * lines] + got[2 * lines :]


def own_kernel(layout, kept, out, tables, acc):
    lines = out.shape[0] * out.shape[1]
    out[...] = kept[0:lines].reshape(out.shape)
    tables[...] = kept[lines : lines + 8]
    acc[...] = moments_of(layout, kept[lines + 8 :])


def more_kernel(layout, started, entries, acc):
    acc[...] = started[...] + moments_of(layout, entries[...])


def by_core(act):
    segment = lax.axis_index("segment")

    @pl.when(segment == 0)
    def _():
        act(0, lambda reach: slice(STEPS, STEPS + reach), lambda reach: slice(0, STEPS))

    @pl.when(segment == 1)
    def _():
        act(1, lambda reach: slice(0, reach), lambda reach: slice(reach, reach + STEPS))


def join_kernel(layout, *refs):
    cx, cz, cy = layout
    kept, got, started, entries, state, ids, times, edge, dense = refs
    reach = reach_of(cz)
    half = cx * cz // 2
    total = started[...] + moments_of(layout, entries[...])
    for c in range(6):
        for k in range(2):
            added = total[c * half : (c + 1) * half, k * cy : (k + 1) * cy]
            dense[c, k * half : (k + 1) * half] = added

    def join(mine, main, outer):
        main, outer = main(reach), outer(reach)
        first = 0 if mine == 0 else cz - reach
        last = main.start if mine == 0 else main.stop - STEPS
        gone = slice(last, last + STEPS)
        for x in range(cx):
            at = slice(x * reach, (x + 1) * reach)
            for model in range(2):
                rows = kept if model == mine else got
                state[model, :, x, main] = rows[0:9, at]
                ids[model, x, main] = rows[9, at]
            added = dense[:, x * cz + first : x * cz + first + reach]
            state[0, 3:9, x, main] = state[0, 3:9, x, main] + added
            times[x, main] = kept[10, at]
            state[:, :, x, outer] = jnp.zeros((2, 9, STEPS, cy), F32)
            ids[:, x, outer] = jnp.zeros((2, STEPS, cy), F32)
            times[x, outer] = jnp.zeros((STEPS, cy), F32)
            for k in range(21):
                line = slice((k * cx + x) * STEPS, (k * cx + x + 1) * STEPS)
                if k == 20:
                    edge[line] = times[x, gone]
                elif k % 10 == 9:
                    edge[line] = ids[k // 10, x, gone]
                else:
                    edge[line] = state[k // 10, k % 10, x, gone]

    by_core(join)


def by_parity(even, odd, act):
    parity = lax.axis_index("sec") % 2

    @pl.when(parity == 0)
    def _():
        act(*even)

    @pl.when(parity == 1)
    def _():
        act(*odd)


def advance(cx, steps, state, coef, times, given_top=False):
    planes, rows, cy = state.shape[2:]
    lane = lax.broadcasted_iota(jnp.int32, (rows, cy), 1)
    first_lane, last_lane = lane == 0, lane == cy - 1

    def back_y(f):
        return f - jnp.where(first_lane, F32(0.0), pltpu.roll(f, 1, 1))

    def back_z(f):
        return f - pltpu.roll(f, 1, 0)

    def fore_y(f):
        return jnp.where(last_lane, F32(0.0), pltpu.roll(f, cy - 1, 1)) - f

    def fore_z(f):
        return pltpu.roll(f, rows - 1, 0) - f

    def velocity(x):
        inc = [None, None]
        for model in range(2):
            sxx, syy, szz, syz, sxz, sxy = (state[model, 3 + k, x] for k in range(6))
            sxx_p, sxz_p, sxy_p = (state[model, k, x - 1] for k in (3, 7, 8))
            hb = coef[model, 0, x]
            inc[model] = (
                hb * ((sxx - sxx_p) + back_y(sxy) + back_z(sxz)),
                hb * ((sxy - sxy_p) + back_y(syy) + back_z(syz)),
                hb * ((sxz - sxz_p) + back_y(syz) + back_z(szz)),
            )
        for k in range(3):
            state[0, k, x] = state[0, k, x] + inc[0][k]
            state[1, k, x] = (state[1, k, x] + inc[1][k]) + times[x] * inc[0][k]

    for step in range(steps):
        left = steps - 1 - step
        low, high = cx - left, 2 * cx + left
        for x in range(low, high + 1 - (given_top and step == 0)):
            velocity(x)
        for x in range(low, high):
            for model in range(2):
                vx, vy, vz = (state[model, k, x] for k in range(3))
                vx_n, vy_n, vz_n = (state[model, k, x + 1] for k in range(3))
                hl, hm = coef[model, 1, x], coef[model, 2, x]
                exx, eyy, ezz = vx_n - vx, fore_y(vy), fore_z(vz)
                pressure = hl * (exx + eyy + ezz)
                twice = hm + hm
                state[model, 3, x] = state[model, 3, x] + (pressure + twice * exx)
                state[model, 4, x] = state[model, 4, x] + (pressure + twice * eyy)
                state[model, 5, x] = state[model, 5, x] + (pressure + twice * ezz)
                state[model, 6, x] = state[model, 6, x] + hm * (fore_z(vy) + fore_y(vz))
                state[model, 7, x] = state[model, 7, x] + hm * (fore_z(vx) + (vz_n - vz))
                state[model, 8, x] = state[model, 8, x] + hm * (fore_y(vx) + (vy_n - vy))

    return velocity


def look_up(tables, ids):
    lanes = ids.astype(jnp.int32)
    wide = [jnp.broadcast_to(tables[i : i + 1], ids.shape) for i in range(3)]
    return [jnp.take_along_axis(table, lanes, axis=1) for table in wide]


def edge_units(cx, with_ids):
    right, left = [], []
    for model in range(2):
        whole = list(range(10 if with_ids else 9)) + [10] * (with_ids and model == 1)
        for x in range(cx - 1):
            right += [(model, what, x + 1) for what in whole]
            left += [(model, what, x) for what in whole]
        right += [(model, what, 0) for what in (3, 7, 8)]
        left += [(model, what, cx - 1) for what in range(3)]
    return right, left


def cut_edges(cx, rows_of, with_ids, velocity, state, ids, times, to_first, to_second):
    right_units, left_units = edge_units(cx, with_ids)

    def put(to, units, far, right):
        line = slice(0, 0)
        for model, what, x in units if to is not None else ():
            at = rows_of(x == far, right)
            line = slice(line.stop, line.stop + at.stop - at.start)
            if what == 10:
                to[line] = times[cx + x, at]
            elif what == 9:
                to[line] = ids[model, cx + x, at]
            else:
                to[line] = state[model, what, cx + x, at]

    holders = (to_second, to_first), (to_first, to_second)
    by_parity(*holders, lambda left, right: put(right, right_units, 0, True))
    velocity(2 * cx - 1)
    by_parity(*holders, lambda left, right: put(left, left_units, cx - 1, False))


def arrived_kernel(edge, out):
    out[...] = edge[...]


def outer_rows(mine, outer):
    def rows_of(far, right):
        shift = 1 if far and not right and mine == 0 else 0
        return slice(outer.start + shift, outer.stop + shift)

    return rows_of


def reached_rows(cx, done, rows):
    def rows_of(far, right):
        first, last = done, rows - done
        if right:
            return slice(first + (cx if far else 1), last)
        return slice(first + far, last - (cx if far else 1))

    return rows_of


def coefficients(cx, planes, tables, ids, coef):
    for model in range(2):
        for x in planes:
            for i, found in enumerate(look_up(tables, ids[model, x])):
                coef[model, i, x] = found


def inner_kernel(cx, pairing, own_state, own_ids, own_times, tables, to, state, ids, coef, times):
    own = slice(cx, 2 * cx)
    reach = state.shape[3] - STEPS
    state[:, :, own], ids[:, own], times[own] = own_state[...], own_ids[...], own_times[...]
    coefficients(cx, range(2 * cx - 1, 2 * cx), tables, ids, coef)
    velocity = advance(cx, 0, state, coef, times)

    def cut(mine, main, outer):
        rows_of = lambda far, right: main(reach)
        both = (to, None) if pairing == 0 else (None, to)
        cut_edges(cx, rows_of, True, velocity, state, ids, times, *both)

    by_core(cut)


def outer_kernel(
    cx, own_state, own_ids, own_times, halo, tables,
    to_first, to_second, both, coef_out, times_out, state, ids, coef, times,
):
    own = slice(cx, 2 * cx)
    reach = state.shape[3] - STEPS
    state[:, :, own], ids[:, own], times[own] = own_state[...], own_ids[...], own_times[...]

    def join(mine, main, outer):
        for x in range(cx):
            for k in range(21):
                line = halo[(k * cx + x) * STEPS : (k * cx + x + 1) * STEPS]
                if k == 20:
                    times[cx + x, outer(reach)] = line
                elif k % 10 == 9:
                    ids[k // 10, cx + x, outer(reach)] = line
                else:
                    state[k // 10, k % 10, cx + x, outer(reach)] = line

    by_core(join)
    coefficients(cx, range(cx, 2 * cx), tables, ids, coef)
    both[...] = state[:, :, own]
    coef_out[...] = coef[:, :, own]
    times_out[...] = times[own]
    velocity = advance(cx, 0, state, coef, times)

    def cut(mine, main, outer):
        rows_of = outer_rows(mine, outer(reach))
        cut_edges(cx, rows_of, True, velocity, state, ids, times, to_first, to_second)

    by_core(cut)


def next_kernel(cx, done, *refs):
    first = done == 0
    parts = 2 if first else 1
    both_in, coef_in, times_in = refs[0:3]
    edges, refs = refs[3 : 3 + 2 * parts], refs[3 + 2 * parts :]
    if first:
        tables, outs = refs[0], refs[1:]
        state, ids, coef, times = refs[-4:]
    else:
        ids, outs = None, refs
        state, coef, times = refs[-1], coef_in, times_in
    segment = lax.axis_index("segment")
    rows = state.shape[3]
    own = slice(cx, 2 * cx)
    state[:, :, own] = both_in[...]
    right_units, left_units = edge_units(cx, first)

    def get(edge, units, start, rows_of, far, right):
        last = 0
        for model, what, x in units:
            at = rows_of(x == far, right)
            first, last = last, last + at.stop - at.start
            line = edge[first:last]
            if what == 10:
                times[start + x, at] = line
            elif what == 9:
                ids[model, start + x, at] = line
            else:
                state[model, what, start + x, at] = line

    def place(rows_of, pair):
        def put(left, right):
            get(left, right_units, 0, rows_of, 0, True)
            get(right, left_units, 2 * cx, rows_of, cx - 1, False)

        by_parity((pair[1], pair[0]), pair, put)

    if first:

        def place_both(mine, main, outer):
            reach = rows - STEPS
            place(lambda far, right: main(reach), edges[0:2])
            place(outer_rows(mine, outer(reach)), edges[2:4])

        by_core(place_both)
        coef[:, :, own] = coef_in[...]
        times[own] = times_in[...]
        coefficients(cx, (*range(1, cx), *range(2 * cx, 3 * cx - 1)), tables, ids, coef)
    else:
        place(reached_rows(cx, done, rows), edges)
    velocity = advance(cx, cx, state, coef, times, given_top=True)
    if done + cx == STEPS:
        outs[0][...] = state[segment, :, own, STEPS : rows - STEPS]
        outs[1][...] = state[1 - segment, :, own, STEPS : rows - STEPS]
    else:
        outs[2][...] = state[:, :, own]
        if first:
            outs[3][...] = coef[...]
            outs[4][...] = times[...]
        rows_of = reached_rows(cx, done + cx, rows)
        cut_edges(cx, rows_of, False, velocity, state, None, times, outs[0], outs[1])


def home_kernel(mine, brought, out):
    half = mine.shape[2]
    segment = lax.axis_index("segment")

    @pl.when(segment == 0)
    def _():
        out[0, :, :, 0:half] = mine[...]
        out[0, :, :, half:] = brought[...]

    @pl.when(segment == 1)
    def _():
        out[0, :, :, half:] = mine[...]
        out[0, :, :, 0:half] = brought[...]


VMEM = pl.BlockSpec(memory_space=pltpu.VMEM)
HBM = pl.BlockSpec(memory_space=pltpu.HBM)


def call(kernel, name, in_vmem, in_hbm, outs, scratch, copies=0, limit=40 * 2**20, flops=10**7):
    sems = [pltpu.SemaphoreType.DMA((copies,))] * (copies > 0)
    return pl.pallas_call(
        kernel,
        out_shape=[jax.ShapeDtypeStruct(shape, F32) for shape in outs],
        in_specs=[VMEM] * len(in_vmem) + [HBM] * len(in_hbm),
        out_specs=[VMEM] * len(outs),
        scratch_shapes=[pltpu.VMEM(s, F32) if isinstance(s, tuple) else s for s in scratch] + sems,
        compiler_params=pltpu.CompilerParams(vmem_limit_bytes=limit),
        cost_estimate=pl.CostEstimate(flops=flops, bytes_accessed=2**20, transcendentals=0),
        name=name,
    )(*in_vmem, *in_hbm)


def on_device(
    fields, block_ids, buoyancy, lame_lambda, lame_mu, moments, moment_owner, moment_cells, drm_rows
):
    sections, slabs = lax.axis_size("sec"), lax.axis_size("depth")
    layout = cx, cz, cy = fields.shape[2:]
    reach, rows = reach_of(cz), cz // 2 + 2 * STEPS
    assert cx > 1 and STEPS % cx == 0

    def pairs(block, start):
        route = [(i, i + 1) for i in range(start, sections - 1, 2)]
        return lax.ppermute(block, "sec", route + [(j, i) for i, j in route])

    def other(section, k):
        return section ^ k if sections & (sections - 1) == 0 else (section + k) % sections

    def along_depth(block):
        down = [(2 * i + 1, 2 * (i + 1)) for i in range(slabs - 1)]
        return lax.ppermute(block, ("depth", "segment"), down + [(j, i) for i, j in down])

    def swap(block):
        return lax.ppermute(block, "segment", [(0, 1), (1, 0)])

    owner = moment_owner.reshape(-1, cy)
    cells = moment_cells.reshape(-1, cy)
    arguments = (fields, block_ids, moments, owner, cells, drm_rows.reshape(-1, cy))
    entry_lines = 8 * cells.shape[0]
    entries, kept, given = call(
        pack_kernel,
        "pack",
        (),
        (*arguments, buoyancy, lame_lambda, lame_mu),
        [(entry_lines, cy), (11 * cx * reach + 8 + entry_lines, cy), (10, cx * reach, cy)],
        [pltpu.VMEM(a.shape, a.dtype) for a in arguments]
        + [(2, cx, cz, cy), pltpu.SMEM((3, buoyancy.shape[0]), F32)],
        len(arguments) + 3,
        limit=64 * 2**20,
    )
    blocks = [
        lax.ppermute(entries, "sec", [(other(i, k), i) for i in range(sections)])
        for k in (sections - 1, *range(1, sections - 1))
    ]
    got = swap(given)
    acc_shape = (6 * cx * cz // 2, 2 * cy)
    kept, tables, started = call(
        functools.partial(own_kernel, layout),
        "own_moments",
        (kept,),
        (),
        [(11, cx * reach, cy), (8, cy), acc_shape],
        [],
        flops=10**8,
    )
    for block in blocks[:-1]:
        (started,) = call(
            functools.partial(more_kernel, layout),
            "more_moments",
            (started, block),
            (),
            [acc_shape],
            [],
            flops=6 * 10**9,
        )
    own = (cx, rows, cy)
    window = (3 * cx, rows, cy)
    state, ids, times, edge = call(
        functools.partial(join_kernel, layout),
        "join_and_moments",
        (kept, got, started, blocks[-1]),
        (),
        [(2, 9, *own), (2, *own), own, (21 * cx * STEPS, cy)],
        [(6, cx * cz, cy)],
    )
    halo = along_depth(edge)
    work = [(2, 9, *window), (2, *window), (2, 3, *window), window]

    def edges(count, with_ids):
        return [(len(edge_units(cx, with_ids)[0]) * count, cy)] * 2

    def reached_edges(done):
        rows_of = reached_rows(cx, done, rows)
        whole, far = rows_of(False, True), rows_of(True, True)
        lines = 18 * (cx - 1) * (whole.stop - whole.start) + 6 * (far.stop - far.start)
        return [(-(-lines // 8) * 8, cy)] * 2

    def exchange(pair):
        return [pairs(pair[0], 0), pairs(pair[1], 1)]

    got_edges = []
    for pairing, flops in enumerate((10**7, 10**7)):
        (inner,) = call(
            functools.partial(inner_kernel, cx, pairing),
            "inner_edges",
            (state, ids, times, tables),
            (),
            edges(reach, True)[0:1],
            work,
            flops=flops,
        )
        got_edges.append(pairs(inner, pairing))
    (got_edges[0],) = call(
        arrived_kernel, "arrived", got_edges[0:1], (), edges(reach, True)[0:1], [], flops=10**10
    )
    *outer, both, coef, times = call(
        functools.partial(outer_kernel, cx),
        "outer_edges",
        (state, ids, times, halo, tables),
        (),
        edges(STEPS, True) + [(2, 9, *own), (2, 3, *own), own],
        work,
        flops=10**8,
    )
    got_edges += exchange(outer)
    for done in range(0, STEPS, cx):
        first, last = done == 0, done + cx == STEPS
        after = done + cx
        outs = [(9, cx, cz // 2, cy)] * 2
        if not last:
            outs = reached_edges(after) + [(2, 9, *own)]
            outs += [(2, 3, *window), window] * first
        pair = call(
            functools.partial(next_kernel, cx, done),
            "steps",
            (both, coef, times, *got_edges) + (tables,) * first,
            (),
            outs,
            work if first else work[0:1],
        )
        if not last:
            got_edges = exchange(pair[0:2])
            both = pair[2]
            if first:
                coef, times = pair[3:5]
    to_first, to_second = pair[0:2]
    (out,) = call(home_kernel, "home", (to_first, swap(to_second)), (), [fields.shape], [])
    return out


def solution(mesh):
    in_specs = (
        P("segment", None, "sec", "depth", None),
        P("segment", "sec", "depth", None),
        P(),
        P(),
        P(),
        P(None, ("sec", "depth")),
        P(("sec", "depth"), None),
        P(("sec", "depth")),
        P(("sec", "depth")),
    )
    out_specs = P("segment", None, "sec", "depth", None)
    return jax.shard_map(
        on_device, mesh=mesh, in_specs=in_specs, out_specs=out_specs, check_vma=False
    )
```

```python
import functools

import jax
import jax.numpy as jnp
from jax import lax
from jax.experimental import pallas as pl
from jax.experimental.pallas import tpu as pltpu
from jax.sharding import PartitionSpec as P

STEPS = 4
F32 = jnp.float32
BF16 = jnp.bfloat16
NT = (((1,), (1,)), ((), ()))


def one_hot(index, count):
    rows = lax.broadcasted_iota(jnp.int32, (count, index.shape[-1]), 0)
    return jnp.where(rows == index, F32(1.0), F32(0.0))


def split3(value):
    high = value.astype(BF16).astype(F32)
    rest = value - high
    mid = rest.astype(BF16).astype(F32)
    return high, mid, rest - mid


def copy_all(sem, pairs):
    copies = [pltpu.make_async_copy(a, b, sem.at[i]) for i, (a, b) in enumerate(pairs)]
    for copy in copies:
        copy.start()
    for copy in copies:
        copy.wait()


def in_line(rows):
    return jnp.concatenate([rows[i : i + 1, :] for i in range(rows.shape[0])], axis=1)


def reach_of(cz):
    return cz // 2 + STEPS


def pack_kernel(
    fields_in, ids_in, moments_in, owner_in, cells_in, rows_in, buoyancy, lame_lambda, lame_mu,
    entries, kept, given, fields, ids, moments, owner, cells, rows, wide, tables, sem,
):
    cx, cz, cy = ids.shape[1:]
    arguments = [(fields_in, fields), (ids_in, ids), (moments_in, moments), (owner_in, owner)]
    arguments += [(cells_in, cells), (rows_in, rows)]
    arguments += [(t, tables.at[i]) for i, t in enumerate((buoyancy, lame_lambda, lame_mu))]
    copy_all(sem, arguments)
    for i in range(cells.shape[0]):
        at = 8 * i
        entries[at : at + 6] = moments[:, i * cy : (i + 1) * cy]
        entries[at + 6 : at + 7] = owner[i : i + 1, :].astype(F32)
        entries[at + 7 : at + 8] = cells[i : i + 1, :].astype(F32)
    wide[0] = (ids[0] + 1).astype(F32)
    line = in_line(rows[...])
    high = one_hot(line // cy, cx * cz).astype(BF16)
    low = one_hot(line % cy, cy).astype(BF16)
    count = lax.dot_general(high, low, NT, preferred_element_type=F32)
    wide[1] = count.reshape(cx, cz, cy)
    reach = reach_of(cz)
    lines = 11 * cx * reach
    lane = lax.broadcasted_iota(jnp.int32, (1, cy), 1)
    for i in range(3):
        found = jnp.zeros((1, cy), F32)
        for entry in range(tables.shape[1]):
            found = jnp.where(lane == entry + 1, F32(0.5) * tables[i, entry], found)
        kept[lines + i : lines + i + 1] = found
    kept[lines + 3 : lines + 8] = jnp.zeros((5, cy), F32)
    kept[lines + 8 :] = entries[...]

    def cut(first, other):
        for x in range(cx):
            at = slice(x * reach, (x + 1) * reach)
            for k in range(11):
                source = fields.at[0, k] if k < 9 else wide.at[k - 9]
                line = (k * cx + x) * reach
                kept[line : line + reach] = source[x, first : first + reach]
            given[0:9, at] = fields[0, :, x, other : other + reach]
            given[9, at] = wide[0, x, other : other + reach]

    @pl.when(lax.axis_index("segment") == 0)
    def _():
        cut(0, cz - reach)

    @pl.when(lax.axis_index("segment") == 1)
    def _():
        cut(cz - reach, 0)


def moments_of(layout, entries):
    cx, cz, cy = layout
    section = lax.axis_index("sec")
    half = cx * cz // 2
    chunk = [entries[8 * i : 8 * i + 8] for i in range(entries.shape[0] // 8)]
    entry = jnp.concatenate(chunk, axis=1)
    owner = entry[6:7].astype(jnp.int32)
    cell = entry[7:8].astype(jnp.int32)
    line = jnp.where(owner == section, cell // cy, -1)
    upper = line >= half
    high = one_hot(jnp.where(upper, line - half, line), half)
    low = one_hot(jnp.where(upper, cell % cy + cy, cell % cy), 2 * cy).astype(BF16)
    parts = split3(entry[0:6])
    spread = [(high * part[c : c + 1]).astype(BF16) for part in parts for c in range(6)]
    spread = jnp.concatenate(spread, axis=0)
    got = lax.dot_general(spread, low, NT, preferred_element_type=F32)
    lines = 6 * half
    return got[0:lines] + got[lines : 2 * lines] + got[2 * lines :]


def own_kernel(layout, kept, out, tables, acc):
    lines = out.shape[0] * out.shape[1]
    out[...] = kept[0:lines].reshape(out.shape)
    tables[...] = kept[lines : lines + 8]
    acc[...] = moments_of(layout, kept[lines + 8 :])


def more_kernel(layout, started, entries, acc):
    acc[...] = started[...] + moments_of(layout, entries[...])


def by_core(act):
    segment = lax.axis_index("segment")

    @pl.when(segment == 0)
    def _():
        act(0, lambda reach: slice(STEPS, STEPS + reach), lambda reach: slice(0, STEPS))

    @pl.when(segment == 1)
    def _():
        act(1, lambda reach: slice(0, reach), lambda reach: slice(reach, reach + STEPS))


def join_kernel(layout, *refs):
    cx, cz, cy = layout
    kept, got, started, entries, state, ids, times, edge, dense = refs
    reach = reach_of(cz)
    half = cx * cz // 2
    total = started[...] + moments_of(layout, entries[...])
    for c in range(6):
        for k in range(2):
            added = total[c * half : (c + 1) * half, k * cy : (k + 1) * cy]
            dense[c, k * half : (k + 1) * half] = added

    def join(mine, main, outer):
        main, outer = main(reach), outer(reach)
        first = 0 if mine == 0 else cz - reach
        last = main.start if mine == 0 else main.stop - STEPS
        gone = slice(last, last + STEPS)
        for x in range(cx):
            at = slice(x * reach, (x + 1) * reach)
            for model in range(2):
                rows = kept if model == mine else got
                state[model, :, x, main] = rows[0:9, at]
                ids[model, x, main] = rows[9, at]
            added = dense[:, x * cz + first : x * cz + first + reach]
            state[0, 3:9, x, main] = state[0, 3:9, x, main] + added
            times[x, main] = kept[10, at]
            state[:, :, x, outer] = jnp.zeros((2, 9, STEPS, cy), F32)
            ids[:, x, outer] = jnp.zeros((2, STEPS, cy), F32)
            times[x, outer] = jnp.zeros((STEPS, cy), F32)
            for k in range(21):
                line = slice((k * cx + x) * STEPS, (k * cx + x + 1) * STEPS)
                if k == 20:
                    edge[line] = times[x, gone]
                elif k % 10 == 9:
                    edge[line] = ids[k // 10, x, gone]
                else:
                    edge[line] = state[k // 10, k % 10, x, gone]

    by_core(join)


def by_parity(even, odd, act):
    parity = lax.axis_index("sec") % 2

    @pl.when(parity == 0)
    def _():
        act(*even)

    @pl.when(parity == 1)
    def _():
        act(*odd)


def advance(cx, steps, state, coef, times, given_top=False):
    planes, rows, cy = state.shape[2:]
    lane = lax.broadcasted_iota(jnp.int32, (rows, cy), 1)
    first_lane, last_lane = lane == 0, lane == cy - 1

    def back_y(f):
        return f - jnp.where(first_lane, F32(0.0), pltpu.roll(f, 1, 1))

    def back_z(f):
        return f - pltpu.roll(f, 1, 0)

    def fore_y(f):
        return jnp.where(last_lane, F32(0.0), pltpu.roll(f, cy - 1, 1)) - f

    def fore_z(f):
        return pltpu.roll(f, rows - 1, 0) - f

    def velocity(x):
        inc = [None, None]
        for model in range(2):
            sxx, syy, szz, syz, sxz, sxy = (state[model, 3 + k, x] for k in range(6))
            sxx_p, sxz_p, sxy_p = (state[model, k, x - 1] for k in (3, 7, 8))
            hb = coef[model, 0, x]
            inc[model] = (
                hb * ((sxx - sxx_p) + back_y(sxy) + back_z(sxz)),
                hb * ((sxy - sxy_p) + back_y(syy) + back_z(syz)),
                hb * ((sxz - sxz_p) + back_y(syz) + back_z(szz)),
            )
        for k in range(3):
            state[0, k, x] = state[0, k, x] + inc[0][k]
            state[1, k, x] = (state[1, k, x] + inc[1][k]) + times[x] * inc[0][k]

    for step in range(steps):
        left = steps - 1 - step
        low, high = cx - left, 2 * cx + left
        for x in range(low, high + 1 - (given_top and step == 0)):
            velocity(x)
        for x in range(low, high):
            for model in range(2):
                vx, vy, vz = (state[model, k, x] for k in range(3))
                vx_n, vy_n, vz_n = (state[model, k, x + 1] for k in range(3))
                hl, hm = coef[model, 1, x], coef[model, 2, x]
                exx, eyy, ezz = vx_n - vx, fore_y(vy), fore_z(vz)
                pressure = hl * (exx + eyy + ezz)
                twice = hm + hm
                state[model, 3, x] = state[model, 3, x] + (pressure + twice * exx)
                state[model, 4, x] = state[model, 4, x] + (pressure + twice * eyy)
                state[model, 5, x] = state[model, 5, x] + (pressure + twice * ezz)
                state[model, 6, x] = state[model, 6, x] + hm * (fore_z(vy) + fore_y(vz))
                state[model, 7, x] = state[model, 7, x] + hm * (fore_z(vx) + (vz_n - vz))
                state[model, 8, x] = state[model, 8, x] + hm * (fore_y(vx) + (vy_n - vy))

    return velocity


def look_up(tables, ids):
    lanes = ids.astype(jnp.int32)
    wide = [jnp.broadcast_to(tables[i : i + 1], ids.shape) for i in range(3)]
    return [jnp.take_along_axis(table, lanes, axis=1) for table in wide]


def edge_units(cx, with_ids):
    right, left = [], []
    for model in range(2):
        whole = list(range(10 if with_ids else 9)) + [10] * (with_ids and model == 1)
        for x in range(cx - 1):
            right += [(model, what, x + 1) for what in whole]
            left += [(model, what, x) for what in whole]
        right += [(model, what, 0) for what in (3, 7, 8)]
        left += [(model, what, cx - 1) for what in range(3)]
    return right, left


def cut_edges(cx, rows_of, with_ids, velocity, state, ids, times, to_first, to_second):
    right_units, left_units = edge_units(cx, with_ids)

    def put(to, units, far, right):
        line = slice(0, 0)
        for model, what, x in units:
            at = rows_of(x == far, right)
            line = slice(line.stop, line.stop + at.stop - at.start)
            if what == 10:
                to[line] = times[cx + x, at]
            elif what == 9:
                to[line] = ids[model, cx + x, at]
            else:
                to[line] = state[model, what, cx + x, at]

    holders = (to_second, to_first), (to_first, to_second)
    by_parity(*holders, lambda left, right: put(right, right_units, 0, True))
    velocity(2 * cx - 1)
    by_parity(*holders, lambda left, right: put(left, left_units, cx - 1, False))


def outer_rows(mine, outer):
    def rows_of(far, right):
        shift = 1 if far and not right and mine == 0 else 0
        return slice(outer.start + shift, outer.stop + shift)

    return rows_of


def reached_rows(cx, done, rows):
    def rows_of(far, right):
        first, last = done, rows - done
        if right:
            return slice(first + (cx if far else 1), last)
        return slice(first + far, last - (cx if far else 1))

    return rows_of


def coefficients(cx, planes, tables, ids, coef):
    for model in range(2):
        for x in planes:
            for i, found in enumerate(look_up(tables, ids[model, x])):
                coef[model, i, x] = found


def inner_kernel(cx, own_state, own_ids, own_times, tables, to_first, to_second, state, ids, coef, times):
    own = slice(cx, 2 * cx)
    reach = state.shape[3] - STEPS
    state[:, :, own], ids[:, own], times[own] = own_state[...], own_ids[...], own_times[...]
    coefficients(cx, range(2 * cx - 1, 2 * cx), tables, ids, coef)
    velocity = advance(cx, 0, state, coef, times)

    def cut(mine, main, outer):
        rows_of = lambda far, right: main(reach)
        cut_edges(cx, rows_of, True, velocity, state, ids, times, to_first, to_second)

    by_core(cut)


def outer_kernel(
    cx, own_state, own_ids, own_times, from_above, from_below, tables,
    to_first, to_second, both, coef_out, times_out, state, ids, coef, times,
):
    own = slice(cx, 2 * cx)
    reach = state.shape[3] - STEPS
    state[:, :, own], ids[:, own], times[own] = own_state[...], own_ids[...], own_times[...]

    def join(mine, main, outer):
        halo = from_above if mine == 0 else from_below
        for x in range(cx):
            for k in range(21):
                line = halo[(k * cx + x) * STEPS : (k * cx + x + 1) * STEPS]
                if k == 20:
                    times[cx + x, outer(reach)] = line
                elif k % 10 == 9:
                    ids[k // 10, cx + x, outer(reach)] = line
                else:
                    state[k // 10, k % 10, cx + x, outer(reach)] = line

    by_core(join)
    coefficients(cx, range(cx, 2 * cx), tables, ids, coef)
    both[...] = state[:, :, own]
    coef_out[...] = coef[:, :, own]
    times_out[...] = times[own]
    velocity = advance(cx, 0, state, coef, times)

    def cut(mine, main, outer):
        rows_of = outer_rows(mine, outer(reach))
        cut_edges(cx, rows_of, True, velocity, state, ids, times, to_first, to_second)

    by_core(cut)


def next_kernel(cx, done, *refs):
    first = done == 0
    parts = 2 if first else 1
    both_in, coef_in, times_in = refs[0:3]
    edges, refs = refs[3 : 3 + 2 * parts], refs[3 + 2 * parts :]
    if first:
        tables, outs = refs[0], refs[1:]
        state, ids, coef, times = refs[-4:]
    else:
        ids, outs = None, refs
        state, coef, times = refs[-1], coef_in, times_in
    segment = lax.axis_index("segment")
    rows = state.shape[3]
    own = slice(cx, 2 * cx)
    state[:, :, own] = both_in[...]
    right_units, left_units = edge_units(cx, first)

    def get(edge, units, start, rows_of, far, right):
        last = 0
        for model, what, x in units:
            at = rows_of(x == far, right)
            first, last = last, last + at.stop - at.start
            line = edge[first:last]
            if what == 10:
                times[start + x, at] = line
            elif what == 9:
                ids[model, start + x, at] = line
            else:
                state[model, what, start + x, at] = line

    def place(rows_of, pair):
        def put(left, right):
            get(left, right_units, 0, rows_of, 0, True)
            get(right, left_units, 2 * cx, rows_of, cx - 1, False)

        by_parity((pair[1], pair[0]), pair, put)

    if first:

        def place_both(mine, main, outer):
            reach = rows - STEPS
            place(lambda far, right: main(reach), edges[0:2])
            place(outer_rows(mine, outer(reach)), edges[2:4])

        by_core(place_both)
        coef[:, :, own] = coef_in[...]
        times[own] = times_in[...]
        coefficients(cx, (*range(1, cx), *range(2 * cx, 3 * cx - 1)), tables, ids, coef)
    else:
        place(reached_rows(cx, done, rows), edges)
    velocity = advance(cx, cx, state, coef, times, given_top=True)
    if done + cx == STEPS:
        outs[0][...] = state[segment, :, own, STEPS : rows - STEPS]
        outs[1][...] = state[1 - segment, :, own, STEPS : rows - STEPS]
    else:
        outs[2][...] = state[:, :, own]
        if first:
            outs[3][...] = coef[...]
            outs[4][...] = times[...]
        rows_of = reached_rows(cx, done + cx, rows)
        cut_edges(cx, rows_of, False, velocity, state, None, times, outs[0], outs[1])


def home_kernel(mine, brought, out):
    half = mine.shape[2]
    segment = lax.axis_index("segment")

    @pl.when(segment == 0)
    def _():
        out[0, :, :, 0:half] = mine[...]
        out[0, :, :, half:] = brought[...]

    @pl.when(segment == 1)
    def _():
        out[0, :, :, half:] = mine[...]
        out[0, :, :, 0:half] = brought[...]


VMEM = pl.BlockSpec(memory_space=pltpu.VMEM)
HBM = pl.BlockSpec(memory_space=pltpu.HBM)


def call(kernel, name, in_vmem, in_hbm, outs, scratch, copies=0, limit=40 * 2**20, flops=10**7):
    sems = [pltpu.SemaphoreType.DMA((copies,))] * (copies > 0)
    return pl.pallas_call(
        kernel,
        out_shape=[jax.ShapeDtypeStruct(shape, F32) for shape in outs],
        in_specs=[VMEM] * len(in_vmem) + [HBM] * len(in_hbm),
        out_specs=[VMEM] * len(outs),
        scratch_shapes=[pltpu.VMEM(s, F32) if isinstance(s, tuple) else s for s in scratch] + sems,
        compiler_params=pltpu.CompilerParams(vmem_limit_bytes=limit),
        cost_estimate=pl.CostEstimate(flops=flops, bytes_accessed=2**20, transcendentals=0),
        name=name,
    )(*in_vmem, *in_hbm)


def on_device(
    fields, block_ids, buoyancy, lame_lambda, lame_mu, moments, moment_owner, moment_cells, drm_rows
):
    sections, slabs = lax.axis_size("sec"), lax.axis_size("depth")
    layout = cx, cz, cy = fields.shape[2:]
    reach, rows = reach_of(cz), cz // 2 + 2 * STEPS
    assert cx > 1 and STEPS % cx == 0

    def pairs(block, start):
        route = [(i, i + 1) for i in range(start, sections - 1, 2)]
        return lax.ppermute(block, "sec", route + [(j, i) for i, j in route])

    def other(section, k):
        return section ^ k if sections & (sections - 1) == 0 else (section + k) % sections

    def along_depth(block):
        down = [(2 * i + 1, 2 * (i + 1)) for i in range(slabs - 1)]
        routes = down, [(j, i) for i, j in down]
        return [lax.ppermute(block, ("depth", "segment"), route) for route in routes]

    def swap(block):
        return lax.ppermute(block, "segment", [(0, 1), (1, 0)])

    owner = moment_owner.reshape(-1, cy)
    cells = moment_cells.reshape(-1, cy)
    arguments = (fields, block_ids, moments, owner, cells, drm_rows.reshape(-1, cy))
    entry_lines = 8 * cells.shape[0]
    entries, kept, given = call(
        pack_kernel,
        "pack",
        (),
        (*arguments, buoyancy, lame_lambda, lame_mu),
        [(entry_lines, cy), (11 * cx * reach + 8 + entry_lines, cy), (10, cx * reach, cy)],
        [pltpu.VMEM(a.shape, a.dtype) for a in arguments]
        + [(2, cx, cz, cy), pltpu.SMEM((3, buoyancy.shape[0]), F32)],
        len(arguments) + 3,
        limit=64 * 2**20,
    )
    blocks = [
        lax.ppermute(entries, "sec", [(other(i, k), i) for i in range(sections)])
        for k in (sections - 1, *range(1, sections - 1))
    ]
    got = swap(given)
    acc_shape = (6 * cx * cz // 2, 2 * cy)
    kept, tables, started = call(
        functools.partial(own_kernel, layout),
        "own_moments",
        (kept,),
        (),
        [(11, cx * reach, cy), (8, cy), acc_shape],
        [],
        flops=10**8,
    )
    for block in blocks[:-1]:
        (started,) = call(
            functools.partial(more_kernel, layout),
            "more_moments",
            (started, block),
            (),
            [acc_shape],
            [],
            flops=6 * 10**9,
        )
    own = (cx, rows, cy)
    window = (3 * cx, rows, cy)
    state, ids, times, edge = call(
        functools.partial(join_kernel, layout),
        "join_and_moments",
        (kept, got, started, blocks[-1]),
        (),
        [(2, 9, *own), (2, *own), own, (21 * cx * STEPS, cy)],
        [(6, cx * cz, cy)],
    )
    halos = along_depth(edge)
    work = [(2, 9, *window), (2, *window), (2, 3, *window), window]

    def edges(count, with_ids):
        return [(len(edge_units(cx, with_ids)[0]) * count, cy)] * 2

    def reached_edges(done):
        rows_of = reached_rows(cx, done, rows)
        whole, far = rows_of(False, True), rows_of(True, True)
        lines = 18 * (cx - 1) * (whole.stop - whole.start) + 6 * (far.stop - far.start)
        return [(-(-lines // 8) * 8, cy)] * 2

    def exchange(pair):
        return [pairs(pair[0], 0), pairs(pair[1], 1)]

    inner = call(
        functools.partial(inner_kernel, cx),
        "inner_edges",
        (state, ids, times, tables),
        (),
        edges(reach, True),
        work,
        flops=10**9,
    )
    got_edges = exchange(inner)
    *outer, both, coef, times = call(
        functools.partial(outer_kernel, cx),
        "outer_edges",
        (state, ids, times, *halos, tables),
        (),
        edges(STEPS, True) + [(2, 9, *own), (2, 3, *own), own],
        work,
        flops=4 * 10**9,
    )
    got_edges += exchange(outer)
    for done in range(0, STEPS, cx):
        first, last = done == 0, done + cx == STEPS
        after = done + cx
        outs = [(9, cx, cz // 2, cy)] * 2
        if not last:
            outs = reached_edges(after) + [(2, 9, *own)]
            outs += [(2, 3, *window), window] * first
        pair = call(
            functools.partial(next_kernel, cx, done),
            "steps",
            (both, coef, times, *got_edges) + (tables,) * first,
            (),
            outs,
            work if first else work[0:1],
        )
        if not last:
            got_edges = exchange(pair[0:2])
            both = pair[2]
            if first:
                coef, times = pair[3:5]
    to_first, to_second = pair[0:2]
    (out,) = call(home_kernel, "home", (to_first, swap(to_second)), (), [fields.shape], [])
    return out


def solution(mesh):
    in_specs = (
        P("segment", None, "sec", "depth", None),
        P("segment", "sec", "depth", None),
        P(),
        P(),
        P(),
        P(None, ("sec", "depth")),
        P(("sec", "depth"), None),
        P(("sec", "depth")),
        P(("sec", "depth")),
    )
    out_specs = P("segment", None, "sec", "depth", None)
    return jax.shard_map(
        on_device, mesh=mesh, in_specs=in_specs, out_specs=out_specs, check_vma=False
    )
```

```python
import functools

import jax
import jax.numpy as jnp
from jax import lax
from jax.experimental import pallas as pl
from jax.experimental.pallas import tpu as pltpu
from jax.sharding import PartitionSpec as P

STEPS = 4
F32 = jnp.float32
BF16 = jnp.bfloat16
NT = (((1,), (1,)), ((), ()))


def one_hot(index, count):
    rows = lax.broadcasted_iota(jnp.int32, (count, index.shape[-1]), 0)
    return jnp.where(rows == index, F32(1.0), F32(0.0))


def split3(value):
    high = value.astype(BF16).astype(F32)
    rest = value - high
    mid = rest.astype(BF16).astype(F32)
    return high, mid, rest - mid


def copy_all(sem, pairs):
    copies = [pltpu.make_async_copy(a, b, sem.at[i]) for i, (a, b) in enumerate(pairs)]
    for copy in copies:
        copy.start()
    for copy in copies:
        copy.wait()


def in_line(rows):
    return jnp.concatenate([rows[i : i + 1, :] for i in range(rows.shape[0])], axis=1)


def reach_of(cz):
    return cz // 2 + STEPS


def pack_kernel(
    fields_in, ids_in, moments_in, owner_in, cells_in, rows_in, buoyancy, lame_lambda, lame_mu,
    entries, kept, given, fields, ids, moments, owner, cells, rows, wide, tables, sem,
):
    cx, cz, cy = ids.shape[1:]
    arguments = [(fields_in, fields), (ids_in, ids), (moments_in, moments), (owner_in, owner)]
    arguments += [(cells_in, cells), (rows_in, rows)]
    arguments += [(t, tables.at[i]) for i, t in enumerate((buoyancy, lame_lambda, lame_mu))]
    copy_all(sem, arguments)
    for i in range(cells.shape[0]):
        at = 8 * i
        entries[at : at + 6] = moments[:, i * cy : (i + 1) * cy]
        entries[at + 6 : at + 7] = owner[i : i + 1, :].astype(F32)
        entries[at + 7 : at + 8] = cells[i : i + 1, :].astype(F32)
    wide[0] = (ids[0] + 1).astype(F32)
    line = in_line(rows[...])
    high = one_hot(line // cy, cx * cz).astype(BF16)
    low = one_hot(line % cy, cy).astype(BF16)
    count = lax.dot_general(high, low, NT, preferred_element_type=F32)
    wide[1] = count.reshape(cx, cz, cy)
    reach = reach_of(cz)
    lines = 11 * cx * reach
    lane = lax.broadcasted_iota(jnp.int32, (1, cy), 1)
    for i in range(3):
        found = jnp.zeros((1, cy), F32)
        for entry in range(tables.shape[1]):
            found = jnp.where(lane == entry + 1, F32(0.5) * tables[i, entry], found)
        kept[lines + i : lines + i + 1] = found
    kept[lines + 3 : lines + 8] = jnp.zeros((5, cy), F32)
    kept[lines + 8 :] = entries[...]

    def cut(first, other):
        for x in range(cx):
            at = slice(x * reach, (x + 1) * reach)
            for k in range(11):
                source = fields.at[0, k] if k < 9 else wide.at[k - 9]
                line = (k * cx + x) * reach
                kept[line : line + reach] = source[x, first : first + reach]
            given[0:9, at] = fields[0, :, x, other : other + reach]
            given[9, at] = wide[0, x, other : other + reach]

    @pl.when(lax.axis_index("segment") == 0)
    def _():
        cut(0, cz - reach)

    @pl.when(lax.axis_index("segment") == 1)
    def _():
        cut(cz - reach, 0)


def moments_of(layout, entries):
    cx, cz, cy = layout
    section = lax.axis_index("sec")
    half = cx * cz // 2
    chunk = [entries[8 * i : 8 * i + 8] for i in range(entries.shape[0] // 8)]
    entry = jnp.concatenate(chunk, axis=1)
    owner = entry[6:7].astype(jnp.int32)
    cell = entry[7:8].astype(jnp.int32)
    line = jnp.where(owner == section, cell // cy, -1)
    upper = line >= half
    high = one_hot(jnp.where(upper, line - half, line), half)
    low = one_hot(jnp.where(upper, cell % cy + cy, cell % cy), 2 * cy).astype(BF16)
    parts = split3(entry[0:6])
    spread = [(high * part[c : c + 1]).astype(BF16) for part in parts for c in range(6)]
    spread = jnp.concatenate(spread, axis=0)
    got = lax.dot_general(spread, low, NT, preferred_element_type=F32)
    lines = 6 * half
    return got[0:lines] + got[lines : 2 * lines] + got[2 * lines :]


def own_kernel(layout, kept, out, tables, acc):
    lines = out.shape[0] * out.shape[1]
    out[...] = kept[0:lines].reshape(out.shape)
    tables[...] = kept[lines : lines + 8]
    acc[...] = moments_of(layout, kept[lines + 8 :])


def more_kernel(layout, started, entries, acc):
    acc[...] = started[...] + moments_of(layout, entries[...])


def by_core(act):
    segment = lax.axis_index("segment")

    @pl.when(segment == 0)
    def _():
        act(0, lambda reach: slice(STEPS, STEPS + reach), lambda reach: slice(0, STEPS))

    @pl.when(segment == 1)
    def _():
        act(1, lambda reach: slice(0, reach), lambda reach: slice(reach, reach + STEPS))


def join_kernel(layout, *refs):
    cx, cz, cy = layout
    kept, got, started, entries, state, ids, times, edge, dense = refs
    reach = reach_of(cz)
    half = cx * cz // 2
    total = started[...] + moments_of(layout, entries[...])
    for c in range(6):
        for k in range(2):
            added = total[c * half : (c + 1) * half, k * cy : (k + 1) * cy]
            dense[c, k * half : (k + 1) * half] = added

    def join(mine, main, outer):
        main, outer = main(reach), outer(reach)
        first = 0 if mine == 0 else cz - reach
        last = main.start if mine == 0 else main.stop - STEPS
        gone = slice(last, last + STEPS)
        for x in range(cx):
            at = slice(x * reach, (x + 1) * reach)
            for model in range(2):
                rows = kept if model == mine else got
                state[model, :, x, main] = rows[0:9, at]
                ids[model, x, main] = rows[9, at]
            added = dense[:, x * cz + first : x * cz + first + reach]
            state[0, 3:9, x, main] = state[0, 3:9, x, main] + added
            times[x, main] = kept[10, at]
            state[:, :, x, outer] = jnp.zeros((2, 9, STEPS, cy), F32)
            ids[:, x, outer] = jnp.zeros((2, STEPS, cy), F32)
            times[x, outer] = jnp.zeros((STEPS, cy), F32)
            for k in range(21):
                line = slice((k * cx + x) * STEPS, (k * cx + x + 1) * STEPS)
                if k == 20:
                    edge[line] = times[x, gone]
                elif k % 10 == 9:
                    edge[line] = ids[k // 10, x, gone]
                else:
                    edge[line] = state[k // 10, k % 10, x, gone]

    by_core(join)


def by_parity(even, odd, act):
    parity = lax.axis_index("sec") % 2

    @pl.when(parity == 0)
    def _():
        act(*even)

    @pl.when(parity == 1)
    def _():
        act(*odd)


def advance(cx, steps, state, coef, times, given_top=False):
    planes, rows, cy = state.shape[2:]
    lane = lax.broadcasted_iota(jnp.int32, (rows, cy), 1)
    first_lane, last_lane = lane == 0, lane == cy - 1

    def back_y(f):
        return f - jnp.where(first_lane, F32(0.0), pltpu.roll(f, 1, 1))

    def back_z(f):
        return f - pltpu.roll(f, 1, 0)

    def fore_y(f):
        return jnp.where(last_lane, F32(0.0), pltpu.roll(f, cy - 1, 1)) - f

    def fore_z(f):
        return pltpu.roll(f, rows - 1, 0) - f

    def velocity(x):
        inc = [None, None]
        for model in range(2):
            sxx, syy, szz, syz, sxz, sxy = (state[model, 3 + k, x] for k in range(6))
            sxx_p, sxz_p, sxy_p = (state[model, k, x - 1] for k in (3, 7, 8))
            hb = coef[model, 0, x]
            inc[model] = (
                hb * ((sxx - sxx_p) + back_y(sxy) + back_z(sxz)),
                hb * ((sxy - sxy_p) + back_y(syy) + back_z(syz)),
                hb * ((sxz - sxz_p) + back_y(syz) + back_z(szz)),
            )
        for k in range(3):
            state[0, k, x] = state[0, k, x] + inc[0][k]
            state[1, k, x] = (state[1, k, x] + inc[1][k]) + times[x] * inc[0][k]

    for step in range(steps):
        left = steps - 1 - step
        low, high = cx - left, 2 * cx + left
        for x in range(low, high + 1 - (given_top and step == 0)):
            velocity(x)
        for x in range(low, high):
            for model in range(2):
                vx, vy, vz = (state[model, k, x] for k in range(3))
                vx_n, vy_n, vz_n = (state[model, k, x + 1] for k in range(3))
                hl, hm = coef[model, 1, x], coef[model, 2, x]
                exx, eyy, ezz = vx_n - vx, fore_y(vy), fore_z(vz)
                pressure = hl * (exx + eyy + ezz)
                twice = hm + hm
                state[model, 3, x] = state[model, 3, x] + (pressure + twice * exx)
                state[model, 4, x] = state[model, 4, x] + (pressure + twice * eyy)
                state[model, 5, x] = state[model, 5, x] + (pressure + twice * ezz)
                state[model, 6, x] = state[model, 6, x] + hm * (fore_z(vy) + fore_y(vz))
                state[model, 7, x] = state[model, 7, x] + hm * (fore_z(vx) + (vz_n - vz))
                state[model, 8, x] = state[model, 8, x] + hm * (fore_y(vx) + (vy_n - vy))

    return velocity


def look_up(tables, ids):
    lanes = ids.astype(jnp.int32)
    wide = [jnp.broadcast_to(tables[i : i + 1], ids.shape) for i in range(3)]
    return [jnp.take_along_axis(table, lanes, axis=1) for table in wide]


def edge_units(cx, with_ids):
    right, left = [], []
    for model in range(2):
        whole = list(range(10 if with_ids else 9)) + [10] * (with_ids and model == 1)
        for x in range(cx - 1):
            right += [(model, what, x + 1) for what in whole]
            left += [(model, what, x) for what in whole]
        right += [(model, what, 0) for what in (3, 7, 8)]
        left += [(model, what, cx - 1) for what in range(3)]
    return right, left


def cut_edges(cx, rows_of, with_ids, velocity, state, ids, times, to_first, to_second):
    right_units, left_units = edge_units(cx, with_ids)

    def put(to, units, far, right):
        line = slice(0, 0)
        for model, what, x in units:
            at = rows_of(x == far, right)
            line = slice(line.stop, line.stop + at.stop - at.start)
            if what == 10:
                to[line] = times[cx + x, at]
            elif what == 9:
                to[line] = ids[model, cx + x, at]
            else:
                to[line] = state[model, what, cx + x, at]

    holders = (to_second, to_first), (to_first, to_second)
    by_parity(*holders, lambda left, right: put(right, right_units, 0, True))
    velocity(2 * cx - 1)
    by_parity(*holders, lambda left, right: put(left, left_units, cx - 1, False))


def outer_rows(mine, outer):
    def rows_of(far, right):
        shift = 1 if far and not right and mine == 0 else 0
        return slice(outer.start + shift, outer.stop + shift)

    return rows_of


def reached_rows(cx, done, rows):
    def rows_of(far, right):
        first, last = done, rows - done
        if right:
            return slice(first + (cx if far else 1), last)
        return slice(first + far, last - (cx if far else 1))

    return rows_of


def coefficients(cx, planes, tables, ids, coef):
    for model in range(2):
        for x in planes:
            for i, found in enumerate(look_up(tables, ids[model, x])):
                coef[model, i, x] = found


def inner_kernel(cx, own_state, own_ids, own_times, tables, to_first, to_second, state, ids, coef, times):
    own = slice(cx, 2 * cx)
    reach = state.shape[3] - STEPS
    state[:, :, own], ids[:, own], times[own] = own_state[...], own_ids[...], own_times[...]
    coefficients(cx, range(2 * cx - 1, 2 * cx), tables, ids, coef)
    velocity = advance(cx, 0, state, coef, times)

    def cut(mine, main, outer):
        rows_of = lambda far, right: main(reach)
        cut_edges(cx, rows_of, True, velocity, state, ids, times, to_first, to_second)

    by_core(cut)


def outer_kernel(
    cx, own_state, own_ids, own_times, halo, tables,
    to_first, to_second, both, coef_out, times_out, state, ids, coef, times,
):
    own = slice(cx, 2 * cx)
    reach = state.shape[3] - STEPS
    state[:, :, own], ids[:, own], times[own] = own_state[...], own_ids[...], own_times[...]

    def join(mine, main, outer):
        for x in range(cx):
            for k in range(21):
                line = halo[(k * cx + x) * STEPS : (k * cx + x + 1) * STEPS]
                if k == 20:
                    times[cx + x, outer(reach)] = line
                elif k % 10 == 9:
                    ids[k // 10, cx + x, outer(reach)] = line
                else:
                    state[k // 10, k % 10, cx + x, outer(reach)] = line

    by_core(join)
    coefficients(cx, range(cx, 2 * cx), tables, ids, coef)
    both[...] = state[:, :, own]
    coef_out[...] = coef[:, :, own]
    times_out[...] = times[own]
    velocity = advance(cx, 0, state, coef, times)

    def cut(mine, main, outer):
        rows_of = outer_rows(mine, outer(reach))
        cut_edges(cx, rows_of, True, velocity, state, ids, times, to_first, to_second)

    by_core(cut)


def next_kernel(cx, done, *refs):
    first = done == 0
    parts = 2 if first else 1
    both_in, coef_in, times_in = refs[0:3]
    edges, refs = refs[3 : 3 + 2 * parts], refs[3 + 2 * parts :]
    if first:
        tables, outs = refs[0], refs[1:]
        state, ids, coef, times = refs[-4:]
    else:
        ids, outs = None, refs
        state, coef, times = refs[-1], coef_in, times_in
    segment = lax.axis_index("segment")
    rows = state.shape[3]
    own = slice(cx, 2 * cx)
    state[:, :, own] = both_in[...]
    right_units, left_units = edge_units(cx, first)

    def get(edge, units, start, rows_of, far, right):
        last = 0
        for model, what, x in units:
            at = rows_of(x == far, right)
            first, last = last, last + at.stop - at.start
            line = edge[first:last]
            if what == 10:
                times[start + x, at] = line
            elif what == 9:
                ids[model, start + x, at] = line
            else:
                state[model, what, start + x, at] = line

    def place(rows_of, pair):
        def put(left, right):
            get(left, right_units, 0, rows_of, 0, True)
            get(right, left_units, 2 * cx, rows_of, cx - 1, False)

        by_parity((pair[1], pair[0]), pair, put)

    if first:

        def place_both(mine, main, outer):
            reach = rows - STEPS
            place(lambda far, right: main(reach), edges[0:2])
            place(outer_rows(mine, outer(reach)), edges[2:4])

        by_core(place_both)
        coef[:, :, own] = coef_in[...]
        times[own] = times_in[...]
        coefficients(cx, (*range(1, cx), *range(2 * cx, 3 * cx - 1)), tables, ids, coef)
    else:
        place(reached_rows(cx, done, rows), edges)
    velocity = advance(cx, cx, state, coef, times, given_top=True)
    if done + cx == STEPS:
        outs[0][...] = state[segment, :, own, STEPS : rows - STEPS]
        outs[1][...] = state[1 - segment, :, own, STEPS : rows - STEPS]
    else:
        outs[2][...] = state[:, :, own]
        if first:
            outs[3][...] = coef[...]
            outs[4][...] = times[...]
        rows_of = reached_rows(cx, done + cx, rows)
        cut_edges(cx, rows_of, False, velocity, state, None, times, outs[0], outs[1])


def home_kernel(mine, brought, out):
    half = mine.shape[2]
    segment = lax.axis_index("segment")

    @pl.when(segment == 0)
    def _():
        out[0, :, :, 0:half] = mine[...]
        out[0, :, :, half:] = brought[...]

    @pl.when(segment == 1)
    def _():
        out[0, :, :, half:] = mine[...]
        out[0, :, :, 0:half] = brought[...]


VMEM = pl.BlockSpec(memory_space=pltpu.VMEM)
HBM = pl.BlockSpec(memory_space=pltpu.HBM)


def call(kernel, name, in_vmem, in_hbm, outs, scratch, copies=0, limit=40 * 2**20, flops=10**7):
    sems = [pltpu.SemaphoreType.DMA((copies,))] * (copies > 0)
    return pl.pallas_call(
        kernel,
        out_shape=[jax.ShapeDtypeStruct(shape, F32) for shape in outs],
        in_specs=[VMEM] * len(in_vmem) + [HBM] * len(in_hbm),
        out_specs=[VMEM] * len(outs),
        scratch_shapes=[pltpu.VMEM(s, F32) if isinstance(s, tuple) else s for s in scratch] + sems,
        compiler_params=pltpu.CompilerParams(vmem_limit_bytes=limit),
        cost_estimate=pl.CostEstimate(flops=flops, bytes_accessed=2**20, transcendentals=0),
        name=name,
    )(*in_vmem, *in_hbm)


def on_device(
    fields, block_ids, buoyancy, lame_lambda, lame_mu, moments, moment_owner, moment_cells, drm_rows
):
    sections, slabs = lax.axis_size("sec"), lax.axis_size("depth")
    layout = cx, cz, cy = fields.shape[2:]
    reach, rows = reach_of(cz), cz // 2 + 2 * STEPS
    assert cx > 1 and STEPS % cx == 0

    def pairs(block, start):
        route = [(i, i + 1) for i in range(start, sections - 1, 2)]
        return lax.ppermute(block, "sec", route + [(j, i) for i, j in route])

    def other(section, k):
        return section ^ k if sections & (sections - 1) == 0 else (section + k) % sections

    def along_depth(block):
        down = [(2 * i + 1, 2 * (i + 1)) for i in range(slabs - 1)]
        return lax.ppermute(block, ("depth", "segment"), down + [(j, i) for i, j in down])

    def swap(block):
        return lax.ppermute(block, "segment", [(0, 1), (1, 0)])

    owner = moment_owner.reshape(-1, cy)
    cells = moment_cells.reshape(-1, cy)
    arguments = (fields, block_ids, moments, owner, cells, drm_rows.reshape(-1, cy))
    entry_lines = 8 * cells.shape[0]
    entries, kept, given = call(
        pack_kernel,
        "pack",
        (),
        (*arguments, buoyancy, lame_lambda, lame_mu),
        [(entry_lines, cy), (11 * cx * reach + 8 + entry_lines, cy), (10, cx * reach, cy)],
        [pltpu.VMEM(a.shape, a.dtype) for a in arguments]
        + [(2, cx, cz, cy), pltpu.SMEM((3, buoyancy.shape[0]), F32)],
        len(arguments) + 3,
        limit=64 * 2**20,
    )
    blocks = [
        lax.ppermute(entries, "sec", [(other(i, k), i) for i in range(sections)])
        for k in reversed(range(1, sections))
    ]
    got = swap(given)
    acc_shape = (6 * cx * cz // 2, 2 * cy)
    kept, tables, started = call(
        functools.partial(own_kernel, layout),
        "own_moments",
        (kept,),
        (),
        [(11, cx * reach, cy), (8, cy), acc_shape],
        [],
        flops=10**8,
    )
    for block, flops in zip(blocks[:-1], (10**8,) + (6 * 10**9,) * sections):
        (started,) = call(
            functools.partial(more_kernel, layout),
            "more_moments",
            (started, block),
            (),
            [acc_shape],
            [],
            flops=flops,
        )
    own = (cx, rows, cy)
    window = (3 * cx, rows, cy)
    state, ids, times, edge = call(
        functools.partial(join_kernel, layout),
        "join_and_moments",
        (kept, got, started, blocks[-1]),
        (),
        [(2, 9, *own), (2, *own), own, (21 * cx * STEPS, cy)],
        [(6, cx * cz, cy)],
    )
    halo = along_depth(edge)
    work = [(2, 9, *window), (2, *window), (2, 3, *window), window]

    def edges(count, with_ids):
        return [(len(edge_units(cx, with_ids)[0]) * count, cy)] * 2

    def reached_edges(done):
        rows_of = reached_rows(cx, done, rows)
        whole, far = rows_of(False, True), rows_of(True, True)
        lines = 18 * (cx - 1) * (whole.stop - whole.start) + 6 * (far.stop - far.start)
        return [(-(-lines // 8) * 8, cy)] * 2

    def exchange(pair):
        return [pairs(pair[0], 0), pairs(pair[1], 1)]

    inner = call(
        functools.partial(inner_kernel, cx),
        "inner_edges",
        (state, ids, times, tables),
        (),
        edges(reach, True),
        work,
        flops=10**9,
    )
    got_edges = exchange(inner)
    *outer, both, coef, times = call(
        functools.partial(outer_kernel, cx),
        "outer_edges",
        (state, ids, times, halo, tables),
        (),
        edges(STEPS, True) + [(2, 9, *own), (2, 3, *own), own],
        work,
        flops=4 * 10**9,
    )
    got_edges += exchange(outer)
    for done in range(0, STEPS, cx):
        first, last = done == 0, done + cx == STEPS
        after = done + cx
        outs = [(9, cx, cz // 2, cy)] * 2
        if not last:
            outs = reached_edges(after) + [(2, 9, *own)]
            outs += [(2, 3, *window), window] * first
        pair = call(
            functools.partial(next_kernel, cx, done),
            "steps",
            (both, coef, times, *got_edges) + (tables,) * first,
            (),
            outs,
            work if first else work[0:1],
        )
        if not last:
            got_edges = exchange(pair[0:2])
            both = pair[2]
            if first:
                coef, times = pair[3:5]
    to_first, to_second = pair[0:2]
    (out,) = call(home_kernel, "home", (to_first, swap(to_second)), (), [fields.shape], [])
    return out


def solution(mesh):
    in_specs = (
        P("segment", None, "sec", "depth", None),
        P("segment", "sec", "depth", None),
        P(),
        P(),
        P(),
        P(None, ("sec", "depth")),
        P(("sec", "depth"), None),
        P(("sec", "depth")),
        P(("sec", "depth")),
    )
    out_specs = P("segment", None, "sec", "depth", None)
    return jax.shard_map(
        on_device, mesh=mesh, in_specs=in_specs, out_specs=out_specs, check_vma=False
    )
```

```python
import functools

import jax
import jax.numpy as jnp
from jax import lax
from jax.experimental import pallas as pl
from jax.experimental.pallas import tpu as pltpu
from jax.sharding import PartitionSpec as P

STEPS = 4
F32 = jnp.float32
BF16 = jnp.bfloat16
NT = (((1,), (1,)), ((), ()))


def one_hot(index, count):
    rows = lax.broadcasted_iota(jnp.int32, (count, index.shape[-1]), 0)
    return jnp.where(rows == index, F32(1.0), F32(0.0))


def split3(value):
    high = value.astype(BF16).astype(F32)
    rest = value - high
    mid = rest.astype(BF16).astype(F32)
    return high, mid, rest - mid


def copy_all(sem, pairs):
    copies = [pltpu.make_async_copy(a, b, sem.at[i]) for i, (a, b) in enumerate(pairs)]
    for copy in copies:
        copy.start()
    for copy in copies:
        copy.wait()


def in_line(rows):
    return jnp.concatenate([rows[i : i + 1, :] for i in range(rows.shape[0])], axis=1)


def reach_of(cz):
    return cz // 2 + STEPS


def pack_kernel(
    fields_in, ids_in, moments_in, owner_in, cells_in, rows_in, buoyancy, lame_lambda, lame_mu,
    entries, kept, given, fields, ids, moments, owner, cells, rows, wide, tables, sem,
):
    cx, cz, cy = ids.shape[1:]
    arguments = [(fields_in, fields), (ids_in, ids), (moments_in, moments), (owner_in, owner)]
    arguments += [(cells_in, cells), (rows_in, rows)]
    arguments += [(t, tables.at[i]) for i, t in enumerate((buoyancy, lame_lambda, lame_mu))]
    copy_all(sem, arguments)
    for i in range(cells.shape[0]):
        at = 8 * i
        entries[at : at + 6] = moments[:, i * cy : (i + 1) * cy]
        entries[at + 6 : at + 7] = owner[i : i + 1, :].astype(F32)
        entries[at + 7 : at + 8] = cells[i : i + 1, :].astype(F32)
    wide[0] = (ids[0] + 1).astype(F32)
    line = in_line(rows[...])
    high = one_hot(line // cy, cx * cz).astype(BF16)
    low = one_hot(line % cy, cy).astype(BF16)
    count = lax.dot_general(high, low, NT, preferred_element_type=F32)
    wide[1] = count.reshape(cx, cz, cy)
    reach = reach_of(cz)
    lines = 11 * cx * reach
    lane = lax.broadcasted_iota(jnp.int32, (1, cy), 1)
    for i in range(3):
        found = jnp.zeros((1, cy), F32)
        for entry in range(tables.shape[1]):
            found = jnp.where(lane == entry + 1, F32(0.5) * tables[i, entry], found)
        kept[lines + i : lines + i + 1] = found
    kept[lines + 3 : lines + 8] = jnp.zeros((5, cy), F32)
    kept[lines + 8 :] = entries[...]

    def cut(first, other):
        for x in range(cx):
            at = slice(x * reach, (x + 1) * reach)
            for k in range(11):
                source = fields.at[0, k] if k < 9 else wide.at[k - 9]
                line = (k * cx + x) * reach
                kept[line : line + reach] = source[x, first : first + reach]
            given[0:9, at] = fields[0, :, x, other : other + reach]
            given[9, at] = wide[0, x, other : other + reach]

    @pl.when(lax.axis_index("segment") == 0)
    def _():
        cut(0, cz - reach)

    @pl.when(lax.axis_index("segment") == 1)
    def _():
        cut(cz - reach, 0)


def moments_of(layout, entries):
    cx, cz, cy = layout
    section = lax.axis_index("sec")
    half = cx * cz // 2
    chunk = [entries[8 * i : 8 * i + 8] for i in range(entries.shape[0] // 8)]
    entry = jnp.concatenate(chunk, axis=1)
    owner = entry[6:7].astype(jnp.int32)
    cell = entry[7:8].astype(jnp.int32)
    line = jnp.where(owner == section, cell // cy, -1)
    upper = line >= half
    high = one_hot(jnp.where(upper, line - half, line), half)
    low = one_hot(jnp.where(upper, cell % cy + cy, cell % cy), 2 * cy).astype(BF16)
    parts = split3(entry[0:6])
    spread = [(high * part[c : c + 1]).astype(BF16) for part in parts for c in range(6)]
    spread = jnp.concatenate(spread, axis=0)
    got = lax.dot_general(spread, low, NT, preferred_element_type=F32)
    lines = 6 * half
    return got[0:lines] + got[lines : 2 * lines] + got[2 * lines :]


def own_kernel(layout, kept, out, tables, acc):
    lines = out.shape[0] * out.shape[1]
    out[...] = kept[0:lines].reshape(out.shape)
    tables[...] = kept[lines : lines + 8]
    acc[...] = moments_of(layout, kept[lines + 8 :])


def more_kernel(layout, started, entries, acc):
    acc[...] = started[...] + moments_of(layout, entries[...])


def by_core(act):
    segment = lax.axis_index("segment")

    @pl.when(segment == 0)
    def _():
        act(0, lambda reach: slice(STEPS, STEPS + reach), lambda reach: slice(0, STEPS))

    @pl.when(segment == 1)
    def _():
        act(1, lambda reach: slice(0, reach), lambda reach: slice(reach, reach + STEPS))


def join_kernel(layout, *refs):
    cx, cz, cy = layout
    kept, got, started, entries, state, ids, times, edge, dense = refs
    reach = reach_of(cz)
    half = cx * cz // 2
    total = started[...] + moments_of(layout, entries[...])
    for c in range(6):
        for k in range(2):
            added = total[c * half : (c + 1) * half, k * cy : (k + 1) * cy]
            dense[c, k * half : (k + 1) * half] = added

    def join(mine, main, outer):
        main, outer = main(reach), outer(reach)
        first = 0 if mine == 0 else cz - reach
        last = main.start if mine == 0 else main.stop - STEPS
        gone = slice(last, last + STEPS)
        for x in range(cx):
            at = slice(x * reach, (x + 1) * reach)
            for model in range(2):
                rows = kept if model == mine else got
                state[model, :, x, main] = rows[0:9, at]
                ids[model, x, main] = rows[9, at]
            added = dense[:, x * cz + first : x * cz + first + reach]
            state[0, 3:9, x, main] = state[0, 3:9, x, main] + added
            times[x, main] = kept[10, at]
            state[:, :, x, outer] = jnp.zeros((2, 9, STEPS, cy), F32)
            ids[:, x, outer] = jnp.zeros((2, STEPS, cy), F32)
            times[x, outer] = jnp.zeros((STEPS, cy), F32)
            for k in range(21):
                line = slice((k * cx + x) * STEPS, (k * cx + x + 1) * STEPS)
                if k == 20:
                    edge[line] = times[x, gone]
                elif k % 10 == 9:
                    edge[line] = ids[k // 10, x, gone]
                else:
                    edge[line] = state[k // 10, k % 10, x, gone]

    by_core(join)


def by_parity(even, odd, act):
    parity = lax.axis_index("sec") % 2

    @pl.when(parity == 0)
    def _():
        act(*even)

    @pl.when(parity == 1)
    def _():
        act(*odd)


def advance(cx, steps, state, coef, times, given_top=False):
    planes, rows, cy = state.shape[2:]
    lane = lax.broadcasted_iota(jnp.int32, (rows, cy), 1)
    first_lane, last_lane = lane == 0, lane == cy - 1

    def back_y(f):
        return f - jnp.where(first_lane, F32(0.0), pltpu.roll(f, 1, 1))

    def back_z(f):
        return f - pltpu.roll(f, 1, 0)

    def fore_y(f):
        return jnp.where(last_lane, F32(0.0), pltpu.roll(f, cy - 1, 1)) - f

    def fore_z(f):
        return pltpu.roll(f, rows - 1, 0) - f

    def velocity(x):
        inc = [None, None]
        for model in range(2):
            sxx, syy, szz, syz, sxz, sxy = (state[model, 3 + k, x] for k in range(6))
            sxx_p, sxz_p, sxy_p = (state[model, k, x - 1] for k in (3, 7, 8))
            hb = coef[model, 0, x]
            inc[model] = (
                hb * ((sxx - sxx_p) + back_y(sxy) + back_z(sxz)),
                hb * ((sxy - sxy_p) + back_y(syy) + back_z(syz)),
                hb * ((sxz - sxz_p) + back_y(syz) + back_z(szz)),
            )
        for k in range(3):
            state[0, k, x] = state[0, k, x] + inc[0][k]
            state[1, k, x] = (state[1, k, x] + inc[1][k]) + times[x] * inc[0][k]

    for step in range(steps):
        left = steps - 1 - step
        low, high = cx - left, 2 * cx + left
        for x in range(low, high + 1 - (given_top and step == 0)):
            velocity(x)
        for x in range(low, high):
            for model in range(2):
                vx, vy, vz = (state[model, k, x] for k in range(3))
                vx_n, vy_n, vz_n = (state[model, k, x + 1] for k in range(3))
                hl, hm = coef[model, 1, x], coef[model, 2, x]
                exx, eyy, ezz = vx_n - vx, fore_y(vy), fore_z(vz)
                pressure = hl * (exx + eyy + ezz)
                twice = hm + hm
                state[model, 3, x] = state[model, 3, x] + (pressure + twice * exx)
                state[model, 4, x] = state[model, 4, x] + (pressure + twice * eyy)
                state[model, 5, x] = state[model, 5, x] + (pressure + twice * ezz)
                state[model, 6, x] = state[model, 6, x] + hm * (fore_z(vy) + fore_y(vz))
                state[model, 7, x] = state[model, 7, x] + hm * (fore_z(vx) + (vz_n - vz))
                state[model, 8, x] = state[model, 8, x] + hm * (fore_y(vx) + (vy_n - vy))

    return velocity


def look_up(tables, ids):
    lanes = ids.astype(jnp.int32)
    wide = [jnp.broadcast_to(tables[i : i + 1], ids.shape) for i in range(3)]
    return [jnp.take_along_axis(table, lanes, axis=1) for table in wide]


def edge_units(cx, with_ids):
    right, left = [], []
    for model in range(2):
        whole = list(range(10 if with_ids else 9)) + [10] * (with_ids and model == 1)
        for x in range(cx - 1):
            right += [(model, what, x + 1) for what in whole]
            left += [(model, what, x) for what in whole]
        right += [(model, what, 0) for what in (3, 7, 8)]
        left += [(model, what, cx - 1) for what in range(3)]
    return right, left


def cut_edges(cx, rows_of, with_ids, velocity, state, ids, times, to_first, to_second):
    right_units, left_units = edge_units(cx, with_ids)

    def put(to, units, far, right):
        line = slice(0, 0)
        for model, what, x in units:
            at = rows_of(x == far, right)
            line = slice(line.stop, line.stop + at.stop - at.start)
            if what == 10:
                to[line] = times[cx + x, at]
            elif what == 9:
                to[line] = ids[model, cx + x, at]
            else:
                to[line] = state[model, what, cx + x, at]

    holders = (to_second, to_first), (to_first, to_second)
    by_parity(*holders, lambda left, right: put(right, right_units, 0, True))
    velocity(2 * cx - 1)
    by_parity(*holders, lambda left, right: put(left, left_units, cx - 1, False))


def outer_rows(mine, outer):
    def rows_of(far, right):
        shift = 1 if far and not right and mine == 0 else 0
        return slice(outer.start + shift, outer.stop + shift)

    return rows_of


def reached_rows(cx, done, rows):
    def rows_of(far, right):
        first, last = done, rows - done
        if right:
            return slice(first + (cx if far else 1), last)
        return slice(first + far, last - (cx if far else 1))

    return rows_of


def coefficients(cx, planes, tables, ids, coef):
    for model in range(2):
        for x in planes:
            for i, found in enumerate(look_up(tables, ids[model, x])):
                coef[model, i, x] = found


def inner_kernel(cx, own_state, own_ids, own_times, tables, to_first, to_second, state, ids, coef, times):
    own = slice(cx, 2 * cx)
    reach = state.shape[3] - STEPS
    state[:, :, own], ids[:, own], times[own] = own_state[...], own_ids[...], own_times[...]
    coefficients(cx, range(2 * cx - 1, 2 * cx), tables, ids, coef)
    velocity = advance(cx, 0, state, coef, times)

    def cut(mine, main, outer):
        rows_of = lambda far, right: main(reach)
        cut_edges(cx, rows_of, True, velocity, state, ids, times, to_first, to_second)

    by_core(cut)


def outer_kernel(
    cx, own_state, own_ids, own_times, halo, tables,
    to_first, to_second, both, coef_out, times_out, state, ids, coef, times,
):
    own = slice(cx, 2 * cx)
    reach = state.shape[3] - STEPS
    state[:, :, own], ids[:, own], times[own] = own_state[...], own_ids[...], own_times[...]

    def join(mine, main, outer):
        for x in range(cx):
            for k in range(21):
                line = halo[(k * cx + x) * STEPS : (k * cx + x + 1) * STEPS]
                if k == 20:
                    times[cx + x, outer(reach)] = line
                elif k % 10 == 9:
                    ids[k // 10, cx + x, outer(reach)] = line
                else:
                    state[k // 10, k % 10, cx + x, outer(reach)] = line

    by_core(join)
    coefficients(cx, range(cx, 2 * cx), tables, ids, coef)
    both[...] = state[:, :, own]
    coef_out[...] = coef[:, :, own]
    times_out[...] = times[own]
    velocity = advance(cx, 0, state, coef, times)

    def cut(mine, main, outer):
        rows_of = outer_rows(mine, outer(reach))
        cut_edges(cx, rows_of, True, velocity, state, ids, times, to_first, to_second)

    by_core(cut)


def next_kernel(cx, done, *refs):
    first = done == 0
    parts = 2 if first else 1
    both_in, coef_in, times_in = refs[0:3]
    edges, refs = refs[3 : 3 + 2 * parts], refs[3 + 2 * parts :]
    if first:
        tables, outs = refs[0], refs[1:]
        state, ids, coef, times = refs[-4:]
    else:
        ids, outs = None, refs
        state, coef, times = refs[-1], coef_in, times_in
    segment = lax.axis_index("segment")
    rows = state.shape[3]
    own = slice(cx, 2 * cx)
    state[:, :, own] = both_in[...]
    right_units, left_units = edge_units(cx, first)

    def get(edge, units, start, rows_of, far, right):
        last = 0
        for model, what, x in units:
            at = rows_of(x == far, right)
            first, last = last, last + at.stop - at.start
            line = edge[first:last]
            if what == 10:
                times[start + x, at] = line
            elif what == 9:
                ids[model, start + x, at] = line
            else:
                state[model, what, start + x, at] = line

    def place(rows_of, pair):
        def put(left, right):
            get(left, right_units, 0, rows_of, 0, True)
            get(right, left_units, 2 * cx, rows_of, cx - 1, False)

        by_parity((pair[1], pair[0]), pair, put)

    if first:

        def place_both(mine, main, outer):
            reach = rows - STEPS
            place(lambda far, right: main(reach), edges[0:2])
            place(outer_rows(mine, outer(reach)), edges[2:4])

        by_core(place_both)
        coef[:, :, own] = coef_in[...]
        times[own] = times_in[...]
        coefficients(cx, (*range(1, cx), *range(2 * cx, 3 * cx - 1)), tables, ids, coef)
    else:
        place(reached_rows(cx, done, rows), edges)
    velocity = advance(cx, cx, state, coef, times, given_top=True)
    if done + cx == STEPS:
        outs[0][...] = state[segment, :, own, STEPS : rows - STEPS]
        outs[1][...] = state[1 - segment, :, own, STEPS : rows - STEPS]
    else:
        outs[2][...] = state[:, :, own]
        if first:
            outs[3][...] = coef[...]
            outs[4][...] = times[...]
        rows_of = reached_rows(cx, done + cx, rows)
        cut_edges(cx, rows_of, False, velocity, state, None, times, outs[0], outs[1])


def home_kernel(mine, brought, out):
    half = mine.shape[2]
    segment = lax.axis_index("segment")

    @pl.when(segment == 0)
    def _():
        out[0, :, :, 0:half] = mine[...]
        out[0, :, :, half:] = brought[...]

    @pl.when(segment == 1)
    def _():
        out[0, :, :, half:] = mine[...]
        out[0, :, :, 0:half] = brought[...]


VMEM = pl.BlockSpec(memory_space=pltpu.VMEM)
HBM = pl.BlockSpec(memory_space=pltpu.HBM)


def call(kernel, name, in_vmem, in_hbm, outs, scratch, copies=0, limit=40 * 2**20, flops=10**7):
    sems = [pltpu.SemaphoreType.DMA((copies,))] * (copies > 0)
    return pl.pallas_call(
        kernel,
        out_shape=[jax.ShapeDtypeStruct(shape, F32) for shape in outs],
        in_specs=[VMEM] * len(in_vmem) + [HBM] * len(in_hbm),
        out_specs=[VMEM] * len(outs),
        scratch_shapes=[pltpu.VMEM(s, F32) if isinstance(s, tuple) else s for s in scratch] + sems,
        compiler_params=pltpu.CompilerParams(vmem_limit_bytes=limit),
        cost_estimate=pl.CostEstimate(flops=flops, bytes_accessed=2**20, transcendentals=0),
        name=name,
    )(*in_vmem, *in_hbm)


def on_device(
    fields, block_ids, buoyancy, lame_lambda, lame_mu, moments, moment_owner, moment_cells, drm_rows
):
    sections, slabs = lax.axis_size("sec"), lax.axis_size("depth")
    layout = cx, cz, cy = fields.shape[2:]
    reach, rows = reach_of(cz), cz // 2 + 2 * STEPS
    assert cx > 1 and STEPS % cx == 0

    def pairs(block, start):
        route = [(i, i + 1) for i in range(start, sections - 1, 2)]
        return lax.ppermute(block, "sec", route + [(j, i) for i, j in route])

    def other(section, k):
        return section ^ k if sections & (sections - 1) == 0 else (section + k) % sections

    def along_depth(block):
        down = [(2 * i + 1, 2 * (i + 1)) for i in range(slabs - 1)]
        return lax.ppermute(block, ("depth", "segment"), down + [(j, i) for i, j in down])

    def swap(block):
        return lax.ppermute(block, "segment", [(0, 1), (1, 0)])

    owner = moment_owner.reshape(-1, cy)
    cells = moment_cells.reshape(-1, cy)
    arguments = (fields, block_ids, moments, owner, cells, drm_rows.reshape(-1, cy))
    entry_lines = 8 * cells.shape[0]
    entries, kept, given = call(
        pack_kernel,
        "pack",
        (),
        (*arguments, buoyancy, lame_lambda, lame_mu),
        [(entry_lines, cy), (11 * cx * reach + 8 + entry_lines, cy), (10, cx * reach, cy)],
        [pltpu.VMEM(a.shape, a.dtype) for a in arguments]
        + [(2, cx, cz, cy), pltpu.SMEM((3, buoyancy.shape[0]), F32)],
        len(arguments) + 3,
        limit=64 * 2**20,
    )
    blocks = [
        lax.ppermute(entries, "sec", [(other(i, k), i) for i in range(sections)])
        for k in (*range(2, sections), 1)[: sections - 1]
    ]
    got = swap(given)
    acc_shape = (6 * cx * cz // 2, 2 * cy)
    kept, tables, started = call(
        functools.partial(own_kernel, layout),
        "own_moments",
        (kept,),
        (),
        [(11, cx * reach, cy), (8, cy), acc_shape],
        [],
        flops=10**8,
    )
    for block, flops in zip(blocks[:-1], (10**8,) + (6 * 10**9,) * sections):
        (started,) = call(
            functools.partial(more_kernel, layout),
            "more_moments",
            (started, block),
            (),
            [acc_shape],
            [],
            flops=flops,
        )
    own = (cx, rows, cy)
    window = (3 * cx, rows, cy)
    state, ids, times, edge = call(
        functools.partial(join_kernel, layout),
        "join_and_moments",
        (kept, got, started, blocks[-1]),
        (),
        [(2, 9, *own), (2, *own), own, (21 * cx * STEPS, cy)],
        [(6, cx * cz, cy)],
    )
    halo = along_depth(edge)
    work = [(2, 9, *window), (2, *window), (2, 3, *window), window]

    def edges(count, with_ids):
        return [(len(edge_units(cx, with_ids)[0]) * count, cy)] * 2

    def reached_edges(done):
        rows_of = reached_rows(cx, done, rows)
        whole, far = rows_of(False, True), rows_of(True, True)
        lines = 18 * (cx - 1) * (whole.stop - whole.start) + 6 * (far.stop - far.start)
        return [(-(-lines // 8) * 8, cy)] * 2

    def exchange(pair):
        return [pairs(pair[0], 0), pairs(pair[1], 1)]

    inner = call(
        functools.partial(inner_kernel, cx),
        "inner_edges",
        (state, ids, times, tables),
        (),
        edges(reach, True),
        work,
        flops=10**9,
    )
    got_edges = exchange(inner)
    *outer, both, coef, times = call(
        functools.partial(outer_kernel, cx),
        "outer_edges",
        (state, ids, times, halo, tables),
        (),
        edges(STEPS, True) + [(2, 9, *own), (2, 3, *own), own],
        work,
        flops=4 * 10**9,
    )
    got_edges += exchange(outer)
    for done in range(0, STEPS, cx):
        first, last = done == 0, done + cx == STEPS
        after = done + cx
        outs = [(9, cx, cz // 2, cy)] * 2
        if not last:
            outs = reached_edges(after) + [(2, 9, *own)]
            outs += [(2, 3, *window), window] * first
        pair = call(
            functools.partial(next_kernel, cx, done),
            "steps",
            (both, coef, times, *got_edges) + (tables,) * first,
            (),
            outs,
            work if first else work[0:1],
        )
        if not last:
            got_edges = exchange(pair[0:2])
            both = pair[2]
            if first:
                coef, times = pair[3:5]
    to_first, to_second = pair[0:2]
    (out,) = call(home_kernel, "home", (to_first, swap(to_second)), (), [fields.shape], [])
    return out


def solution(mesh):
    in_specs = (
        P("segment", None, "sec", "depth", None),
        P("segment", "sec", "depth", None),
        P(),
        P(),
        P(),
        P(None, ("sec", "depth")),
        P(("sec", "depth"), None),
        P(("sec", "depth")),
        P(("sec", "depth")),
    )
    out_specs = P("segment", None, "sec", "depth", None)
    return jax.shard_map(
        on_device, mesh=mesh, in_specs=in_specs, out_specs=out_specs, check_vma=False
    )
```

```python
import functools

import jax
import jax.numpy as jnp
from jax import lax
from jax.experimental import pallas as pl
from jax.experimental.pallas import tpu as pltpu
from jax.sharding import PartitionSpec as P

STEPS = 4
F32 = jnp.float32
BF16 = jnp.bfloat16
NT = (((1,), (1,)), ((), ()))


def one_hot(index, count):
    rows = lax.broadcasted_iota(jnp.int32, (count, index.shape[-1]), 0)
    return jnp.where(rows == index, F32(1.0), F32(0.0))


def split3(value):
    high = value.astype(BF16).astype(F32)
    rest = value - high
    mid = rest.astype(BF16).astype(F32)
    return high, mid, rest - mid


def copy_all(sem, pairs):
    copies = [pltpu.make_async_copy(a, b, sem.at[i]) for i, (a, b) in enumerate(pairs)]
    for copy in copies:
        copy.start()
    for copy in copies:
        copy.wait()


def in_line(rows):
    return jnp.concatenate([rows[i : i + 1, :] for i in range(rows.shape[0])], axis=1)


def reach_of(cz):
    return cz // 2 + STEPS


def pack_kernel(
    fields_in, ids_in, moments_in, owner_in, cells_in, rows_in, buoyancy, lame_lambda, lame_mu,
    entries, kept, given, fields, ids, moments, owner, cells, rows, wide, tables, sem,
):
    cx, cz, cy = ids.shape[1:]
    arguments = [(fields_in, fields), (ids_in, ids), (moments_in, moments), (owner_in, owner)]
    arguments += [(cells_in, cells), (rows_in, rows)]
    arguments += [(t, tables.at[i]) for i, t in enumerate((buoyancy, lame_lambda, lame_mu))]
    copy_all(sem, arguments)
    for i in range(cells.shape[0]):
        at = 8 * i
        entries[at : at + 6] = moments[:, i * cy : (i + 1) * cy]
        entries[at + 6 : at + 7] = owner[i : i + 1, :].astype(F32)
        entries[at + 7 : at + 8] = cells[i : i + 1, :].astype(F32)
    wide[0] = (ids[0] + 1).astype(F32)
    line = in_line(rows[...])
    high = one_hot(line // cy, cx * cz).astype(BF16)
    low = one_hot(line % cy, cy).astype(BF16)
    count = lax.dot_general(high, low, NT, preferred_element_type=F32)
    wide[1] = count.reshape(cx, cz, cy)
    reach = reach_of(cz)
    lines = 11 * cx * reach
    lane = lax.broadcasted_iota(jnp.int32, (1, cy), 1)
    for i in range(3):
        found = jnp.zeros((1, cy), F32)
        for entry in range(tables.shape[1]):
            found = jnp.where(lane == entry + 1, F32(0.5) * tables[i, entry], found)
        kept[lines + i : lines + i + 1] = found
    kept[lines + 3 : lines + 8] = jnp.zeros((5, cy), F32)
    kept[lines + 8 :] = entries[...]

    def cut(first, other):
        for x in range(cx):
            at = slice(x * reach, (x + 1) * reach)
            for k in range(11):
                source = fields.at[0, k] if k < 9 else wide.at[k - 9]
                line = (k * cx + x) * reach
                kept[line : line + reach] = source[x, first : first + reach]
            given[0:9, at] = fields[0, :, x, other : other + reach]
            given[9, at] = wide[0, x, other : other + reach]

    @pl.when(lax.axis_index("segment") == 0)
    def _():
        cut(0, cz - reach)

    @pl.when(lax.axis_index("segment") == 1)
    def _():
        cut(cz - reach, 0)


def moments_of(layout, entries):
    cx, cz, cy = layout
    section = lax.axis_index("sec")
    half = cx * cz // 2
    chunk = [entries[8 * i : 8 * i + 8] for i in range(entries.shape[0] // 8)]
    entry = jnp.concatenate(chunk, axis=1)
    owner = entry[6:7].astype(jnp.int32)
    cell = entry[7:8].astype(jnp.int32)
    line = jnp.where(owner == section, cell // cy, -1)
    upper = line >= half
    high = one_hot(jnp.where(upper, line - half, line), half)
    low = one_hot(jnp.where(upper, cell % cy + cy, cell % cy), 2 * cy).astype(BF16)
    parts = split3(entry[0:6])
    spread = [(high * part[c : c + 1]).astype(BF16) for part in parts for c in range(6)]
    spread = jnp.concatenate(spread, axis=0)
    got = lax.dot_general(spread, low, NT, preferred_element_type=F32)
    lines = 6 * half
    return got[0:lines] + got[lines : 2 * lines] + got[2 * lines :]


def own_kernel(layout, kept, out, tables, acc):
    lines = out.shape[0] * out.shape[1]
    out[...] = kept[0:lines].reshape(out.shape)
    tables[...] = kept[lines : lines + 8]
    acc[...] = moments_of(layout, kept[lines + 8 :])


def more_kernel(layout, started, entries, acc):
    acc[...] = started[...] + moments_of(layout, entries[...])


def by_core(act):
    segment = lax.axis_index("segment")

    @pl.when(segment == 0)
    def _():
        act(0, lambda reach: slice(STEPS, STEPS + reach), lambda reach: slice(0, STEPS))

    @pl.when(segment == 1)
    def _():
        act(1, lambda reach: slice(0, reach), lambda reach: slice(reach, reach + STEPS))


def join_kernel(layout, *refs):
    cx, cz, cy = layout
    kept, got, started, entries, state, ids, times, edge, dense = refs
    reach = reach_of(cz)
    half = cx * cz // 2
    total = started[...] + moments_of(layout, entries[...])
    for c in range(6):
        for k in range(2):
            added = total[c * half : (c + 1) * half, k * cy : (k + 1) * cy]
            dense[c, k * half : (k + 1) * half] = added

    def join(mine, main, outer):
        main, outer = main(reach), outer(reach)
        first = 0 if mine == 0 else cz - reach
        last = main.start if mine == 0 else main.stop - STEPS
        gone = slice(last, last + STEPS)
        for x in range(cx):
            at = slice(x * reach, (x + 1) * reach)
            for model in range(2):
                rows = kept if model == mine else got
                state[model, :, x, main] = rows[0:9, at]
                ids[model, x, main] = rows[9, at]
            added = dense[:, x * cz + first : x * cz + first + reach]
            state[0, 3:9, x, main] = state[0, 3:9, x, main] + added
            times[x, main] = kept[10, at]
            state[:, :, x, outer] = jnp.zeros((2, 9, STEPS, cy), F32)
            ids[:, x, outer] = jnp.zeros((2, STEPS, cy), F32)
            times[x, outer] = jnp.zeros((STEPS, cy), F32)
            for k in range(21):
                line = slice((k * cx + x) * STEPS, (k * cx + x + 1) * STEPS)
                if k == 20:
                    edge[line] = times[x, gone]
                elif k % 10 == 9:
                    edge[line] = ids[k // 10, x, gone]
                else:
                    edge[line] = state[k // 10, k % 10, x, gone]

    by_core(join)


def by_parity(even, odd, act):
    parity = lax.axis_index("sec") % 2

    @pl.when(parity == 0)
    def _():
        act(*even)

    @pl.when(parity == 1)
    def _():
        act(*odd)


def advance(cx, steps, state, coef, times, given_top=False):
    planes, rows, cy = state.shape[2:]
    lane = lax.broadcasted_iota(jnp.int32, (rows, cy), 1)
    first_lane, last_lane = lane == 0, lane == cy - 1

    def back_y(f):
        return f - jnp.where(first_lane, F32(0.0), pltpu.roll(f, 1, 1))

    def back_z(f):
        return f - pltpu.roll(f, 1, 0)

    def fore_y(f):
        return jnp.where(last_lane, F32(0.0), pltpu.roll(f, cy - 1, 1)) - f

    def fore_z(f):
        return pltpu.roll(f, rows - 1, 0) - f

    def velocity(x):
        inc = [None, None]
        for model in range(2):
            sxx, syy, szz, syz, sxz, sxy = (state[model, 3 + k, x] for k in range(6))
            sxx_p, sxz_p, sxy_p = (state[model, k, x - 1] for k in (3, 7, 8))
            hb = coef[model, 0, x]
            inc[model] = (
                hb * ((sxx - sxx_p) + back_y(sxy) + back_z(sxz)),
                hb * ((sxy - sxy_p) + back_y(syy) + back_z(syz)),
                hb * ((sxz - sxz_p) + back_y(syz) + back_z(szz)),
            )
        for k in range(3):
            state[0, k, x] = state[0, k, x] + inc[0][k]
            state[1, k, x] = (state[1, k, x] + inc[1][k]) + times[x] * inc[0][k]

    for step in range(steps):
        left = steps - 1 - step
        low, high = cx - left, 2 * cx + left
        for x in range(low, high + 1 - (given_top and step == 0)):
            velocity(x)
        for x in range(low, high):
            for model in range(2):
                vx, vy, vz = (state[model, k, x] for k in range(3))
                vx_n, vy_n, vz_n = (state[model, k, x + 1] for k in range(3))
                hl, hm = coef[model, 1, x], coef[model, 2, x]
                exx, eyy, ezz = vx_n - vx, fore_y(vy), fore_z(vz)
                pressure = hl * (exx + eyy + ezz)
                twice = hm + hm
                state[model, 3, x] = state[model, 3, x] + (pressure + twice * exx)
                state[model, 4, x] = state[model, 4, x] + (pressure + twice * eyy)
                state[model, 5, x] = state[model, 5, x] + (pressure + twice * ezz)
                state[model, 6, x] = state[model, 6, x] + hm * (fore_z(vy) + fore_y(vz))
                state[model, 7, x] = state[model, 7, x] + hm * (fore_z(vx) + (vz_n - vz))
                state[model, 8, x] = state[model, 8, x] + hm * (fore_y(vx) + (vy_n - vy))

    return velocity


def look_up(tables, ids):
    lanes = ids.astype(jnp.int32)
    wide = [jnp.broadcast_to(tables[i : i + 1], ids.shape) for i in range(3)]
    return [jnp.take_along_axis(table, lanes, axis=1) for table in wide]


def edge_units(cx, with_ids):
    right, left = [], []
    for model in range(2):
        whole = list(range(10 if with_ids else 9)) + [10] * (with_ids and model == 1)
        for x in range(cx - 1):
            right += [(model, what, x + 1) for what in whole]
            left += [(model, what, x) for what in whole]
        right += [(model, what, 0) for what in (3, 7, 8)]
        left += [(model, what, cx - 1) for what in range(3)]
    return right, left


def cut_edges(cx, rows_of, with_ids, velocity, state, ids, times, to_first, to_second):
    right_units, left_units = edge_units(cx, with_ids)

    def put(to, units, far, right):
        to, pairing = to
        line = slice(0, 0)
        for model, what, x in units:
            at = rows_of(x == far, right, pairing)
            line = slice(line.stop, line.stop + at.stop - at.start)
            if what == 10:
                to[line] = times[cx + x, at]
            elif what == 9:
                to[line] = ids[model, cx + x, at]
            else:
                to[line] = state[model, what, cx + x, at]

    first, second = (to_first, 0), (to_second, 1)
    holders = (second, first), (first, second)
    by_parity(*holders, lambda left, right: put(right, right_units, 0, True))
    velocity(2 * cx - 1)
    by_parity(*holders, lambda left, right: put(left, left_units, cx - 1, False))


def inner_rows(mine, main):
    def rows_of(far, right, pairing):
        short = STEPS * (pairing == 0)
        if mine == 0:
            return slice(main.start + short, main.stop)
        return slice(main.start, main.stop - short)

    return rows_of


def outer_rows(mine, outer):
    def rows_of(far, right, pairing):
        more = STEPS * (pairing == 0)
        if mine == 1:
            return slice(outer.start - more, outer.stop)
        shift = 1 if far and not right else 0
        return slice(outer.start + shift, outer.stop + more + shift)

    return rows_of


def reached_rows(cx, done, rows):
    def rows_of(far, right, pairing=0):
        first, last = done, rows - done
        if right:
            return slice(first + (cx if far else 1), last)
        return slice(first + far, last - (cx if far else 1))

    return rows_of


def coefficients(cx, planes, tables, ids, coef):
    for model in range(2):
        for x in planes:
            for i, found in enumerate(look_up(tables, ids[model, x])):
                coef[model, i, x] = found


def inner_kernel(cx, own_state, own_ids, own_times, tables, to_first, to_second, state, ids, coef, times):
    own = slice(cx, 2 * cx)
    reach = state.shape[3] - STEPS
    state[:, :, own], ids[:, own], times[own] = own_state[...], own_ids[...], own_times[...]
    coefficients(cx, range(2 * cx - 1, 2 * cx), tables, ids, coef)
    velocity = advance(cx, 0, state, coef, times)

    def cut(mine, main, outer):
        rows_of = inner_rows(mine, main(reach))
        cut_edges(cx, rows_of, True, velocity, state, ids, times, to_first, to_second)

    by_core(cut)


def outer_kernel(
    cx, own_state, own_ids, own_times, halo, tables,
    to_first, to_second, both, coef_out, times_out, state, ids, coef, times,
):
    own = slice(cx, 2 * cx)
    reach = state.shape[3] - STEPS
    state[:, :, own], ids[:, own], times[own] = own_state[...], own_ids[...], own_times[...]

    def join(mine, main, outer):
        for x in range(cx):
            for k in range(21):
                line = halo[(k * cx + x) * STEPS : (k * cx + x + 1) * STEPS]
                if k == 20:
                    times[cx + x, outer(reach)] = line
                elif k % 10 == 9:
                    ids[k // 10, cx + x, outer(reach)] = line
                else:
                    state[k // 10, k % 10, cx + x, outer(reach)] = line

    by_core(join)
    coefficients(cx, range(cx, 2 * cx), tables, ids, coef)
    both[...] = state[:, :, own]
    coef_out[...] = coef[:, :, own]
    times_out[...] = times[own]
    velocity = advance(cx, 0, state, coef, times)

    def cut(mine, main, outer):
        rows_of = outer_rows(mine, outer(reach))
        cut_edges(cx, rows_of, True, velocity, state, ids, times, to_first, to_second)

    by_core(cut)


def next_kernel(cx, done, *refs):
    first = done == 0
    parts = 2 if first else 1
    both_in, coef_in, times_in = refs[0:3]
    edges, refs = refs[3 : 3 + 2 * parts], refs[3 + 2 * parts :]
    if first:
        tables, outs = refs[0], refs[1:]
        state, ids, coef, times = refs[-4:]
    else:
        ids, outs = None, refs
        state, coef, times = refs[-1], coef_in, times_in
    segment = lax.axis_index("segment")
    rows = state.shape[3]
    own = slice(cx, 2 * cx)
    state[:, :, own] = both_in[...]
    right_units, left_units = edge_units(cx, first)

    def get(edge, units, start, rows_of, far, right):
        edge, pairing = edge
        last = 0
        for model, what, x in units:
            at = rows_of(x == far, right, pairing)
            first, last = last, last + at.stop - at.start
            line = edge[first:last]
            if what == 10:
                times[start + x, at] = line
            elif what == 9:
                ids[model, start + x, at] = line
            else:
                state[model, what, start + x, at] = line

    def place(rows_of, pair):
        def put(left, right):
            get(left, right_units, 0, rows_of, 0, True)
            get(right, left_units, 2 * cx, rows_of, cx - 1, False)

        early, late = (pair[0], 0), (pair[1], 1)
        by_parity((late, early), (early, late), put)

    if first:

        def place_both(mine, main, outer):
            reach = rows - STEPS
            place(inner_rows(mine, main(reach)), edges[0:2])
            place(outer_rows(mine, outer(reach)), edges[2:4])

        by_core(place_both)
        coef[:, :, own] = coef_in[...]
        times[own] = times_in[...]
        coefficients(cx, (*range(1, cx), *range(2 * cx, 3 * cx - 1)), tables, ids, coef)
    else:
        place(reached_rows(cx, done, rows), edges)
    velocity = advance(cx, cx, state, coef, times, given_top=True)
    if done + cx == STEPS:
        outs[0][...] = state[segment, :, own, STEPS : rows - STEPS]
        outs[1][...] = state[1 - segment, :, own, STEPS : rows - STEPS]
    else:
        outs[2][...] = state[:, :, own]
        if first:
            outs[3][...] = coef[...]
            outs[4][...] = times[...]
        rows_of = reached_rows(cx, done + cx, rows)
        cut_edges(cx, rows_of, False, velocity, state, None, times, outs[0], outs[1])


def home_kernel(mine, brought, out):
    half = mine.shape[2]
    segment = lax.axis_index("segment")

    @pl.when(segment == 0)
    def _():
        out[0, :, :, 0:half] = mine[...]
        out[0, :, :, half:] = brought[...]

    @pl.when(segment == 1)
    def _():
        out[0, :, :, half:] = mine[...]
        out[0, :, :, 0:half] = brought[...]


VMEM = pl.BlockSpec(memory_space=pltpu.VMEM)
HBM = pl.BlockSpec(memory_space=pltpu.HBM)


def call(kernel, name, in_vmem, in_hbm, outs, scratch, copies=0, limit=40 * 2**20, flops=10**7):
    sems = [pltpu.SemaphoreType.DMA((copies,))] * (copies > 0)
    return pl.pallas_call(
        kernel,
        out_shape=[jax.ShapeDtypeStruct(shape, F32) for shape in outs],
        in_specs=[VMEM] * len(in_vmem) + [HBM] * len(in_hbm),
        out_specs=[VMEM] * len(outs),
        scratch_shapes=[pltpu.VMEM(s, F32) if isinstance(s, tuple) else s for s in scratch] + sems,
        compiler_params=pltpu.CompilerParams(vmem_limit_bytes=limit),
        cost_estimate=pl.CostEstimate(flops=flops, bytes_accessed=2**20, transcendentals=0),
        name=name,
    )(*in_vmem, *in_hbm)


def on_device(
    fields, block_ids, buoyancy, lame_lambda, lame_mu, moments, moment_owner, moment_cells, drm_rows
):
    sections, slabs = lax.axis_size("sec"), lax.axis_size("depth")
    layout = cx, cz, cy = fields.shape[2:]
    reach, rows = reach_of(cz), cz // 2 + 2 * STEPS
    assert cx > 1 and STEPS % cx == 0

    def pairs(block, start):
        route = [(i, i + 1) for i in range(start, sections - 1, 2)]
        return lax.ppermute(block, "sec", route + [(j, i) for i, j in route])

    def other(section, k):
        return section ^ k if sections & (sections - 1) == 0 else (section + k) % sections

    def along_depth(block):
        down = [(2 * i + 1, 2 * (i + 1)) for i in range(slabs - 1)]
        return lax.ppermute(block, ("depth", "segment"), down + [(j, i) for i, j in down])

    def swap(block):
        return lax.ppermute(block, "segment", [(0, 1), (1, 0)])

    owner = moment_owner.reshape(-1, cy)
    cells = moment_cells.reshape(-1, cy)
    arguments = (fields, block_ids, moments, owner, cells, drm_rows.reshape(-1, cy))
    entry_lines = 8 * cells.shape[0]
    entries, kept, given = call(
        pack_kernel,
        "pack",
        (),
        (*arguments, buoyancy, lame_lambda, lame_mu),
        [(entry_lines, cy), (11 * cx * reach + 8 + entry_lines, cy), (10, cx * reach, cy)],
        [pltpu.VMEM(a.shape, a.dtype) for a in arguments]
        + [(2, cx, cz, cy), pltpu.SMEM((3, buoyancy.shape[0]), F32)],
        len(arguments) + 3,
        limit=64 * 2**20,
    )
    blocks = [
        lax.ppermute(entries, "sec", [(other(i, k), i) for i in range(sections)])
        for k in (sections - 1, *range(1, sections - 1))
    ]
    got = swap(given)
    acc_shape = (6 * cx * cz // 2, 2 * cy)
    kept, tables, started = call(
        functools.partial(own_kernel, layout),
        "own_moments",
        (kept,),
        (),
        [(11, cx * reach, cy), (8, cy), acc_shape],
        [],
        flops=10**8,
    )
    for block in blocks[:-1]:
        (started,) = call(
            functools.partial(more_kernel, layout),
            "more_moments",
            (started, block),
            (),
            [acc_shape],
            [],
            flops=6 * 10**9,
        )
    own = (cx, rows, cy)
    window = (3 * cx, rows, cy)
    state, ids, times, edge = call(
        functools.partial(join_kernel, layout),
        "join_and_moments",
        (kept, got, started, blocks[-1]),
        (),
        [(2, 9, *own), (2, *own), own, (21 * cx * STEPS, cy)],
        [(6, cx * cz, cy)],
    )
    halo = along_depth(edge)
    work = [(2, 9, *window), (2, *window), (2, 3, *window), window]

    def edges(*counts):
        return [(len(edge_units(cx, True)[0]) * count, cy) for count in counts]

    def reached_edges(done):
        rows_of = reached_rows(cx, done, rows)
        whole, far = rows_of(False, True), rows_of(True, True)
        lines = 18 * (cx - 1) * (whole.stop - whole.start) + 6 * (far.stop - far.start)
        return [(-(-lines // 8) * 8, cy)] * 2

    def exchange(pair):
        return [pairs(pair[0], 0), pairs(pair[1], 1)]

    inner = call(
        functools.partial(inner_kernel, cx),
        "inner_edges",
        (state, ids, times, tables),
        (),
        edges(reach - STEPS, reach),
        work,
        flops=10**9,
    )
    got_edges = exchange(inner)
    *outer, both, coef, times = call(
        functools.partial(outer_kernel, cx),
        "outer_edges",
        (state, ids, times, halo, tables),
        (),
        edges(2 * STEPS, STEPS) + [(2, 9, *own), (2, 3, *own), own],
        work,
        flops=4 * 10**9,
    )
    got_edges += exchange(outer)
    for done in range(0, STEPS, cx):
        first, last = done == 0, done + cx == STEPS
        after = done + cx
        outs = [(9, cx, cz // 2, cy)] * 2
        if not last:
            outs = reached_edges(after) + [(2, 9, *own)]
            outs += [(2, 3, *window), window] * first
        pair = call(
            functools.partial(next_kernel, cx, done),
            "steps",
            (both, coef, times, *got_edges) + (tables,) * first,
            (),
            outs,
            work if first else work[0:1],
        )
        if not last:
            got_edges = exchange(pair[0:2])
            both = pair[2]
            if first:
                coef, times = pair[3:5]
    to_first, to_second = pair[0:2]
    (out,) = call(home_kernel, "home", (to_first, swap(to_second)), (), [fields.shape], [])
    return out


def solution(mesh):
    in_specs = (
        P("segment", None, "sec", "depth", None),
        P("segment", "sec", "depth", None),
        P(),
        P(),
        P(),
        P(None, ("sec", "depth")),
        P(("sec", "depth"), None),
        P(("sec", "depth")),
        P(("sec", "depth")),
    )
    out_specs = P("segment", None, "sec", "depth", None)
    return jax.shard_map(
        on_device, mesh=mesh, in_specs=in_specs, out_specs=out_specs, check_vma=False
    )
```

```python
import functools

import jax
import jax.numpy as jnp
from jax import lax
from jax.experimental import pallas as pl
from jax.experimental.pallas import tpu as pltpu
from jax.sharding import PartitionSpec as P

STEPS = 4
F32 = jnp.float32
BF16 = jnp.bfloat16
NT = (((1,), (1,)), ((), ()))


def one_hot(index, count):
    rows = lax.broadcasted_iota(jnp.int32, (count, index.shape[-1]), 0)
    return jnp.where(rows == index, F32(1.0), F32(0.0))


def split3(value):
    high = value.astype(BF16).astype(F32)
    rest = value - high
    mid = rest.astype(BF16).astype(F32)
    return high, mid, rest - mid


def copy_all(sem, pairs):
    copies = [pltpu.make_async_copy(a, b, sem.at[i]) for i, (a, b) in enumerate(pairs)]
    for copy in copies:
        copy.start()
    for copy in copies:
        copy.wait()


def in_line(rows):
    return jnp.concatenate([rows[i : i + 1, :] for i in range(rows.shape[0])], axis=1)


def reach_of(cz):
    return cz // 2 + STEPS


def pack_kernel(
    fields_in, ids_in, moments_in, owner_in, cells_in, rows_in, buoyancy, lame_lambda, lame_mu,
    entries, kept, given, fields, ids, moments, owner, cells, rows, wide, tables, sem,
):
    cx, cz, cy = ids.shape[1:]
    arguments = [(fields_in, fields), (ids_in, ids), (moments_in, moments), (owner_in, owner)]
    arguments += [(cells_in, cells), (rows_in, rows)]
    arguments += [(t, tables.at[i]) for i, t in enumerate((buoyancy, lame_lambda, lame_mu))]
    copy_all(sem, arguments)
    for i in range(cells.shape[0]):
        at = 8 * i
        entries[at : at + 6] = moments[:, i * cy : (i + 1) * cy]
        entries[at + 6 : at + 7] = owner[i : i + 1, :].astype(F32)
        entries[at + 7 : at + 8] = cells[i : i + 1, :].astype(F32)
    wide[0] = (ids[0] + 1).astype(F32)
    line = in_line(rows[...])
    high = one_hot(line // cy, cx * cz).astype(BF16)
    low = one_hot(line % cy, cy).astype(BF16)
    count = lax.dot_general(high, low, NT, preferred_element_type=F32)
    wide[1] = count.reshape(cx, cz, cy)
    reach = reach_of(cz)
    lines = 11 * cx * reach
    lane = lax.broadcasted_iota(jnp.int32, (1, cy), 1)
    for i in range(3):
        found = jnp.zeros((1, cy), F32)
        for entry in range(tables.shape[1]):
            found = jnp.where(lane == entry + 1, F32(0.5) * tables[i, entry], found)
        kept[lines + i : lines + i + 1] = found
    kept[lines + 3 : lines + 8] = jnp.zeros((5, cy), F32)
    kept[lines + 8 :] = entries[...]

    def cut(first, other):
        for x in range(cx):
            at = slice(x * reach, (x + 1) * reach)
            for k in range(11):
                source = fields.at[0, k] if k < 9 else wide.at[k - 9]
                line = (k * cx + x) * reach
                kept[line : line + reach] = source[x, first : first + reach]
            given[0:9, at] = fields[0, :, x, other : other + reach]
            given[9, at] = wide[0, x, other : other + reach]

    @pl.when(lax.axis_index("segment") == 0)
    def _():
        cut(0, cz - reach)

    @pl.when(lax.axis_index("segment") == 1)
    def _():
        cut(cz - reach, 0)


def moments_of(layout, entries):
    cx, cz, cy = layout
    section = lax.axis_index("sec")
    half = cx * cz // 2
    chunk = [entries[8 * i : 8 * i + 8] for i in range(entries.shape[0] // 8)]
    entry = jnp.concatenate(chunk, axis=1)
    owner = entry[6:7].astype(jnp.int32)
    cell = entry[7:8].astype(jnp.int32)
    line = jnp.where(owner == section, cell // cy, -1)
    upper = line >= half
    high = one_hot(jnp.where(upper, line - half, line), half)
    low = one_hot(jnp.where(upper, cell % cy + cy, cell % cy), 2 * cy).astype(BF16)
    parts = split3(entry[0:6])
    spread = [(high * part[c : c + 1]).astype(BF16) for part in parts for c in range(6)]
    spread = jnp.concatenate(spread, axis=0)
    got = lax.dot_general(spread, low, NT, preferred_element_type=F32)
    lines = 6 * half
    return got[0:lines] + got[lines : 2 * lines] + got[2 * lines :]


def own_kernel(layout, kept, out, tables, acc):
    lines = out.shape[0] * out.shape[1]
    out[...] = kept[0:lines].reshape(out.shape)
    tables[...] = kept[lines : lines + 8]
    acc[...] = moments_of(layout, kept[lines + 8 :])


def more_kernel(layout, started, entries, acc):
    acc[...] = started[...] + moments_of(layout, entries[...])


def by_core(act):
    segment = lax.axis_index("segment")

    @pl.when(segment == 0)
    def _():
        act(0, lambda reach: slice(STEPS, STEPS + reach), lambda reach: slice(0, STEPS))

    @pl.when(segment == 1)
    def _():
        act(1, lambda reach: slice(0, reach), lambda reach: slice(reach, reach + STEPS))


def join_kernel(layout, *refs):
    cx, cz, cy = layout
    kept, got, started, entries, state, ids, times, edge, dense = refs
    reach = reach_of(cz)
    half = cx * cz // 2
    total = started[...] + moments_of(layout, entries[...])
    for c in range(6):
        for k in range(2):
            added = total[c * half : (c + 1) * half, k * cy : (k + 1) * cy]
            dense[c, k * half : (k + 1) * half] = added

    def join(mine, main, outer):
        main, outer = main(reach), outer(reach)
        first = 0 if mine == 0 else cz - reach
        last = main.start if mine == 0 else main.stop - STEPS
        gone = slice(last, last + STEPS)
        for x in range(cx):
            at = slice(x * reach, (x + 1) * reach)
            for model in range(2):
                rows = kept if model == mine else got
                state[model, :, x, main] = rows[0:9, at]
                ids[model, x, main] = rows[9, at]
            added = dense[:, x * cz + first : x * cz + first + reach]
            state[0, 3:9, x, main] = state[0, 3:9, x, main] + added
            times[x, main] = kept[10, at]
            state[:, :, x, outer] = jnp.zeros((2, 9, STEPS, cy), F32)
            ids[:, x, outer] = jnp.zeros((2, STEPS, cy), F32)
            times[x, outer] = jnp.zeros((STEPS, cy), F32)
            for k in range(21):
                line = slice((k * cx + x) * STEPS, (k * cx + x + 1) * STEPS)
                if k == 20:
                    edge[line] = times[x, gone]
                elif k % 10 == 9:
                    edge[line] = ids[k // 10, x, gone]
                else:
                    edge[line] = state[k // 10, k % 10, x, gone]

    by_core(join)


def by_parity(even, odd, act):
    parity = lax.axis_index("sec") % 2

    @pl.when(parity == 0)
    def _():
        act(*even)

    @pl.when(parity == 1)
    def _():
        act(*odd)


def advance(cx, steps, state, coef, times, given_top=False):
    planes, rows, cy = state.shape[2:]
    lane = lax.broadcasted_iota(jnp.int32, (rows, cy), 1)
    first_lane, last_lane = lane == 0, lane == cy - 1

    def back_y(f):
        return f - jnp.where(first_lane, F32(0.0), pltpu.roll(f, 1, 1))

    def back_z(f):
        return f - pltpu.roll(f, 1, 0)

    def fore_y(f):
        return jnp.where(last_lane, F32(0.0), pltpu.roll(f, cy - 1, 1)) - f

    def fore_z(f):
        return pltpu.roll(f, rows - 1, 0) - f

    def velocity(x):
        inc = [None, None]
        for model in range(2):
            sxx, syy, szz, syz, sxz, sxy = (state[model, 3 + k, x] for k in range(6))
            sxx_p, sxz_p, sxy_p = (state[model, k, x - 1] for k in (3, 7, 8))
            hb = coef[model, 0, x]
            inc[model] = (
                hb * ((sxx - sxx_p) + back_y(sxy) + back_z(sxz)),
                hb * ((sxy - sxy_p) + back_y(syy) + back_z(syz)),
                hb * ((sxz - sxz_p) + back_y(syz) + back_z(szz)),
            )
        for k in range(3):
            state[0, k, x] = state[0, k, x] + inc[0][k]
            state[1, k, x] = (state[1, k, x] + inc[1][k]) + times[x] * inc[0][k]

    for step in range(steps):
        left = steps - 1 - step
        low, high = cx - left, 2 * cx + left
        for x in range(low, high + 1 - (given_top and step == 0)):
            velocity(x)
        for x in range(low, high):
            for model in range(2):
                vx, vy, vz = (state[model, k, x] for k in range(3))
                vx_n, vy_n, vz_n = (state[model, k, x + 1] for k in range(3))
                hl, hm = coef[model, 1, x], coef[model, 2, x]
                exx, eyy, ezz = vx_n - vx, fore_y(vy), fore_z(vz)
                pressure = hl * (exx + eyy + ezz)
                twice = hm + hm
                state[model, 3, x] = state[model, 3, x] + (pressure + twice * exx)
                state[model, 4, x] = state[model, 4, x] + (pressure + twice * eyy)
                state[model, 5, x] = state[model, 5, x] + (pressure + twice * ezz)
                state[model, 6, x] = state[model, 6, x] + hm * (fore_z(vy) + fore_y(vz))
                state[model, 7, x] = state[model, 7, x] + hm * (fore_z(vx) + (vz_n - vz))
                state[model, 8, x] = state[model, 8, x] + hm * (fore_y(vx) + (vy_n - vy))

    return velocity


def look_up(tables, ids):
    lanes = ids.astype(jnp.int32)
    wide = [jnp.broadcast_to(tables[i : i + 1], ids.shape) for i in range(3)]
    return [jnp.take_along_axis(table, lanes, axis=1) for table in wide]


def edge_units(cx, with_ids):
    right, left = [], []
    for model in range(2):
        whole = list(range(10 if with_ids else 9)) + [10] * (with_ids and model == 1)
        for x in range(cx - 1):
            right += [(model, what, x + 1) for what in whole]
            left += [(model, what, x) for what in whole]
        right += [(model, what, 0) for what in (3, 7, 8)]
        left += [(model, what, cx - 1) for what in range(3)]
    return right, left


def cut_edges(cx, rows_of, with_ids, velocity, state, ids, times, to_first, to_second):
    right_units, left_units = edge_units(cx, with_ids)

    def put(to, units, far, right):
        line = slice(0, 0)
        for model, what, x in units:
            at = rows_of(x == far, right)
            line = slice(line.stop, line.stop + at.stop - at.start)
            if what == 10:
                to[line] = times[cx + x, at]
            elif what == 9:
                to[line] = ids[model, cx + x, at]
            else:
                to[line] = state[model, what, cx + x, at]

    holders = (to_second, to_first), (to_first, to_second)
    by_parity(*holders, lambda left, right: put(right, right_units, 0, True))
    velocity(2 * cx - 1)
    by_parity(*holders, lambda left, right: put(left, left_units, cx - 1, False))


def outer_rows(mine, outer):
    def rows_of(far, right):
        shift = 1 if far and not right and mine == 0 else 0
        return slice(outer.start + shift, outer.stop + shift)

    return rows_of


def reached_rows(cx, done, rows):
    def rows_of(far, right):
        first, last = done, rows - done
        if right:
            return slice(first + (cx if far else 1), last)
        return slice(first + far, last - (cx if far else 1))

    return rows_of


def coefficients(cx, planes, tables, ids, coef):
    for model in range(2):
        for x in planes:
            for i, found in enumerate(look_up(tables, ids[model, x])):
                coef[model, i, x] = found


def inner_kernel(cx, own_state, own_ids, own_times, tables, to_first, to_second, state, ids, coef, times):
    own = slice(cx, 2 * cx)
    reach = state.shape[3] - STEPS
    state[:, :, own], ids[:, own], times[own] = own_state[...], own_ids[...], own_times[...]
    coefficients(cx, range(2 * cx - 1, 2 * cx), tables, ids, coef)
    velocity = advance(cx, 0, state, coef, times)

    def cut(mine, main, outer):
        rows_of = lambda far, right: main(reach)
        cut_edges(cx, rows_of, True, velocity, state, ids, times, to_first, to_second)

    by_core(cut)


def outer_kernel(
    cx, own_state, own_ids, own_times, halo, tables,
    to_first, to_second, both, coef_out, times_out, state, ids, coef, times,
):
    own = slice(cx, 2 * cx)
    reach = state.shape[3] - STEPS
    state[:, :, own], ids[:, own], times[own] = own_state[...], own_ids[...], own_times[...]

    slab = lax.axis_index("depth")

    def join(mine, main, outer):
        inside = slab > 0 if mine == 0 else slab < lax.axis_size("depth") - 1
        inside = jnp.where(inside, F32(1.0), F32(0.0))
        for x in range(cx):
            for k in range(21):
                line = inside * halo[(k * cx + x) * STEPS : (k * cx + x + 1) * STEPS]
                if k == 20:
                    times[cx + x, outer(reach)] = line
                elif k % 10 == 9:
                    ids[k // 10, cx + x, outer(reach)] = line
                else:
                    state[k // 10, k % 10, cx + x, outer(reach)] = line

    by_core(join)
    coefficients(cx, range(cx, 2 * cx), tables, ids, coef)
    both[...] = state[:, :, own]
    coef_out[...] = coef[:, :, own]
    times_out[...] = times[own]
    velocity = advance(cx, 0, state, coef, times)

    def cut(mine, main, outer):
        rows_of = outer_rows(mine, outer(reach))
        cut_edges(cx, rows_of, True, velocity, state, ids, times, to_first, to_second)

    by_core(cut)


def next_kernel(cx, done, *refs):
    first = done == 0
    parts = 2 if first else 1
    both_in, coef_in, times_in = refs[0:3]
    edges, refs = refs[3 : 3 + 2 * parts], refs[3 + 2 * parts :]
    if first:
        tables, outs = refs[0], refs[1:]
        state, ids, coef, times = refs[-4:]
    else:
        ids, outs = None, refs
        state, coef, times = refs[-1], coef_in, times_in
    segment = lax.axis_index("segment")
    rows = state.shape[3]
    own = slice(cx, 2 * cx)
    state[:, :, own] = both_in[...]
    right_units, left_units = edge_units(cx, first)

    section = lax.axis_index("sec")
    has_left = jnp.where(section > 0, F32(1.0), F32(0.0))
    has_right = jnp.where(section < lax.axis_size("sec") - 1, F32(1.0), F32(0.0))

    def get(edge, units, start, rows_of, far, right):
        inside = has_left if right else has_right
        last = 0
        for model, what, x in units:
            at = rows_of(x == far, right)
            first, last = last, last + at.stop - at.start
            line = inside * edge[first:last]
            if what == 10:
                times[start + x, at] = line
            elif what == 9:
                ids[model, start + x, at] = line
            else:
                state[model, what, start + x, at] = line

    def place(rows_of, pair):
        def put(left, right):
            get(left, right_units, 0, rows_of, 0, True)
            get(right, left_units, 2 * cx, rows_of, cx - 1, False)

        by_parity((pair[1], pair[0]), pair, put)

    if first:

        def place_both(mine, main, outer):
            reach = rows - STEPS
            place(lambda far, right: main(reach), edges[0:2])
            place(outer_rows(mine, outer(reach)), edges[2:4])

        by_core(place_both)
        coef[:, :, own] = coef_in[...]
        times[own] = times_in[...]
        coefficients(cx, (*range(1, cx), *range(2 * cx, 3 * cx - 1)), tables, ids, coef)
    else:
        place(reached_rows(cx, done, rows), edges)
    velocity = advance(cx, cx, state, coef, times, given_top=True)
    if done + cx == STEPS:
        outs[0][...] = state[segment, :, own, STEPS : rows - STEPS]
        outs[1][...] = state[1 - segment, :, own, STEPS : rows - STEPS]
    else:
        outs[2][...] = state[:, :, own]
        if first:
            outs[3][...] = coef[...]
            outs[4][...] = times[...]
        rows_of = reached_rows(cx, done + cx, rows)
        cut_edges(cx, rows_of, False, velocity, state, None, times, outs[0], outs[1])


def home_kernel(mine, brought, out):
    half = mine.shape[2]
    segment = lax.axis_index("segment")

    @pl.when(segment == 0)
    def _():
        out[0, :, :, 0:half] = mine[...]
        out[0, :, :, half:] = brought[...]

    @pl.when(segment == 1)
    def _():
        out[0, :, :, half:] = mine[...]
        out[0, :, :, 0:half] = brought[...]


def swaps(start, count):
    route = {i: i for i in range(count)}
    for i in range(start, count - 1, 2):
        route[i], route[i + 1] = i + 1, i
    return list(route.items())


VMEM = pl.BlockSpec(memory_space=pltpu.VMEM)
HBM = pl.BlockSpec(memory_space=pltpu.HBM)


def call(kernel, name, in_vmem, in_hbm, outs, scratch, copies=0, limit=40 * 2**20, flops=10**7):
    sems = [pltpu.SemaphoreType.DMA((copies,))] * (copies > 0)
    return pl.pallas_call(
        kernel,
        out_shape=[jax.ShapeDtypeStruct(shape, F32) for shape in outs],
        in_specs=[VMEM] * len(in_vmem) + [HBM] * len(in_hbm),
        out_specs=[VMEM] * len(outs),
        scratch_shapes=[pltpu.VMEM(s, F32) if isinstance(s, tuple) else s for s in scratch] + sems,
        compiler_params=pltpu.CompilerParams(vmem_limit_bytes=limit),
        cost_estimate=pl.CostEstimate(flops=flops, bytes_accessed=2**20, transcendentals=0),
        name=name,
    )(*in_vmem, *in_hbm)


def on_device(
    fields, block_ids, buoyancy, lame_lambda, lame_mu, moments, moment_owner, moment_cells, drm_rows
):
    sections, slabs = lax.axis_size("sec"), lax.axis_size("depth")
    layout = cx, cz, cy = fields.shape[2:]
    reach, rows = reach_of(cz), cz // 2 + 2 * STEPS
    assert cx > 1 and STEPS % cx == 0

    def pairs(block, start):
        return lax.ppermute(block, "sec", swaps(start, sections))

    def other(section, k):
        return section ^ k if sections & (sections - 1) == 0 else (section + k) % sections

    def along_depth(block):
        return lax.ppermute(block, ("depth", "segment"), swaps(1, 2 * slabs))

    def swap(block):
        return lax.ppermute(block, "segment", [(0, 1), (1, 0)])

    owner = moment_owner.reshape(-1, cy)
    cells = moment_cells.reshape(-1, cy)
    arguments = (fields, block_ids, moments, owner, cells, drm_rows.reshape(-1, cy))
    entry_lines = 8 * cells.shape[0]
    entries, kept, given = call(
        pack_kernel,
        "pack",
        (),
        (*arguments, buoyancy, lame_lambda, lame_mu),
        [(entry_lines, cy), (11 * cx * reach + 8 + entry_lines, cy), (10, cx * reach, cy)],
        [pltpu.VMEM(a.shape, a.dtype) for a in arguments]
        + [(2, cx, cz, cy), pltpu.SMEM((3, buoyancy.shape[0]), F32)],
        len(arguments) + 3,
        limit=64 * 2**20,
    )
    blocks = [
        lax.ppermute(entries, "sec", [(other(i, k), i) for i in range(sections)])
        for k in (sections - 1, *range(1, sections - 1))
    ]
    got = swap(given)
    acc_shape = (6 * cx * cz // 2, 2 * cy)
    kept, tables, started = call(
        functools.partial(own_kernel, layout),
        "own_moments",
        (kept,),
        (),
        [(11, cx * reach, cy), (8, cy), acc_shape],
        [],
        flops=10**8,
    )
    for block in blocks[:-1]:
        (started,) = call(
            functools.partial(more_kernel, layout),
            "more_moments",
            (started, block),
            (),
            [acc_shape],
            [],
            flops=6 * 10**9,
        )
    own = (cx, rows, cy)
    window = (3 * cx, rows, cy)
    state, ids, times, edge = call(
        functools.partial(join_kernel, layout),
        "join_and_moments",
        (kept, got, started, blocks[-1]),
        (),
        [(2, 9, *own), (2, *own), own, (21 * cx * STEPS, cy)],
        [(6, cx * cz, cy)],
    )
    halo = along_depth(edge)
    work = [(2, 9, *window), (2, *window), (2, 3, *window), window]

    def edges(count, with_ids):
        return [(len(edge_units(cx, with_ids)[0]) * count, cy)] * 2

    def reached_edges(done):
        rows_of = reached_rows(cx, done, rows)
        whole, far = rows_of(False, True), rows_of(True, True)
        lines = 18 * (cx - 1) * (whole.stop - whole.start) + 6 * (far.stop - far.start)
        return [(-(-lines // 8) * 8, cy)] * 2

    def exchange(pair):
        return [pairs(pair[0], 0), pairs(pair[1], 1)]

    inner = call(
        functools.partial(inner_kernel, cx),
        "inner_edges",
        (state, ids, times, tables),
        (),
        edges(reach, True),
        work,
        flops=10**9,
    )
    got_edges = exchange(inner)
    *outer, both, coef, times = call(
        functools.partial(outer_kernel, cx),
        "outer_edges",
        (state, ids, times, halo, tables),
        (),
        edges(STEPS, True) + [(2, 9, *own), (2, 3, *own), own],
        work,
        flops=4 * 10**9,
    )
    got_edges += exchange(outer)
    for done in range(0, STEPS, cx):
        first, last = done == 0, done + cx == STEPS
        after = done + cx
        outs = [(9, cx, cz // 2, cy)] * 2
        if not last:
            outs = reached_edges(after) + [(2, 9, *own)]
            outs += [(2, 3, *window), window] * first
        pair = call(
            functools.partial(next_kernel, cx, done),
            "steps",
            (both, coef, times, *got_edges) + (tables,) * first,
            (),
            outs,
            work if first else work[0:1],
        )
        if not last:
            got_edges = exchange(pair[0:2])
            both = pair[2]
            if first:
                coef, times = pair[3:5]
    to_first, to_second = pair[0:2]
    (out,) = call(home_kernel, "home", (to_first, swap(to_second)), (), [fields.shape], [])
    return out


def solution(mesh):
    in_specs = (
        P("segment", None, "sec", "depth", None),
        P("segment", "sec", "depth", None),
        P(),
        P(),
        P(),
        P(None, ("sec", "depth")),
        P(("sec", "depth"), None),
        P(("sec", "depth")),
        P(("sec", "depth")),
    )
    out_specs = P("segment", None, "sec", "depth", None)
    return jax.shard_map(
        on_device, mesh=mesh, in_specs=in_specs, out_specs=out_specs, check_vma=False
    )
```

```python
import functools

import jax
import jax.numpy as jnp
from jax import lax
from jax.experimental import pallas as pl
from jax.experimental.pallas import tpu as pltpu
from jax.sharding import PartitionSpec as P

STEPS = 4
F32 = jnp.float32
BF16 = jnp.bfloat16
NT = (((1,), (1,)), ((), ()))


def one_hot(index, count):
    rows = lax.broadcasted_iota(jnp.int32, (count, index.shape[-1]), 0)
    return jnp.where(rows == index, F32(1.0), F32(0.0))


def split3(value):
    high = value.astype(BF16).astype(F32)
    rest = value - high
    mid = rest.astype(BF16).astype(F32)
    return high, mid, rest - mid


def copy_all(sem, pairs):
    copies = [pltpu.make_async_copy(a, b, sem.at[i]) for i, (a, b) in enumerate(pairs)]
    for copy in copies:
        copy.start()
    for copy in copies:
        copy.wait()


def in_line(rows):
    return jnp.concatenate([rows[i : i + 1, :] for i in range(rows.shape[0])], axis=1)


def reach_of(cz):
    return cz // 2 + STEPS


def pack_kernel(
    fields_in, ids_in, moments_in, owner_in, cells_in, rows_in, buoyancy, lame_lambda, lame_mu,
    entries, kept, given, fields, ids, moments, owner, cells, rows, wide, tables, sem,
):
    cx, cz, cy = ids.shape[1:]
    arguments = [(fields_in, fields), (ids_in, ids), (moments_in, moments), (owner_in, owner)]
    arguments += [(cells_in, cells), (rows_in, rows)]
    arguments += [(t, tables.at[i]) for i, t in enumerate((buoyancy, lame_lambda, lame_mu))]
    copy_all(sem, arguments)
    for i in range(cells.shape[0]):
        at = 8 * i
        entries[at : at + 6] = moments[:, i * cy : (i + 1) * cy]
        entries[at + 6 : at + 7] = owner[i : i + 1, :].astype(F32)
        entries[at + 7 : at + 8] = cells[i : i + 1, :].astype(F32)
    wide[0] = (ids[0] + 1).astype(F32)
    line = in_line(rows[...])
    high = one_hot(line // cy, cx * cz).astype(BF16)
    low = one_hot(line % cy, cy).astype(BF16)
    count = lax.dot_general(high, low, NT, preferred_element_type=F32)
    wide[1] = count.reshape(cx, cz, cy)
    reach = reach_of(cz)
    lines = 11 * cx * reach
    lane = lax.broadcasted_iota(jnp.int32, (1, cy), 1)
    for i in range(3):
        found = jnp.zeros((1, cy), F32)
        for entry in range(tables.shape[1]):
            found = jnp.where(lane == entry + 1, F32(0.5) * tables[i, entry], found)
        kept[lines + i : lines + i + 1] = found
    kept[lines + 3 : lines + 8] = jnp.zeros((5, cy), F32)
    kept[lines + 8 :] = entries[...]

    def cut(first, other):
        for x in range(cx):
            at = slice(x * reach, (x + 1) * reach)
            for k in range(11):
                source = fields.at[0, k] if k < 9 else wide.at[k - 9]
                line = (k * cx + x) * reach
                kept[line : line + reach] = source[x, first : first + reach]
            given[0:9, at] = fields[0, :, x, other : other + reach]
            given[9, at] = wide[0, x, other : other + reach]

    @pl.when(lax.axis_index("segment") == 0)
    def _():
        cut(0, cz - reach)

    @pl.when(lax.axis_index("segment") == 1)
    def _():
        cut(cz - reach, 0)


def moments_of(layout, entries):
    cx, cz, cy = layout
    section = lax.axis_index("sec")
    half = cx * cz // 2
    chunk = [entries[8 * i : 8 * i + 8] for i in range(entries.shape[0] // 8)]
    entry = jnp.concatenate(chunk, axis=1)
    owner = entry[6:7].astype(jnp.int32)
    cell = entry[7:8].astype(jnp.int32)
    line = jnp.where(owner == section, cell // cy, -1)
    upper = line >= half
    high = one_hot(jnp.where(upper, line - half, line), half)
    low = one_hot(jnp.where(upper, cell % cy + cy, cell % cy), 2 * cy).astype(BF16)
    parts = split3(entry[0:6])
    spread = [(high * part[c : c + 1]).astype(BF16) for part in parts for c in range(6)]
    spread = jnp.concatenate(spread, axis=0)
    got = lax.dot_general(spread, low, NT, preferred_element_type=F32)
    lines = 6 * half
    return got[0:lines] + got[lines : 2 * lines] + got[2 * lines :]


def own_kernel(layout, kept, out, tables, acc):
    lines = out.shape[0] * out.shape[1]
    out[...] = kept[0:lines].reshape(out.shape)
    tables[...] = kept[lines : lines + 8]
    acc[...] = moments_of(layout, kept[lines + 8 :])


def more_kernel(layout, started, entries, acc):
    acc[...] = started[...] + moments_of(layout, entries[...])


def by_core(act):
    segment = lax.axis_index("segment")

    @pl.when(segment == 0)
    def _():
        act(0, lambda reach: slice(STEPS, STEPS + reach), lambda reach: slice(0, STEPS))

    @pl.when(segment == 1)
    def _():
        act(1, lambda reach: slice(0, reach), lambda reach: slice(reach, reach + STEPS))


def join_kernel(layout, *refs):
    cx, cz, cy = layout
    kept, got, started, entries, state, ids, times, edge, dense = refs
    reach = reach_of(cz)
    half = cx * cz // 2
    total = started[...] + moments_of(layout, entries[...])
    for c in range(6):
        for k in range(2):
            added = total[c * half : (c + 1) * half, k * cy : (k + 1) * cy]
            dense[c, k * half : (k + 1) * half] = added

    def join(mine, main, outer):
        main, outer = main(reach), outer(reach)
        first = 0 if mine == 0 else cz - reach
        last = main.start if mine == 0 else main.stop - STEPS
        gone = slice(last, last + STEPS)
        for x in range(cx):
            at = slice(x * reach, (x + 1) * reach)
            for model in range(2):
                rows = kept if model == mine else got
                state[model, :, x, main] = rows[0:9, at]
                ids[model, x, main] = rows[9, at]
            added = dense[:, x * cz + first : x * cz + first + reach]
            state[0, 3:9, x, main] = state[0, 3:9, x, main] + added
            times[x, main] = kept[10, at]
            state[:, :, x, outer] = jnp.zeros((2, 9, STEPS, cy), F32)
            ids[:, x, outer] = jnp.zeros((2, STEPS, cy), F32)
            times[x, outer] = jnp.zeros((STEPS, cy), F32)
            for k in range(21):
                line = slice((k * cx + x) * STEPS, (k * cx + x + 1) * STEPS)
                if k == 20:
                    edge[line] = times[x, gone]
                elif k % 10 == 9:
                    edge[line] = ids[k // 10, x, gone]
                else:
                    edge[line] = state[k // 10, k % 10, x, gone]

    by_core(join)


def by_parity(even, odd, act):
    parity = lax.axis_index("sec") % 2

    @pl.when(parity == 0)
    def _():
        act(*even)

    @pl.when(parity == 1)
    def _():
        act(*odd)


def advance(cx, steps, state, coef, times, given_top=False):
    planes, rows, cy = state.shape[2:]
    lane = lax.broadcasted_iota(jnp.int32, (rows, cy), 1)
    first_lane, last_lane = lane == 0, lane == cy - 1

    def back_y(f):
        return f - jnp.where(first_lane, F32(0.0), pltpu.roll(f, 1, 1))

    def back_z(f):
        return f - pltpu.roll(f, 1, 0)

    def fore_y(f):
        return jnp.where(last_lane, F32(0.0), pltpu.roll(f, cy - 1, 1)) - f

    def fore_z(f):
        return pltpu.roll(f, rows - 1, 0) - f

    def velocity(x):
        inc = [None, None]
        for model in range(2):
            sxx, syy, szz, syz, sxz, sxy = (state[model, 3 + k, x] for k in range(6))
            sxx_p, sxz_p, sxy_p = (state[model, k, x - 1] for k in (3, 7, 8))
            hb = coef[model, 0, x]
            inc[model] = (
                hb * ((sxx - sxx_p) + back_y(sxy) + back_z(sxz)),
                hb * ((sxy - sxy_p) + back_y(syy) + back_z(syz)),
                hb * ((sxz - sxz_p) + back_y(syz) + back_z(szz)),
            )
        for k in range(3):
            state[0, k, x] = state[0, k, x] + inc[0][k]
            state[1, k, x] = (state[1, k, x] + inc[1][k]) + times[x] * inc[0][k]

    for step in range(steps):
        left = steps - 1 - step
        low, high = cx - left, 2 * cx + left
        for x in range(low, high + 1 - (given_top and step == 0)):
            velocity(x)
        for x in range(low, high):
            for model in range(2):
                vx, vy, vz = (state[model, k, x] for k in range(3))
                vx_n, vy_n, vz_n = (state[model, k, x + 1] for k in range(3))
                hl, hm = coef[model, 1, x], coef[model, 2, x]
                exx, eyy, ezz = vx_n - vx, fore_y(vy), fore_z(vz)
                pressure = hl * (exx + eyy + ezz)
                twice = hm + hm
                state[model, 3, x] = state[model, 3, x] + (pressure + twice * exx)
                state[model, 4, x] = state[model, 4, x] + (pressure + twice * eyy)
                state[model, 5, x] = state[model, 5, x] + (pressure + twice * ezz)
                state[model, 6, x] = state[model, 6, x] + hm * (fore_z(vy) + fore_y(vz))
                state[model, 7, x] = state[model, 7, x] + hm * (fore_z(vx) + (vz_n - vz))
                state[model, 8, x] = state[model, 8, x] + hm * (fore_y(vx) + (vy_n - vy))

    return velocity


def look_up(tables, ids):
    lanes = ids.astype(jnp.int32)
    wide = [jnp.broadcast_to(tables[i : i + 1], ids.shape) for i in range(3)]
    return [jnp.take_along_axis(table, lanes, axis=1) for table in wide]


def edge_units(cx, with_ids):
    right, left = [], []
    for model in range(2):
        whole = list(range(10 if with_ids else 9)) + [10] * (with_ids and model == 1)
        for x in range(cx - 1):
            right += [(model, what, x + 1) for what in whole]
            left += [(model, what, x) for what in whole]
        right += [(model, what, 0) for what in (3, 7, 8)]
        left += [(model, what, cx - 1) for what in range(3)]
    return right, left


def cut_edges(cx, rows_of, with_ids, velocity, state, ids, times, to_first, to_second):
    right_units, left_units = edge_units(cx, with_ids)

    def put(to, units, far, right):
        line = slice(0, 0)
        for model, what, x in units:
            at = rows_of(x == far, right)
            line = slice(line.stop, line.stop + at.stop - at.start)
            if what == 10:
                to[line] = times[cx + x, at]
            elif what == 9:
                to[line] = ids[model, cx + x, at]
            else:
                to[line] = state[model, what, cx + x, at]

    holders = (to_second, to_first), (to_first, to_second)
    by_parity(*holders, lambda left, right: put(right, right_units, 0, True))
    velocity(2 * cx - 1)
    by_parity(*holders, lambda left, right: put(left, left_units, cx - 1, False))


def outer_rows(mine, outer):
    def rows_of(far, right):
        shift = 1 if far and not right and mine == 0 else 0
        return slice(outer.start + shift, outer.stop + shift)

    return rows_of


def reached_rows(cx, done, rows):
    def rows_of(far, right):
        first, last = done, rows - done
        if right:
            return slice(first + (cx if far else 1), last)
        return slice(first + far, last - (cx if far else 1))

    return rows_of


def coefficients(cx, planes, tables, ids, coef):
    for model in range(2):
        for x in planes:
            for i, found in enumerate(look_up(tables, ids[model, x])):
                coef[model, i, x] = found


def inner_kernel(cx, own_state, own_ids, own_times, tables, to_first, to_second, state, ids, coef, times):
    own = slice(cx, 2 * cx)
    reach = state.shape[3] - STEPS
    state[:, :, own], ids[:, own], times[own] = own_state[...], own_ids[...], own_times[...]
    coefficients(cx, range(2 * cx - 1, 2 * cx), tables, ids, coef)
    velocity = advance(cx, 0, state, coef, times)

    def cut(mine, main, outer):
        rows_of = lambda far, right: main(reach)
        cut_edges(cx, rows_of, True, velocity, state, ids, times, to_first, to_second)

    by_core(cut)


def outer_kernel(
    cx, own_state, own_ids, own_times, halo, tables,
    to_first, to_second, both, coef_out, times_out, state, ids, coef, times,
):
    own = slice(cx, 2 * cx)
    reach = state.shape[3] - STEPS
    state[:, :, own], ids[:, own], times[own] = own_state[...], own_ids[...], own_times[...]

    slab = lax.axis_index("depth")

    def join(mine, main, outer):
        inside = slab > 0 if mine == 0 else slab < lax.axis_size("depth") - 1
        inside = jnp.where(inside, F32(1.0), F32(0.0))
        for x in range(cx):
            for k in range(21):
                line = inside * halo[(k * cx + x) * STEPS : (k * cx + x + 1) * STEPS]
                if k == 20:
                    times[cx + x, outer(reach)] = line
                elif k % 10 == 9:
                    ids[k // 10, cx + x, outer(reach)] = line
                else:
                    state[k // 10, k % 10, cx + x, outer(reach)] = line

    by_core(join)
    coefficients(cx, range(cx, 2 * cx), tables, ids, coef)
    both[...] = state[:, :, own]
    coef_out[...] = coef[:, :, own]
    times_out[...] = times[own]
    velocity = advance(cx, 0, state, coef, times)

    def cut(mine, main, outer):
        rows_of = outer_rows(mine, outer(reach))
        cut_edges(cx, rows_of, True, velocity, state, ids, times, to_first, to_second)

    by_core(cut)


def next_kernel(cx, done, *refs):
    first = done == 0
    parts = 2 if first else 1
    both_in, coef_in, times_in = refs[0:3]
    edges, refs = refs[3 : 3 + 2 * parts], refs[3 + 2 * parts :]
    if first:
        tables, outs = refs[0], refs[1:]
        state, ids, coef, times = refs[-4:]
    else:
        ids, outs = None, refs
        state, coef, times = refs[-1], coef_in, times_in
    segment = lax.axis_index("segment")
    rows = state.shape[3]
    own = slice(cx, 2 * cx)
    state[:, :, own] = both_in[...]
    right_units, left_units = edge_units(cx, first)

    section = lax.axis_index("sec")
    has_left = jnp.where(section > 0, F32(1.0), F32(0.0))
    has_right = jnp.where(section < lax.axis_size("sec") - 1, F32(1.0), F32(0.0))

    def get(edge, units, start, rows_of, far, right):
        inside = has_left if right else has_right
        last = 0
        for model, what, x in units:
            at = rows_of(x == far, right)
            first, last = last, last + at.stop - at.start
            line = inside * edge[first:last]
            if what == 10:
                times[start + x, at] = line
            elif what == 9:
                ids[model, start + x, at] = line
            else:
                state[model, what, start + x, at] = line

    def place(rows_of, pair):
        def put(left, right):
            get(left, right_units, 0, rows_of, 0, True)
            get(right, left_units, 2 * cx, rows_of, cx - 1, False)

        by_parity((pair[1], pair[0]), pair, put)

    if first:

        def place_both(mine, main, outer):
            reach = rows - STEPS
            place(lambda far, right: main(reach), edges[0:2])
            place(outer_rows(mine, outer(reach)), edges[2:4])

        by_core(place_both)
        coef[:, :, own] = coef_in[...]
        times[own] = times_in[...]
        coefficients(cx, (*range(1, cx), *range(2 * cx, 3 * cx - 1)), tables, ids, coef)
    else:
        place(reached_rows(cx, done, rows), edges)
    velocity = advance(cx, cx, state, coef, times, given_top=True)
    if done + cx == STEPS:
        outs[0][...] = state[segment, :, own, STEPS : rows - STEPS]
        outs[1][...] = state[1 - segment, :, own, STEPS : rows - STEPS]
    else:
        outs[2][...] = state[:, :, own]
        if first:
            outs[3][...] = coef[...]
            outs[4][...] = times[...]
        rows_of = reached_rows(cx, done + cx, rows)
        cut_edges(cx, rows_of, False, velocity, state, None, times, outs[0], outs[1])


def home_kernel(mine, brought, out):
    half = mine.shape[2]
    segment = lax.axis_index("segment")

    @pl.when(segment == 0)
    def _():
        out[0, :, :, 0:half] = mine[...]
        out[0, :, :, half:] = brought[...]

    @pl.when(segment == 1)
    def _():
        out[0, :, :, half:] = mine[...]
        out[0, :, :, 0:half] = brought[...]


def swaps(start, count):
    route = {i: i for i in range(count)}
    for i in range(start, count - 1, 2):
        route[i], route[i + 1] = i + 1, i
    return list(route.items())


VMEM = pl.BlockSpec(memory_space=pltpu.VMEM)
HBM = pl.BlockSpec(memory_space=pltpu.HBM)


def call(kernel, name, in_vmem, in_hbm, outs, scratch, copies=0, limit=40 * 2**20, flops=10**7):
    sems = [pltpu.SemaphoreType.DMA((copies,))] * (copies > 0)
    return pl.pallas_call(
        kernel,
        out_shape=[jax.ShapeDtypeStruct(shape, F32) for shape in outs],
        in_specs=[VMEM] * len(in_vmem) + [HBM] * len(in_hbm),
        out_specs=[VMEM] * len(outs),
        scratch_shapes=[pltpu.VMEM(s, F32) if isinstance(s, tuple) else s for s in scratch] + sems,
        compiler_params=pltpu.CompilerParams(vmem_limit_bytes=limit),
        cost_estimate=pl.CostEstimate(flops=flops, bytes_accessed=2**20, transcendentals=0),
        name=name,
    )(*in_vmem, *in_hbm)


def on_device(
    fields, block_ids, buoyancy, lame_lambda, lame_mu, moments, moment_owner, moment_cells, drm_rows
):
    sections, slabs = lax.axis_size("sec"), lax.axis_size("depth")
    layout = cx, cz, cy = fields.shape[2:]
    reach, rows = reach_of(cz), cz // 2 + 2 * STEPS
    assert cx > 1 and STEPS % cx == 0

    def pairs(block, start):
        route = []
        for i, j in swaps(start, sections):
            route += [(2 * i + k, 2 * j + (k if i != j else 1 - k)) for k in range(2)]
        return lax.ppermute(block, ("sec", "segment"), route)

    def other(section, k):
        return section ^ k if sections & (sections - 1) == 0 else (section + k) % sections

    def along_depth(block):
        ends = [(0, 2 * slabs - 1), (2 * slabs - 1, 0)]
        route = [(i, j) for i, j in swaps(1, 2 * slabs) if i != j] + ends
        return lax.ppermute(block, ("depth", "segment"), route)

    def swap(block):
        return lax.ppermute(block, "segment", [(0, 1), (1, 0)])

    owner = moment_owner.reshape(-1, cy)
    cells = moment_cells.reshape(-1, cy)
    arguments = (fields, block_ids, moments, owner, cells, drm_rows.reshape(-1, cy))
    entry_lines = 8 * cells.shape[0]
    entries, kept, given = call(
        pack_kernel,
        "pack",
        (),
        (*arguments, buoyancy, lame_lambda, lame_mu),
        [(entry_lines, cy), (11 * cx * reach + 8 + entry_lines, cy), (10, cx * reach, cy)],
        [pltpu.VMEM(a.shape, a.dtype) for a in arguments]
        + [(2, cx, cz, cy), pltpu.SMEM((3, buoyancy.shape[0]), F32)],
        len(arguments) + 3,
        limit=64 * 2**20,
    )
    blocks = [
        lax.ppermute(entries, "sec", [(other(i, k), i) for i in range(sections)])
        for k in (sections - 1, *range(1, sections - 1))
    ]
    got = swap(given)
    acc_shape = (6 * cx * cz // 2, 2 * cy)
    kept, tables, started = call(
        functools.partial(own_kernel, layout),
        "own_moments",
        (kept,),
        (),
        [(11, cx * reach, cy), (8, cy), acc_shape],
        [],
        flops=10**8,
    )
    for block in blocks[:-1]:
        (started,) = call(
            functools.partial(more_kernel, layout),
            "more_moments",
            (started, block),
            (),
            [acc_shape],
            [],
            flops=6 * 10**9,
        )
    own = (cx, rows, cy)
    window = (3 * cx, rows, cy)
    state, ids, times, edge = call(
        functools.partial(join_kernel, layout),
        "join_and_moments",
        (kept, got, started, blocks[-1]),
        (),
        [(2, 9, *own), (2, *own), own, (21 * cx * STEPS, cy)],
        [(6, cx * cz, cy)],
    )
    halo = along_depth(edge)
    work = [(2, 9, *window), (2, *window), (2, 3, *window), window]

    def edges(count, with_ids):
        return [(len(edge_units(cx, with_ids)[0]) * count, cy)] * 2

    def reached_edges(done):
        rows_of = reached_rows(cx, done, rows)
        whole, far = rows_of(False, True), rows_of(True, True)
        lines = 18 * (cx - 1) * (whole.stop - whole.start) + 6 * (far.stop - far.start)
        return [(-(-lines // 8) * 8, cy)] * 2

    def exchange(pair):
        return [pairs(pair[0], 0), pairs(pair[1], 1)]

    inner = call(
        functools.partial(inner_kernel, cx),
        "inner_edges",
        (state, ids, times, tables),
        (),
        edges(reach, True),
        work,
        flops=10**9,
    )
    got_edges = exchange(inner)
    *outer, both, coef, times = call(
        functools.partial(outer_kernel, cx),
        "outer_edges",
        (state, ids, times, halo, tables),
        (),
        edges(STEPS, True) + [(2, 9, *own), (2, 3, *own), own],
        work,
        flops=4 * 10**9,
    )
    got_edges += exchange(outer)
    for done in range(0, STEPS, cx):
        first, last = done == 0, done + cx == STEPS
        after = done + cx
        outs = [(9, cx, cz // 2, cy)] * 2
        if not last:
            outs = reached_edges(after) + [(2, 9, *own)]
            outs += [(2, 3, *window), window] * first
        pair = call(
            functools.partial(next_kernel, cx, done),
            "steps",
            (both, coef, times, *got_edges) + (tables,) * first,
            (),
            outs,
            work if first else work[0:1],
        )
        if not last:
            got_edges = exchange(pair[0:2])
            both = pair[2]
            if first:
                coef, times = pair[3:5]
    to_first, to_second = pair[0:2]
    (out,) = call(home_kernel, "home", (to_first, swap(to_second)), (), [fields.shape], [])
    return out


def solution(mesh):
    in_specs = (
        P("segment", None, "sec", "depth", None),
        P("segment", "sec", "depth", None),
        P(),
        P(),
        P(),
        P(None, ("sec", "depth")),
        P(("sec", "depth"), None),
        P(("sec", "depth")),
        P(("sec", "depth")),
    )
    out_specs = P("segment", None, "sec", "depth", None)
    return jax.shard_map(
        on_device, mesh=mesh, in_specs=in_specs, out_specs=out_specs, check_vma=False
    )
```

```python
import functools

import jax
import jax.numpy as jnp
from jax import lax
from jax.experimental import pallas as pl
from jax.experimental.pallas import tpu as pltpu
from jax.sharding import PartitionSpec as P

STEPS = 4
F32 = jnp.float32
BF16 = jnp.bfloat16
NT = (((1,), (1,)), ((), ()))


def one_hot(index, count):
    rows = lax.broadcasted_iota(jnp.int32, (count, index.shape[-1]), 0)
    return jnp.where(rows == index, F32(1.0), F32(0.0))


def split3(value):
    high = value.astype(BF16).astype(F32)
    rest = value - high
    mid = rest.astype(BF16).astype(F32)
    return high, mid, rest - mid


def copy_all(sem, pairs):
    copies = [pltpu.make_async_copy(a, b, sem.at[i]) for i, (a, b) in enumerate(pairs)]
    for copy in copies:
        copy.start()
    for copy in copies:
        copy.wait()


def in_line(rows):
    return jnp.concatenate([rows[i : i + 1, :] for i in range(rows.shape[0])], axis=1)


def reach_of(cz):
    return cz // 2 + STEPS


def pack_kernel(
    fields_in, ids_in, moments_in, owner_in, cells_in, rows_in, buoyancy, lame_lambda, lame_mu,
    entries, kept, given, fields, ids, moments, owner, cells, rows, wide, tables, sem,
):
    cx, cz, cy = ids.shape[1:]
    arguments = [(fields_in, fields), (ids_in, ids), (moments_in, moments), (owner_in, owner)]
    arguments += [(cells_in, cells), (rows_in, rows)]
    arguments += [(t, tables.at[i]) for i, t in enumerate((buoyancy, lame_lambda, lame_mu))]
    copy_all(sem, arguments)
    for i in range(cells.shape[0]):
        at = 8 * i
        entries[at : at + 6] = moments[:, i * cy : (i + 1) * cy]
        entries[at + 6 : at + 7] = owner[i : i + 1, :].astype(F32)
        entries[at + 7 : at + 8] = cells[i : i + 1, :].astype(F32)
    wide[0] = (ids[0] + 1).astype(F32)
    line = in_line(rows[...])
    high = one_hot(line // cy, cx * cz).astype(BF16)
    low = one_hot(line % cy, cy).astype(BF16)
    count = lax.dot_general(high, low, NT, preferred_element_type=F32)
    wide[1] = count.reshape(cx, cz, cy)
    reach = reach_of(cz)
    lines = 11 * cx * reach
    lane = lax.broadcasted_iota(jnp.int32, (1, cy), 1)
    for i in range(3):
        found = jnp.zeros((1, cy), F32)
        for entry in range(tables.shape[1]):
            found = jnp.where(lane == entry + 1, F32(0.5) * tables[i, entry], found)
        kept[lines + i : lines + i + 1] = found
    kept[lines + 3 : lines + 8] = jnp.zeros((5, cy), F32)
    kept[lines + 8 :] = entries[...]

    def cut(first, other):
        for x in range(cx):
            at = slice(x * reach, (x + 1) * reach)
            for k in range(11):
                source = fields.at[0, k] if k < 9 else wide.at[k - 9]
                line = (k * cx + x) * reach
                kept[line : line + reach] = source[x, first : first + reach]
            given[0:9, at] = fields[0, :, x, other : other + reach]
            given[9, at] = wide[0, x, other : other + reach]

    @pl.when(lax.axis_index("segment") == 0)
    def _():
        cut(0, cz - reach)

    @pl.when(lax.axis_index("segment") == 1)
    def _():
        cut(cz - reach, 0)


def moments_of(layout, entries):
    cx, cz, cy = layout
    section = lax.axis_index("sec")
    half = cx * cz // 2
    chunk = [entries[8 * i : 8 * i + 8] for i in range(entries.shape[0] // 8)]
    entry = jnp.concatenate(chunk, axis=1)
    owner = entry[6:7].astype(jnp.int32)
    cell = entry[7:8].astype(jnp.int32)
    line = jnp.where(owner == section, cell // cy, -1)
    upper = line >= half
    high = one_hot(jnp.where(upper, line - half, line), half)
    low = one_hot(jnp.where(upper, cell % cy + cy, cell % cy), 2 * cy).astype(BF16)
    parts = split3(entry[0:6])
    spread = [(high * part[c : c + 1]).astype(BF16) for part in parts for c in range(6)]
    spread = jnp.concatenate(spread, axis=0)
    got = lax.dot_general(spread, low, NT, preferred_element_type=F32)
    lines = 6 * half
    return got[0:lines] + got[lines : 2 * lines] + got[2 * lines :]


def own_kernel(layout, kept, out, tables, acc):
    lines = out.shape[0] * out.shape[1]
    out[...] = kept[0:lines].reshape(out.shape)
    tables[...] = kept[lines : lines + 8]
    acc[...] = moments_of(layout, kept[lines + 8 :])


def more_kernel(layout, started, entries, acc):
    acc[...] = started[...] + moments_of(layout, entries[...])


def by_core(act):
    segment = lax.axis_index("segment")

    @pl.when(segment == 0)
    def _():
        act(0, lambda reach: slice(STEPS, STEPS + reach), lambda reach: slice(0, STEPS))

    @pl.when(segment == 1)
    def _():
        act(1, lambda reach: slice(0, reach), lambda reach: slice(reach, reach + STEPS))


def join_kernel(layout, *refs):
    cx, cz, cy = layout
    kept, got, started, entries, state, ids, times, edge, dense = refs
    reach = reach_of(cz)
    half = cx * cz // 2
    total = started[...] + moments_of(layout, entries[...])
    for c in range(6):
        for k in range(2):
            added = total[c * half : (c + 1) * half, k * cy : (k + 1) * cy]
            dense[c, k * half : (k + 1) * half] = added

    def join(mine, main, outer):
        main, outer = main(reach), outer(reach)
        first = 0 if mine == 0 else cz - reach
        last = main.start if mine == 0 else main.stop - STEPS
        gone = slice(last, last + STEPS)
        for x in range(cx):
            at = slice(x * reach, (x + 1) * reach)
            for model in range(2):
                rows = kept if model == mine else got
                state[model, :, x, main] = rows[0:9, at]
                ids[model, x, main] = rows[9, at]
            added = dense[:, x * cz + first : x * cz + first + reach]
            state[0, 3:9, x, main] = state[0, 3:9, x, main] + added
            times[x, main] = kept[10, at]
            state[:, :, x, outer] = jnp.zeros((2, 9, STEPS, cy), F32)
            ids[:, x, outer] = jnp.zeros((2, STEPS, cy), F32)
            times[x, outer] = jnp.zeros((STEPS, cy), F32)
            for k in range(21):
                line = slice((k * cx + x) * STEPS, (k * cx + x + 1) * STEPS)
                if k == 20:
                    edge[line] = times[x, gone]
                elif k % 10 == 9:
                    edge[line] = ids[k // 10, x, gone]
                else:
                    edge[line] = state[k // 10, k % 10, x, gone]

    by_core(join)


def by_parity(even, odd, act):
    parity = lax.axis_index("sec") % 2

    @pl.when(parity == 0)
    def _():
        act(*even)

    @pl.when(parity == 1)
    def _():
        act(*odd)


def advance(cx, steps, state, coef, times, given_top=False):
    planes, rows, cy = state.shape[2:]
    lane = lax.broadcasted_iota(jnp.int32, (rows, cy), 1)
    first_lane, last_lane = lane == 0, lane == cy - 1

    def back_y(f):
        return f - jnp.where(first_lane, F32(0.0), pltpu.roll(f, 1, 1))

    def back_z(f):
        return f - pltpu.roll(f, 1, 0)

    def fore_y(f):
        return jnp.where(last_lane, F32(0.0), pltpu.roll(f, cy - 1, 1)) - f

    def fore_z(f):
        return pltpu.roll(f, rows - 1, 0) - f

    def velocity(x):
        inc = [None, None]
        for model in range(2):
            sxx, syy, szz, syz, sxz, sxy = (state[model, 3 + k, x] for k in range(6))
            sxx_p, sxz_p, sxy_p = (state[model, k, x - 1] for k in (3, 7, 8))
            hb = coef[model, 0, x]
            inc[model] = (
                hb * ((sxx - sxx_p) + back_y(sxy) + back_z(sxz)),
                hb * ((sxy - sxy_p) + back_y(syy) + back_z(syz)),
                hb * ((sxz - sxz_p) + back_y(syz) + back_z(szz)),
            )
        for k in range(3):
            state[0, k, x] = state[0, k, x] + inc[0][k]
            state[1, k, x] = (state[1, k, x] + inc[1][k]) + times[x] * inc[0][k]

    for step in range(steps):
        left = steps - 1 - step
        low, high = cx - left, 2 * cx + left
        for x in range(low, high + 1 - (given_top and step == 0)):
            velocity(x)
        for x in range(low, high):
            for model in range(2):
                vx, vy, vz = (state[model, k, x] for k in range(3))
                vx_n, vy_n, vz_n = (state[model, k, x + 1] for k in range(3))
                hl, hm = coef[model, 1, x], coef[model, 2, x]
                exx, eyy, ezz = vx_n - vx, fore_y(vy), fore_z(vz)
                pressure = hl * (exx + eyy + ezz)
                twice = hm + hm
                state[model, 3, x] = state[model, 3, x] + (pressure + twice * exx)
                state[model, 4, x] = state[model, 4, x] + (pressure + twice * eyy)
                state[model, 5, x] = state[model, 5, x] + (pressure + twice * ezz)
                state[model, 6, x] = state[model, 6, x] + hm * (fore_z(vy) + fore_y(vz))
                state[model, 7, x] = state[model, 7, x] + hm * (fore_z(vx) + (vz_n - vz))
                state[model, 8, x] = state[model, 8, x] + hm * (fore_y(vx) + (vy_n - vy))

    return velocity


def look_up(tables, ids):
    lanes = ids.astype(jnp.int32)
    wide = [jnp.broadcast_to(tables[i : i + 1], ids.shape) for i in range(3)]
    return [jnp.take_along_axis(table, lanes, axis=1) for table in wide]


def edge_units(cx, with_ids):
    right, left = [], []
    for model in range(2):
        whole = list(range(10 if with_ids else 9)) + [10] * (with_ids and model == 1)
        for x in range(cx - 1):
            right += [(model, what, x + 1) for what in whole]
            left += [(model, what, x) for what in whole]
        right += [(model, what, 0) for what in (3, 7, 8)]
        left += [(model, what, cx - 1) for what in range(3)]
    return right, left


def cut_edges(cx, rows_of, with_ids, velocity, state, ids, times, to_first, to_second):
    right_units, left_units = edge_units(cx, with_ids)

    def put(to, units, far, right):
        line = slice(0, 0)
        for model, what, x in units:
            at = rows_of(x == far, right)
            line = slice(line.stop, line.stop + at.stop - at.start)
            if what == 10:
                to[line] = times[cx + x, at]
            elif what == 9:
                to[line] = ids[model, cx + x, at]
            else:
                to[line] = state[model, what, cx + x, at]

    holders = (to_second, to_first), (to_first, to_second)
    by_parity(*holders, lambda left, right: put(right, right_units, 0, True))
    velocity(2 * cx - 1)
    by_parity(*holders, lambda left, right: put(left, left_units, cx - 1, False))


def outer_rows(mine, outer):
    def rows_of(far, right):
        shift = 1 if far and not right and mine == 0 else 0
        return slice(outer.start + shift, outer.stop + shift)

    return rows_of


def reached_rows(cx, done, rows):
    def rows_of(far, right):
        first, last = done, rows - done
        if right:
            return slice(first + (cx if far else 1), last)
        return slice(first + far, last - (cx if far else 1))

    return rows_of


def coefficients(cx, planes, tables, ids, coef):
    for model in range(2):
        for x in planes:
            for i, found in enumerate(look_up(tables, ids[model, x])):
                coef[model, i, x] = found


def inner_kernel(cx, own_state, own_ids, own_times, tables, to_first, to_second, state, ids, coef, times):
    own = slice(cx, 2 * cx)
    reach = state.shape[3] - STEPS
    state[:, :, own], ids[:, own], times[own] = own_state[...], own_ids[...], own_times[...]
    coefficients(cx, range(2 * cx - 1, 2 * cx), tables, ids, coef)
    velocity = advance(cx, 0, state, coef, times)

    def cut(mine, main, outer):
        rows_of = lambda far, right: main(reach)
        cut_edges(cx, rows_of, True, velocity, state, ids, times, to_first, to_second)

    by_core(cut)


def outer_kernel(
    cx, own_state, own_ids, own_times, halo, tables,
    to_first, to_second, both, coef_out, times_out, state, ids, coef, times,
):
    own = slice(cx, 2 * cx)
    reach = state.shape[3] - STEPS
    state[:, :, own], ids[:, own], times[own] = own_state[...], own_ids[...], own_times[...]

    slab = lax.axis_index("depth")

    def join(mine, main, outer):
        inside = slab > 0 if mine == 0 else slab < lax.axis_size("depth") - 1
        inside = jnp.where(inside, F32(1.0), F32(0.0))
        for x in range(cx):
            for k in range(21):
                line = inside * halo[(k * cx + x) * STEPS : (k * cx + x + 1) * STEPS]
                if k == 20:
                    times[cx + x, outer(reach)] = line
                elif k % 10 == 9:
                    ids[k // 10, cx + x, outer(reach)] = line
                else:
                    state[k // 10, k % 10, cx + x, outer(reach)] = line

    by_core(join)
    coefficients(cx, range(cx, 2 * cx), tables, ids, coef)
    both[...] = state[:, :, own]
    coef_out[...] = coef[:, :, own]
    times_out[...] = times[own]
    velocity = advance(cx, 0, state, coef, times)

    def cut(mine, main, outer):
        rows_of = outer_rows(mine, outer(reach))
        cut_edges(cx, rows_of, True, velocity, state, ids, times, to_first, to_second)

    by_core(cut)


def next_kernel(cx, done, *refs):
    first = done == 0
    parts = 2 if first else 1
    both_in, coef_in, times_in = refs[0:3]
    edges, refs = refs[3 : 3 + 2 * parts], refs[3 + 2 * parts :]
    if first:
        tables, outs = refs[0], refs[1:]
        state, ids, coef, times = refs[-4:]
    else:
        ids, outs = None, refs
        state, coef, times = refs[-1], coef_in, times_in
    segment = lax.axis_index("segment")
    rows = state.shape[3]
    own = slice(cx, 2 * cx)
    state[:, :, own] = both_in[...]
    right_units, left_units = edge_units(cx, first)

    section = lax.axis_index("sec")
    has_left = jnp.where(section > 0, F32(1.0), F32(0.0))
    has_right = jnp.where(section < lax.axis_size("sec") - 1, F32(1.0), F32(0.0))

    def get(edge, units, start, rows_of, far, right):
        inside = has_left if right else has_right
        last = 0
        for model, what, x in units:
            at = rows_of(x == far, right)
            first, last = last, last + at.stop - at.start
            line = inside * edge[first:last]
            if what == 10:
                times[start + x, at] = line
            elif what == 9:
                ids[model, start + x, at] = line
            else:
                state[model, what, start + x, at] = line

    def place(rows_of, pair):
        def put(left, right):
            get(left, right_units, 0, rows_of, 0, True)
            get(right, left_units, 2 * cx, rows_of, cx - 1, False)

        by_parity((pair[1], pair[0]), pair, put)

    if first:

        def place_both(mine, main, outer):
            reach = rows - STEPS
            place(lambda far, right: main(reach), edges[0:2])
            place(outer_rows(mine, outer(reach)), edges[2:4])

        by_core(place_both)
        coef[:, :, own] = coef_in[...]
        times[own] = times_in[...]
        coefficients(cx, (*range(1, cx), *range(2 * cx, 3 * cx - 1)), tables, ids, coef)
    else:
        place(reached_rows(cx, done, rows), edges)
    velocity = advance(cx, cx, state, coef, times, given_top=True)
    if done + cx == STEPS:
        outs[0][...] = state[segment, :, own, STEPS : rows - STEPS]
        outs[1][...] = state[1 - segment, :, own, STEPS : rows - STEPS]
    else:
        outs[2][...] = state[:, :, own]
        if first:
            outs[3][...] = coef[...]
            outs[4][...] = times[...]
        rows_of = reached_rows(cx, done + cx, rows)
        cut_edges(cx, rows_of, False, velocity, state, None, times, outs[0], outs[1])


def home_kernel(mine, brought, out):
    half = mine.shape[2]
    segment = lax.axis_index("segment")

    @pl.when(segment == 0)
    def _():
        out[0, :, :, 0:half] = mine[...]
        out[0, :, :, half:] = brought[...]

    @pl.when(segment == 1)
    def _():
        out[0, :, :, half:] = mine[...]
        out[0, :, :, 0:half] = brought[...]


def swaps(start, count):
    route = {i: i for i in range(count)}
    for i in range(start, count - 1, 2):
        route[i], route[i + 1] = i + 1, i
    return list(route.items())


VMEM = pl.BlockSpec(memory_space=pltpu.VMEM)
HBM = pl.BlockSpec(memory_space=pltpu.HBM)


def call(kernel, name, in_vmem, in_hbm, outs, scratch, copies=0, limit=40 * 2**20, flops=10**7):
    sems = [pltpu.SemaphoreType.DMA((copies,))] * (copies > 0)
    return pl.pallas_call(
        kernel,
        out_shape=[jax.ShapeDtypeStruct(shape, F32) for shape in outs],
        in_specs=[VMEM] * len(in_vmem) + [HBM] * len(in_hbm),
        out_specs=[VMEM] * len(outs),
        scratch_shapes=[pltpu.VMEM(s, F32) if isinstance(s, tuple) else s for s in scratch] + sems,
        compiler_params=pltpu.CompilerParams(vmem_limit_bytes=limit),
        cost_estimate=pl.CostEstimate(flops=flops, bytes_accessed=2**20, transcendentals=0),
        name=name,
    )(*in_vmem, *in_hbm)


def on_device(
    fields, block_ids, buoyancy, lame_lambda, lame_mu, moments, moment_owner, moment_cells, drm_rows
):
    sections, slabs = lax.axis_size("sec"), lax.axis_size("depth")
    layout = cx, cz, cy = fields.shape[2:]
    reach, rows = reach_of(cz), cz // 2 + 2 * STEPS
    assert cx > 1 and STEPS % cx == 0

    def pairs(block, start):
        route = []
        for i, j in swaps(start, sections):
            route += [(2 * i + k, 2 * j + (k if i != j else 1 - k)) for k in range(2)]
        return lax.ppermute(block, ("sec", "segment"), route)

    def other(section, k):
        return section ^ k if sections & (sections - 1) == 0 else (section + k) % sections

    def along_depth(block):
        line = 2 * slabs
        route = []
        for s, partner in swaps(0, sections):
            route += [(s * line + i, (s if i != j else partner) * line + j) for i, j in swaps(1, line)]
        return lax.ppermute(block, ("sec", "depth", "segment"), route)

    def swap(block):
        return lax.ppermute(block, "segment", [(0, 1), (1, 0)])

    owner = moment_owner.reshape(-1, cy)
    cells = moment_cells.reshape(-1, cy)
    arguments = (fields, block_ids, moments, owner, cells, drm_rows.reshape(-1, cy))
    entry_lines = 8 * cells.shape[0]
    entries, kept, given = call(
        pack_kernel,
        "pack",
        (),
        (*arguments, buoyancy, lame_lambda, lame_mu),
        [(entry_lines, cy), (11 * cx * reach + 8 + entry_lines, cy), (10, cx * reach, cy)],
        [pltpu.VMEM(a.shape, a.dtype) for a in arguments]
        + [(2, cx, cz, cy), pltpu.SMEM((3, buoyancy.shape[0]), F32)],
        len(arguments) + 3,
        limit=64 * 2**20,
    )
    blocks = [
        lax.ppermute(entries, "sec", [(other(i, k), i) for i in range(sections)])
        for k in (sections - 1, *range(1, sections - 1))
    ]
    got = swap(given)
    acc_shape = (6 * cx * cz // 2, 2 * cy)
    kept, tables, started = call(
        functools.partial(own_kernel, layout),
        "own_moments",
        (kept,),
        (),
        [(11, cx * reach, cy), (8, cy), acc_shape],
        [],
        flops=10**8,
    )
    for block in blocks[:-1]:
        (started,) = call(
            functools.partial(more_kernel, layout),
            "more_moments",
            (started, block),
            (),
            [acc_shape],
            [],
            flops=6 * 10**9,
        )
    own = (cx, rows, cy)
    window = (3 * cx, rows, cy)
    state, ids, times, edge = call(
        functools.partial(join_kernel, layout),
        "join_and_moments",
        (kept, got, started, blocks[-1]),
        (),
        [(2, 9, *own), (2, *own), own, (21 * cx * STEPS, cy)],
        [(6, cx * cz, cy)],
    )
    halo = along_depth(edge)
    work = [(2, 9, *window), (2, *window), (2, 3, *window), window]

    def edges(count, with_ids):
        return [(len(edge_units(cx, with_ids)[0]) * count, cy)] * 2

    def reached_edges(done):
        rows_of = reached_rows(cx, done, rows)
        whole, far = rows_of(False, True), rows_of(True, True)
        lines = 18 * (cx - 1) * (whole.stop - whole.start) + 6 * (far.stop - far.start)
        return [(-(-lines // 8) * 8, cy)] * 2

    def exchange(pair):
        return [pairs(pair[0], 0), pairs(pair[1], 1)]

    inner = call(
        functools.partial(inner_kernel, cx),
        "inner_edges",
        (state, ids, times, tables),
        (),
        edges(reach, True),
        work,
        flops=10**9,
    )
    got_edges = exchange(inner)
    *outer, both, coef, times = call(
        functools.partial(outer_kernel, cx),
        "outer_edges",
        (state, ids, times, halo, tables),
        (),
        edges(STEPS, True) + [(2, 9, *own), (2, 3, *own), own],
        work,
        flops=4 * 10**9,
    )
    got_edges += exchange(outer)
    for done in range(0, STEPS, cx):
        first, last = done == 0, done + cx == STEPS
        after = done + cx
        outs = [(9, cx, cz // 2, cy)] * 2
        if not last:
            outs = reached_edges(after) + [(2, 9, *own)]
            outs += [(2, 3, *window), window] * first
        pair = call(
            functools.partial(next_kernel, cx, done),
            "steps",
            (both, coef, times, *got_edges) + (tables,) * first,
            (),
            outs,
            work if first else work[0:1],
        )
        if not last:
            got_edges = exchange(pair[0:2])
            both = pair[2]
            if first:
                coef, times = pair[3:5]
    to_first, to_second = pair[0:2]
    (out,) = call(home_kernel, "home", (to_first, swap(to_second)), (), [fields.shape], [])
    return out


def solution(mesh):
    in_specs = (
        P("segment", None, "sec", "depth", None),
        P("segment", "sec", "depth", None),
        P(),
        P(),
        P(),
        P(None, ("sec", "depth")),
        P(("sec", "depth"), None),
        P(("sec", "depth")),
        P(("sec", "depth")),
    )
    out_specs = P("segment", None, "sec", "depth", None)
    return jax.shard_map(
        on_device, mesh=mesh, in_specs=in_specs, out_specs=out_specs, check_vma=False
    )
```

```python
import functools

import jax
import jax.numpy as jnp
from jax import lax
from jax.experimental import pallas as pl
from jax.experimental.pallas import tpu as pltpu
from jax.sharding import PartitionSpec as P

STEPS = 4
F32 = jnp.float32
BF16 = jnp.bfloat16
NT = (((1,), (1,)), ((), ()))


def one_hot(index, count):
    rows = lax.broadcasted_iota(jnp.int32, (count, index.shape[-1]), 0)
    return jnp.where(rows == index, F32(1.0), F32(0.0))


def split3(value):
    high = value.astype(BF16).astype(F32)
    rest = value - high
    mid = rest.astype(BF16).astype(F32)
    return high, mid, rest - mid


def copy_all(sem, pairs):
    copies = [pltpu.make_async_copy(a, b, sem.at[i]) for i, (a, b) in enumerate(pairs)]
    for copy in copies:
        copy.start()
    for copy in copies:
        copy.wait()


def in_line(rows):
    return jnp.concatenate([rows[i : i + 1, :] for i in range(rows.shape[0])], axis=1)


def reach_of(cz):
    return cz // 2 + STEPS


def pack_kernel(
    fields_in, ids_in, moments_in, owner_in, cells_in, rows_in, buoyancy, lame_lambda, lame_mu,
    entries, kept, given, fields, ids, moments, owner, cells, rows, wide, tables, sem,
):
    cx, cz, cy = ids.shape[1:]
    arguments = [(fields_in, fields), (ids_in, ids), (moments_in, moments), (owner_in, owner)]
    arguments += [(cells_in, cells), (rows_in, rows)]
    arguments += [(t, tables.at[i]) for i, t in enumerate((buoyancy, lame_lambda, lame_mu))]
    copy_all(sem, arguments)
    for i in range(cells.shape[0]):
        at = 8 * i
        entries[at : at + 6] = moments[:, i * cy : (i + 1) * cy]
        entries[at + 6 : at + 7] = owner[i : i + 1, :].astype(F32)
        entries[at + 7 : at + 8] = cells[i : i + 1, :].astype(F32)
    wide[0] = (ids[0] + 1).astype(F32)
    line = in_line(rows[...])
    high = one_hot(line // cy, cx * cz).astype(BF16)
    low = one_hot(line % cy, cy).astype(BF16)
    count = lax.dot_general(high, low, NT, preferred_element_type=F32)
    wide[1] = count.reshape(cx, cz, cy)
    reach = reach_of(cz)
    lines = 11 * cx * reach
    lane = lax.broadcasted_iota(jnp.int32, (1, cy), 1)
    for i in range(3):
        found = jnp.zeros((1, cy), F32)
        for entry in range(tables.shape[1]):
            found = jnp.where(lane == entry + 1, F32(0.5) * tables[i, entry], found)
        kept[lines + i : lines + i + 1] = found
    kept[lines + 3 : lines + 8] = jnp.zeros((5, cy), F32)
    kept[lines + 8 :] = entries[...]

    def cut(first, other):
        for x in range(cx):
            at = slice(x * reach, (x + 1) * reach)
            for k in range(11):
                source = fields.at[0, k] if k < 9 else wide.at[k - 9]
                line = (k * cx + x) * reach
                kept[line : line + reach] = source[x, first : first + reach]
            given[0:9, at] = fields[0, :, x, other : other + reach]
            given[9, at] = wide[0, x, other : other + reach]

    @pl.when(lax.axis_index("segment") == 0)
    def _():
        cut(0, cz - reach)

    @pl.when(lax.axis_index("segment") == 1)
    def _():
        cut(cz - reach, 0)


def moments_of(layout, entries):
    cx, cz, cy = layout
    section = lax.axis_index("sec")
    half = cx * cz // 2
    chunk = [entries[8 * i : 8 * i + 8] for i in range(entries.shape[0] // 8)]
    entry = jnp.concatenate(chunk, axis=1)
    owner = entry[6:7].astype(jnp.int32)
    cell = entry[7:8].astype(jnp.int32)
    line = jnp.where(owner == section, cell // cy, -1)
    upper = line >= half
    high = one_hot(jnp.where(upper, line - half, line), half)
    low = one_hot(jnp.where(upper, cell % cy + cy, cell % cy), 2 * cy).astype(BF16)
    parts = split3(entry[0:6])
    spread = [(high * part[c : c + 1]).astype(BF16) for part in parts for c in range(6)]
    spread = jnp.concatenate(spread, axis=0)
    got = lax.dot_general(spread, low, NT, preferred_element_type=F32)
    lines = 6 * half
    return got[0:lines] + got[lines : 2 * lines] + got[2 * lines :]


def own_kernel(layout, kept, out, tables, acc):
    lines = out.shape[0] * out.shape[1]
    out[...] = kept[0:lines].reshape(out.shape)
    tables[...] = kept[lines : lines + 8]
    acc[...] = moments_of(layout, kept[lines + 8 :])


def more_kernel(layout, started, entries, acc):
    acc[...] = started[...] + moments_of(layout, entries[...])


def by_core(act):
    segment = lax.axis_index("segment")

    @pl.when(segment == 0)
    def _():
        act(0, lambda reach: slice(STEPS, STEPS + reach), lambda reach: slice(0, STEPS))

    @pl.when(segment == 1)
    def _():
        act(1, lambda reach: slice(0, reach), lambda reach: slice(reach, reach + STEPS))


def join_kernel(layout, *refs):
    cx, cz, cy = layout
    kept, got, started, entries, state, ids, times, edge, dense = refs
    reach = reach_of(cz)
    half = cx * cz // 2
    total = started[...] + moments_of(layout, entries[...])
    for c in range(6):
        for k in range(2):
            added = total[c * half : (c + 1) * half, k * cy : (k + 1) * cy]
            dense[c, k * half : (k + 1) * half] = added

    def join(mine, main, outer):
        main, outer = main(reach), outer(reach)
        first = 0 if mine == 0 else cz - reach
        last = main.start if mine == 0 else main.stop - STEPS
        gone = slice(last, last + STEPS)
        for x in range(cx):
            at = slice(x * reach, (x + 1) * reach)
            for model in range(2):
                rows = kept if model == mine else got
                state[model, :, x, main] = rows[0:9, at]
                ids[model, x, main] = rows[9, at]
            added = dense[:, x * cz + first : x * cz + first + reach]
            state[0, 3:9, x, main] = state[0, 3:9, x, main] + added
            times[x, main] = kept[10, at]
            state[:, :, x, outer] = jnp.zeros((2, 9, STEPS, cy), F32)
            ids[:, x, outer] = jnp.zeros((2, STEPS, cy), F32)
            times[x, outer] = jnp.zeros((STEPS, cy), F32)
            for k in range(21):
                line = slice((k * cx + x) * STEPS, (k * cx + x + 1) * STEPS)
                if k == 20:
                    edge[line] = times[x, gone]
                elif k % 10 == 9:
                    edge[line] = ids[k // 10, x, gone]
                else:
                    edge[line] = state[k // 10, k % 10, x, gone]

    by_core(join)


def by_parity(even, odd, act):
    parity = lax.axis_index("sec") % 2

    @pl.when(parity == 0)
    def _():
        act(*even)

    @pl.when(parity == 1)
    def _():
        act(*odd)


def advance(cx, steps, state, coef, times, given_top=False):
    planes, rows, cy = state.shape[2:]
    lane = lax.broadcasted_iota(jnp.int32, (rows, cy), 1)
    first_lane, last_lane = lane == 0, lane == cy - 1

    def back_y(f):
        return f - jnp.where(first_lane, F32(0.0), pltpu.roll(f, 1, 1))

    def back_z(f):
        return f - pltpu.roll(f, 1, 0)

    def fore_y(f):
        return jnp.where(last_lane, F32(0.0), pltpu.roll(f, cy - 1, 1)) - f

    def fore_z(f):
        return pltpu.roll(f, rows - 1, 0) - f

    def velocity(x):
        inc = [None, None]
        for model in range(2):
            sxx, syy, szz, syz, sxz, sxy = (state[model, 3 + k, x] for k in range(6))
            sxx_p, sxz_p, sxy_p = (state[model, k, x - 1] for k in (3, 7, 8))
            hb = coef[model, 0, x]
            inc[model] = (
                hb * ((sxx - sxx_p) + back_y(sxy) + back_z(sxz)),
                hb * ((sxy - sxy_p) + back_y(syy) + back_z(syz)),
                hb * ((sxz - sxz_p) + back_y(syz) + back_z(szz)),
            )
        for k in range(3):
            state[0, k, x] = state[0, k, x] + inc[0][k]
            state[1, k, x] = (state[1, k, x] + inc[1][k]) + times[x] * inc[0][k]

    for step in range(steps):
        left = steps - 1 - step
        low, high = cx - left, 2 * cx + left
        for x in range(low, high + 1 - (given_top and step == 0)):
            velocity(x)
        for x in range(low, high):
            for model in range(2):
                vx, vy, vz = (state[model, k, x] for k in range(3))
                vx_n, vy_n, vz_n = (state[model, k, x + 1] for k in range(3))
                hl, hm = coef[model, 1, x], coef[model, 2, x]
                exx, eyy, ezz = vx_n - vx, fore_y(vy), fore_z(vz)
                pressure = hl * (exx + eyy + ezz)
                twice = hm + hm
                state[model, 3, x] = state[model, 3, x] + (pressure + twice * exx)
                state[model, 4, x] = state[model, 4, x] + (pressure + twice * eyy)
                state[model, 5, x] = state[model, 5, x] + (pressure + twice * ezz)
                state[model, 6, x] = state[model, 6, x] + hm * (fore_z(vy) + fore_y(vz))
                state[model, 7, x] = state[model, 7, x] + hm * (fore_z(vx) + (vz_n - vz))
                state[model, 8, x] = state[model, 8, x] + hm * (fore_y(vx) + (vy_n - vy))

    return velocity


def look_up(tables, ids):
    lanes = ids.astype(jnp.int32)
    wide = [jnp.broadcast_to(tables[i : i + 1], ids.shape) for i in range(3)]
    return [jnp.take_along_axis(table, lanes, axis=1) for table in wide]


def edge_units(cx, with_ids):
    right, left = [], []
    for model in range(2):
        whole = list(range(10 if with_ids else 9)) + [10] * (with_ids and model == 1)
        for x in range(cx - 1):
            right += [(model, what, x + 1) for what in whole]
            left += [(model, what, x) for what in whole]
        right += [(model, what, 0) for what in (3, 7, 8)]
        left += [(model, what, cx - 1) for what in range(3)]
    return right, left


def cut_edges(cx, rows_of, with_ids, velocity, state, ids, times, to_first, to_second):
    right_units, left_units = edge_units(cx, with_ids)

    def put(to, units, far, right):
        line = slice(0, 0)
        for model, what, x in units if to is not None else ():
            at = rows_of(x == far, right)
            line = slice(line.stop, line.stop + at.stop - at.start)
            if what == 10:
                to[line] = times[cx + x, at]
            elif what == 9:
                to[line] = ids[model, cx + x, at]
            else:
                to[line] = state[model, what, cx + x, at]

    holders = (to_second, to_first), (to_first, to_second)
    by_parity(*holders, lambda left, right: put(right, right_units, 0, True))
    velocity(2 * cx - 1)
    by_parity(*holders, lambda left, right: put(left, left_units, cx - 1, False))


def arrived_kernel(edge, out):
    out[...] = edge[...]


def outer_rows(mine, outer):
    def rows_of(far, right):
        shift = 1 if far and not right and mine == 0 else 0
        return slice(outer.start + shift, outer.stop + shift)

    return rows_of


def reached_rows(cx, done, rows):
    def rows_of(far, right):
        first, last = done, rows - done
        if right:
            return slice(first + (cx if far else 1), last)
        return slice(first + far, last - (cx if far else 1))

    return rows_of


def coefficients(cx, planes, tables, ids, coef):
    for model in range(2):
        for x in planes:
            for i, found in enumerate(look_up(tables, ids[model, x])):
                coef[model, i, x] = found


def inner_kernel(cx, pairing, own_state, own_ids, own_times, tables, to, state, ids, coef, times):
    own = slice(cx, 2 * cx)
    reach = state.shape[3] - STEPS
    state[:, :, own], ids[:, own], times[own] = own_state[...], own_ids[...], own_times[...]
    coefficients(cx, range(2 * cx - 1, 2 * cx), tables, ids, coef)
    velocity = advance(cx, 0, state, coef, times)

    def cut(mine, main, outer):
        rows_of = lambda far, right: main(reach)
        both = (to, None) if pairing == 0 else (None, to)
        cut_edges(cx, rows_of, True, velocity, state, ids, times, *both)

    by_core(cut)


def outer_kernel(
    cx, own_state, own_ids, own_times, halo, tables,
    to_first, to_second, both, coef_out, times_out, state, ids, coef, times,
):
    own = slice(cx, 2 * cx)
    reach = state.shape[3] - STEPS
    state[:, :, own], ids[:, own], times[own] = own_state[...], own_ids[...], own_times[...]

    slab = lax.axis_index("depth")

    def join(mine, main, outer):
        inside = slab > 0 if mine == 0 else slab < lax.axis_size("depth") - 1
        inside = jnp.where(inside, F32(1.0), F32(0.0))
        for x in range(cx):
            for k in range(21):
                line = inside * halo[(k * cx + x) * STEPS : (k * cx + x + 1) * STEPS]
                if k == 20:
                    times[cx + x, outer(reach)] = line
                elif k % 10 == 9:
                    ids[k // 10, cx + x, outer(reach)] = line
                else:
                    state[k // 10, k % 10, cx + x, outer(reach)] = line

    by_core(join)
    coefficients(cx, range(cx, 2 * cx), tables, ids, coef)
    both[...] = state[:, :, own]
    coef_out[...] = coef[:, :, own]
    times_out[...] = times[own]
    velocity = advance(cx, 0, state, coef, times)

    def cut(mine, main, outer):
        rows_of = outer_rows(mine, outer(reach))
        cut_edges(cx, rows_of, True, velocity, state, ids, times, to_first, to_second)

    by_core(cut)


def next_kernel(cx, done, *refs):
    first = done == 0
    parts = 2 if first else 1
    both_in, coef_in, times_in = refs[0:3]
    edges, refs = refs[3 : 3 + 2 * parts], refs[3 + 2 * parts :]
    if first:
        tables, outs = refs[0], refs[1:]
        state, ids, coef, times = refs[-4:]
    else:
        ids, outs = None, refs
        state, coef, times = refs[-1], coef_in, times_in
    segment = lax.axis_index("segment")
    rows = state.shape[3]
    own = slice(cx, 2 * cx)
    state[:, :, own] = both_in[...]
    right_units, left_units = edge_units(cx, first)

    section = lax.axis_index("sec")
    has_left = jnp.where(section > 0, F32(1.0), F32(0.0))
    has_right = jnp.where(section < lax.axis_size("sec") - 1, F32(1.0), F32(0.0))

    def get(edge, units, start, rows_of, far, right):
        inside = has_left if right else has_right
        last = 0
        for model, what, x in units:
            at = rows_of(x == far, right)
            first, last = last, last + at.stop - at.start
            line = inside * edge[first:last]
            if what == 10:
                times[start + x, at] = line
            elif what == 9:
                ids[model, start + x, at] = line
            else:
                state[model, what, start + x, at] = line

    def place(rows_of, pair):
        def put(left, right):
            get(left, right_units, 0, rows_of, 0, True)
            get(right, left_units, 2 * cx, rows_of, cx - 1, False)

        by_parity((pair[1], pair[0]), pair, put)

    if first:

        def place_both(mine, main, outer):
            reach = rows - STEPS
            place(lambda far, right: main(reach), edges[0:2])
            place(outer_rows(mine, outer(reach)), edges[2:4])

        by_core(place_both)
        coef[:, :, own] = coef_in[...]
        times[own] = times_in[...]
        coefficients(cx, (*range(1, cx), *range(2 * cx, 3 * cx - 1)), tables, ids, coef)
    else:
        place(reached_rows(cx, done, rows), edges)
    velocity = advance(cx, cx, state, coef, times, given_top=True)
    if done + cx == STEPS:
        outs[0][...] = state[segment, :, own, STEPS : rows - STEPS]
        outs[1][...] = state[1 - segment, :, own, STEPS : rows - STEPS]
    else:
        outs[2][...] = state[:, :, own]
        if first:
            outs[3][...] = coef[...]
            outs[4][...] = times[...]
        rows_of = reached_rows(cx, done + cx, rows)
        cut_edges(cx, rows_of, False, velocity, state, None, times, outs[0], outs[1])


def home_kernel(mine, brought, out):
    half = mine.shape[2]
    segment = lax.axis_index("segment")

    @pl.when(segment == 0)
    def _():
        out[0, :, :, 0:half] = mine[...]
        out[0, :, :, half:] = brought[...]

    @pl.when(segment == 1)
    def _():
        out[0, :, :, half:] = mine[...]
        out[0, :, :, 0:half] = brought[...]


def swaps(start, count):
    route = {i: i for i in range(count)}
    for i in range(start, count - 1, 2):
        route[i], route[i + 1] = i + 1, i
    return list(route.items())


VMEM = pl.BlockSpec(memory_space=pltpu.VMEM)
HBM = pl.BlockSpec(memory_space=pltpu.HBM)


def call(kernel, name, in_vmem, in_hbm, outs, scratch, copies=0, limit=40 * 2**20, flops=10**7):
    sems = [pltpu.SemaphoreType.DMA((copies,))] * (copies > 0)
    return pl.pallas_call(
        kernel,
        out_shape=[jax.ShapeDtypeStruct(shape, F32) for shape in outs],
        in_specs=[VMEM] * len(in_vmem) + [HBM] * len(in_hbm),
        out_specs=[VMEM] * len(outs),
        scratch_shapes=[pltpu.VMEM(s, F32) if isinstance(s, tuple) else s for s in scratch] + sems,
        compiler_params=pltpu.CompilerParams(vmem_limit_bytes=limit),
        cost_estimate=pl.CostEstimate(flops=flops, bytes_accessed=2**20, transcendentals=0),
        name=name,
    )(*in_vmem, *in_hbm)


def on_device(
    fields, block_ids, buoyancy, lame_lambda, lame_mu, moments, moment_owner, moment_cells, drm_rows
):
    sections, slabs = lax.axis_size("sec"), lax.axis_size("depth")
    layout = cx, cz, cy = fields.shape[2:]
    reach, rows = reach_of(cz), cz // 2 + 2 * STEPS
    assert cx > 1 and STEPS % cx == 0

    def pairs(block, start):
        route = []
        for i, j in swaps(start, sections):
            route += [(2 * i + k, 2 * j + (k if i != j else 1 - k)) for k in range(2)]
        return lax.ppermute(block, ("sec", "segment"), route)

    def other(section, k):
        return section ^ k if sections & (sections - 1) == 0 else (section + k) % sections

    def along_depth(block):
        line = 2 * slabs
        route = []
        for s, partner in swaps(0, sections):
            route += [(s * line + i, (s if i != j else partner) * line + j) for i, j in swaps(1, line)]
        return lax.ppermute(block, ("sec", "depth", "segment"), route)

    def swap(block):
        return lax.ppermute(block, "segment", [(0, 1), (1, 0)])

    owner = moment_owner.reshape(-1, cy)
    cells = moment_cells.reshape(-1, cy)
    arguments = (fields, block_ids, moments, owner, cells, drm_rows.reshape(-1, cy))
    entry_lines = 8 * cells.shape[0]
    entries, kept, given = call(
        pack_kernel,
        "pack",
        (),
        (*arguments, buoyancy, lame_lambda, lame_mu),
        [(entry_lines, cy), (11 * cx * reach + 8 + entry_lines, cy), (10, cx * reach, cy)],
        [pltpu.VMEM(a.shape, a.dtype) for a in arguments]
        + [(2, cx, cz, cy), pltpu.SMEM((3, buoyancy.shape[0]), F32)],
        len(arguments) + 3,
        limit=64 * 2**20,
    )
    blocks = [
        lax.ppermute(entries, "sec", [(other(i, k), i) for i in range(sections)])
        for k in (sections - 1, *range(1, sections - 1))
    ]
    got = swap(given)
    acc_shape = (6 * cx * cz // 2, 2 * cy)
    kept, tables, started = call(
        functools.partial(own_kernel, layout),
        "own_moments",
        (kept,),
        (),
        [(11, cx * reach, cy), (8, cy), acc_shape],
        [],
        flops=10**8,
    )
    for block in blocks[:-1]:
        (started,) = call(
            functools.partial(more_kernel, layout),
            "more_moments",
            (started, block),
            (),
            [acc_shape],
            [],
            flops=6 * 10**9,
        )
    own = (cx, rows, cy)
    window = (3 * cx, rows, cy)
    state, ids, times, edge = call(
        functools.partial(join_kernel, layout),
        "join_and_moments",
        (kept, got, started, blocks[-1]),
        (),
        [(2, 9, *own), (2, *own), own, (21 * cx * STEPS, cy)],
        [(6, cx * cz, cy)],
    )
    halo = along_depth(edge)
    work = [(2, 9, *window), (2, *window), (2, 3, *window), window]

    def edges(count, with_ids):
        return [(len(edge_units(cx, with_ids)[0]) * count, cy)] * 2

    def reached_edges(done):
        rows_of = reached_rows(cx, done, rows)
        whole, far = rows_of(False, True), rows_of(True, True)
        lines = 18 * (cx - 1) * (whole.stop - whole.start) + 6 * (far.stop - far.start)
        return [(-(-lines // 8) * 8, cy)] * 2

    def exchange(pair):
        return [pairs(pair[0], 0), pairs(pair[1], 1)]

    got_edges = []
    for pairing, flops in enumerate((10**7, 10**7)):
        (inner,) = call(
            functools.partial(inner_kernel, cx, pairing),
            "inner_edges",
            (state, ids, times, tables),
            (),
            edges(reach, True)[0:1],
            work,
            flops=flops,
        )
        got_edges.append(pairs(inner, pairing))
    (got_edges[0],) = call(
        arrived_kernel, "arrived", got_edges[0:1], (), edges(reach, True)[0:1], [], flops=10**10
    )
    *outer, both, coef, times = call(
        functools.partial(outer_kernel, cx),
        "outer_edges",
        (state, ids, times, halo, tables),
        (),
        edges(STEPS, True) + [(2, 9, *own), (2, 3, *own), own],
        work,
        flops=10**8,
    )
    got_edges += exchange(outer)
    for done in range(0, STEPS, cx):
        first, last = done == 0, done + cx == STEPS
        after = done + cx
        outs = [(9, cx, cz // 2, cy)] * 2
        if not last:
            outs = reached_edges(after) + [(2, 9, *own)]
            outs += [(2, 3, *window), window] * first
        pair = call(
            functools.partial(next_kernel, cx, done),
            "steps",
            (both, coef, times, *got_edges) + (tables,) * first,
            (),
            outs,
            work if first else work[0:1],
        )
        if not last:
            got_edges = exchange(pair[0:2])
            both = pair[2]
            if first:
                coef, times = pair[3:5]
    to_first, to_second = pair[0:2]
    (out,) = call(home_kernel, "home", (to_first, swap(to_second)), (), [fields.shape], [])
    return out


def solution(mesh):
    in_specs = (
        P("segment", None, "sec", "depth", None),
        P("segment", "sec", "depth", None),
        P(),
        P(),
        P(),
        P(None, ("sec", "depth")),
        P(("sec", "depth"), None),
        P(("sec", "depth")),
        P(("sec", "depth")),
    )
    out_specs = P("segment", None, "sec", "depth", None)
    return jax.shard_map(
        on_device, mesh=mesh, in_specs=in_specs, out_specs=out_specs, check_vma=False
    )
```

```python
import functools

import jax
import jax.numpy as jnp
from jax import lax
from jax.experimental import pallas as pl
from jax.experimental.pallas import tpu as pltpu
from jax.sharding import PartitionSpec as P

STEPS = 4
F32 = jnp.float32
BF16 = jnp.bfloat16
NT = (((1,), (1,)), ((), ()))


def one_hot(index, count):
    rows = lax.broadcasted_iota(jnp.int32, (count, index.shape[-1]), 0)
    return jnp.where(rows == index, F32(1.0), F32(0.0))


def split3(value):
    high = value.astype(BF16).astype(F32)
    rest = value - high
    mid = rest.astype(BF16).astype(F32)
    return high, mid, rest - mid


def copy_all(sem, pairs):
    copies = [pltpu.make_async_copy(a, b, sem.at[i]) for i, (a, b) in enumerate(pairs)]
    for copy in copies:
        copy.start()
    for copy in copies:
        copy.wait()


def in_line(rows):
    return jnp.concatenate([rows[i : i + 1, :] for i in range(rows.shape[0])], axis=1)


def reach_of(cz):
    return cz // 2 + STEPS


def pack_kernel(
    fields_in, ids_in, moments_in, owner_in, cells_in, rows_in, buoyancy, lame_lambda, lame_mu,
    entries, kept, given, fields, ids, moments, owner, cells, rows, wide, tables, sem,
):
    cx, cz, cy = ids.shape[1:]
    arguments = [(fields_in, fields), (ids_in, ids), (moments_in, moments), (owner_in, owner)]
    arguments += [(cells_in, cells), (rows_in, rows)]
    arguments += [(t, tables.at[i]) for i, t in enumerate((buoyancy, lame_lambda, lame_mu))]
    copy_all(sem, arguments)
    for i in range(cells.shape[0]):
        at = 8 * i
        entries[at : at + 6] = moments[:, i * cy : (i + 1) * cy]
        entries[at + 6 : at + 7] = owner[i : i + 1, :].astype(F32)
        entries[at + 7 : at + 8] = cells[i : i + 1, :].astype(F32)
    wide[0] = (ids[0] + 1).astype(F32)
    line = in_line(rows[...])
    high = one_hot(line // cy, cx * cz).astype(BF16)
    low = one_hot(line % cy, cy).astype(BF16)
    count = lax.dot_general(high, low, NT, preferred_element_type=F32)
    wide[1] = count.reshape(cx, cz, cy)
    reach = reach_of(cz)
    lines = 11 * cx * reach
    lane = lax.broadcasted_iota(jnp.int32, (1, cy), 1)
    for i in range(3):
        found = jnp.zeros((1, cy), F32)
        for entry in range(tables.shape[1]):
            found = jnp.where(lane == entry + 1, F32(0.5) * tables[i, entry], found)
        kept[lines + i : lines + i + 1] = found
    kept[lines + 3 : lines + 8] = jnp.zeros((5, cy), F32)
    kept[lines + 8 :] = entries[...]

    def cut(first, other):
        for x in range(cx):
            at = slice(x * reach, (x + 1) * reach)
            for k in range(11):
                source = fields.at[0, k] if k < 9 else wide.at[k - 9]
                line = (k * cx + x) * reach
                kept[line : line + reach] = source[x, first : first + reach]
            given[0:9, at] = fields[0, :, x, other : other + reach]
            given[9, at] = wide[0, x, other : other + reach]

    @pl.when(lax.axis_index("segment") == 0)
    def _():
        cut(0, cz - reach)

    @pl.when(lax.axis_index("segment") == 1)
    def _():
        cut(cz - reach, 0)


def moments_of(layout, entries):
    cx, cz, cy = layout
    section = lax.axis_index("sec")
    half = cx * cz // 2
    chunk = [entries[8 * i : 8 * i + 8] for i in range(entries.shape[0] // 8)]
    entry = jnp.concatenate(chunk, axis=1)
    owner = entry[6:7].astype(jnp.int32)
    cell = entry[7:8].astype(jnp.int32)
    line = jnp.where(owner == section, cell // cy, -1)
    upper = line >= half
    high = one_hot(jnp.where(upper, line - half, line), half)
    low = one_hot(jnp.where(upper, cell % cy + cy, cell % cy), 2 * cy).astype(BF16)
    parts = split3(entry[0:6])
    spread = [(high * part[c : c + 1]).astype(BF16) for part in parts for c in range(6)]
    spread = jnp.concatenate(spread, axis=0)
    got = lax.dot_general(spread, low, NT, preferred_element_type=F32)
    lines = 6 * half
    return got[0:lines] + got[lines : 2 * lines] + got[2 * lines :]


def own_kernel(layout, kept, out, tables, acc):
    lines = out.shape[0] * out.shape[1]
    out[...] = kept[0:lines].reshape(out.shape)
    tables[...] = kept[lines : lines + 8]
    acc[...] = moments_of(layout, kept[lines + 8 :])


def more_kernel(layout, started, entries, acc):
    acc[...] = started[...] + moments_of(layout, entries[...])


def by_core(act):
    segment = lax.axis_index("segment")

    @pl.when(segment == 0)
    def _():
        act(0, lambda reach: slice(STEPS, STEPS + reach), lambda reach: slice(0, STEPS))

    @pl.when(segment == 1)
    def _():
        act(1, lambda reach: slice(0, reach), lambda reach: slice(reach, reach + STEPS))


def join_kernel(layout, *refs):
    cx, cz, cy = layout
    kept, got, started, entries, state, ids, times, edge, dense = refs
    reach = reach_of(cz)
    half = cx * cz // 2
    total = started[...] + moments_of(layout, entries[...])
    for c in range(6):
        for k in range(2):
            added = total[c * half : (c + 1) * half, k * cy : (k + 1) * cy]
            dense[c, k * half : (k + 1) * half] = added

    def join(mine, main, outer):
        main, outer = main(reach), outer(reach)
        first = 0 if mine == 0 else cz - reach
        last = main.start if mine == 0 else main.stop - STEPS
        gone = slice(last, last + STEPS)
        for x in range(cx):
            at = slice(x * reach, (x + 1) * reach)
            for model in range(2):
                rows = kept if model == mine else got
                state[model, :, x, main] = rows[0:9, at]
                ids[model, x, main] = rows[9, at]
            added = dense[:, x * cz + first : x * cz + first + reach]
            state[0, 3:9, x, main] = state[0, 3:9, x, main] + added
            times[x, main] = kept[10, at]
            state[:, :, x, outer] = jnp.zeros((2, 9, STEPS, cy), F32)
            ids[:, x, outer] = jnp.zeros((2, STEPS, cy), F32)
            times[x, outer] = jnp.zeros((STEPS, cy), F32)
            for k in range(21):
                line = slice((k * cx + x) * STEPS, (k * cx + x + 1) * STEPS)
                if k == 20:
                    edge[line] = times[x, gone]
                elif k % 10 == 9:
                    edge[line] = ids[k // 10, x, gone]
                else:
                    edge[line] = state[k // 10, k % 10, x, gone]

    by_core(join)


def by_parity(even, odd, act):
    parity = lax.axis_index("sec") % 2

    @pl.when(parity == 0)
    def _():
        act(*even)

    @pl.when(parity == 1)
    def _():
        act(*odd)


def advance(cx, steps, state, coef, times, given_top=False):
    planes, rows, cy = state.shape[2:]
    lane = lax.broadcasted_iota(jnp.int32, (rows, cy), 1)
    first_lane, last_lane = lane == 0, lane == cy - 1

    def back_y(f):
        return f - jnp.where(first_lane, F32(0.0), pltpu.roll(f, 1, 1))

    def back_z(f):
        return f - pltpu.roll(f, 1, 0)

    def fore_y(f):
        return jnp.where(last_lane, F32(0.0), pltpu.roll(f, cy - 1, 1)) - f

    def fore_z(f):
        return pltpu.roll(f, rows - 1, 0) - f

    def velocity(x):
        inc = [None, None]
        for model in range(2):
            sxx, syy, szz, syz, sxz, sxy = (state[model, 3 + k, x] for k in range(6))
            sxx_p, sxz_p, sxy_p = (state[model, k, x - 1] for k in (3, 7, 8))
            hb = coef[model, 0, x]
            inc[model] = (
                hb * ((sxx - sxx_p) + back_y(sxy) + back_z(sxz)),
                hb * ((sxy - sxy_p) + back_y(syy) + back_z(syz)),
                hb * ((sxz - sxz_p) + back_y(syz) + back_z(szz)),
            )
        for k in range(3):
            state[0, k, x] = state[0, k, x] + inc[0][k]
            state[1, k, x] = (state[1, k, x] + inc[1][k]) + times[x] * inc[0][k]

    for step in range(steps):
        left = steps - 1 - step
        low, high = cx - left, 2 * cx + left
        for x in range(low, high + 1 - (given_top and step == 0)):
            velocity(x)
        for x in range(low, high):
            for model in range(2):
                vx, vy, vz = (state[model, k, x] for k in range(3))
                vx_n, vy_n, vz_n = (state[model, k, x + 1] for k in range(3))
                hl, hm = coef[model, 1, x], coef[model, 2, x]
                exx, eyy, ezz = vx_n - vx, fore_y(vy), fore_z(vz)
                pressure = hl * (exx + eyy + ezz)
                twice = hm + hm
                state[model, 3, x] = state[model, 3, x] + (pressure + twice * exx)
                state[model, 4, x] = state[model, 4, x] + (pressure + twice * eyy)
                state[model, 5, x] = state[model, 5, x] + (pressure + twice * ezz)
                state[model, 6, x] = state[model, 6, x] + hm * (fore_z(vy) + fore_y(vz))
                state[model, 7, x] = state[model, 7, x] + hm * (fore_z(vx) + (vz_n - vz))
                state[model, 8, x] = state[model, 8, x] + hm * (fore_y(vx) + (vy_n - vy))

    return velocity


def look_up(tables, ids):
    lanes = ids.astype(jnp.int32)
    wide = [jnp.broadcast_to(tables[i : i + 1], ids.shape) for i in range(3)]
    return [jnp.take_along_axis(table, lanes, axis=1) for table in wide]


def edge_units(cx, with_ids):
    right, left = [], []
    for model in range(2):
        whole = list(range(10 if with_ids else 9)) + [10] * (with_ids and model == 1)
        for x in range(cx - 1):
            right += [(model, what, x + 1) for what in whole]
            left += [(model, what, x) for what in whole]
        right += [(model, what, 0) for what in (3, 7, 8)]
        left += [(model, what, cx - 1) for what in range(3)]
    return right, left


def cut_edges(cx, rows_of, with_ids, velocity, state, ids, times, to_first, to_second):
    right_units, left_units = edge_units(cx, with_ids)

    def put(to, units, far, right):
        line = slice(0, 0)
        for model, what, x in units:
            at = rows_of(x == far, right)
            line = slice(line.stop, line.stop + at.stop - at.start)
            if what == 10:
                to[line] = times[cx + x, at]
            elif what == 9:
                to[line] = ids[model, cx + x, at]
            else:
                to[line] = state[model, what, cx + x, at]

    holders = (to_second, to_first), (to_first, to_second)
    by_parity(*holders, lambda left, right: put(right, right_units, 0, True))
    velocity(2 * cx - 1)
    by_parity(*holders, lambda left, right: put(left, left_units, cx - 1, False))


def outer_rows(mine, outer):
    def rows_of(far, right):
        shift = 1 if far and not right and mine == 0 else 0
        return slice(outer.start + shift, outer.stop + shift)

    return rows_of


def reached_rows(cx, done, rows):
    def rows_of(far, right):
        first, last = done, rows - done
        if right:
            return slice(first + (cx if far else 1), last)
        return slice(first + far, last - (cx if far else 1))

    return rows_of


def coefficients(cx, planes, tables, ids, coef):
    for model in range(2):
        for x in planes:
            for i, found in enumerate(look_up(tables, ids[model, x])):
                coef[model, i, x] = found


def inner_kernel(cx, own_state, own_ids, own_times, tables, to_first, to_second, state, ids, coef, times):
    own = slice(cx, 2 * cx)
    reach = state.shape[3] - STEPS
    state[:, :, own], ids[:, own], times[own] = own_state[...], own_ids[...], own_times[...]
    coefficients(cx, range(2 * cx - 1, 2 * cx), tables, ids, coef)
    velocity = advance(cx, 0, state, coef, times)

    def cut(mine, main, outer):
        rows_of = lambda far, right: main(reach)
        cut_edges(cx, rows_of, True, velocity, state, ids, times, to_first, to_second)

    by_core(cut)


def outer_kernel(
    cx, own_state, own_ids, own_times, halo, tables,
    to_first, to_second, both, coef_out, times_out, state, ids, coef, times,
):
    own = slice(cx, 2 * cx)
    reach = state.shape[3] - STEPS
    state[:, :, own], ids[:, own], times[own] = own_state[...], own_ids[...], own_times[...]

    slab = lax.axis_index("depth")

    def join(mine, main, outer):
        inside = slab > 0 if mine == 0 else slab < lax.axis_size("depth") - 1
        inside = jnp.where(inside, F32(1.0), F32(0.0))
        for x in range(cx):
            for k in range(21):
                line = inside * halo[(k * cx + x) * STEPS : (k * cx + x + 1) * STEPS]
                if k == 20:
                    times[cx + x, outer(reach)] = line
                elif k % 10 == 9:
                    ids[k // 10, cx + x, outer(reach)] = line
                else:
                    state[k // 10, k % 10, cx + x, outer(reach)] = line

    by_core(join)
    coefficients(cx, range(cx, 2 * cx), tables, ids, coef)
    both[...] = state[:, :, own]
    coef_out[...] = coef[:, :, own]
    times_out[...] = times[own]
    velocity = advance(cx, 0, state, coef, times)

    def cut(mine, main, outer):
        rows_of = outer_rows(mine, outer(reach))
        cut_edges(cx, rows_of, True, velocity, state, ids, times, to_first, to_second)

    by_core(cut)


def next_kernel(cx, done, *refs):
    first = done == 0
    parts = 2 if first else 1
    both_in, coef_in, times_in = refs[0:3]
    edges, refs = refs[3 : 3 + 2 * parts], refs[3 + 2 * parts :]
    if first:
        tables, outs = refs[0], refs[1:]
        state, ids, coef, times = refs[-4:]
    else:
        ids, outs = None, refs
        state, coef, times = refs[-1], coef_in, times_in
    segment = lax.axis_index("segment")
    rows = state.shape[3]
    own = slice(cx, 2 * cx)
    state[:, :, own] = both_in[...]
    right_units, left_units = edge_units(cx, first)

    section = lax.axis_index("sec")
    has_left = jnp.where(section > 0, F32(1.0), F32(0.0))
    has_right = jnp.where(section < lax.axis_size("sec") - 1, F32(1.0), F32(0.0))

    def get(edge, units, start, rows_of, far, right):
        inside = has_left if right else has_right
        last = 0
        for model, what, x in units:
            at = rows_of(x == far, right)
            first, last = last, last + at.stop - at.start
            line = inside * edge[first:last]
            if what == 10:
                times[start + x, at] = line
            elif what == 9:
                ids[model, start + x, at] = line
            else:
                state[model, what, start + x, at] = line

    def place(rows_of, pair):
        def put(left, right):
            get(left, right_units, 0, rows_of, 0, True)
            get(right, left_units, 2 * cx, rows_of, cx - 1, False)

        by_parity((pair[1], pair[0]), pair, put)

    if first:

        def place_both(mine, main, outer):
            reach = rows - STEPS
            place(lambda far, right: main(reach), edges[0:2])
            place(outer_rows(mine, outer(reach)), edges[2:4])

        by_core(place_both)
        coef[:, :, own] = coef_in[...]
        times[own] = times_in[...]
        coefficients(cx, (*range(1, cx), *range(2 * cx, 3 * cx - 1)), tables, ids, coef)
    else:
        place(reached_rows(cx, done, rows), edges)
    velocity = advance(cx, cx, state, coef, times, given_top=True)
    if done + cx == STEPS:
        outs[0][...] = state[segment, :, own, STEPS : rows - STEPS]
        outs[1][...] = state[1 - segment, :, own, STEPS : rows - STEPS]
    else:
        outs[2][...] = state[:, :, own]
        if first:
            outs[3][...] = coef[...]
            outs[4][...] = times[...]
        rows_of = reached_rows(cx, done + cx, rows)
        cut_edges(cx, rows_of, False, velocity, state, None, times, outs[0], outs[1])


def home_kernel(mine, brought, out):
    half = mine.shape[2]
    segment = lax.axis_index("segment")

    @pl.when(segment == 0)
    def _():
        out[0, :, :, 0:half] = mine[...]
        out[0, :, :, half:] = brought[...]

    @pl.when(segment == 1)
    def _():
        out[0, :, :, half:] = mine[...]
        out[0, :, :, 0:half] = brought[...]


def swaps(start, count):
    route = {i: i for i in range(count)}
    for i in range(start, count - 1, 2):
        route[i], route[i + 1] = i + 1, i
    return list(route.items())


VMEM = pl.BlockSpec(memory_space=pltpu.VMEM)
HBM = pl.BlockSpec(memory_space=pltpu.HBM)


def call(kernel, name, in_vmem, in_hbm, outs, scratch, copies=0, limit=40 * 2**20, flops=10**7):
    sems = [pltpu.SemaphoreType.DMA((copies,))] * (copies > 0)
    return pl.pallas_call(
        kernel,
        out_shape=[jax.ShapeDtypeStruct(shape, F32) for shape in outs],
        in_specs=[VMEM] * len(in_vmem) + [HBM] * len(in_hbm),
        out_specs=[VMEM] * len(outs),
        scratch_shapes=[pltpu.VMEM(s, F32) if isinstance(s, tuple) else s for s in scratch] + sems,
        compiler_params=pltpu.CompilerParams(vmem_limit_bytes=limit),
        cost_estimate=pl.CostEstimate(flops=flops, bytes_accessed=2**20, transcendentals=0),
        name=name,
    )(*in_vmem, *in_hbm)


def on_device(
    fields, block_ids, buoyancy, lame_lambda, lame_mu, moments, moment_owner, moment_cells, drm_rows
):
    sections, slabs = lax.axis_size("sec"), lax.axis_size("depth")
    layout = cx, cz, cy = fields.shape[2:]
    reach, rows = reach_of(cz), cz // 2 + 2 * STEPS
    assert cx > 1 and STEPS % cx == 0

    def pairs(block, start):
        route = []
        for i, j in swaps(start, sections):
            route += [(2 * i + k, 2 * j + (k if i != j else 1 - k)) for k in range(2)]
        return lax.ppermute(block, ("sec", "segment"), route)

    def other(section, k):
        return section ^ k if sections & (sections - 1) == 0 else (section + k) % sections

    def along_depth(block):
        line = 2 * slabs
        route = []
        for s, partner in swaps(0, sections):
            route += [(s * line + i, (s if i != j else partner) * line + j) for i, j in swaps(1, line)]
        return lax.ppermute(block, ("sec", "depth", "segment"), route)

    def swap(block):
        return lax.ppermute(block, "segment", [(0, 1), (1, 0)])

    owner = moment_owner.reshape(-1, cy)
    cells = moment_cells.reshape(-1, cy)
    arguments = (fields, block_ids, moments, owner, cells, drm_rows.reshape(-1, cy))
    entry_lines = 8 * cells.shape[0]
    entries, kept, given = call(
        pack_kernel,
        "pack",
        (),
        (*arguments, buoyancy, lame_lambda, lame_mu),
        [(entry_lines, cy), (11 * cx * reach + 8 + entry_lines, cy), (10, cx * reach, cy)],
        [pltpu.VMEM(a.shape, a.dtype) for a in arguments]
        + [(2, cx, cz, cy), pltpu.SMEM((3, buoyancy.shape[0]), F32)],
        len(arguments) + 3,
        limit=64 * 2**20,
    )
    blocks = [
        lax.ppermute(entries, "sec", [(other(i, k), i) for i in range(sections)])
        for k in dict.fromkeys((*range(2, sections - 1), 1, sections - 1))
    ]
    got = swap(given)
    acc_shape = (6 * cx * cz // 2, 2 * cy)
    kept, tables, started = call(
        functools.partial(own_kernel, layout),
        "own_moments",
        (kept,),
        (),
        [(11, cx * reach, cy), (8, cy), acc_shape],
        [],
        flops=10**8,
    )
    for block in blocks[:-1]:
        (started,) = call(
            functools.partial(more_kernel, layout),
            "more_moments",
            (started, block),
            (),
            [acc_shape],
            [],
            flops=6 * 10**9,
        )
    own = (cx, rows, cy)
    window = (3 * cx, rows, cy)
    state, ids, times, edge = call(
        functools.partial(join_kernel, layout),
        "join_and_moments",
        (kept, got, started, blocks[-1]),
        (),
        [(2, 9, *own), (2, *own), own, (21 * cx * STEPS, cy)],
        [(6, cx * cz, cy)],
    )
    halo = along_depth(edge)
    work = [(2, 9, *window), (2, *window), (2, 3, *window), window]

    def edges(count, with_ids):
        return [(len(edge_units(cx, with_ids)[0]) * count, cy)] * 2

    def reached_edges(done):
        rows_of = reached_rows(cx, done, rows)
        whole, far = rows_of(False, True), rows_of(True, True)
        lines = 18 * (cx - 1) * (whole.stop - whole.start) + 6 * (far.stop - far.start)
        return [(-(-lines // 8) * 8, cy)] * 2

    def exchange(pair):
        return [pairs(pair[0], 0), pairs(pair[1], 1)]

    inner = call(
        functools.partial(inner_kernel, cx),
        "inner_edges",
        (state, ids, times, tables),
        (),
        edges(reach, True),
        work,
        flops=10**9,
    )
    got_edges = exchange(inner)
    *outer, both, coef, times = call(
        functools.partial(outer_kernel, cx),
        "outer_edges",
        (state, ids, times, halo, tables),
        (),
        edges(STEPS, True) + [(2, 9, *own), (2, 3, *own), own],
        work,
        flops=4 * 10**9,
    )
    got_edges += exchange(outer)
    for done in range(0, STEPS, cx):
        first, last = done == 0, done + cx == STEPS
        after = done + cx
        outs = [(9, cx, cz // 2, cy)] * 2
        if not last:
            outs = reached_edges(after) + [(2, 9, *own)]
            outs += [(2, 3, *window), window] * first
        pair = call(
            functools.partial(next_kernel, cx, done),
            "steps",
            (both, coef, times, *got_edges) + (tables,) * first,
            (),
            outs,
            work if first else work[0:1],
        )
        if not last:
            got_edges = exchange(pair[0:2])
            both = pair[2]
            if first:
                coef, times = pair[3:5]
    to_first, to_second = pair[0:2]
    (out,) = call(home_kernel, "home", (to_first, swap(to_second)), (), [fields.shape], [])
    return out


def solution(mesh):
    in_specs = (
        P("segment", None, "sec", "depth", None),
        P("segment", "sec", "depth", None),
        P(),
        P(),
        P(),
        P(None, ("sec", "depth")),
        P(("sec", "depth"), None),
        P(("sec", "depth")),
        P(("sec", "depth")),
    )
    out_specs = P("segment", None, "sec", "depth", None)
    return jax.shard_map(
        on_device, mesh=mesh, in_specs=in_specs, out_specs=out_specs, check_vma=False
    )
```
